32 devices in a mesh: seq: 4 (over x, core), fsdp: 8 (over z, y).
Axes of the slice: x: 2, y: 2, z: 4, core: 2. Of those that a mesh axis runs over, the one named last changes fastest.
Arguments:
- inputs: bfloat16 [16, 1568, 1024], P('fsdp', 'seq'), may hold values from -7 to 7
- cotangent: bfloat16 [16, 1568, 1024], P('fsdp', 'seq'), may hold values from -6 to 6
- valid: int32 [16, 1568], P('fsdp'), may hold values from 0 to 1, as said below
- ln1_gain: bfloat16 [1024], P('fsdp'), may hold values from 0.25 to 1.75
- ln1_bias: bfloat16 [1024], P('fsdp'), may hold values from -1.75 to 1.75
- qkv_weight: bfloat16 [1024, 3072], P('fsdp'), may hold values from -0.1875 to 0.1875
- q_bias: bfloat16 [1024], P('fsdp'), may hold values from -3 to 3
- v_bias: bfloat16 [1024], P('fsdp'), may hold values from -0.3125 to 0.3125
- out_weight: bfloat16 [1024, 1024], P('fsdp'), may hold values from -2 to 2
- out_bias: bfloat16 [1024], P('fsdp'), may hold values from -1.75 to 1.75
- ln2_gain: bfloat16 [1024], P('fsdp'), may hold values from 0.25 to 1.75
- ln2_bias: bfloat16 [1024], P('fsdp'), may hold values from -1.75 to 1.75
- fc1_weight: bfloat16 [1024, 4096], P('fsdp'), may hold values from -0.1875 to 0.1875
- fc1_bias: bfloat16 [4096], P('fsdp'), may hold values from -1.75 to 1.75
- fc2_weight: bfloat16 [4096, 1024], P('fsdp'), may hold values from -0.09375 to 0.09375
- fc2_bias: bfloat16 [1024], P('fsdp'), may hold values from -1.75 to 1.75
Outputs:
- output: bfloat16 [16, 1568, 1024], P('fsdp', 'seq')
- input_grad: bfloat16 [16, 1568, 1024], P('fsdp', 'seq')
- ln1_gain_grad: float32 [1024], P('fsdp')
- ln1_bias_grad: float32 [1024], P('fsdp')
- qkv_weight_grad: float32 [1024, 3072], P('fsdp')
- q_bias_grad: float32 [1024], P('fsdp')
- v_bias_grad: float32 [1024], P('fsdp')
- out_weight_grad: float32 [1024, 1024], P('fsdp')
- out_bias_grad: float32 [1024], P('fsdp')
- ln2_gain_grad: float32 [1024], P('fsdp')
- ln2_bias_grad: float32 [1024], P('fsdp')
- fc1_weight_grad: float32 [1024, 4096], P('fsdp')
- fc1_bias_grad: float32 [4096], P('fsdp')
- fc2_weight_grad: float32 [4096, 1024], P('fsdp')
- fc2_bias_grad: float32 [1024], P('fsdp')
- branch_rms: float32 [3], replicated
The draws below stay inside these ranges and needn't reach their ends.
Inputs may be any that keep to these rules, and one draw needn't show every extreme that they name: In every clip the valid tokens are a leading run of 392 tokens or more; some clip is valid in all its tokens.
All inputs are finite; a program needn't handle non-finite values.
Results may differ from the reference program's by a relative error of at most 0.015.
Values may be sent and summed in bfloat16 or wider, within the bound.
No kernel may reach another device: no remote copies, remote signals or barrier semaphores. Data moves between devices by JAX's collectives and lax.ppermute only.
A program may use at most 192 MiB of HBM per device.

```python
from functools import partial
import jax
import jax.numpy as jnp
from jax import lax

D = 1024
HEADS = 16
HEAD = 64
FF = 4096
L_CLIP = 1568
CLIPS = 16


def draw_valid(key, part):
    clip_index = jnp.arange(CLIPS, dtype=jnp.int32)
    span_clips = max(CLIPS - 1, 1)
    least_len = L_CLIP // 4
    base_len = least_len + (L_CLIP - least_len) * clip_index // span_clips
    jitter_len = jax.random.randint(key, (CLIPS,), 0, L_CLIP // 8 + 1, dtype=jnp.int32)
    lengths_all = jnp.minimum(base_len + jitter_len, L_CLIP)
    positions = jnp.arange(L_CLIP, dtype=jnp.int32)
    return (positions[None, :] < lengths_all[:, None]).astype(jnp.int32)


def draw_inputs(key, part):
    noise_key = jax.random.fold_in(key, 7)
    clip_frac = jnp.arange(CLIPS, dtype=jnp.float32) / float(max(CLIPS - 1, 1))
    token_frac = jnp.arange(L_CLIP, dtype=jnp.float32) / float(max(L_CLIP - 1, 1))
    clip_scale = 0.7 + 0.7 * clip_frac
    token_scale = 0.5 + 1.5 * token_frac
    noise = jax.random.truncated_normal(noise_key, -2.1, 2.1, (CLIPS, L_CLIP, D), jnp.float32)
    values = noise * clip_scale[:, None, None] * token_scale[None, :, None]
    return values.astype(jnp.bfloat16)


def spiked(entries, stream_key, source, target, blocks, factor):
    owner, partner = [(jnp.arange(entries.shape[dim]) // (entries.shape[dim] // blocks)).reshape([-1 if axis == dim else 1 for axis in range(entries.ndim)]) for dim in (source, target)]
    chosen = jax.random.permutation(stream_key, blocks)[partner]
    strong = (owner == chosen) | (owner == (partner + blocks // 2) % blocks)
    return jnp.where(strong, factor * entries, entries)


def shard_levels(stream_key, shape, cuts, low, top_value):
    loudness, own = 1.0, jax.random.fold_in(stream_key, 6)
    for position, parts in cuts:
        steps = jnp.exp(jax.random.uniform(jax.random.fold_in(own, position), (parts,), jnp.float32, low / len(cuts), top_value / len(cuts)))
        loudness = loudness * jnp.repeat(steps, shape[position] // parts).reshape([-1 if axis == position else 1 for axis in range(len(shape))])
    return loudness


def gaussian(key, dims, width, reach, cuts=(), kind=jnp.bfloat16):
    entries = width * jax.random.normal(key, dims, jnp.float32)
    if cuts:
        entries = entries * shard_levels(key, dims, cuts, -0.22, 0.18)
    return jnp.clip(entries, -reach, reach).astype(kind)


def heavy_noise(rng, dims, deviation, reach, cuts, heavy, kind=jnp.bfloat16):
    entries = deviation * jax.random.normal(rng, dims, jnp.float32)
    if cuts:
        entries = entries * shard_levels(rng, dims, cuts, -0.22, 0.18)
    return jnp.clip(spiked(entries, jax.random.fold_in(rng, 3), *heavy), -reach, reach).astype(kind)


def setup_inputs(seed: int = 0) -> dict:
    keys = jax.random.split(jax.random.key(seed), 17)
    return {
        "inputs": draw_inputs(jax.random.fold_in(keys[16], 71), 0),
        "cotangent": heavy_noise(keys[1], (CLIPS, L_CLIP, D), 1.0, 6.0, ((0, 8), (1, 4)), (0, 2, 8, 2.0)),
        "valid": draw_valid(jax.random.fold_in(keys[16], 71), 0),
        "ln1_gain": jnp.clip(1.0 + 0.15 * jax.random.normal(keys[3], (D,), jnp.float32), 0.25, 1.75).astype(jnp.bfloat16),
        "ln1_bias": gaussian(keys[4], (D,), 0.3, 1.75, ((0, 8),)),
        "qkv_weight": gaussian(keys[5], (D, 3 * D), D ** -0.5, 0.1875, ((0, 8),)),
        "q_bias": gaussian(keys[6], (D,), 0.5, 3.0, ((0, 8),)),
        "v_bias": gaussian(keys[7], (D,), 0.05, 0.3125, ((0, 8),)),
        "out_weight": gaussian(keys[8], (D, D), (max(D * 16 // L_CLIP, 1)) ** -0.5, 2.0, ((0, 8),)),
        "out_bias": gaussian(keys[9], (D,), 0.3, 1.75, ((0, 8),)),
        "ln2_gain": jnp.clip(1.0 + 0.15 * jax.random.normal(keys[10], (D,), jnp.float32), 0.25, 1.75).astype(jnp.bfloat16),
        "ln2_bias": gaussian(keys[11], (D,), 0.3, 1.75, ((0, 8),)),
        "fc1_weight": gaussian(keys[12], (D, FF), D ** -0.5, 0.1875, ((0, 8),)),
        "fc1_bias": gaussian(keys[13], (FF,), 0.3, 1.75, ((0, 8),)),
        "fc2_weight": gaussian(keys[14], (FF, D), FF ** -0.5, 0.09375, ((0, 8),)),
        "fc2_bias": gaussian(keys[15], (D,), 0.3, 1.75, ((0, 8),)),
    }


@jax.custom_vjp
def low(v):
    return lax.optimization_barrier(v.astype(jnp.bfloat16)).astype(jnp.float32)

@jax.custom_vjp
def low_back(v):
    return v

def low_keep(v):
    return (low(v), None)

def low_pass(kept, grad):
    return (grad,)

def back_keep(v):
    return (v, None)

def back_low(kept, grad):
    return (low(grad),)
low.defvjp(low_keep, low_pass)
low_back.defvjp(back_keep, back_low)
EPS = 1e-06
exact_mode = lax.Precision.HIGHEST

def matmul(left, right):
    return jnp.dot(left, right, precision=exact_mode)

def layer_norm(values, gain, bias):
    center = values - lax.optimization_barrier(jnp.mean(values, axis=-1, keepdims=True))
    spread = lax.optimization_barrier(jnp.mean(center * center, axis=-1, keepdims=True))
    return center * lax.rsqrt(spread + EPS) * gain + bias

def gelu_exact(values):
    return jax.nn.gelu(values, approximate=False)

def head_attend(pieces):
    queries, key_rows, value_rows, keep_row = pieces
    scores = low_back(matmul(queries, key_rows.T))
    scores = jnp.where(keep_row[None, :] > 0.5, scores, -1e+30)
    probs = low(jax.nn.softmax(scores, axis=-1))
    return low_back(low(matmul(probs, value_rows)))

def layer(inputs, params, keep_row):
    ln1_gain, ln1_bias, qkv_weight, q_bias, v_bias, out_weight, out_bias, ln2_gain, ln2_bias, fc1_weight, fc1_bias, fc2_weight, fc2_bias = params
    length = inputs.shape[0]
    h_one = low(layer_norm(inputs, ln1_gain, ln1_bias))
    mixed = matmul(h_one, qkv_weight)
    queries = low_back(low((mixed[:, :D] + q_bias) * HEAD ** (-0.5)))
    key_rows = low_back(low(mixed[:, D:2 * D]))
    value_rows = low_back(low(mixed[:, 2 * D:] + v_bias))

    def split_heads(values):
        return values.reshape(length, HEADS, HEAD).transpose(1, 0, 2)
    keeps = jnp.broadcast_to(keep_row, (HEADS, length))
    context = lax.map(jax.checkpoint(head_attend), (split_heads(queries), split_heads(key_rows), split_heads(value_rows), keeps))
    context = context.transpose(1, 0, 2).reshape(length, D)
    attn_branch = low_back(matmul(context, out_weight) + out_bias)
    residual_mid = inputs + attn_branch
    h_two = low(layer_norm(residual_mid, ln2_gain, ln2_bias))
    hidden = low_back(matmul(h_two, fc1_weight) + fc1_bias)
    active = low(gelu_exact(hidden))
    mlp_branch = matmul(active, fc2_weight) + fc2_bias
    return (residual_mid + mlp_branch, (attn_branch, mlp_branch))

def reference(inputs, cotangent, valid, ln1_gain, ln1_bias, qkv_weight, q_bias, v_bias, out_weight, out_bias, ln2_gain, ln2_bias, fc1_weight, fc1_bias, fc2_weight, fc2_bias):
    params = tuple((p.astype(jnp.float32) for p in (ln1_gain, ln1_bias, qkv_weight, q_bias, v_bias, out_weight, out_bias, ln2_gain, ln2_bias, fc1_weight, fc1_bias, fc2_weight, fc2_bias)))
    clip_inputs = inputs.astype(jnp.float32)
    clip_grads = cotangent.astype(jnp.float32)
    keeps = valid.astype(jnp.float32)

    def one_clip(carry, item):
        grad_sums, square_sums = carry
        clip_in, clip_grad, keep_row = item
        result, pull, aux = jax.vjp(partial(layer, keep_row=keep_row), clip_in, params, has_aux=True)
        attn_branch, mlp_branch = aux
        grad_in, grad_params = pull(clip_grad)
        weight = keep_row[:, None]
        squares = jnp.stack([jnp.sum(weight * result * result), jnp.sum(weight * attn_branch * attn_branch), jnp.sum(weight * mlp_branch * mlp_branch)])
        grad_sums = tuple((a + b for a, b in zip(grad_sums, grad_params)))
        return ((grad_sums, square_sums + squares), (result.astype(jnp.bfloat16), grad_in.astype(jnp.bfloat16)))
    start = (tuple((jnp.zeros(p.shape, jnp.float32) for p in params)), jnp.zeros((3,), jnp.float32))
    (grads, square_sums), (output, input_grad) = lax.scan(one_clip, start, (clip_inputs, clip_grads, keeps))
    count = jnp.sum(keeps) * D
    branch_rms = jnp.sqrt(square_sums / count)
    return (output, input_grad, grads[0], grads[1], grads[2], grads[3], grads[4], grads[5], grads[6], grads[7], grads[8], grads[9], grads[10], grads[11], grads[12], branch_rms)
```

```python
from functools import partial

import jax
import jax.numpy as jnp
from jax import lax
from jax.experimental import pallas as pl
from jax.experimental.pallas import tpu as pltpu
from jax.sharding import PartitionSpec as P

HEADS = 16
HEAD = 64
PAIR = 2 * HEAD
EPS = 1e-06
MASKED = -1e30
VMEM_BYTES = 56 * 2**20
BF16 = jnp.bfloat16
F32 = jnp.float32
NN = (((1,), (0,)), ((), ()))
NT = (((1,), (1,)), ((), ()))
TN = (((0,), (0,)), ((), ()))


def dot(left, right, dims=NN):
    return lax.dot_general(left, right, dims, preferred_element_type=F32)


def lanes_of(shape):
    return lax.broadcasted_iota(jnp.int32, shape, len(shape) - 1)


def three_parts(column):
    high = column.astype(BF16).astype(F32)
    rest = column - high
    middle = rest.astype(BF16).astype(F32)
    return high, middle, rest - middle


def block_rows(length):
    for rows in (224, 112, 16):
        if length % rows == 0:
            return rows
    return length


def attend_kernel(q_ref, k_ref, v_ref, key_base_ref, context_ref, query_ref):
    length = q_ref.shape[0]
    rows = block_rows(length)
    low = lanes_of((length, PAIR)) < HEAD
    keys, values, key_base = k_ref[...], v_ref[...], key_base_ref[...]
    ones = jnp.ones((length, PAIR), BF16)
    keys_of = [jnp.where(low, keys, key_base), jnp.where(low, key_base, keys)]
    values_of = [jnp.where(low, values, ones), jnp.where(low, ones, values)]
    lane = lanes_of((rows, PAIR))
    low_rows = lane < HEAD
    for step in range(length // rows):
        span = slice(step * rows, (step + 1) * rows)
        queries = q_ref[span, :]
        results = []
        for head in range(2):
            base = HEAD * (1 - head)
            own = low_rows if head == 0 else jnp.logical_not(low_rows)
            unit = jnp.where(lane == base, 1.0, 0.0)
            scores = dot(jnp.where(own, queries, unit.astype(BF16)), keys_of[head], NT)
            highest = jnp.max(scores, axis=1, keepdims=True)
            weights = jnp.exp(scores - highest).astype(BF16)
            mixed = dot(weights, values_of[head])
            total = mixed[:, base : base + 1]
            high, middle, rest = three_parts(-(highest + jnp.log(total)))
            extra = jnp.where(lane == base + 3, rest, unit)
            extra = jnp.where(lane == base + 2, middle, extra)
            extra = jnp.where(lane == base + 1, high, extra)
            query_ref[head, span, :] = jnp.where(own, queries, extra.astype(BF16))
            results.append(mixed / total)
        context_ref[span, :] = jnp.where(low_rows, results[0], results[1]).astype(BF16)


def attend(mixed, key_base):
    length, width = mixed.shape
    pairs = width // (3 * PAIR)
    tile = lambda place: pl.BlockSpec((length, PAIR), place)
    scores_size = 2 * pairs * length * length
    return pl.pallas_call(
        attend_kernel,
        grid=(pairs,),
        in_specs=[
            tile(lambda i: (0, i)),
            tile(lambda i: (0, pairs + i)),
            tile(lambda i: (0, 2 * pairs + i)),
            tile(lambda i: (0, 0)),
        ],
        out_specs=[tile(lambda i: (0, i)), pl.BlockSpec((2, length, PAIR), lambda i: (i, 0, 0))],
        out_shape=[
            jax.ShapeDtypeStruct((length, pairs * PAIR), BF16),
            jax.ShapeDtypeStruct((2 * pairs, length, PAIR), BF16),
        ],
        compiler_params=pltpu.CompilerParams(vmem_limit_bytes=VMEM_BYTES),
        cost_estimate=pl.CostEstimate(
            flops=16 * scores_size * HEAD, bytes_accessed=8 * 2**20, transcendentals=scores_size
        ),
        name="attend",
    )(mixed, mixed, mixed, key_base)


def attend_back_kernel(
    query_ref, k_ref, v_ref, grad_ref, context_ref, key_base_ref, grad_q_ref, grad_k_ref, grad_v_ref
):
    length = k_ref.shape[0]
    rows = block_rows(length)
    low = lanes_of((length, PAIR)) < HEAD
    keys, values, key_base = k_ref[...], v_ref[...], key_base_ref[...]
    ones = jnp.ones((length, PAIR), BF16)
    lane = lanes_of((rows, PAIR))
    low_rows = lane < HEAD
    steps = length // rows
    grad_q, grad_k, grad_v = [], [], []
    for head in range(2):
        base = HEAD * (1 - head)
        own = low if head == 0 else jnp.logical_not(low)
        own_rows = low_rows if head == 0 else jnp.logical_not(low_rows)
        head_keys = jnp.where(own, keys, key_base)
        head_values = jnp.where(own, values, ones)
        sum_k = jnp.zeros((length, PAIR), F32)
        sum_v = jnp.zeros((length, PAIR), F32)
        for step in range(steps):
            span = slice(step * rows, (step + 1) * rows)
            queries = query_ref[head, span, :]
            grads = grad_ref[span, :]
            product = grads.astype(F32) * context_ref[span, :].astype(F32)
            inner = jnp.sum(jnp.where(own_rows, product, 0.0), axis=1, keepdims=True)
            high, middle, rest = three_parts(-inner)
            extra = jnp.where(lane == base + 2, rest, 0.0)
            extra = jnp.where(lane == base + 1, middle, extra)
            extra = jnp.where(lane == base, high, extra)
            head_grads = jnp.where(own_rows, grads, extra.astype(BF16))
            probs = jnp.exp(dot(head_keys, queries, NT))
            grad_scores = (probs * dot(head_values, head_grads, NT)).astype(BF16)
            sum_v = sum_v + dot(probs.astype(BF16), grads)
            sum_k = sum_k + dot(grad_scores, queries)
            part = dot(grad_scores, keys, TN)
            if head == 0:
                grad_q.append(part)
            else:
                both = jnp.where(low_rows, grad_q[step], part).astype(BF16)
                grad_q_ref[span, :] = both * (HEAD ** (-0.5))
        grad_k.append(sum_k)
        grad_v.append(sum_v)
    grad_k_ref[...] = jnp.where(low, grad_k[0], grad_k[1]).astype(BF16)
    grad_v_ref[...] = jnp.where(low, grad_v[0], grad_v[1]).astype(BF16)


def attend_back(queries, mixed, grad_context, context, key_base):
    length, width = mixed.shape
    pairs = width // (3 * PAIR)
    tile = lambda place: pl.BlockSpec((length, PAIR), place)
    scores_size = 2 * pairs * length * length
    return pl.pallas_call(
        attend_back_kernel,
        grid=(pairs,),
        in_specs=[
            pl.BlockSpec((2, length, PAIR), lambda i: (i, 0, 0)),
            tile(lambda i: (0, pairs + i)),
            tile(lambda i: (0, 2 * pairs + i)),
            tile(lambda i: (0, i)),
            tile(lambda i: (0, i)),
            tile(lambda i: (0, 0)),
        ],
        out_specs=[tile(lambda i: (0, i))] * 3,
        out_shape=[jax.ShapeDtypeStruct((length, pairs * PAIR), BF16)] * 3,
        compiler_params=pltpu.CompilerParams(vmem_limit_bytes=VMEM_BYTES),
        cost_estimate=pl.CostEstimate(
            flops=40 * scores_size * HEAD, bytes_accessed=12 * 2**20, transcendentals=scores_size
        ),
        name="attend_back",
    )(queries, mixed, mixed, grad_context, context, key_base)


def normalize(values):
    center = values - jnp.mean(values, axis=-1, keepdims=True)
    spread = jnp.mean(center * center, axis=-1, keepdims=True)
    scale = lax.rsqrt(spread + EPS)
    return center * scale, scale


def normalize_back(normal, scale, grad, gain):
    inner = grad * gain
    first = jnp.mean(inner, axis=-1, keepdims=True)
    second = jnp.mean(inner * normal, axis=-1, keepdims=True)
    return scale * (inner - first - normal * second)


def gelu_both(values):
    half = 0.5 * (1.0 + lax.erf(values * (0.5**0.5)))
    density = jnp.exp(-0.5 * values * values) * (0.5 / jnp.pi) ** 0.5
    return values * half, half + values * density


def column_sum(values):
    return jnp.sum(values, axis=0, dtype=F32)


def swap_core(values):
    return lax.ppermute(values, "seq", [(0, 1), (1, 0), (2, 3), (3, 2)])


def swap_chip(values):
    return lax.ppermute(values, "seq", [(0, 2), (2, 0), (1, 3), (3, 1)])


def with_partner(values):
    return jnp.concatenate([values, swap_core(values)], axis=0)


def sum_partner(partial_sums):
    half = partial_sums.shape[0] // 2
    received = swap_core(partial_sums[half:].astype(BF16))
    return partial_sums[:half] + received.astype(F32)


def gather_rows(values):
    return lax.all_gather(values, "fsdp", axis=0, tiled=True)


def scatter_rows(values):
    return lax.psum_scatter(values.astype(BF16), "fsdp", scatter_dimension=0, tiled=True)


def in_core_order(own, other, core, axis):
    first = jnp.where(core == 0, own, other)
    second = jnp.where(core == 0, other, own)
    return first, second


def body(
    inputs,
    cotangent,
    valid,
    ln1_gain,
    ln1_bias,
    qkv_weight,
    q_bias,
    v_bias,
    out_weight,
    out_bias,
    ln2_gain,
    ln2_bias,
    fc1_weight,
    fc1_bias,
    fc2_weight,
    fc2_bias,
):
    clips, rows, width = inputs.shape
    groups = lax.axis_size("fsdp")
    place = lax.axis_index("seq")
    group = lax.axis_index("fsdp")
    chip, core = place // 2, place % 2
    half = width // 2
    hidden_rows = fc2_weight.shape[0]
    half_rows = hidden_rows // 2
    own_rows = clips * rows
    scale_factor = HEAD ** (-0.5)

    def take(values, index):
        return lax.dynamic_index_in_dim(values, index, 0, keepdims=False)

    def own_clip(values):
        mine = take(values, chip)
        return jnp.concatenate([mine, swap_chip(take(values, 1 - chip))], axis=0)

    def all_clips(values):
        mine, back = values[:rows], swap_chip(values[rows:])
        first = jnp.where(chip == 0, mine, back)
        second = jnp.where(chip == 0, back, mine)
        return jnp.stack([first, second])

    vectors = (ln1_gain, ln1_bias, q_bias, v_bias, out_bias, ln2_gain, ln2_bias, fc2_bias, fc1_bias)
    packed = lax.all_gather(jnp.concatenate(vectors), "fsdp", axis=0)
    own_width = width // groups
    wide = [
        packed[:, i * own_width : (i + 1) * own_width].reshape(width).astype(F32) for i in range(8)
    ]
    gain_one, bias_one, bias_q, bias_v, bias_out, gain_two, bias_two, bias_fc2 = wide
    bias_fc1 = take(
        jnp.moveaxis(packed[:, 8 * own_width :].reshape(groups, 2, half_rows), 1, 0), core
    )
    bias_fc1 = bias_fc1.reshape(groups * half_rows).astype(F32)
    bias_q, bias_v = take(bias_q.reshape(2, half), core), take(bias_v.reshape(2, half), core)

    own_qkv = lax.dynamic_index_in_dim(
        qkv_weight.reshape(own_width, 3, 2, half), core, 2, keepdims=False
    ).reshape(own_width, 3 * half)
    full_qkv = gather_rows(own_qkv)
    full_out = lax.dynamic_slice_in_dim(gather_rows(out_weight), core * half, half, 0)
    own_fc1 = lax.dynamic_index_in_dim(
        fc1_weight.reshape(own_width, groups, 2, half_rows), core, 2, keepdims=False
    ).reshape(own_width, groups * half_rows)
    full_fc1 = gather_rows(own_fc1)
    full_fc2 = gather_rows(lax.dynamic_slice_in_dim(fc2_weight, core * half_rows, half_rows, 0))

    own_inputs = own_clip(inputs)
    own_grads = own_clip(cotangent)
    all_inputs = with_partner(own_inputs)
    all_grads = with_partner(own_grads)
    clip_valid = take(valid, chip).reshape(2 * clips, rows)
    own_valid = jnp.concatenate([take(clip_valid, place), take(clip_valid, place ^ 2)])
    other_valid = jnp.concatenate([take(clip_valid, place ^ 1), take(clip_valid, place ^ 3)])
    key_valid = jnp.concatenate([own_valid, other_valid])
    lane = jnp.arange(PAIR) % HEAD
    key_mask = jnp.where(key_valid > 0, 0.0, MASKED)[:, None]
    key_base = jnp.where(lane == 0, key_mask, jnp.where(lane < 4, 1.0, 0.0)).astype(BF16)

    normal_one = normalize(all_inputs.astype(F32))[0]
    h_one = (normal_one * gain_one + bias_one).astype(BF16)
    product = dot(h_one, full_qkv)
    mixed = jnp.concatenate(
        [
            ((product[:, :half] + bias_q) * scale_factor).astype(BF16),
            product[:, half : 2 * half].astype(BF16),
            (product[:, 2 * half :] + bias_v).astype(BF16),
        ],
        axis=1,
    )
    context, queries = attend(mixed, key_base)
    attn_branch = sum_partner(dot(context, full_out)) + bias_out
    residual_mid = own_inputs.astype(F32) + attn_branch
    normal_two, scale_two = normalize(residual_mid)
    h_two = with_partner((normal_two * gain_two + bias_two).astype(BF16))
    active, slope = gelu_both(dot(h_two, full_fc1) + bias_fc1)
    active, slope = active.astype(BF16), slope.astype(BF16)
    mlp_branch = sum_partner(dot(active, full_fc2)) + bias_fc2
    residual_out = residual_mid + mlp_branch
    output = all_clips(residual_out.astype(BF16))
    counted = own_valid.astype(F32)[:, None]
    squares = jnp.stack(
        [
            jnp.sum(counted * residual_out * residual_out),
            jnp.sum(counted * attn_branch * attn_branch),
            jnp.sum(counted * mlp_branch * mlp_branch),
            jnp.sum(counted),
        ]
    )

    grad_fc2 = scatter_rows(dot(active, all_grads, TN))
    grad_hidden = (dot(all_grads, full_fc2, NT) * slope.astype(F32)).astype(BF16)
    grad_fc1 = scatter_rows(dot(h_two, grad_hidden, TN))
    grad_h_two = sum_partner(dot(grad_hidden, full_fc1, NT))
    grad_residual = own_grads.astype(F32) + normalize_back(
        normal_two, scale_two, grad_h_two, gain_two
    )
    own_grad_attn = grad_residual.astype(BF16)
    grad_attn = with_partner(own_grad_attn)
    grad_out = dot(context, grad_attn, TN).astype(BF16)
    kept = lax.dynamic_slice_in_dim(grad_out, core * half, half, 1)
    received = swap_core(lax.dynamic_slice_in_dim(grad_out, (1 - core) * half, half, 1))
    grad_out = scatter_rows(jnp.concatenate(in_core_order(kept, received, core, 0), axis=0))
    grad_context = dot(grad_attn, full_out, NT).astype(BF16)
    grad_q, grad_k, grad_v = attend_back(queries, mixed, grad_context, context, key_base)
    grad_mixed = jnp.concatenate([grad_q, grad_k, grad_v], axis=1)
    grad_qkv = scatter_rows(dot(h_one, grad_mixed, TN))
    grad_h_one = sum_partner(dot(grad_mixed, full_qkv, NT))
    own_normal, own_scale = normalize(own_inputs.astype(F32))
    input_grad = all_clips(
        (grad_residual + normalize_back(own_normal, own_scale, grad_h_one, gain_one)).astype(BF16)
    )

    def by_core(values):
        full = jnp.zeros((2, values.shape[0]), F32)
        return lax.dynamic_update_index_in_dim(full, values, core, 0).reshape(-1)

    mixed_sums = column_sum(grad_mixed)
    vector_grads = [
        column_sum(grad_h_one * own_normal),
        column_sum(grad_h_one),
        by_core(mixed_sums[:half]),
        by_core(mixed_sums[2 * half :]),
        column_sum(own_grad_attn),
        column_sum(grad_h_two * normal_two),
        column_sum(grad_h_two),
        column_sum(own_grads),
    ]
    hidden_sums = jnp.zeros((groups, 2, half_rows), F32)
    hidden_sums = lax.dynamic_update_index_in_dim(
        hidden_sums, column_sum(grad_hidden).reshape(groups, half_rows), core, 1
    )
    flat = jnp.concatenate(vector_grads + [hidden_sums.reshape(-1), squares])
    flat = lax.psum(flat, ("seq", "fsdp"))
    totals = flat[-4:]
    branch_rms = jnp.sqrt(totals[:3] / (totals[3] * width))
    own_vectors = [
        lax.dynamic_slice_in_dim(flat, i * width + group * own_width, own_width) for i in range(8)
    ]
    own_hidden = lax.dynamic_slice_in_dim(flat, 8 * width + group * hidden_rows, hidden_rows)

    def finish(values):
        values = (values.astype(F32) + swap_chip(values).astype(F32)).astype(BF16)
        return in_core_order(values, swap_core(values), core, 0)

    qkv_parts = [part.reshape(own_width, 3, 1, half) for part in finish(grad_qkv)]
    qkv_grad = jnp.concatenate(qkv_parts, axis=2).reshape(own_width, 3 * width).astype(F32)
    out_grad = jnp.concatenate(finish(grad_out), axis=1).astype(F32)
    fc1_parts = [part.reshape(own_width, groups, 1, half_rows) for part in finish(grad_fc1)]
    fc1_grad = jnp.concatenate(fc1_parts, axis=2).reshape(own_width, -1).astype(F32)
    fc2_grad = jnp.concatenate(finish(grad_fc2), axis=0).astype(F32)
    return (
        output,
        input_grad,
        own_vectors[0],
        own_vectors[1],
        qkv_grad,
        own_vectors[2],
        own_vectors[3],
        out_grad,
        own_vectors[4],
        own_vectors[5],
        own_vectors[6],
        fc1_grad,
        own_hidden,
        fc2_grad,
        own_vectors[7],
        branch_rms,
    )


def solution(mesh):
    tokens, rows, vector = P("fsdp", "seq", None), P("fsdp", None), P("fsdp")
    return jax.shard_map(
        body,
        mesh=mesh,
        in_specs=(
            tokens,
            tokens,
            rows,
            vector,
            vector,
            rows,
            vector,
            vector,
            rows,
            vector,
            vector,
            vector,
            rows,
            vector,
            rows,
            vector,
        ),
        out_specs=(
            tokens,
            tokens,
            vector,
            vector,
            rows,
            vector,
            vector,
            rows,
            vector,
            vector,
            vector,
            rows,
            vector,
            rows,
            vector,
            P(),
        ),
        check_vma=False,
    )
```

```python
from functools import partial

import jax
import jax.numpy as jnp
from jax import lax
from jax.experimental import pallas as pl
from jax.experimental.pallas import tpu as pltpu
from jax.sharding import PartitionSpec as P

HEADS = 16
HEAD = 64
PAIR = 2 * HEAD
EPS = 1e-06
MASKED = -1e30
VMEM_BYTES = 56 * 2**20
BF16 = jnp.bfloat16
F32 = jnp.float32
NN = (((1,), (0,)), ((), ()))
NT = (((1,), (1,)), ((), ()))
TN = (((0,), (0,)), ((), ()))
SMALL_COST = pl.CostEstimate(flops=10**7, bytes_accessed=2**20, transcendentals=0)


def dot(left, right, dims=NN):
    return lax.dot_general(left, right, dims, preferred_element_type=F32)


def lanes_of(shape):
    return lax.broadcasted_iota(jnp.int32, shape, len(shape) - 1)


def three_parts(column):
    high = column.astype(BF16).astype(F32)
    rest = column - high
    middle = rest.astype(BF16).astype(F32)
    return high, middle, rest - middle


def block_rows(length):
    for rows in (224, 112, 16):
        if length % rows == 0:
            return rows
    return length


def attend_kernel(q_ref, k_ref, v_ref, key_base_ref, *refs):
    context_ref, query_ref = refs[-2:]
    length = q_ref.shape[0]
    rows = block_rows(length)
    low = lanes_of((length, PAIR)) < HEAD
    keys, values, key_base = k_ref[...], v_ref[...], key_base_ref[...]
    ones = jnp.ones((length, PAIR), BF16)
    keys_of = [jnp.where(low, keys, key_base), jnp.where(low, key_base, keys)]
    values_of = [jnp.where(low, values, ones), jnp.where(low, ones, values)]
    lane = lanes_of((rows, PAIR))
    low_rows = lane < HEAD
    for step in range(length // rows):
        span = slice(step * rows, (step + 1) * rows)
        queries = q_ref[span, :]
        results = []
        for head in range(2):
            base = HEAD * (1 - head)
            own = low_rows if head == 0 else jnp.logical_not(low_rows)
            unit = jnp.where(lane == base, 1.0, 0.0)
            scores = dot(jnp.where(own, queries, unit.astype(BF16)), keys_of[head], NT)
            highest = jnp.max(scores, axis=1, keepdims=True)
            weights = jnp.exp(scores - highest).astype(BF16)
            mixed = dot(weights, values_of[head])
            total = mixed[:, base : base + 1]
            high, middle, rest = three_parts(-(highest + jnp.log(total)))
            extra = jnp.where(lane == base + 3, rest, unit)
            extra = jnp.where(lane == base + 2, middle, extra)
            extra = jnp.where(lane == base + 1, high, extra)
            query_ref[head, span, :] = jnp.where(own, queries, extra.astype(BF16))
            results.append(mixed / total)
        context_ref[span, :] = jnp.where(low_rows, results[0], results[1]).astype(BF16)


def attend(mixed, key_base, pair, context, place, places):
    length = mixed.shape[0]
    tile = lambda column: pl.BlockSpec((length, PAIR), lambda i: (0, column))
    in_specs = [tile(3 * pair), tile(3 * pair + 1), tile(3 * pair + 2), tile(0)]
    operands = (mixed, mixed, mixed, key_base)
    aliases = {}
    if context is not None:
        in_specs.append(pl.BlockSpec(memory_space=pl.ANY))
        operands += (context,)
        aliases = {4: 0}
    return pl.pallas_call(
        attend_kernel,
        grid=(1,),
        in_specs=in_specs,
        out_specs=[tile(place), pl.BlockSpec((2, length, PAIR), lambda i: (0, 0, 0))],
        out_shape=[
            jax.ShapeDtypeStruct((length, places * PAIR), BF16),
            jax.ShapeDtypeStruct((2, length, PAIR), BF16),
        ],
        input_output_aliases=aliases,
        compiler_params=pltpu.CompilerParams(vmem_limit_bytes=VMEM_BYTES),
        cost_estimate=SMALL_COST,
        name="attend",
    )(*operands)


def attend_back_kernel(query_ref, k_ref, v_ref, grad_ref, context_ref, key_base_ref, *refs):
    grad_mixed_ref, sums_ref = refs[-2:]
    length = k_ref.shape[0]
    rows = block_rows(length)
    low = lanes_of((length, PAIR)) < HEAD
    keys, values, key_base = k_ref[...], v_ref[...], key_base_ref[...]
    ones = jnp.ones((length, PAIR), BF16)
    lane = lanes_of((rows, PAIR))
    low_rows = lane < HEAD
    steps = length // rows
    grad_q, grad_k, grad_v = [], [], []
    sum_q = jnp.zeros((1, PAIR), F32)
    for head in range(2):
        base = HEAD * (1 - head)
        own = low if head == 0 else jnp.logical_not(low)
        own_rows = low_rows if head == 0 else jnp.logical_not(low_rows)
        head_keys = jnp.where(own, keys, key_base)
        head_values = jnp.where(own, values, ones)
        sum_k = jnp.zeros((length, PAIR), F32)
        sum_v = jnp.zeros((length, PAIR), F32)
        for step in range(steps):
            span = slice(step * rows, (step + 1) * rows)
            queries = query_ref[head, span, :]
            grads = grad_ref[span, :]
            product = grads.astype(F32) * context_ref[span, :].astype(F32)
            inner = jnp.sum(jnp.where(own_rows, product, 0.0), axis=1, keepdims=True)
            high, middle, rest = three_parts(-inner)
            extra = jnp.where(lane == base + 2, rest, 0.0)
            extra = jnp.where(lane == base + 1, middle, extra)
            extra = jnp.where(lane == base, high, extra)
            head_grads = jnp.where(own_rows, grads, extra.astype(BF16))
            probs = jnp.exp(dot(head_keys, queries, NT))
            grad_scores = (probs * dot(head_values, head_grads, NT)).astype(BF16)
            sum_v = sum_v + dot(probs.astype(BF16), grads)
            sum_k = sum_k + dot(grad_scores, queries)
            part = dot(grad_scores, keys, TN)
            if head == 0:
                grad_q.append(part)
            else:
                both = jnp.where(low_rows, grad_q[step], part).astype(BF16)
                both = both * (HEAD ** (-0.5))
                grad_mixed_ref[span, :PAIR] = both
                sum_q = sum_q + jnp.sum(both.astype(F32), axis=0, keepdims=True)
        grad_k.append(sum_k)
        grad_v.append(sum_v)
    grad_mixed_ref[:, PAIR : 2 * PAIR] = jnp.where(low, grad_k[0], grad_k[1]).astype(BF16)
    both = jnp.where(low, grad_v[0], grad_v[1]).astype(BF16)
    grad_mixed_ref[:, 2 * PAIR :] = both
    sums_ref[0:1, :] = sum_q
    sums_ref[1:2, :] = jnp.sum(both.astype(F32), axis=0, keepdims=True)


def attend_back(queries, mixed, grad_context, context, key_base, pair, place, grad_mixed):
    length = mixed.shape[0]
    tile = lambda column: pl.BlockSpec((length, PAIR), lambda i: (0, column))
    in_specs = [
        pl.BlockSpec((2, length, PAIR), lambda i: (0, 0, 0)),
        tile(3 * pair + 1),
        tile(3 * pair + 2),
        tile(place),
        tile(place),
        tile(0),
    ]
    operands = (queries, mixed, mixed, grad_context, context, key_base)
    aliases = {}
    if grad_mixed is not None:
        in_specs.append(pl.BlockSpec(memory_space=pl.ANY))
        operands += (grad_mixed,)
        aliases = {6: 0}
    return pl.pallas_call(
        attend_back_kernel,
        grid=(1,),
        in_specs=in_specs,
        out_specs=[
            pl.BlockSpec((length, 3 * PAIR), lambda i: (0, pair)),
            pl.BlockSpec((2, PAIR), lambda i: (0, 0)),
        ],
        out_shape=[
            jax.ShapeDtypeStruct((length, 6 * PAIR), BF16),
            jax.ShapeDtypeStruct((2, PAIR), F32),
        ],
        input_output_aliases=aliases,
        compiler_params=pltpu.CompilerParams(vmem_limit_bytes=VMEM_BYTES),
        cost_estimate=SMALL_COST,
        name="attend_back",
    )(*operands)


def normalize(values):
    center = values - jnp.mean(values, axis=-1, keepdims=True)
    spread = jnp.mean(center * center, axis=-1, keepdims=True)
    scale = lax.rsqrt(spread + EPS)
    return center * scale, scale


def normalize_back(normal, scale, grad, gain):
    inner = grad * gain
    first = jnp.mean(inner, axis=-1, keepdims=True)
    second = jnp.mean(inner * normal, axis=-1, keepdims=True)
    return scale * (inner - first - normal * second)


def gelu_both(values):
    half = 0.5 * (1.0 + lax.erf(values * (0.5**0.5)))
    density = jnp.exp(-0.5 * values * values) * (0.5 / jnp.pi) ** 0.5
    return values * half, half + values * density


def column_sum(values):
    return jnp.sum(values, axis=0, dtype=F32)


def swap_core(values):
    return lax.ppermute(values, "seq", [(0, 1), (1, 0), (2, 3), (3, 2)])


def swap_chip(values):
    return lax.ppermute(values, "seq", [(0, 2), (2, 0), (1, 3), (3, 1)])


def with_partner(values):
    return jnp.concatenate([values, swap_core(values)], axis=0)


def sum_partner(partial_sums):
    half = partial_sums.shape[0] // 2
    received = swap_core(partial_sums[half:].astype(BF16))
    return partial_sums[:half] + received.astype(F32)


def swap_group(values, bit):
    return lax.ppermute(values, "fsdp", [(i, i ^ bit) for i in range(8)])


def order_kernel(count, *refs):
    pieces, full_ref, sems = refs[:count], refs[count], refs[-1]
    group = lax.axis_index("fsdp")
    rows = full_ref.shape[0] // count
    copies = []
    for relative, piece in enumerate(pieces):
        start = pl.multiple_of((group ^ relative) * rows, rows)
        copies.append(
            pltpu.make_async_copy(
                piece.at[pl.ds(0, rows)], full_ref.at[pl.ds(start, rows)], sems.at[relative]
            )
        )
    for copy in copies:
        copy.start()
    if len(refs) > count + 2:
        own_width, core = 128, lax.rem(lax.axis_index("seq"), 2)
        wide_ref, bias_ref = refs[count + 1], refs[count + 2]
        for relative, piece in enumerate(pieces):
            place = group ^ relative
            columns = pl.ds(pl.multiple_of(place * own_width, own_width), own_width)
            extra = piece[rows : rows + 8, :].astype(F32)
            lines = [
                extra[k : k + 1, own_width * n : own_width * (n + 1)]
                for k in range(2)
                for n in range(6)
            ]
            for n in range(8):
                wide_ref[n : n + 1, columns] = lines[n]
            for n in range(2):
                start = pl.multiple_of((place * 2 + n) * own_width, own_width)
                bias_ref[:, pl.ds(start, own_width)] = jnp.where(
                    core == 0, lines[8 + n], lines[10 + n]
                )
    for copy in copies:
        copy.wait()


def in_order(pieces, rows, with_vectors=False):
    count, columns = len(pieces), pieces[0].shape[1]
    out_specs = [pl.BlockSpec(memory_space=pl.ANY)]
    out_shape = [jax.ShapeDtypeStruct((count * rows, columns), pieces[0].dtype)]
    if with_vectors:
        out_specs += [pl.BlockSpec(memory_space=pltpu.VMEM)] * 2
        out_shape += [jax.ShapeDtypeStruct((8, 1024), F32), jax.ShapeDtypeStruct((1, 2048), F32)]
    result = pl.pallas_call(
        partial(order_kernel, count),
        in_specs=[pl.BlockSpec(memory_space=pltpu.VMEM)] * count,
        out_specs=out_specs,
        out_shape=out_shape,
        scratch_shapes=[pltpu.SemaphoreType.DMA((count,))],
        compiler_params=pltpu.CompilerParams(vmem_limit_bytes=16 * 2**20),
        cost_estimate=pl.CostEstimate(
            flops=0, bytes_accessed=4 * count * rows * columns, transcendentals=0
        ),
        name="in_order",
    )(*pieces)
    return result if with_vectors else result[0]


def own_kernel(qkv_ref, out_ref, *refs):
    vector_refs, (first_ref, second_ref) = refs[:-2], refs[-2:]
    core = lax.rem(lax.axis_index("seq"), 2)
    rows = qkv_ref.shape[0]
    for n in range(3):
        for pair in range(4):
            block_ref = second_ref if pair >= 2 else first_ref
            start = pl.multiple_of((8 * n + pair + 4 * core) * PAIR, PAIR)
            target = (3 * (pair % 2) + n) * PAIR
            block_ref[:rows, target : target + PAIR] = qkv_ref[:, pl.ds(start, PAIR)]
    out_half = out_ref.shape[1] // 2
    start = pl.multiple_of(core * out_half, out_half)
    second_ref[:, 6 * PAIR :] = out_ref[:, pl.ds(start, out_half)]
    lines = []
    for ref in vector_refs:
        vector = ref[...].astype(F32).reshape(ref.shape[0] // PAIR, PAIR)
        lines += [vector[n : n + 1] for n in range(ref.shape[0] // PAIR)]
    row = lax.broadcasted_iota(jnp.int32, (8, PAIR), 0)
    for n in range(6):
        block = jnp.where(row == 0, lines[n], jnp.where(row == 1, lines[n + 6], 0.0))
        first_ref[rows:, PAIR * n : PAIR * (n + 1)] = block.astype(BF16)


def own_qkv_blocks(qkv_weight, out_weight, vectors):
    rows, columns = qkv_weight.shape[0], qkv_weight.shape[1] // 4
    out_half = out_weight.shape[1] // 2
    return pl.pallas_call(
        own_kernel,
        in_specs=[pl.BlockSpec(memory_space=pltpu.VMEM)] * (2 + len(vectors)),
        out_specs=[pl.BlockSpec(memory_space=pltpu.VMEM)] * 2,
        out_shape=[
            jax.ShapeDtypeStruct((rows + 8, columns), BF16),
            jax.ShapeDtypeStruct((rows, columns + out_half), BF16),
        ],
        cost_estimate=SMALL_COST,
        name="own_qkv",
    )(qkv_weight, out_weight, *vectors)


def after(values, *others):
    return lax.optimization_barrier((values,) + others)[0] if others else values


class Gather:
    SOURCE = {4: 0, 2: 0, 1: 0, 6: 4, 3: 2, 5: 4, 7: 6}
    STEP = {4: 4, 2: 2, 1: 1, 6: 2, 3: 1, 5: 1, 7: 1}

    def __init__(self, own):
        self.pieces = [own] + [None] * 7
        self.grouped = lax.axis_size("fsdp") == 8

    def send(self, *parts, ready=()):
        if not self.grouped:
            return
        sources = [self.pieces[self.SOURCE[part]] for part in parts]
        if ready:
            sources = lax.optimization_barrier(tuple(sources) + tuple(ready))
        for part, source in zip(parts, sources):
            self.pieces[part] = swap_group(source, self.STEP[part])

    def got(self, *parts):
        return tuple(self.pieces[part] for part in parts) if self.grouped else ()

    def result(self):
        if not self.grouped:
            return lax.all_gather(self.pieces[0], "fsdp", axis=0, tiled=True)
        return in_order(self.pieces, self.pieces[0].shape[0])


def add_low(left, right):
    return (left.astype(F32) + right.astype(F32)).astype(BF16)


def split_kernel(full_ref, *refs):
    sems = refs[2]
    group = lax.axis_index("fsdp")
    rows = full_ref.shape[0] // 8
    copies = []
    for n in range(8):
        far, near, side = n % 2, (n // 2) % 2, n // 4
        start = pl.multiple_of((group ^ (4 * far + 2 * near + side)) * rows, rows)
        target = refs[side].at[pl.ds((n % 4) * rows, rows)]
        copies.append(
            pltpu.make_async_copy(full_ref.at[pl.ds(start, rows)], target, sems.at[n])
        )
    for copy in copies:
        copy.start()
    for copy in copies:
        copy.wait()


def split_blocks(values):
    rows, columns = values.shape
    return pl.pallas_call(
        split_kernel,
        in_specs=[pl.BlockSpec(memory_space=pltpu.VMEM)],
        out_specs=[pl.BlockSpec(memory_space=pl.ANY)] * 2,
        out_shape=[jax.ShapeDtypeStruct((rows // 2, columns), values.dtype)] * 2,
        scratch_shapes=[pltpu.SemaphoreType.DMA((8,))],
        compiler_params=pltpu.CompilerParams(vmem_limit_bytes=16 * 2**20),
        cost_estimate=SMALL_COST,
        name="split_blocks",
    )(values)


class Scatter:
    def __init__(self, values, *ready, halves=None):
        self.grouped = lax.axis_size("fsdp") == 8
        self.halved = halves is not None
        values = values.astype(BF16)
        if self.halved:
            self.kept, self.sent = halves
            self.crossed = swap_chip(self.sent)
        elif self.grouped:
            self.keep, self.side_send = split_blocks(values)
            self.side = swap_group(after(self.side_send, *ready), 1)
        else:
            self.sums = lax.psum_scatter(values, "fsdp", scatter_dimension=0, tiled=True)

    def cross(self, *ready):
        values = add_low(self.kept, after(self.crossed, *ready))
        if self.grouped:
            self.keep, self.side_send = split_blocks(values)
            self.side = swap_group(self.side_send, 1)
        else:
            self.sums = lax.psum_scatter(values, "fsdp", scatter_dimension=0, tiled=True)

    def got(self, *names):
        return tuple(getattr(self, name) for name in names if hasattr(self, name))

    def step(self, name, next_name, bit, ready):
        if self.grouped:
            received = after(getattr(self, name), *ready)
            half = self.keep.shape[0] // 2
            send = add_low(self.keep[half:], received[half:])
            self.keep = add_low(self.keep[:half], received[:half])
            setattr(self, next_name, swap_group(send, bit))

    def near(self, *ready):
        self.step("side", "near_sums", 2, ready)

    def far(self, *ready):
        self.step("near_sums", "far_sums", 4, ready)

    def chips(self, *ready):
        if self.grouped:
            self.sums = add_low(self.keep, after(self.far_sums, *ready))
        self.other_chip = swap_chip(self.sums)

    def cores(self, *ready):
        other_chip = after(self.other_chip, *ready)
        if self.halved:
            chip = lax.axis_index("seq") // 2
            first = jnp.where(chip == 0, self.sums, other_chip)
            second = jnp.where(chip == 0, other_chip, self.sums)
            self.total = jnp.concatenate([first, second], axis=1)
        else:
            self.total = add_low(self.sums, other_chip)
        self.other_core = swap_core(self.total)

    def finish(self):
        self.near()
        self.far()
        self.chips()
        self.cores()


def take(values, index):
    return lax.dynamic_index_in_dim(values, index, 0, keepdims=False)


def in_core_order(own, other, core, axis):
    first = jnp.where(core == 0, own, other)
    second = jnp.where(core == 0, other, own)
    return first, second


def body(
    inputs,
    cotangent,
    valid,
    ln1_gain,
    ln1_bias,
    qkv_weight,
    q_bias,
    v_bias,
    out_weight,
    out_bias,
    ln2_gain,
    ln2_bias,
    fc1_weight,
    fc1_bias,
    fc2_weight,
    fc2_bias,
):
    clips, rows, width = inputs.shape
    groups = lax.axis_size("fsdp")
    place = lax.axis_index("seq")
    group = lax.axis_index("fsdp")
    chip, core = place // 2, place % 2
    half = width // 2
    hidden_rows = fc2_weight.shape[0]
    half_rows = hidden_rows // 2
    own_rows = clips * rows
    scale_factor = HEAD ** (-0.5)

    def all_clips(values):
        mine, back = values[:rows], swap_chip(values[rows:])
        first = jnp.where(chip == 0, mine, back)
        second = jnp.where(chip == 0, back, mine)
        return jnp.stack([first, second])

    own_width = width // groups
    vectors = (ln1_gain, ln1_bias, q_bias, v_bias, out_bias, ln2_gain, ln2_bias, fc2_bias, fc1_bias)
    quarter = half // 2
    row_width = 3 * quarter
    used = 8 * own_width + fc1_bias.shape[0]
    if groups == 8:
        own_first, own_second = own_qkv_blocks(qkv_weight, out_weight, vectors)
    else:
        by_head = qkv_weight.reshape(own_width, 3, 2, 2, 2, PAIR)
        by_head = lax.dynamic_index_in_dim(by_head, core, 2, keepdims=False)
        by_head = by_head.transpose(0, 2, 3, 1, 4).reshape(own_width, 2, row_width)
        out_columns = lax.dynamic_slice_in_dim(out_weight, core * half, half, 1)
        own_first = by_head[:, 0]
        own_second = jnp.concatenate([by_head[:, 1], out_columns], axis=1)

    own_fc1 = lax.dynamic_index_in_dim(
        fc1_weight.reshape(own_width, groups, 2, half_rows), core, 2, keepdims=False
    ).reshape(own_width, groups * half_rows)
    own_fc2 = lax.dynamic_slice_in_dim(fc2_weight, core * half_rows, half_rows, 0)

    qkv_a, qkv_b = Gather(own_first), Gather(own_second)
    fc1_gather, fc2_gather = Gather(own_fc1), Gather(own_fc2)
    qkv_a.send(4, 2, 1)
    other_inputs = swap_chip(after(take(inputs, 1 - chip), own_first))
    qkv_a.send(6, 3, 5, ready=qkv_a.got(4, 2, 1) + (own_fc1, own_fc2))
    qkv_b.send(4, ready=qkv_a.got(4, 2, 1))
    qkv_a.send(7, ready=qkv_a.got(6, 3, 5))
    other_inputs = after(other_inputs, *qkv_a.got(6, 3, 5))
    qkv_b.send(2, 1, ready=qkv_a.got(6, 3, 5))
    own_inputs = jnp.concatenate([take(inputs, chip), other_inputs], axis=0)
    all_inputs = with_partner(own_inputs)
    if groups == 8:
        qkv_first, wide, bias_fc1 = in_order(qkv_a.pieces, own_width, True)
    else:
        qkv_first = qkv_a.result()
        packed = lax.all_gather(jnp.concatenate(vectors), "fsdp", axis=0)
        wide = [
            packed[:, i * own_width : (i + 1) * own_width].reshape(width).astype(F32)
            for i in range(8)
        ]
        bias_fc1 = packed[:, 8 * own_width : used].reshape(groups, 2, half_rows)
        bias_fc1 = take(jnp.moveaxis(bias_fc1, 1, 0), core)
        bias_fc1 = bias_fc1.reshape(groups * half_rows).astype(F32)
    gain_one, bias_one, bias_q, bias_v, bias_out, gain_two, bias_two, bias_fc2 = [
        wide[i] for i in range(8)
    ]
    bias_q = take(bias_q.reshape(2, 2, 2, PAIR), core)
    bias_v = take(bias_v.reshape(2, 2, 2, PAIR), core)
    bias_mixed = jnp.stack([bias_q, jnp.zeros_like(bias_q), bias_v], axis=2).reshape(2, row_width)
    scale_mixed = jnp.array([scale_factor, 1.0, 1.0] * 2, F32).repeat(PAIR)
    clip_valid = take(valid, chip).reshape(2 * clips, rows)
    own_valid = jnp.concatenate([take(clip_valid, place), take(clip_valid, place ^ 2)])
    other_valid = jnp.concatenate([take(clip_valid, place ^ 1), take(clip_valid, place ^ 3)])
    key_valid = jnp.concatenate([own_valid, other_valid])
    lane = jnp.arange(PAIR) % HEAD
    key_mask = jnp.where(key_valid > 0, 0.0, MASKED)[:, None]
    key_base = jnp.where(lane == 0, key_mask, jnp.where(lane < 4, 1.0, 0.0)).astype(BF16)


    def project(weight, i):
        return ((dot(h_one, weight) + bias_mixed[i]) * scale_mixed).astype(BF16)

    normal_one = normalize(all_inputs.astype(F32))[0]
    h_one = (normal_one * gain_one + bias_one).astype(BF16)
    mixed = [project(qkv_first, 0)]
    context, queries = [], []

    def attend_pair(pair, *ready):
        before = context[-1] if context else None
        base = after(key_base, *ready)
        results = attend(mixed[pair // 2], base, pair % 2, before, pair, 4)
        context.append(results[0])
        queries.append(results[1])

    ready = (mixed[0],) + qkv_b.got(4, 2, 1)
    qkv_b.send(6, 3, 5, ready=ready)
    fc1_gather.send(4, ready=ready)
    attend_pair(0, *ready)
    ready = (queries[0],) + qkv_b.got(6, 3, 5)
    qkv_b.send(7, ready=ready)
    fc1_gather.send(2, 1, ready=ready)
    attend_pair(1, *ready)
    second_columns = qkv_b.result()
    mixed.append(project(second_columns[:, :row_width], 1))
    ready = (queries[1], mixed[1]) + fc1_gather.got(4, 2, 1)
    fc1_gather.send(6, 3, 5, ready=ready)
    fc2_gather.send(4, ready=ready)
    kept = lax.dynamic_slice(second_columns, (core * half, row_width), (half, half))
    received = lax.dynamic_slice(second_columns, ((1 - core) * half, row_width), (half, half))
    received = swap_core(after(received, mixed[1]))
    attend_pair(2, kept, *ready)
    ready = (queries[2], received) + fc1_gather.got(6, 3, 5)
    fc1_gather.send(7, ready=ready)
    fc2_gather.send(2, ready=ready)
    other_grads = swap_chip(after(take(cotangent, 1 - chip), *ready))
    attend_pair(3, *ready)
    own_grads = jnp.concatenate([take(cotangent, chip), after(other_grads, queries[3])], axis=0)
    full_out = jnp.concatenate(in_core_order(kept, received, core, 1), axis=1)
    full_qkv = (qkv_first, second_columns[:, :row_width])
    ready = (own_grads, queries[3]) + fc2_gather.got(4, 2)
    all_context = after(context[3], *ready)
    fc2_gather.send(1, 3, 6, ready=ready)
    attn_branch = sum_partner(dot(all_context, full_out)) + bias_out
    residual_mid = own_inputs.astype(F32) + attn_branch
    normal_two, scale_two = normalize(residual_mid)
    h_two = with_partner((normal_two * gain_two + bias_two).astype(BF16))
    all_grads = with_partner(after(own_grads, residual_mid))
    full_fc1 = fc1_gather.result()
    h_two = after(h_two, *fc2_gather.got(1, 3, 6))
    fc2_gather.send(5, ready=(h_two,))
    active, slope = gelu_both(dot(h_two, full_fc1) + bias_fc1)
    active, slope = active.astype(BF16), slope.astype(BF16)
    active = after(active, *fc2_gather.got(5))
    fc2_gather.send(7, ready=(active,))
    fc2_product = dot(active, all_grads, TN).astype(BF16)
    fc2_scatter = Scatter(fc2_product)

    full_fc2 = fc2_gather.result()
    late_grads = after(all_grads, *fc2_scatter.got("keep"))
    grad_hidden = (dot(late_grads, full_fc2, NT) * slope.astype(F32)).astype(BF16)
    fc1_product = dot(h_two, grad_hidden, TN).astype(BF16)
    fc1_half = fc1_product.shape[1] // 2
    fc1_halves = [
        lax.dynamic_slice_in_dim(fc1_product, part * fc1_half, fc1_half, 1)
        for part in (chip, 1 - chip)
    ]
    fc1_scatter = Scatter(fc1_product, halves=fc1_halves)
    mlp_branch = sum_partner(dot(after(active, fc1_scatter.sent), full_fc2)) + bias_fc2
    residual_out = residual_mid + mlp_branch
    counted = own_valid.astype(F32)[:, None]
    squares = jnp.stack(
        [
            jnp.sum(counted * residual_out * residual_out),
            jnp.sum(counted * attn_branch * attn_branch),
            jnp.sum(counted * mlp_branch * mlp_branch),
            jnp.sum(counted),
        ]
    )
    low_output = residual_out.astype(BF16)
    grad_h_two = sum_partner(dot(after(grad_hidden, residual_out), full_fc1, NT))
    grad_residual = own_grads.astype(F32) + normalize_back(
        normal_two, scale_two, grad_h_two, gain_two
    )
    own_grad_attn = grad_residual.astype(BF16)
    grad_attn = with_partner(own_grad_attn)
    grad_out = dot(all_context, grad_attn, TN).astype(BF16)
    kept = lax.dynamic_slice_in_dim(grad_out, core * half, half, 1)
    received = swap_core(lax.dynamic_slice_in_dim(grad_out, (1 - core) * half, half, 1))
    grad_context = dot(grad_attn, full_out, NT).astype(BF16)
    halves, sums = [None, None], []

    def back_pair(pair, *ready):
        grad_mixed, parts = attend_back(
            queries[pair],
            mixed[pair // 2],
            grad_context,
            all_context,
            after(key_base, *ready),
            pair % 2,
            pair,
            halves[pair // 2],
        )
        halves[pair // 2] = grad_mixed
        sums.append(parts)

    back_pair(0, grad_context)
    grad_out = jnp.concatenate(
        in_core_order(kept, after(received, grad_context), core, 0), axis=0
    )
    ready = (sums[0], fc1_scatter.crossed) + fc2_scatter.got("side")
    fc2_scatter.near(*ready)
    fc1_scatter.cross(*ready)
    output = all_clips(after(low_output, *ready))
    back_pair(1, grad_out, *ready, *fc2_scatter.got("keep"), *fc1_scatter.got("keep"))
    early = jnp.concatenate([dot(h_one, halves[0], TN).astype(BF16), grad_out], axis=1)
    ready = (sums[1],) + fc2_scatter.got("near_sums") + fc1_scatter.got("side")
    fc2_scatter.far(*ready)
    fc1_scatter.near(*ready)
    early_scatter = Scatter(early, *ready)
    ready += fc2_scatter.got("keep") + fc1_scatter.got("keep") + early_scatter.got("keep")
    back_pair(2, *ready)
    ready = (sums[2], output) + fc2_scatter.got("far_sums") + fc1_scatter.got("near_sums")
    fc2_scatter.chips(*ready)
    fc1_scatter.far(*ready)
    back_pair(3, *ready, fc2_scatter.sums, *fc1_scatter.got("keep"))
    ready = (sums[3], fc2_scatter.other_chip) + fc1_scatter.got("far_sums")
    ready += early_scatter.got("side")
    fc1_scatter.chips(*ready)
    fc2_scatter.cores(*ready)
    early_scatter.near(*ready)
    late_scatter = Scatter(dot(after(h_one, fc1_scatter.sums, *ready), halves[1], TN))
    ready = late_scatter.got("keep")
    grad_h_one = sum_partner(
        dot(after(halves[0], *ready), full_qkv[0], NT) + dot(halves[1], full_qkv[1], NT)
    )
    own_normal, own_scale = normalize(own_inputs.astype(F32))
    input_grad = all_clips(
        (grad_residual + normalize_back(own_normal, own_scale, grad_h_one, gain_one)).astype(BF16)
    )

    def by_core(values):
        full = jnp.zeros((2, values.shape[0]), F32)
        return lax.dynamic_update_index_in_dim(full, values, core, 0).reshape(-1)

    vector_grads = [
        column_sum(grad_h_one * own_normal),
        column_sum(grad_h_one),
        by_core(jnp.concatenate([part[0] for part in sums])),
        by_core(jnp.concatenate([part[1] for part in sums])),
        column_sum(own_grad_attn),
        column_sum(grad_h_two * normal_two),
        column_sum(grad_h_two),
        column_sum(own_grads),
    ]
    hidden_sums = jnp.zeros((groups, 2, half_rows), F32)
    hidden_sums = lax.dynamic_update_index_in_dim(
        hidden_sums, column_sum(grad_hidden).reshape(groups, half_rows), core, 1
    )
    by_group = [part.reshape(groups, own_width) for part in vector_grads]
    by_group.append(hidden_sums.reshape(groups, hidden_rows))
    by_group.append(jnp.broadcast_to(squares, (groups, 4)))
    by_group = jnp.concatenate(by_group, axis=1).astype(BF16)
    by_group = jnp.pad(by_group, ((0, 0), (0, 16 * PAIR - by_group.shape[1])))
    vector_scatter = Scatter(by_group.reshape(groups * 16, PAIR))
    ready = vector_scatter.got("keep")
    late_scatter.near(*ready)
    early_scatter.far(*ready)
    vector_scatter.near()
    fc1_scatter.cores(*ready)
    late_scatter.far()
    vector_scatter.far()
    early_scatter.chips()
    vector_scatter.chips()
    late_scatter.chips()
    early_scatter.cores()
    vector_scatter.cores()
    late_scatter.cores()

    def in_columns(values, other, blocks):
        size = values.shape[1] // blocks
        parts = in_core_order(values, other, core, 0)
        parts = [part.reshape(own_width, blocks, 1, size) for part in parts]
        return jnp.concatenate(parts, axis=2).reshape(own_width, -1).astype(F32)

    fc2_grad = in_core_order(fc2_scatter.total, fc2_scatter.other_core, core, 0)
    fc2_grad = jnp.concatenate(fc2_grad, axis=0).astype(F32)
    fc1_grad = in_columns(fc1_scatter.total, fc1_scatter.other_core, groups)
    early, early_other = early_scatter.total, early_scatter.other_core
    late, late_other = late_scatter.total, late_scatter.other_core
    out_grad = in_columns(early[:, row_width:], early_other[:, row_width:], 1)

    def both_halves(left, right):
        left = left[:, :row_width].reshape(own_width, 1, 2, 3, PAIR)
        right = right.reshape(own_width, 1, 2, 3, PAIR)
        both = jnp.concatenate([left, right], axis=1).transpose(0, 3, 1, 2, 4)
        return both.reshape(own_width, 3 * half)

    qkv_grad = in_columns(both_halves(early, late), both_halves(early_other, late_other), 3)
    flat = vector_scatter.total.astype(F32) + vector_scatter.other_core.astype(F32)
    flat = flat.reshape(-1)
    own_vectors = [flat[i * own_width : (i + 1) * own_width] for i in range(8)]
    own_hidden = flat[8 * own_width : used]
    totals = flat[used : used + 4]
    branch_rms = jnp.sqrt(totals[:3] / (totals[3] * width))
    return (
        output,
        input_grad,
        own_vectors[0],
        own_vectors[1],
        qkv_grad,
        own_vectors[2],
        own_vectors[3],
        out_grad,
        own_vectors[4],
        own_vectors[5],
        own_vectors[6],
        fc1_grad,
        own_hidden,
        fc2_grad,
        own_vectors[7],
        branch_rms,
    )


def solution(mesh):
    tokens, rows, vector = P("fsdp", "seq", None), P("fsdp", None), P("fsdp")
    return jax.shard_map(
        body,
        mesh=mesh,
        in_specs=(
            tokens,
            tokens,
            rows,
            vector,
            vector,
            rows,
            vector,
            vector,
            rows,
            vector,
            vector,
            vector,
            rows,
            vector,
            rows,
            vector,
        ),
        out_specs=(
            tokens,
            tokens,
            vector,
            vector,
            rows,
            vector,
            vector,
            rows,
            vector,
            vector,
            vector,
            rows,
            vector,
            rows,
            vector,
            P(),
        ),
        check_vma=False,
    )
```

```python
from functools import partial

import jax
import jax.numpy as jnp
from jax import lax
from jax.experimental import pallas as pl
from jax.experimental.pallas import tpu as pltpu
from jax.sharding import PartitionSpec as P

HEADS = 16
HEAD = 64
PAIR = 2 * HEAD
EPS = 1e-06
MASKED = -1e30
VMEM_BYTES = 56 * 2**20
BF16 = jnp.bfloat16
F32 = jnp.float32
NN = (((1,), (0,)), ((), ()))
NT = (((1,), (1,)), ((), ()))
TN = (((0,), (0,)), ((), ()))
SMALL_COST = pl.CostEstimate(flops=10**7, bytes_accessed=2**20, transcendentals=0)


def dot(left, right, dims=NN):
    return lax.dot_general(left, right, dims, preferred_element_type=F32)


def lanes_of(shape):
    return lax.broadcasted_iota(jnp.int32, shape, len(shape) - 1)


def three_parts(column):
    high = column.astype(BF16).astype(F32)
    rest = column - high
    middle = rest.astype(BF16).astype(F32)
    return high, middle, rest - middle


def block_rows(length, *sizes):
    for rows in sizes + (224, 112, 16):
        if length % rows == 0:
            return rows
    return length


def attend_kernel(q_ref, k_ref, v_ref, key_base_ref, *refs):
    context_ref, query_ref = refs[-2:]
    length = q_ref.shape[0]
    rows = block_rows(length, 392)
    low = lanes_of((length, PAIR)) < HEAD
    keys, values, key_base = k_ref[...], v_ref[...], key_base_ref[...]
    ones = jnp.ones((length, PAIR), BF16)
    keys_of = [jnp.where(low, keys, key_base), jnp.where(low, key_base, keys)]
    values_of = [jnp.where(low, values, ones), jnp.where(low, ones, values)]
    lane = lanes_of((rows, PAIR))
    low_rows = lane < HEAD
    for step in range(length // rows):
        span = slice(step * rows, (step + 1) * rows)
        queries = q_ref[span, :]
        results = []
        for head in range(2):
            base = HEAD * (1 - head)
            own = low_rows if head == 0 else jnp.logical_not(low_rows)
            unit = jnp.where(lane == base, 1.0, 0.0)
            scores = dot(jnp.where(own, queries, unit.astype(BF16)), keys_of[head], NT)
            highest = jnp.max(scores, axis=1, keepdims=True)
            weights = jnp.exp(scores - highest).astype(BF16)
            mixed = dot(weights, values_of[head])
            total = mixed[:, base : base + 1]
            high, middle, rest = three_parts(-(highest + jnp.log(total)))
            extra = jnp.where(lane == base + 3, rest, unit)
            extra = jnp.where(lane == base + 2, middle, extra)
            extra = jnp.where(lane == base + 1, high, extra)
            query_ref[head, span, :] = jnp.where(own, queries, extra.astype(BF16))
            results.append(mixed / total)
        context_ref[span, :] = jnp.where(low_rows, results[0], results[1]).astype(BF16)


def attend(mixed, key_base, pair, context, place, places):
    length = mixed.shape[0]
    tile = lambda column: pl.BlockSpec((length, PAIR), lambda i: (0, column))
    in_specs = [tile(3 * pair), tile(3 * pair + 1), tile(3 * pair + 2), tile(0)]
    operands = (mixed, mixed, mixed, key_base)
    aliases = {}
    if context is not None:
        in_specs.append(pl.BlockSpec(memory_space=pl.ANY))
        operands += (context,)
        aliases = {4: 0}
    return pl.pallas_call(
        attend_kernel,
        grid=(1,),
        in_specs=in_specs,
        out_specs=[tile(place), pl.BlockSpec((2, length, PAIR), lambda i: (0, 0, 0))],
        out_shape=[
            jax.ShapeDtypeStruct((length, places * PAIR), BF16),
            jax.ShapeDtypeStruct((2, length, PAIR), BF16),
        ],
        input_output_aliases=aliases,
        compiler_params=pltpu.CompilerParams(vmem_limit_bytes=VMEM_BYTES),
        cost_estimate=SMALL_COST,
        name="attend",
    )(*operands)


def attend_back_kernel(query_ref, k_ref, v_ref, grad_ref, context_ref, key_base_ref, *refs):
    grad_mixed_ref, sums_ref = refs[-2:]
    length = k_ref.shape[0]
    rows = block_rows(length)
    low = lanes_of((length, PAIR)) < HEAD
    keys, values, key_base = k_ref[...], v_ref[...], key_base_ref[...]
    ones = jnp.ones((length, PAIR), BF16)
    lane = lanes_of((rows, PAIR))
    low_rows = lane < HEAD
    steps = length // rows
    grad_q, grad_k, grad_v = [], [], []
    sum_q = jnp.zeros((1, PAIR), F32)
    for head in range(2):
        base = HEAD * (1 - head)
        own = low if head == 0 else jnp.logical_not(low)
        own_rows = low_rows if head == 0 else jnp.logical_not(low_rows)
        head_keys = jnp.where(own, keys, key_base)
        head_values = jnp.where(own, values, ones)
        sum_k = jnp.zeros((length, PAIR), F32)
        sum_v = jnp.zeros((length, PAIR), F32)
        for step in range(steps):
            span = slice(step * rows, (step + 1) * rows)
            queries = query_ref[head, span, :]
            grads = grad_ref[span, :]
            product = grads.astype(F32) * context_ref[span, :].astype(F32)
            inner = jnp.sum(jnp.where(own_rows, product, 0.0), axis=1, keepdims=True)
            high, middle, rest = three_parts(-inner)
            extra = jnp.where(lane == base + 2, rest, 0.0)
            extra = jnp.where(lane == base + 1, middle, extra)
            extra = jnp.where(lane == base, high, extra)
            head_grads = jnp.where(own_rows, grads, extra.astype(BF16))
            probs = jnp.exp(dot(head_keys, queries, NT))
            grad_scores = (probs * dot(head_values, head_grads, NT)).astype(BF16)
            sum_v = sum_v + dot(probs.astype(BF16), grads)
            sum_k = sum_k + dot(grad_scores, queries)
            part = dot(grad_scores, keys, TN)
            if head == 0:
                grad_q.append(part)
            else:
                both = jnp.where(low_rows, grad_q[step], part).astype(BF16)
                both = both * (HEAD ** (-0.5))
                grad_mixed_ref[span, :PAIR] = both
                sum_q = sum_q + jnp.sum(both.astype(F32), axis=0, keepdims=True)
        grad_k.append(sum_k)
        grad_v.append(sum_v)
    grad_mixed_ref[:, PAIR : 2 * PAIR] = jnp.where(low, grad_k[0], grad_k[1]).astype(BF16)
    both = jnp.where(low, grad_v[0], grad_v[1]).astype(BF16)
    grad_mixed_ref[:, 2 * PAIR :] = both
    sums_ref[0:1, :] = sum_q
    sums_ref[1:2, :] = jnp.sum(both.astype(F32), axis=0, keepdims=True)


def attend_back(queries, mixed, grad_context, context, key_base, pair, place, grad_mixed):
    length = mixed.shape[0]
    tile = lambda column: pl.BlockSpec((length, PAIR), lambda i: (0, column))
    in_specs = [
        pl.BlockSpec((2, length, PAIR), lambda i: (0, 0, 0)),
        tile(3 * pair + 1),
        tile(3 * pair + 2),
        tile(place),
        tile(place),
        tile(0),
    ]
    operands = (queries, mixed, mixed, grad_context, context, key_base)
    aliases = {}
    if grad_mixed is not None:
        in_specs.append(pl.BlockSpec(memory_space=pl.ANY))
        operands += (grad_mixed,)
        aliases = {6: 0}
    return pl.pallas_call(
        attend_back_kernel,
        grid=(1,),
        in_specs=in_specs,
        out_specs=[
            pl.BlockSpec((length, 3 * PAIR), lambda i: (0, pair)),
            pl.BlockSpec((2, PAIR), lambda i: (0, 0)),
        ],
        out_shape=[
            jax.ShapeDtypeStruct((length, 6 * PAIR), BF16),
            jax.ShapeDtypeStruct((2, PAIR), F32),
        ],
        input_output_aliases=aliases,
        compiler_params=pltpu.CompilerParams(vmem_limit_bytes=VMEM_BYTES),
        cost_estimate=SMALL_COST,
        name="attend_back",
    )(*operands)


def normalize(values):
    center = values - jnp.mean(values, axis=-1, keepdims=True)
    spread = jnp.mean(center * center, axis=-1, keepdims=True)
    scale = lax.rsqrt(spread + EPS)
    return center * scale, scale


def normalize_back(normal, scale, grad, gain):
    inner = grad * gain
    first = jnp.mean(inner, axis=-1, keepdims=True)
    second = jnp.mean(inner * normal, axis=-1, keepdims=True)
    return scale * (inner - first - normal * second)


def gelu_both(values):
    half = 0.5 * (1.0 + lax.erf(values * (0.5**0.5)))
    density = jnp.exp(-0.5 * values * values) * (0.5 / jnp.pi) ** 0.5
    return values * half, half + values * density


def column_sum(values):
    return jnp.sum(values, axis=0, dtype=F32)


def swap_core(values):
    return lax.ppermute(values, "seq", [(0, 1), (1, 0), (2, 3), (3, 2)])


def swap_chip(values):
    return lax.ppermute(values, "seq", [(0, 2), (2, 0), (1, 3), (3, 1)])


def with_partner(values):
    return jnp.concatenate([values, swap_core(values)], axis=0)


def sum_partner(pairs, dims):
    half = pairs[0][0].shape[0] // 2
    other = sum(dot(left[half:], right, dims) for left, right in pairs).astype(BF16)
    received = swap_core(other)
    own = [after(left[:half], other) for left, _ in pairs]
    total = sum(dot(left, right, dims) for left, (_, right) in zip(own, pairs))
    return total + received.astype(F32)


def swap_group(values, bit):
    return lax.ppermute(values, "fsdp", [(i, i ^ bit) for i in range(8)])


def order_kernel(count, *refs):
    pieces, full_ref, held, arrived, sent = refs[:count], refs[count], *refs[-3:]
    group = lax.axis_index("fsdp")
    rows = full_ref.shape[0] // count
    loads = [
        pltpu.make_async_copy(piece, held.at[relative], arrived.at[relative])
        for relative, piece in enumerate(pieces)
    ]
    for load in loads:
        load.start()
    stores = []
    for relative in range(count):
        start = pl.multiple_of((group ^ relative) * rows, rows)
        store = pltpu.make_async_copy(
            held.at[relative, pl.ds(0, rows)], full_ref.at[pl.ds(start, rows)], sent.at[relative]
        )
        loads[relative].wait()
        store.start()
        stores.append(store)
    if len(refs) > count + 4:
        own_width, core = 128, lax.rem(lax.axis_index("seq"), 2)
        wide_ref, bias_ref = refs[count + 1], refs[count + 2]
        for relative in range(count):
            place = group ^ relative
            columns = pl.ds(pl.multiple_of(place * own_width, own_width), own_width)
            extra = held[relative, rows : rows + 8, :].astype(F32)
            lines = [
                extra[k : k + 1, own_width * n : own_width * (n + 1)]
                for k in range(2)
                for n in range(6)
            ]
            for n in range(8):
                wide_ref[n : n + 1, columns] = lines[n]
            for n in range(2):
                start = pl.multiple_of((place * 2 + n) * own_width, own_width)
                bias_ref[:, pl.ds(start, own_width)] = jnp.where(
                    core == 0, lines[8 + n], lines[10 + n]
                )
    for store in stores:
        store.wait()


def in_order(pieces, rows, with_vectors=False):
    count, columns = len(pieces), pieces[0].shape[1]
    out_specs = [pl.BlockSpec(memory_space=pl.ANY)]
    out_shape = [jax.ShapeDtypeStruct((count * rows, columns), pieces[0].dtype)]
    if with_vectors:
        out_specs += [pl.BlockSpec(memory_space=pltpu.VMEM)] * 2
        out_shape += [jax.ShapeDtypeStruct((8, 1024), F32), jax.ShapeDtypeStruct((1, 2048), F32)]
    result = pl.pallas_call(
        partial(order_kernel, count),
        in_specs=[pl.BlockSpec(memory_space=pl.ANY)] * count,
        out_specs=out_specs,
        out_shape=out_shape,
        scratch_shapes=[
            pltpu.VMEM((count,) + pieces[0].shape, pieces[0].dtype),
            pltpu.SemaphoreType.DMA((count,)),
            pltpu.SemaphoreType.DMA((count,)),
        ],
        compiler_params=pltpu.CompilerParams(vmem_limit_bytes=16 * 2**20),
        cost_estimate=SMALL_COST,
        name="in_order",
    )(*pieces)
    return result if with_vectors else result[0]


def own_kernel(qkv_ref, out_ref, *refs):
    vector_refs, (first_ref, second_ref) = refs[:-2], refs[-2:]
    core = lax.rem(lax.axis_index("seq"), 2)
    rows = qkv_ref.shape[0]
    for n in range(3):
        for pair in range(4):
            block_ref = second_ref if pair >= 2 else first_ref
            start = pl.multiple_of((8 * n + pair + 4 * core) * PAIR, PAIR)
            target = (3 * (pair % 2) + n) * PAIR
            block_ref[:rows, target : target + PAIR] = qkv_ref[:, pl.ds(start, PAIR)]
    out_half = out_ref.shape[1] // 2
    start = pl.multiple_of(core * out_half, out_half)
    second_ref[:, 6 * PAIR :] = out_ref[:, pl.ds(start, out_half)]
    lines = []
    for ref in vector_refs:
        vector = ref[...].astype(F32).reshape(ref.shape[0] // PAIR, PAIR)
        lines += [vector[n : n + 1] for n in range(ref.shape[0] // PAIR)]
    row = lax.broadcasted_iota(jnp.int32, (8, PAIR), 0)
    for n in range(6):
        block = jnp.where(row == 0, lines[n], jnp.where(row == 1, lines[n + 6], 0.0))
        first_ref[rows:, PAIR * n : PAIR * (n + 1)] = block.astype(BF16)


def own_qkv_blocks(qkv_weight, out_weight, vectors):
    rows, columns = qkv_weight.shape[0], qkv_weight.shape[1] // 4
    out_half = out_weight.shape[1] // 2
    return pl.pallas_call(
        own_kernel,
        in_specs=[pl.BlockSpec(memory_space=pltpu.VMEM)] * (2 + len(vectors)),
        out_specs=[pl.BlockSpec(memory_space=pltpu.VMEM)] * 2,
        out_shape=[
            jax.ShapeDtypeStruct((rows + 8, columns), BF16),
            jax.ShapeDtypeStruct((rows, columns + out_half), BF16),
        ],
        cost_estimate=SMALL_COST,
        name="own_qkv",
    )(qkv_weight, out_weight, *vectors)


def after(values, *others):
    return lax.optimization_barrier((values,) + others)[0] if others else values


class Gather:
    SOURCE = {4: 0, 2: 0, 1: 0, 6: 4, 3: 2, 5: 4, 7: 6}
    STEP = {4: 4, 2: 2, 1: 1, 6: 2, 3: 1, 5: 1, 7: 1}

    def __init__(self, own):
        self.pieces = [own] + [None] * 7
        self.grouped = lax.axis_size("fsdp") == 8

    def send(self, *parts, ready=()):
        if not self.grouped:
            return
        sources = [self.pieces[self.SOURCE[part]] for part in parts]
        if ready:
            sources = lax.optimization_barrier(tuple(sources) + tuple(ready))
        for part, source in zip(parts, sources):
            self.pieces[part] = swap_group(source, self.STEP[part])

    def got(self, *parts):
        return tuple(self.pieces[part] for part in parts) if self.grouped else ()

    def result(self):
        if not self.grouped:
            return lax.all_gather(self.pieces[0], "fsdp", axis=0, tiled=True)
        return in_order(self.pieces, self.pieces[0].shape[0])


def add_low(left, right):
    return (left.astype(F32) + right.astype(F32)).astype(BF16)


def split_kernel(full_ref, *refs):
    sems = refs[2]
    group = lax.axis_index("fsdp")
    rows = full_ref.shape[0] // 8
    copies = []
    for n in range(8):
        far, near, side = n % 2, (n // 2) % 2, n // 4
        start = pl.multiple_of((group ^ (4 * far + 2 * near + side)) * rows, rows)
        target = refs[side].at[pl.ds((n % 4) * rows, rows)]
        copies.append(
            pltpu.make_async_copy(full_ref.at[pl.ds(start, rows)], target, sems.at[n])
        )
    for copy in copies:
        copy.start()
    for copy in copies:
        copy.wait()


def split_blocks(values):
    rows, columns = values.shape
    return pl.pallas_call(
        split_kernel,
        in_specs=[pl.BlockSpec(memory_space=pltpu.VMEM)],
        out_specs=[pl.BlockSpec(memory_space=pl.ANY)] * 2,
        out_shape=[jax.ShapeDtypeStruct((rows // 2, columns), values.dtype)] * 2,
        scratch_shapes=[pltpu.SemaphoreType.DMA((8,))],
        compiler_params=pltpu.CompilerParams(vmem_limit_bytes=16 * 2**20),
        cost_estimate=SMALL_COST,
        name="split_blocks",
    )(values)


class Scatter:
    def __init__(self, values, *ready, halves=None):
        self.grouped = lax.axis_size("fsdp") == 8
        self.halved = halves is not None
        values = values.astype(BF16)
        if self.halved:
            self.kept, self.sent = halves
            self.crossed = swap_chip(self.sent)
        elif self.grouped:
            self.keep, self.side_send = split_blocks(values)
            self.side = swap_group(after(self.side_send, *ready), 1)
        else:
            self.sums = lax.psum_scatter(values, "fsdp", scatter_dimension=0, tiled=True)

    def cross(self, *ready):
        values = add_low(self.kept, after(self.crossed, *ready))
        if self.grouped:
            self.keep, self.side_send = split_blocks(values)
            self.side = swap_group(self.side_send, 1)
        else:
            self.sums = lax.psum_scatter(values, "fsdp", scatter_dimension=0, tiled=True)

    def got(self, *names):
        return tuple(getattr(self, name) for name in names if hasattr(self, name))

    def step(self, name, next_name, bit, ready):
        if self.grouped:
            received = after(getattr(self, name), *ready)
            half = self.keep.shape[0] // 2
            send = add_low(self.keep[half:], received[half:])
            self.keep = add_low(self.keep[:half], received[:half])
            setattr(self, next_name, swap_group(send, bit))

    def near(self, *ready):
        self.step("side", "near_sums", 2, ready)

    def far(self, *ready):
        self.step("near_sums", "far_sums", 4, ready)

    def chips(self, *ready):
        if self.grouped:
            self.sums = add_low(self.keep, after(self.far_sums, *ready))
        self.other_chip = swap_chip(self.sums)

    def cores(self, *ready):
        other_chip = after(self.other_chip, *ready)
        if self.halved:
            chip = lax.axis_index("seq") // 2
            first = jnp.where(chip == 0, self.sums, other_chip)
            second = jnp.where(chip == 0, other_chip, self.sums)
            self.total = jnp.concatenate([first, second], axis=1)
        else:
            self.total = add_low(self.sums, other_chip)
        self.other_core = swap_core(self.total)

    def finish(self):
        self.near()
        self.far()
        self.chips()
        self.cores()


def take(values, index):
    return lax.dynamic_index_in_dim(values, index, 0, keepdims=False)


def in_core_order(own, other, core, axis):
    first = jnp.where(core == 0, own, other)
    second = jnp.where(core == 0, other, own)
    return first, second


def body(
    inputs,
    cotangent,
    valid,
    ln1_gain,
    ln1_bias,
    qkv_weight,
    q_bias,
    v_bias,
    out_weight,
    out_bias,
    ln2_gain,
    ln2_bias,
    fc1_weight,
    fc1_bias,
    fc2_weight,
    fc2_bias,
):
    clips, rows, width = inputs.shape
    groups = lax.axis_size("fsdp")
    place = lax.axis_index("seq")
    group = lax.axis_index("fsdp")
    chip, core = place // 2, place % 2
    half = width // 2
    hidden_rows = fc2_weight.shape[0]
    half_rows = hidden_rows // 2
    own_rows = clips * rows
    scale_factor = HEAD ** (-0.5)

    def all_clips(values, *ready):
        mine, back = values[:rows], swap_chip(values[rows:])
        back = after(back, *ready)
        first = jnp.where(chip == 0, mine, back)
        second = jnp.where(chip == 0, back, mine)
        return jnp.stack([first, second])

    own_width = width // groups
    vectors = (ln1_gain, ln1_bias, q_bias, v_bias, out_bias, ln2_gain, ln2_bias, fc2_bias, fc1_bias)
    quarter = half // 2
    row_width = 3 * quarter
    used = 8 * own_width + fc1_bias.shape[0]
    if groups == 8:
        own_first, own_second = own_qkv_blocks(qkv_weight, out_weight, vectors)
    else:
        by_head = qkv_weight.reshape(own_width, 3, 2, 2, 2, PAIR)
        by_head = lax.dynamic_index_in_dim(by_head, core, 2, keepdims=False)
        by_head = by_head.transpose(0, 2, 3, 1, 4).reshape(own_width, 2, row_width)
        out_columns = lax.dynamic_slice_in_dim(out_weight, core * half, half, 1)
        own_first = by_head[:, 0]
        own_second = jnp.concatenate([by_head[:, 1], out_columns], axis=1)

    own_fc1 = lax.dynamic_index_in_dim(
        fc1_weight.reshape(own_width, groups, 2, half_rows), core, 2, keepdims=False
    ).reshape(own_width, groups * half_rows)
    own_fc2 = lax.dynamic_slice_in_dim(fc2_weight, core * half_rows, half_rows, 0)

    qkv_a, qkv_b = Gather(own_first), Gather(own_second)
    fc1_gather, fc2_gather = Gather(own_fc1), Gather(own_fc2)
    qkv_a.send(4, 2, 1)
    other_inputs = swap_chip(after(take(inputs, 1 - chip), own_first))
    qkv_a.send(6, 3, 5, ready=qkv_a.got(4, 2, 1) + (own_fc1, own_fc2))
    qkv_b.send(4, ready=qkv_a.got(4, 2, 1))
    qkv_a.send(7, ready=qkv_a.got(6, 3, 5))
    other_inputs = after(other_inputs, *qkv_a.got(6, 3, 5))
    qkv_b.send(2, 1, ready=qkv_a.got(6, 3, 5))
    own_inputs = jnp.concatenate([take(inputs, chip), other_inputs], axis=0)
    all_inputs = with_partner(own_inputs)
    if groups == 8:
        qkv_first, wide, bias_fc1 = in_order(qkv_a.pieces, own_width, True)
    else:
        qkv_first = qkv_a.result()
        packed = lax.all_gather(jnp.concatenate(vectors), "fsdp", axis=0)
        wide = [
            packed[:, i * own_width : (i + 1) * own_width].reshape(width).astype(F32)
            for i in range(8)
        ]
        bias_fc1 = packed[:, 8 * own_width : used].reshape(groups, 2, half_rows)
        bias_fc1 = take(jnp.moveaxis(bias_fc1, 1, 0), core)
        bias_fc1 = bias_fc1.reshape(groups * half_rows).astype(F32)
    gain_one, bias_one, bias_q, bias_v, bias_out, gain_two, bias_two, bias_fc2 = [
        wide[i] for i in range(8)
    ]
    bias_q = take(bias_q.reshape(2, 2, 2, PAIR), core)
    bias_v = take(bias_v.reshape(2, 2, 2, PAIR), core)
    bias_mixed = jnp.stack([bias_q, jnp.zeros_like(bias_q), bias_v], axis=2).reshape(2, row_width)
    scale_mixed = jnp.array([scale_factor, 1.0, 1.0] * 2, F32).repeat(PAIR)
    clip_valid = take(valid, chip).reshape(2 * clips, rows)
    own_valid = jnp.concatenate([take(clip_valid, place), take(clip_valid, place ^ 2)])
    other_valid = jnp.concatenate([take(clip_valid, place ^ 1), take(clip_valid, place ^ 3)])
    key_valid = jnp.concatenate([own_valid, other_valid])
    lane = jnp.arange(PAIR) % HEAD
    key_mask = jnp.where(key_valid > 0, 0.0, MASKED)[:, None]
    key_base = jnp.where(lane == 0, key_mask, jnp.where(lane < 4, 1.0, 0.0)).astype(BF16)


    def project(weight, i):
        return ((dot(h_one, weight) + bias_mixed[i]) * scale_mixed).astype(BF16)

    normal_one = normalize(all_inputs.astype(F32))[0]
    h_one = (normal_one * gain_one + bias_one).astype(BF16)
    mixed = [project(qkv_first, 0)]
    context, queries = [], []

    def attend_pair(pair, *ready):
        before = context[-1] if context else None
        base = after(key_base, *ready)
        results = attend(mixed[pair // 2], base, pair % 2, before, pair, 4)
        context.append(results[0])
        queries.append(results[1])

    ready = (mixed[0],) + qkv_b.got(4, 2, 1)
    qkv_b.send(6, 3, 5, ready=ready)
    fc1_gather.send(4, ready=ready)
    attend_pair(0, *ready)
    ready = (queries[0],) + qkv_b.got(6, 3, 5)
    qkv_b.send(7, ready=ready)
    fc1_gather.send(2, 1, ready=ready)
    attend_pair(1, *ready)
    second_columns = qkv_b.result()
    mixed.append(project(second_columns[:, :row_width], 1))
    ready = (queries[1], mixed[1]) + fc1_gather.got(4, 2, 1)
    fc1_gather.send(6, 3, 5, ready=ready)
    fc2_gather.send(4, ready=ready)
    kept = lax.dynamic_slice(second_columns, (core * half, row_width), (half, half))
    received = lax.dynamic_slice(second_columns, ((1 - core) * half, row_width), (half, half))
    received = swap_core(after(received, mixed[1]))
    attend_pair(2, kept, *ready)
    ready = (queries[2], received) + fc1_gather.got(6, 3, 5)
    fc1_gather.send(7, ready=ready)
    fc2_gather.send(2, ready=ready)
    other_grads = swap_chip(after(take(cotangent, 1 - chip), *ready))
    attend_pair(3, *ready)
    own_grads = jnp.concatenate([take(cotangent, chip), after(other_grads, queries[3])], axis=0)
    full_out = jnp.concatenate(in_core_order(kept, received, core, 1), axis=1)
    full_qkv = (qkv_first, second_columns[:, :row_width])
    ready = (own_grads, queries[3]) + fc2_gather.got(4, 2) + fc1_gather.got(7)
    all_context = after(context[3], *ready)
    fc2_gather.send(1, 3, 6, ready=ready)
    attn_branch = sum_partner([(all_context, full_out)], NN) + bias_out
    residual_mid = own_inputs.astype(F32) + attn_branch
    normal_two, scale_two = normalize(residual_mid)
    h_two = with_partner((normal_two * gain_two + bias_two).astype(BF16))
    all_grads = with_partner(after(own_grads, residual_mid))
    full_fc1 = fc1_gather.result()
    h_two = after(h_two, *fc2_gather.got(1, 3, 6))
    fc2_gather.send(5, ready=(h_two,))
    active, slope = gelu_both(dot(h_two, full_fc1) + bias_fc1)
    active, slope = active.astype(BF16), slope.astype(BF16)
    active = after(active, *fc2_gather.got(5))
    fc2_gather.send(7, ready=(active,))
    fc2_product = dot(active, all_grads, TN).astype(BF16)
    fc2_scatter = Scatter(fc2_product)

    full_fc2 = fc2_gather.result()
    late_grads = after(all_grads, *fc2_scatter.got("keep"))
    grad_hidden = (dot(late_grads, full_fc2, NT) * slope.astype(F32)).astype(BF16)
    fc1_product = dot(h_two, grad_hidden, TN).astype(BF16)
    fc1_half = fc1_product.shape[1] // 2
    fc1_halves = [
        lax.dynamic_slice_in_dim(fc1_product, part * fc1_half, fc1_half, 1)
        for part in (chip, 1 - chip)
    ]
    fc1_scatter = Scatter(fc1_product, halves=fc1_halves)
    mlp_branch = sum_partner([(after(active, fc1_scatter.sent), full_fc2)], NN) + bias_fc2
    residual_out = residual_mid + mlp_branch
    counted = own_valid.astype(F32)[:, None]
    squares = jnp.stack(
        [
            jnp.sum(counted * residual_out * residual_out),
            jnp.sum(counted * attn_branch * attn_branch),
            jnp.sum(counted * mlp_branch * mlp_branch),
            jnp.sum(counted),
        ]
    )
    low_output = residual_out.astype(BF16)
    grad_h_two = sum_partner([(after(grad_hidden, residual_out), full_fc1)], NT)
    grad_residual = own_grads.astype(F32) + normalize_back(
        normal_two, scale_two, grad_h_two, gain_two
    )
    own_grad_attn = grad_residual.astype(BF16)
    grad_attn = with_partner(own_grad_attn)
    grad_out = dot(all_context, grad_attn, TN).astype(BF16)
    kept = lax.dynamic_slice_in_dim(grad_out, core * half, half, 1)
    received = swap_core(lax.dynamic_slice_in_dim(grad_out, (1 - core) * half, half, 1))
    grad_context = dot(grad_attn, full_out, NT).astype(BF16)
    halves, sums = [None, None], []

    def back_pair(pair, *ready):
        grad_mixed, parts = attend_back(
            queries[pair],
            mixed[pair // 2],
            grad_context,
            all_context,
            after(key_base, *ready),
            pair % 2,
            pair,
            halves[pair // 2],
        )
        halves[pair // 2] = grad_mixed
        sums.append(parts)

    back_pair(0, grad_context)
    grad_out = jnp.concatenate(
        in_core_order(kept, after(received, grad_context), core, 0), axis=0
    )
    ready = (sums[0], fc1_scatter.crossed) + fc2_scatter.got("side")
    fc2_scatter.near(*ready)
    fc1_scatter.cross(*ready)
    low_output = after(low_output, *ready)
    back_pair(1, grad_out, *ready, *fc2_scatter.got("keep"), *fc1_scatter.got("keep"))
    early = jnp.concatenate([dot(h_one, halves[0], TN).astype(BF16), grad_out], axis=1)
    ready = (sums[1],) + fc2_scatter.got("near_sums") + fc1_scatter.got("side")
    fc2_scatter.far(*ready)
    fc1_scatter.near(*ready)
    early_scatter = Scatter(early, *ready)
    ready += fc2_scatter.got("keep") + fc1_scatter.got("keep") + early_scatter.got("keep")
    back_pair(2, *ready)
    output = all_clips(low_output, sums[2])
    ready = (sums[2],) + fc2_scatter.got("far_sums") + fc1_scatter.got("near_sums")
    fc2_scatter.chips(*ready)
    fc1_scatter.far(*ready)
    back_pair(3, *ready, fc2_scatter.sums, *fc1_scatter.got("keep"))
    ready = (sums[3], fc2_scatter.other_chip) + fc1_scatter.got("far_sums")
    ready += early_scatter.got("side")
    fc1_scatter.chips(*ready)
    fc2_scatter.cores(*ready)
    early_scatter.near(*ready)
    late_scatter = Scatter(dot(after(h_one, fc1_scatter.sums, *ready), halves[1], TN))
    ready = late_scatter.got("keep")
    grad_h_one = sum_partner(
        [(after(halves[0], *ready), full_qkv[0]), (halves[1], full_qkv[1])], NT
    )
    late_scatter.near()
    grad_h_one = after(grad_h_one, *late_scatter.got("keep"))
    own_normal, own_scale = normalize(own_inputs.astype(F32))
    low_input_grad = (
        grad_residual + normalize_back(own_normal, own_scale, grad_h_one, gain_one)
    ).astype(BF16)
    input_grad = all_clips(low_input_grad)

    def by_core(values):
        full = jnp.zeros((2, values.shape[0]), F32)
        return lax.dynamic_update_index_in_dim(full, values, core, 0).reshape(-1)

    vector_grads = [
        column_sum(grad_h_one * own_normal),
        column_sum(grad_h_one),
        by_core(jnp.concatenate([part[0] for part in sums])),
        by_core(jnp.concatenate([part[1] for part in sums])),
        column_sum(own_grad_attn),
        column_sum(grad_h_two * normal_two),
        column_sum(grad_h_two),
        column_sum(own_grads),
    ]
    hidden_sums = jnp.zeros((groups, 2, half_rows), F32)
    hidden_sums = lax.dynamic_update_index_in_dim(
        hidden_sums, column_sum(grad_hidden).reshape(groups, half_rows), core, 1
    )
    by_group = [part.reshape(groups, own_width) for part in vector_grads]
    by_group.append(hidden_sums.reshape(groups, hidden_rows))
    by_group.append(jnp.broadcast_to(squares, (groups, 4)))
    by_group = jnp.concatenate(by_group, axis=1).astype(BF16)
    by_group = jnp.pad(by_group, ((0, 0), (0, 16 * PAIR - by_group.shape[1])))
    by_group = after(by_group, *late_scatter.got("near_sums"))
    vector_scatter = Scatter(by_group.reshape(groups * 16, PAIR))
    ready = vector_scatter.got("keep")
    early_scatter.far(*ready)
    late_scatter.far(*ready)
    vector_scatter.near()
    fc1_scatter.cores(*ready)
    vector_scatter.far()
    early_scatter.chips()
    vector_scatter.chips()
    late_scatter.chips(input_grad)
    early_scatter.cores()
    vector_scatter.cores()
    late_scatter.cores()

    def in_columns(values, other, blocks):
        size = values.shape[1] // blocks
        parts = in_core_order(values, other, core, 0)
        parts = [part.reshape(own_width, blocks, 1, size) for part in parts]
        return jnp.concatenate(parts, axis=2).reshape(own_width, -1).astype(F32)

    fc2_grad = in_core_order(fc2_scatter.total, fc2_scatter.other_core, core, 0)
    fc2_grad = jnp.concatenate(fc2_grad, axis=0).astype(F32)
    fc1_grad = in_columns(fc1_scatter.total, fc1_scatter.other_core, groups)
    early, early_other = early_scatter.total, early_scatter.other_core
    late, late_other = late_scatter.total, late_scatter.other_core
    out_grad = in_columns(early[:, row_width:], early_other[:, row_width:], 1)

    def both_halves(left, right):
        left = left[:, :row_width].reshape(own_width, 1, 2, 3, PAIR)
        right = right.reshape(own_width, 1, 2, 3, PAIR)
        both = jnp.concatenate([left, right], axis=1).transpose(0, 3, 1, 2, 4)
        return both.reshape(own_width, 3 * half)

    qkv_grad = in_columns(both_halves(early, late), both_halves(early_other, late_other), 3)
    flat = vector_scatter.total.astype(F32) + vector_scatter.other_core.astype(F32)
    flat = flat.reshape(-1)
    own_vectors = [flat[i * own_width : (i + 1) * own_width] for i in range(8)]
    own_hidden = flat[8 * own_width : used]
    totals = flat[used : used + 4]
    branch_rms = jnp.sqrt(totals[:3] / (totals[3] * width))
    return (
        output,
        input_grad,
        own_vectors[0],
        own_vectors[1],
        qkv_grad,
        own_vectors[2],
        own_vectors[3],
        out_grad,
        own_vectors[4],
        own_vectors[5],
        own_vectors[6],
        fc1_grad,
        own_hidden,
        fc2_grad,
        own_vectors[7],
        branch_rms,
    )


def solution(mesh):
    tokens, rows, vector = P("fsdp", "seq", None), P("fsdp", None), P("fsdp")
    return jax.shard_map(
        body,
        mesh=mesh,
        in_specs=(
            tokens,
            tokens,
            rows,
            vector,
            vector,
            rows,
            vector,
            vector,
            rows,
            vector,
            vector,
            vector,
            rows,
            vector,
            rows,
            vector,
        ),
        out_specs=(
            tokens,
            tokens,
            vector,
            vector,
            rows,
            vector,
            vector,
            rows,
            vector,
            vector,
            vector,
            rows,
            vector,
            rows,
            vector,
            P(),
        ),
        check_vma=False,
    )
```

```python
from functools import partial

import jax
import jax.numpy as jnp
from jax import lax
from jax.experimental import pallas as pl
from jax.experimental.pallas import tpu as pltpu
from jax.sharding import PartitionSpec as P

HEADS = 16
HEAD = 64
PAIR = 2 * HEAD
EPS = 1e-06
MASKED = -1e30
VMEM_BYTES = 28 * 2**20
BF16 = jnp.bfloat16
F32 = jnp.float32
NN = (((1,), (0,)), ((), ()))
NT = (((1,), (1,)), ((), ()))
TN = (((0,), (0,)), ((), ()))
SMALL_COST = pl.CostEstimate(flops=10**7, bytes_accessed=2**20, transcendentals=0)


def dot(left, right, dims=NN):
    return lax.dot_general(left, right, dims, preferred_element_type=F32)


def lanes_of(shape):
    return lax.broadcasted_iota(jnp.int32, shape, len(shape) - 1)


def three_parts(column):
    high = column.astype(BF16).astype(F32)
    rest = column - high
    middle = rest.astype(BF16).astype(F32)
    return high, middle, rest - middle


def block_rows(length, *sizes):
    for rows in sizes + (224, 112, 16):
        if length % rows == 0:
            return rows
    return length


def attend_kernel(q_ref, k_ref, v_ref, key_base_ref, *refs):
    context_ref, query_ref = refs[-2:]
    length = q_ref.shape[0]
    rows = block_rows(length, 392)
    low = lanes_of((length, PAIR)) < HEAD
    keys, values, key_base = k_ref[...], v_ref[...], key_base_ref[...]
    ones = jnp.ones((length, PAIR), BF16)
    keys_of = [jnp.where(low, keys, key_base), jnp.where(low, key_base, keys)]
    values_of = [jnp.where(low, values, ones), jnp.where(low, ones, values)]
    lane = lanes_of((rows, PAIR))
    low_rows = lane < HEAD
    for step in range(length // rows):
        span = slice(step * rows, (step + 1) * rows)
        queries = q_ref[span, :]
        results = []
        for head in range(2):
            base = HEAD * (1 - head)
            own = low_rows if head == 0 else jnp.logical_not(low_rows)
            unit = jnp.where(lane == base, 1.0, 0.0)
            scores = dot(jnp.where(own, queries, unit.astype(BF16)), keys_of[head], NT)
            highest = jnp.max(scores, axis=1, keepdims=True)
            weights = jnp.exp(scores - highest).astype(BF16)
            mixed = dot(weights, values_of[head])
            total = mixed[:, base : base + 1]
            high, middle, rest = three_parts(-(highest + jnp.log(total)))
            extra = jnp.where(lane == base + 3, rest, unit)
            extra = jnp.where(lane == base + 2, middle, extra)
            extra = jnp.where(lane == base + 1, high, extra)
            query_ref[head, span, :] = jnp.where(own, queries, extra.astype(BF16))
            results.append(mixed / total)
        context_ref[span, :] = jnp.where(low_rows, results[0], results[1]).astype(BF16)


def attend(mixed, key_base, pair, context, place, places):
    length = mixed.shape[0]
    tile = lambda column: pl.BlockSpec((length, PAIR), lambda i: (0, column))
    in_specs = [tile(3 * pair), tile(3 * pair + 1), tile(3 * pair + 2), tile(0)]
    operands = (mixed, mixed, mixed, key_base)
    aliases = {}
    if context is not None:
        in_specs.append(pl.BlockSpec(memory_space=pl.ANY))
        operands += (context,)
        aliases = {4: 0}
    return pl.pallas_call(
        attend_kernel,
        grid=(1,),
        in_specs=in_specs,
        out_specs=[tile(place), pl.BlockSpec((2, length, PAIR), lambda i: (0, 0, 0))],
        out_shape=[
            jax.ShapeDtypeStruct((length, places * PAIR), BF16),
            jax.ShapeDtypeStruct((2, length, PAIR), BF16),
        ],
        input_output_aliases=aliases,
        compiler_params=pltpu.CompilerParams(vmem_limit_bytes=VMEM_BYTES),
        cost_estimate=SMALL_COST,
        name="attend",
    )(*operands)


def attend_back_kernel(query_ref, k_ref, v_ref, grad_ref, context_ref, key_base_ref, *refs):
    grad_mixed_ref, sums_ref = refs[-2:]
    length = k_ref.shape[0]
    rows = block_rows(length)
    low = lanes_of((length, PAIR)) < HEAD
    keys, values, key_base = k_ref[...], v_ref[...], key_base_ref[...]
    ones = jnp.ones((length, PAIR), BF16)
    lane = lanes_of((rows, PAIR))
    low_rows = lane < HEAD
    steps = length // rows
    grad_q, grad_k, grad_v = [], [], []
    sum_q = jnp.zeros((1, PAIR), F32)
    for head in range(2):
        base = HEAD * (1 - head)
        own = low if head == 0 else jnp.logical_not(low)
        own_rows = low_rows if head == 0 else jnp.logical_not(low_rows)
        head_keys = jnp.where(own, keys, key_base)
        head_values = jnp.where(own, values, ones)
        sum_k = jnp.zeros((length, PAIR), F32)
        sum_v = jnp.zeros((length, PAIR), F32)
        for step in range(steps):
            span = slice(step * rows, (step + 1) * rows)
            queries = query_ref[head, span, :]
            grads = grad_ref[span, :]
            product = grads.astype(F32) * context_ref[span, :].astype(F32)
            inner = jnp.sum(jnp.where(own_rows, product, 0.0), axis=1, keepdims=True)
            high, middle, rest = three_parts(-inner)
            extra = jnp.where(lane == base + 2, rest, 0.0)
            extra = jnp.where(lane == base + 1, middle, extra)
            extra = jnp.where(lane == base, high, extra)
            head_grads = jnp.where(own_rows, grads, extra.astype(BF16))
            probs = jnp.exp(dot(head_keys, queries, NT))
            grad_scores = (probs * dot(head_values, head_grads, NT)).astype(BF16)
            sum_v = sum_v + dot(probs.astype(BF16), grads)
            sum_k = sum_k + dot(grad_scores, queries)
            part = dot(grad_scores, keys, TN)
            if head == 0:
                grad_q.append(part)
            else:
                both = jnp.where(low_rows, grad_q[step], part).astype(BF16)
                both = both * (HEAD ** (-0.5))
                grad_mixed_ref[span, :PAIR] = both
                sum_q = sum_q + jnp.sum(both.astype(F32), axis=0, keepdims=True)
        grad_k.append(sum_k)
        grad_v.append(sum_v)
    grad_mixed_ref[:, PAIR : 2 * PAIR] = jnp.where(low, grad_k[0], grad_k[1]).astype(BF16)
    both = jnp.where(low, grad_v[0], grad_v[1]).astype(BF16)
    grad_mixed_ref[:, 2 * PAIR :] = both
    sums_ref[0:1, :] = sum_q
    sums_ref[1:2, :] = jnp.sum(both.astype(F32), axis=0, keepdims=True)


def attend_back(queries, mixed, grad_context, context, key_base, pair, place, grad_mixed):
    length = mixed.shape[0]
    tile = lambda column: pl.BlockSpec((length, PAIR), lambda i: (0, column))
    in_specs = [
        pl.BlockSpec((2, length, PAIR), lambda i: (0, 0, 0)),
        tile(3 * pair + 1),
        tile(3 * pair + 2),
        tile(place),
        tile(place),
        tile(0),
    ]
    operands = (queries, mixed, mixed, grad_context, context, key_base)
    aliases = {}
    if grad_mixed is not None:
        in_specs.append(pl.BlockSpec(memory_space=pl.ANY))
        operands += (grad_mixed,)
        aliases = {6: 0}
    return pl.pallas_call(
        attend_back_kernel,
        grid=(1,),
        in_specs=in_specs,
        out_specs=[
            pl.BlockSpec((length, 3 * PAIR), lambda i: (0, pair)),
            pl.BlockSpec((2, PAIR), lambda i: (0, 0)),
        ],
        out_shape=[
            jax.ShapeDtypeStruct((length, 6 * PAIR), BF16),
            jax.ShapeDtypeStruct((2, PAIR), F32),
        ],
        input_output_aliases=aliases,
        compiler_params=pltpu.CompilerParams(vmem_limit_bytes=VMEM_BYTES),
        cost_estimate=SMALL_COST,
        name="attend_back",
    )(*operands)


def normalize(values):
    center = values - jnp.mean(values, axis=-1, keepdims=True)
    spread = jnp.mean(center * center, axis=-1, keepdims=True)
    scale = lax.rsqrt(spread + EPS)
    return center * scale, scale


def normalize_back(normal, scale, grad, gain):
    inner = grad * gain
    first = jnp.mean(inner, axis=-1, keepdims=True)
    second = jnp.mean(inner * normal, axis=-1, keepdims=True)
    return scale * (inner - first - normal * second)


def gelu_both(values):
    half = 0.5 * (1.0 + lax.erf(values * (0.5**0.5)))
    density = jnp.exp(-0.5 * values * values) * (0.5 / jnp.pi) ** 0.5
    return values * half, half + values * density


def column_sum(values):
    return jnp.sum(values, axis=0, dtype=F32)


def swap_core(values):
    return lax.ppermute(values, "seq", [(0, 1), (1, 0), (2, 3), (3, 2)])


def swap_chip(values):
    return lax.ppermute(values, "seq", [(0, 2), (2, 0), (1, 3), (3, 1)])


def with_partner(values):
    return jnp.concatenate([values, swap_core(values)], axis=0)


def sum_partner(pairs, dims):
    half = pairs[0][0].shape[0] // 2
    other = sum(dot(left[half:], right, dims) for left, right in pairs).astype(BF16)
    received = swap_core(other)
    own = [after(left[:half], other) for left, _ in pairs]
    total = sum(dot(left, right, dims) for left, (_, right) in zip(own, pairs))
    return total + received.astype(F32)


def swap_group(values, bit):
    return lax.ppermute(values, "fsdp", [(i, i ^ bit) for i in range(8)])


def order_kernel(count, *refs):
    pieces, full_ref, held, arrived, sent = refs[:count], refs[count], *refs[-3:]
    group = lax.axis_index("fsdp")
    rows = full_ref.shape[0] // count
    loads = [
        pltpu.make_async_copy(piece, held.at[relative], arrived.at[relative])
        for relative, piece in enumerate(pieces)
    ]
    for load in loads:
        load.start()
    stores = []
    for relative in range(count):
        start = pl.multiple_of((group ^ relative) * rows, rows)
        store = pltpu.make_async_copy(
            held.at[relative, pl.ds(0, rows)], full_ref.at[pl.ds(start, rows)], sent.at[relative]
        )
        loads[relative].wait()
        store.start()
        stores.append(store)
    if len(refs) > count + 4:
        own_width, core = 128, lax.rem(lax.axis_index("seq"), 2)
        wide_ref, bias_ref = refs[count + 1], refs[count + 2]
        for relative in range(count):
            place = group ^ relative
            columns = pl.ds(pl.multiple_of(place * own_width, own_width), own_width)
            extra = held[relative, rows : rows + 8, :].astype(F32)
            lines = [
                extra[k : k + 1, own_width * n : own_width * (n + 1)]
                for k in range(2)
                for n in range(6)
            ]
            for n in range(8):
                wide_ref[n : n + 1, columns] = lines[n]
            for n in range(2):
                start = pl.multiple_of((place * 2 + n) * own_width, own_width)
                bias_ref[:, pl.ds(start, own_width)] = jnp.where(
                    core == 0, lines[8 + n], lines[10 + n]
                )
    for store in stores:
        store.wait()


def in_order(pieces, rows, with_vectors=False):
    count, columns = len(pieces), pieces[0].shape[1]
    out_specs = [pl.BlockSpec(memory_space=pl.ANY)]
    out_shape = [jax.ShapeDtypeStruct((count * rows, columns), pieces[0].dtype)]
    if with_vectors:
        out_specs += [pl.BlockSpec(memory_space=pltpu.VMEM)] * 2
        out_shape += [jax.ShapeDtypeStruct((8, 1024), F32), jax.ShapeDtypeStruct((1, 2048), F32)]
    result = pl.pallas_call(
        partial(order_kernel, count),
        in_specs=[pl.BlockSpec(memory_space=pl.ANY)] * count,
        out_specs=out_specs,
        out_shape=out_shape,
        scratch_shapes=[
            pltpu.VMEM((count,) + pieces[0].shape, pieces[0].dtype),
            pltpu.SemaphoreType.DMA((count,)),
            pltpu.SemaphoreType.DMA((count,)),
        ],
        compiler_params=pltpu.CompilerParams(vmem_limit_bytes=16 * 2**20),
        cost_estimate=SMALL_COST,
        name="in_order",
    )(*pieces)
    return result if with_vectors else result[0]


def own_kernel(qkv_ref, out_ref, *refs):
    vector_refs, (first_ref, second_ref) = refs[:-2], refs[-2:]
    core = lax.rem(lax.axis_index("seq"), 2)
    rows = qkv_ref.shape[0]
    for n in range(3):
        for pair in range(4):
            block_ref = second_ref if pair >= 2 else first_ref
            start = pl.multiple_of((8 * n + pair + 4 * core) * PAIR, PAIR)
            target = (3 * (pair % 2) + n) * PAIR
            block_ref[:rows, target : target + PAIR] = qkv_ref[:, pl.ds(start, PAIR)]
    out_half = out_ref.shape[1] // 2
    start = pl.multiple_of(core * out_half, out_half)
    second_ref[:, 6 * PAIR :] = out_ref[:, pl.ds(start, out_half)]
    lines = []
    for ref in vector_refs:
        vector = ref[...].astype(F32).reshape(ref.shape[0] // PAIR, PAIR)
        lines += [vector[n : n + 1] for n in range(ref.shape[0] // PAIR)]
    row = lax.broadcasted_iota(jnp.int32, (8, PAIR), 0)
    for n in range(6):
        block = jnp.where(row == 0, lines[n], jnp.where(row == 1, lines[n + 6], 0.0))
        first_ref[rows:, PAIR * n : PAIR * (n + 1)] = block.astype(BF16)


def own_qkv_blocks(qkv_weight, out_weight, vectors):
    rows, columns = qkv_weight.shape[0], qkv_weight.shape[1] // 4
    out_half = out_weight.shape[1] // 2
    return pl.pallas_call(
        own_kernel,
        in_specs=[pl.BlockSpec(memory_space=pltpu.VMEM)] * (2 + len(vectors)),
        out_specs=[pl.BlockSpec(memory_space=pltpu.VMEM)] * 2,
        out_shape=[
            jax.ShapeDtypeStruct((rows + 8, columns), BF16),
            jax.ShapeDtypeStruct((rows, columns + out_half), BF16),
        ],
        cost_estimate=SMALL_COST,
        name="own_qkv",
    )(qkv_weight, out_weight, *vectors)


def after(values, *others):
    return lax.optimization_barrier((values,) + others)[0] if others else values


class Gather:
    SOURCE = {4: 0, 2: 0, 1: 0, 6: 4, 3: 2, 5: 4, 7: 6}
    STEP = {4: 4, 2: 2, 1: 1, 6: 2, 3: 1, 5: 1, 7: 1}

    def __init__(self, own):
        self.pieces = [own] + [None] * 7
        self.grouped = lax.axis_size("fsdp") == 8

    def send(self, *parts, ready=()):
        if not self.grouped:
            return
        sources = [self.pieces[self.SOURCE[part]] for part in parts]
        if ready:
            sources = lax.optimization_barrier(tuple(sources) + tuple(ready))
        for part, source in zip(parts, sources):
            self.pieces[part] = swap_group(source, self.STEP[part])

    def got(self, *parts):
        return tuple(self.pieces[part] for part in parts) if self.grouped else ()

    def result(self):
        if not self.grouped:
            return lax.all_gather(self.pieces[0], "fsdp", axis=0, tiled=True)
        return in_order(self.pieces, self.pieces[0].shape[0])


def add_low(left, right):
    return (left.astype(F32) + right.astype(F32)).astype(BF16)


def split_kernel(full_ref, *refs):
    sems = refs[2]
    group = lax.axis_index("fsdp")
    rows = full_ref.shape[0] // 8
    copies = []
    for n in range(8):
        far, near, side = n % 2, (n // 2) % 2, n // 4
        start = pl.multiple_of((group ^ (4 * far + 2 * near + side)) * rows, rows)
        target = refs[side].at[pl.ds((n % 4) * rows, rows)]
        copies.append(
            pltpu.make_async_copy(full_ref.at[pl.ds(start, rows)], target, sems.at[n])
        )
    for copy in copies:
        copy.start()
    for copy in copies:
        copy.wait()


def split_blocks(values):
    rows, columns = values.shape
    return pl.pallas_call(
        split_kernel,
        in_specs=[pl.BlockSpec(memory_space=pltpu.VMEM)],
        out_specs=[pl.BlockSpec(memory_space=pl.ANY)] * 2,
        out_shape=[jax.ShapeDtypeStruct((rows // 2, columns), values.dtype)] * 2,
        scratch_shapes=[pltpu.SemaphoreType.DMA((8,))],
        compiler_params=pltpu.CompilerParams(vmem_limit_bytes=16 * 2**20),
        cost_estimate=SMALL_COST,
        name="split_blocks",
    )(values)


def pack_kernel(*refs):
    line_refs, sum_refs, squares_ref, packed_ref = refs[:7], refs[7:11], refs[11], refs[12]
    group = lax.axis_index("fsdp")
    core = lax.rem(lax.axis_index("seq"), 2)
    for n in range(8):
        far, near, side = n % 2, (n // 2) % 2, n // 4
        target = group ^ (4 * far + 2 * near + side)
        columns = pl.ds(pl.multiple_of(target * PAIR, PAIR), PAIR)
        mine = (target // 4) == core
        pair = lax.rem(target, 4)
        head_sums = jnp.zeros((2, PAIR), F32)
        for k in range(4):
            head_sums = jnp.where(jnp.logical_and(mine, pair == k), sum_refs[k][...], head_sums)
        rows = [ref[:, columns] for ref in line_refs[:6]]
        rows = rows[:2] + [head_sums] + rows[2:]
        hidden = [
            line_refs[6][:, pl.ds(pl.multiple_of(target * 2 * PAIR + k * PAIR, PAIR), PAIR)]
            for k in range(2)
        ]
        empty = jnp.zeros((1, PAIR), F32)
        rows += [jnp.where(core == 0, part, empty) for part in hidden]
        rows += [jnp.where(core == 0, empty, part) for part in hidden]
        rows.append(squares_ref[...])
        packed_ref[16 * n : 16 * (n + 1), :] = jnp.concatenate(rows, axis=0).astype(BF16)


def pack_lines(lines, sums, squares):
    return pl.pallas_call(
        pack_kernel,
        in_specs=[pl.BlockSpec(memory_space=pltpu.VMEM)] * 12,
        out_specs=pl.BlockSpec(memory_space=pltpu.VMEM),
        out_shape=jax.ShapeDtypeStruct((128, PAIR), BF16),
        cost_estimate=SMALL_COST,
        name="pack_lines",
    )(*lines, *sums, squares)


class Scatter:
    def __init__(self, values, *ready, halves=None, ordered=False):
        self.grouped = lax.axis_size("fsdp") == 8
        self.halved = halves is not None
        values = values.astype(BF16)
        if self.halved:
            self.kept, self.sent = halves
            self.crossed = swap_chip(self.sent)
        elif self.grouped:
            middle = values.shape[0] // 2
            split = (values[:middle], values[middle:]) if ordered else split_blocks(values)
            self.keep, self.side_send = split
            self.side = swap_group(after(self.side_send, *ready), 1)
        else:
            self.sums = lax.psum_scatter(values, "fsdp", scatter_dimension=0, tiled=True)

    def cross(self, *ready):
        values = add_low(self.kept, after(self.crossed, *ready))
        if self.grouped:
            self.keep, self.side_send = split_blocks(values)
            self.side = swap_group(self.side_send, 1)
        else:
            self.sums = lax.psum_scatter(values, "fsdp", scatter_dimension=0, tiled=True)

    def got(self, *names):
        return tuple(getattr(self, name) for name in names if hasattr(self, name))

    def step(self, name, next_name, bit, ready):
        if self.grouped:
            received = after(getattr(self, name), *ready)
            half = self.keep.shape[0] // 2
            send = add_low(self.keep[half:], received[half:])
            self.keep = add_low(self.keep[:half], received[:half])
            setattr(self, next_name, swap_group(send, bit))

    def near(self, *ready):
        self.step("side", "near_sums", 2, ready)

    def far(self, *ready):
        self.step("near_sums", "far_sums", 4, ready)

    def chips(self, *ready):
        if self.grouped:
            self.sums = add_low(self.keep, after(self.far_sums, *ready))
        self.other_chip = swap_chip(self.sums)

    def cores(self, *ready):
        other_chip = after(self.other_chip, *ready)
        if self.halved:
            chip = lax.axis_index("seq") // 2
            first = jnp.where(chip == 0, self.sums, other_chip)
            second = jnp.where(chip == 0, other_chip, self.sums)
            self.total = jnp.concatenate([first, second], axis=1)
        else:
            self.total = add_low(self.sums, other_chip)
        self.other_core = swap_core(self.total)

    def last(self):
        if not self.grouped:
            return self.sums.astype(F32)
        return self.keep.astype(F32) + self.far_sums.astype(F32)


def take(values, index):
    return lax.dynamic_index_in_dim(values, index, 0, keepdims=False)


def in_core_order(own, other, core, axis):
    first = jnp.where(core == 0, own, other)
    second = jnp.where(core == 0, other, own)
    return first, second


def body(
    inputs,
    cotangent,
    valid,
    ln1_gain,
    ln1_bias,
    qkv_weight,
    q_bias,
    v_bias,
    out_weight,
    out_bias,
    ln2_gain,
    ln2_bias,
    fc1_weight,
    fc1_bias,
    fc2_weight,
    fc2_bias,
):
    clips, rows, width = inputs.shape
    groups = lax.axis_size("fsdp")
    place = lax.axis_index("seq")
    group = lax.axis_index("fsdp")
    chip, core = place // 2, place % 2
    half = width // 2
    hidden_rows = fc2_weight.shape[0]
    half_rows = hidden_rows // 2
    own_rows = clips * rows
    scale_factor = HEAD ** (-0.5)

    def all_clips(values, *ready):
        mine, back = values[:rows], swap_chip(values[rows:])
        back = after(back, *ready)
        first = jnp.where(chip == 0, mine, back)
        second = jnp.where(chip == 0, back, mine)
        return jnp.stack([first, second])

    own_width = width // groups
    vectors = (ln1_gain, ln1_bias, q_bias, v_bias, out_bias, ln2_gain, ln2_bias, fc2_bias, fc1_bias)
    quarter = half // 2
    row_width = 3 * quarter
    used = 8 * own_width + fc1_bias.shape[0]
    if groups == 8:
        own_first, own_second = own_qkv_blocks(qkv_weight, out_weight, vectors)
    else:
        by_head = qkv_weight.reshape(own_width, 3, 2, 2, 2, PAIR)
        by_head = lax.dynamic_index_in_dim(by_head, core, 2, keepdims=False)
        by_head = by_head.transpose(0, 2, 3, 1, 4).reshape(own_width, 2, row_width)
        out_columns = lax.dynamic_slice_in_dim(out_weight, core * half, half, 1)
        own_first = by_head[:, 0]
        own_second = jnp.concatenate([by_head[:, 1], out_columns], axis=1)

    fc1_weight, fc2_weight = lax.optimization_barrier((fc1_weight, fc2_weight, own_first))[:2]
    own_fc1 = lax.dynamic_index_in_dim(
        fc1_weight.reshape(own_width, groups, 2, half_rows), core, 2, keepdims=False
    ).reshape(own_width, groups * half_rows)
    own_fc2 = lax.dynamic_slice_in_dim(fc2_weight, core * half_rows, half_rows, 0)

    qkv_a, qkv_b = Gather(own_first), Gather(own_second)
    fc1_gather, fc2_gather = Gather(own_fc1), Gather(own_fc2)
    qkv_a.send(4, 2, 1)
    other_inputs = swap_chip(take(after(inputs, own_fc1), 1 - chip))
    qkv_a.send(6, 3, 5, ready=qkv_a.got(4, 2, 1) + (own_fc1, own_fc2))
    qkv_b.send(4, ready=qkv_a.got(4, 2, 1))
    qkv_a.send(7, ready=qkv_a.got(6, 3, 5))
    other_inputs = after(other_inputs, *qkv_a.got(6, 3, 5))
    qkv_b.send(2, 1, ready=qkv_a.got(6, 3, 5))
    own_inputs = jnp.concatenate([take(inputs, chip), other_inputs], axis=0)
    all_inputs = with_partner(own_inputs)
    if groups == 8:
        qkv_first, wide, bias_fc1 = in_order(qkv_a.pieces, own_width, True)
    else:
        qkv_first = qkv_a.result()
        packed = lax.all_gather(jnp.concatenate(vectors), "fsdp", axis=0)
        wide = [
            packed[:, i * own_width : (i + 1) * own_width].reshape(width).astype(F32)
            for i in range(8)
        ]
        bias_fc1 = packed[:, 8 * own_width : used].reshape(groups, 2, half_rows)
        bias_fc1 = take(jnp.moveaxis(bias_fc1, 1, 0), core)
        bias_fc1 = bias_fc1.reshape(groups * half_rows).astype(F32)
    gain_one, bias_one, bias_q, bias_v, bias_out, gain_two, bias_two, bias_fc2 = [
        wide[i] for i in range(8)
    ]
    bias_q = take(bias_q.reshape(2, 2, 2, PAIR), core)
    bias_v = take(bias_v.reshape(2, 2, 2, PAIR), core)
    bias_mixed = jnp.stack([bias_q, jnp.zeros_like(bias_q), bias_v], axis=2).reshape(2, row_width)
    scale_mixed = jnp.array([scale_factor, 1.0, 1.0] * 2, F32).repeat(PAIR)
    clip_valid = take(valid, chip).reshape(2 * clips, rows)
    own_valid = jnp.concatenate([take(clip_valid, place), take(clip_valid, place ^ 2)])
    other_valid = jnp.concatenate([take(clip_valid, place ^ 1), take(clip_valid, place ^ 3)])
    key_valid = jnp.concatenate([own_valid, other_valid])
    lane = jnp.arange(PAIR) % HEAD
    key_mask = jnp.where(key_valid > 0, 0.0, MASKED)[:, None]
    key_base = jnp.where(lane == 0, key_mask, jnp.where(lane < 4, 1.0, 0.0)).astype(BF16)


    def project(weight, i):
        return ((dot(h_one, weight) + bias_mixed[i]) * scale_mixed).astype(BF16)

    normal_one = normalize(all_inputs.astype(F32))[0]
    h_one = (normal_one * gain_one + bias_one).astype(BF16)
    mixed = [project(qkv_first, 0)]
    context, queries = [], []

    def attend_pair(pair, *ready):
        before = context[-1] if context else None
        base = after(key_base, *ready)
        results = attend(mixed[pair // 2], base, pair % 2, before, pair, 4)
        context.append(results[0])
        queries.append(results[1])

    ready = (mixed[0],) + qkv_b.got(4, 2, 1)
    qkv_b.send(6, 3, 5, ready=ready)
    fc1_gather.send(4, ready=ready)
    attend_pair(0, *ready)
    ready = (queries[0],) + qkv_b.got(6, 3, 5) + fc1_gather.got(4)
    qkv_b.send(7, ready=ready)
    fc1_gather.send(2, 1, 6, 5, ready=ready)
    attend_pair(1, *ready)
    second_columns = qkv_b.result()
    mixed.append(project(second_columns[:, :row_width], 1))
    ready = (queries[1], mixed[1]) + fc1_gather.got(2, 1, 6, 5)
    fc1_gather.send(3, 7, ready=ready)
    fc2_gather.send(4, 2, ready=ready)
    kept = lax.dynamic_slice(second_columns, (core * half, row_width), (half, half))
    received = lax.dynamic_slice(second_columns, ((1 - core) * half, row_width), (half, half))
    received = swap_core(after(received, mixed[1]))
    attend_pair(2, kept, *ready)
    ready = (queries[2], received) + fc1_gather.got(3, 7) + fc2_gather.got(2)
    fc2_gather.send(1, ready=ready)
    fc2_gather.send(3, ready=ready)
    other_grads = swap_chip(after(take(cotangent, 1 - chip), *ready))
    attend_pair(3, *ready)
    own_grads = jnp.concatenate([take(cotangent, chip), after(other_grads, queries[3])], axis=0)
    full_out = jnp.concatenate(in_core_order(kept, received, core, 1), axis=1)
    full_qkv = (qkv_first, second_columns[:, :row_width])
    ready = (own_grads, queries[3]) + fc2_gather.got(4, 1)
    all_context = after(context[3], *ready)
    fc2_gather.send(5, 6, ready=ready)
    attn_branch = sum_partner([(all_context, full_out)], NN) + bias_out
    residual_mid = own_inputs.astype(F32) + attn_branch
    normal_two, scale_two = normalize(residual_mid)
    h_two = (normal_two * gain_two + bias_two).astype(BF16)
    h_two = with_partner(after(h_two, *fc2_gather.got(3)))
    all_grads = with_partner(after(own_grads, residual_mid))
    full_fc1 = fc1_gather.result()
    h_two = after(h_two, *fc2_gather.got(5, 6))
    fc2_gather.send(7, ready=(h_two,))
    active, slope = gelu_both(dot(h_two, full_fc1) + bias_fc1)
    active, slope = active.astype(BF16), slope.astype(BF16)
    fc2_product = dot(active, all_grads, TN).astype(BF16)
    fc2_scatter = Scatter(fc2_product)

    full_fc2 = fc2_gather.result()
    late_grads = after(all_grads, *fc2_scatter.got("keep"))
    grad_hidden = (dot(late_grads, full_fc2, NT) * slope.astype(F32)).astype(BF16)
    fc1_product = dot(h_two, grad_hidden, TN).astype(BF16)
    fc1_half = fc1_product.shape[1] // 2
    fc1_halves = [
        lax.dynamic_slice_in_dim(fc1_product, part * fc1_half, fc1_half, 1)
        for part in (chip, 1 - chip)
    ]
    fc1_scatter = Scatter(fc1_product, halves=fc1_halves)
    grad_h_two = sum_partner([(after(grad_hidden, fc1_scatter.sent), full_fc1)], NT)
    grad_residual = own_grads.astype(F32) + normalize_back(
        normal_two, scale_two, grad_h_two, gain_two
    )
    own_grad_attn = grad_residual.astype(BF16)
    grad_attn = with_partner(own_grad_attn)
    grad_out = dot(all_context, grad_attn, TN).astype(BF16)
    kept = lax.dynamic_slice_in_dim(grad_out, core * half, half, 1)
    received = swap_core(lax.dynamic_slice_in_dim(grad_out, (1 - core) * half, half, 1))
    grad_context = dot(grad_attn, full_out, NT).astype(BF16)
    halves, sums = [None, None], []

    def back_pair(pair, *ready):
        grad_mixed, parts = attend_back(
            queries[pair],
            mixed[pair // 2],
            grad_context,
            all_context,
            after(key_base, *ready),
            pair % 2,
            pair,
            halves[pair // 2],
        )
        halves[pair // 2] = grad_mixed
        sums.append(parts)

    back_pair(0, grad_context)
    grad_out = jnp.concatenate(
        in_core_order(kept, after(received, grad_context), core, 0), axis=0
    )
    ready = (sums[0], fc1_scatter.crossed) + fc2_scatter.got("side")
    fc2_scatter.near(*ready)
    fc1_scatter.cross(*ready)
    back_pair(1, grad_out, *ready, *fc2_scatter.got("keep"), *fc1_scatter.got("keep"))
    early = jnp.concatenate([dot(h_one, halves[0], TN).astype(BF16), grad_out], axis=1)
    ready = (sums[1],) + fc2_scatter.got("near_sums") + fc1_scatter.got("side")
    fc2_scatter.far(*ready)
    fc1_scatter.near(*ready)
    early_scatter = Scatter(early, *ready)
    ready += fc2_scatter.got("keep") + fc1_scatter.got("keep") + early_scatter.got("keep")
    back_pair(2, *ready)
    ready = (sums[2],) + fc2_scatter.got("far_sums") + fc1_scatter.got("near_sums")
    fc2_scatter.chips(*ready)
    fc1_scatter.far(*ready)
    back_pair(3, *ready, fc2_scatter.sums, *fc1_scatter.got("keep"))
    ready = (sums[3], fc2_scatter.other_chip) + fc1_scatter.got("far_sums")
    ready += early_scatter.got("side")
    fc1_scatter.chips(*ready)
    fc2_scatter.cores(*ready)
    early_scatter.near(*ready)
    late_scatter = Scatter(dot(after(h_one, fc1_scatter.sums, *ready), halves[1], TN))
    mlp_branch = sum_partner([(after(active, *late_scatter.got("keep")), full_fc2)], NN) + bias_fc2
    residual_out = residual_mid + mlp_branch
    low_output = residual_out.astype(BF16)
    counted = own_valid.astype(F32)[:, None]
    squares = [
        jnp.sum(column_sum(counted * part * part).reshape(-1, PAIR), axis=0)
        for part in (residual_out, attn_branch, mlp_branch)
    ]
    squares.append(jnp.sum(jnp.pad(own_valid.astype(F32), (0, -own_rows % PAIR)).reshape(-1, PAIR), axis=0))
    late_scatter.near(low_output)
    early_scatter.far(low_output)
    ready = late_scatter.got("keep")
    grad_h_one = sum_partner(
        [(after(halves[n], *ready), full_qkv[n]) for n in range(2)], NT
    )
    late_scatter.far(grad_h_one)
    grad_h_one = after(grad_h_one, *late_scatter.got("keep"))
    own_normal, own_scale = normalize(own_inputs.astype(F32))
    low_input_grad = (
        grad_residual + normalize_back(own_normal, own_scale, grad_h_one, gain_one)
    ).astype(BF16)

    lines = [
        column_sum(grad_h_one * own_normal),
        column_sum(grad_h_one),
        column_sum(own_grad_attn),
        column_sum(grad_h_two * normal_two),
        column_sum(grad_h_two),
        column_sum(own_grads),
        column_sum(grad_hidden),
    ]
    if groups == 8:
        packed = pack_lines([line[None] for line in lines], sums, jnp.stack(squares))
    else:
        def by_core(values):
            full = jnp.zeros((2, values.shape[0]), F32)
            return lax.dynamic_update_index_in_dim(full, values, core, 0).reshape(-1)

        wide = lines[:2] + [by_core(jnp.concatenate([part[n] for part in sums])) for n in range(2)]
        wide = [line.reshape(groups, own_width) for line in wide + lines[2:6]]
        hidden_sums = jnp.zeros((groups, 2, half_rows), F32)
        hidden_sums = lax.dynamic_update_index_in_dim(
            hidden_sums, lines[6].reshape(groups, half_rows), core, 1
        )
        wide.append(hidden_sums.reshape(groups, hidden_rows))
        wide.append(jnp.zeros((groups, 12 * PAIR - used)))
        wide.append(jnp.broadcast_to(jnp.concatenate(squares), (groups, 4 * PAIR)))
        packed = jnp.concatenate(wide, axis=1).astype(BF16).reshape(groups * 16, PAIR)
    packed = add_low(packed, swap_chip(packed))
    packed = add_low(packed, swap_core(packed))
    vector_scatter = Scatter(packed, ordered=True)
    vector_scatter.near()
    early_scatter.chips(packed)
    late_scatter.chips(packed)
    input_grad = all_clips(after(low_input_grad, packed))
    output = all_clips(low_output, packed)
    vector_scatter.far()
    fc1_scatter.cores(packed)
    early_scatter.cores(input_grad)
    late_scatter.cores()

    def in_columns(values, other, blocks):
        size = values.shape[1] // blocks
        parts = in_core_order(values, other, core, 0)
        parts = [part.reshape(own_width, blocks, 1, size) for part in parts]
        return jnp.concatenate(parts, axis=2).reshape(own_width, -1).astype(F32)

    fc2_grad = in_core_order(fc2_scatter.total, fc2_scatter.other_core, core, 0)
    fc2_grad = jnp.concatenate(fc2_grad, axis=0).astype(F32)
    fc1_grad = in_columns(fc1_scatter.total, fc1_scatter.other_core, groups)
    early, early_other = early_scatter.total, early_scatter.other_core
    late, late_other = late_scatter.total, late_scatter.other_core
    out_grad = in_columns(early[:, row_width:], early_other[:, row_width:], 1)

    def both_halves(left, right):
        left = left[:, :row_width].reshape(own_width, 1, 2, 3, PAIR)
        right = right.reshape(own_width, 1, 2, 3, PAIR)
        both = jnp.concatenate([left, right], axis=1).transpose(0, 3, 1, 2, 4)
        return both.reshape(own_width, 3 * half)

    qkv_grad = in_columns(both_halves(early, late), both_halves(early_other, late_other), 3)
    lines = vector_scatter.last()
    flat = lines[:12].reshape(-1)
    own_vectors = [flat[i * own_width : (i + 1) * own_width] for i in range(8)]
    own_hidden = flat[8 * own_width : used]
    totals = jnp.sum(lines[12:], axis=1)
    branch_rms = jnp.sqrt(totals[:3] / (totals[3] * width))
    return (
        output,
        input_grad,
        own_vectors[0],
        own_vectors[1],
        qkv_grad,
        own_vectors[2],
        own_vectors[3],
        out_grad,
        own_vectors[4],
        own_vectors[5],
        own_vectors[6],
        fc1_grad,
        own_hidden,
        fc2_grad,
        own_vectors[7],
        branch_rms,
    )


def solution(mesh):
    tokens, rows, vector = P("fsdp", "seq", None), P("fsdp", None), P("fsdp")
    return jax.shard_map(
        body,
        mesh=mesh,
        in_specs=(
            tokens,
            tokens,
            rows,
            vector,
            vector,
            rows,
            vector,
            vector,
            rows,
            vector,
            vector,
            vector,
            rows,
            vector,
            rows,
            vector,
        ),
        out_specs=(
            tokens,
            tokens,
            vector,
            vector,
            rows,
            vector,
            vector,
            rows,
            vector,
            vector,
            vector,
            rows,
            vector,
            rows,
            vector,
            P(),
        ),
        check_vma=False,
    )
```

```python
from functools import partial

import jax
import jax.numpy as jnp
from jax import lax
from jax.experimental import pallas as pl
from jax.experimental.pallas import tpu as pltpu
from jax.sharding import PartitionSpec as P

HEADS = 16
HEAD = 64
PAIR = 2 * HEAD
EPS = 1e-06
MASKED = -1e30
VMEM_BYTES = 28 * 2**20
BF16 = jnp.bfloat16
F32 = jnp.float32
NN = (((1,), (0,)), ((), ()))
NT = (((1,), (1,)), ((), ()))
TN = (((0,), (0,)), ((), ()))
SMALL_COST = pl.CostEstimate(flops=10**7, bytes_accessed=2**20, transcendentals=0)


def dot(left, right, dims=NN):
    return lax.dot_general(left, right, dims, preferred_element_type=F32)


def lanes_of(shape):
    return lax.broadcasted_iota(jnp.int32, shape, len(shape) - 1)


def three_parts(column):
    high = column.astype(BF16).astype(F32)
    rest = column - high
    middle = rest.astype(BF16).astype(F32)
    return high, middle, rest - middle


def block_rows(length, *sizes):
    for rows in sizes + (224, 112, 16):
        if length % rows == 0:
            return rows
    return length


def attend_kernel(q_ref, k_ref, v_ref, key_base_ref, *refs):
    context_ref, query_ref = refs[-2:]
    length = q_ref.shape[0]
    rows = block_rows(length, 392)
    low = lanes_of((length, PAIR)) < HEAD
    keys, values, key_base = k_ref[...], v_ref[...], key_base_ref[...]
    ones = jnp.ones((length, PAIR), BF16)
    keys_of = [jnp.where(low, keys, key_base), jnp.where(low, key_base, keys)]
    values_of = [jnp.where(low, values, ones), jnp.where(low, ones, values)]
    lane = lanes_of((rows, PAIR))
    low_rows = lane < HEAD
    for step in range(length // rows):
        span = slice(step * rows, (step + 1) * rows)
        queries = q_ref[span, :]
        results = []
        for head in range(2):
            base = HEAD * (1 - head)
            own = low_rows if head == 0 else jnp.logical_not(low_rows)
            unit = jnp.where(lane == base, 1.0, 0.0)
            scores = dot(jnp.where(own, queries, unit.astype(BF16)), keys_of[head], NT)
            highest = jnp.max(scores, axis=1, keepdims=True)
            weights = jnp.exp(scores - highest).astype(BF16)
            mixed = dot(weights, values_of[head])
            total = mixed[:, base : base + 1]
            high, middle, rest = three_parts(-(highest + jnp.log(total)))
            extra = jnp.where(lane == base + 3, rest, unit)
            extra = jnp.where(lane == base + 2, middle, extra)
            extra = jnp.where(lane == base + 1, high, extra)
            query_ref[head, span, :] = jnp.where(own, queries, extra.astype(BF16))
            results.append(mixed / total)
        context_ref[span, :] = jnp.where(low_rows, results[0], results[1]).astype(BF16)


def attend(mixed, key_base, pair, context, place, places):
    length = mixed.shape[0]
    tile = lambda column: pl.BlockSpec((length, PAIR), lambda i: (0, column))
    in_specs = [tile(3 * pair), tile(3 * pair + 1), tile(3 * pair + 2), tile(0)]
    operands = (mixed, mixed, mixed, key_base)
    aliases = {}
    if context is not None:
        in_specs.append(pl.BlockSpec(memory_space=pl.ANY))
        operands += (context,)
        aliases = {4: 0}
    return pl.pallas_call(
        attend_kernel,
        grid=(1,),
        in_specs=in_specs,
        out_specs=[tile(place), pl.BlockSpec((2, length, PAIR), lambda i: (0, 0, 0))],
        out_shape=[
            jax.ShapeDtypeStruct((length, places * PAIR), BF16),
            jax.ShapeDtypeStruct((2, length, PAIR), BF16),
        ],
        input_output_aliases=aliases,
        compiler_params=pltpu.CompilerParams(vmem_limit_bytes=VMEM_BYTES),
        cost_estimate=SMALL_COST,
        name="attend",
    )(*operands)


def attend_back_kernel(query_ref, k_ref, v_ref, grad_ref, context_ref, key_base_ref, *refs):
    grad_mixed_ref, sums_ref = refs[-2:]
    length = k_ref.shape[0]
    rows = block_rows(length)
    low = lanes_of((length, PAIR)) < HEAD
    keys, values, key_base = k_ref[...], v_ref[...], key_base_ref[...]
    ones = jnp.ones((length, PAIR), BF16)
    lane = lanes_of((rows, PAIR))
    low_rows = lane < HEAD
    steps = length // rows
    grad_q, grad_k, grad_v = [], [], []
    sum_q = jnp.zeros((1, PAIR), F32)
    for head in range(2):
        base = HEAD * (1 - head)
        own = low if head == 0 else jnp.logical_not(low)
        own_rows = low_rows if head == 0 else jnp.logical_not(low_rows)
        head_keys = jnp.where(own, keys, key_base)
        head_values = jnp.where(own, values, ones)
        sum_k = jnp.zeros((length, PAIR), F32)
        sum_v = jnp.zeros((length, PAIR), F32)
        for step in range(steps):
            span = slice(step * rows, (step + 1) * rows)
            queries = query_ref[head, span, :]
            grads = grad_ref[span, :]
            product = grads.astype(F32) * context_ref[span, :].astype(F32)
            inner = jnp.sum(jnp.where(own_rows, product, 0.0), axis=1, keepdims=True)
            high, middle, rest = three_parts(-inner)
            extra = jnp.where(lane == base + 2, rest, 0.0)
            extra = jnp.where(lane == base + 1, middle, extra)
            extra = jnp.where(lane == base, high, extra)
            head_grads = jnp.where(own_rows, grads, extra.astype(BF16))
            probs = jnp.exp(dot(head_keys, queries, NT))
            grad_scores = (probs * dot(head_values, head_grads, NT)).astype(BF16)
            sum_v = sum_v + dot(probs.astype(BF16), grads)
            sum_k = sum_k + dot(grad_scores, queries)
            part = dot(grad_scores, keys, TN)
            if head == 0:
                grad_q.append(part)
            else:
                both = jnp.where(low_rows, grad_q[step], part).astype(BF16)
                both = both * (HEAD ** (-0.5))
                grad_mixed_ref[span, :PAIR] = both
                sum_q = sum_q + jnp.sum(both.astype(F32), axis=0, keepdims=True)
        grad_k.append(sum_k)
        grad_v.append(sum_v)
    grad_mixed_ref[:, PAIR : 2 * PAIR] = jnp.where(low, grad_k[0], grad_k[1]).astype(BF16)
    both = jnp.where(low, grad_v[0], grad_v[1]).astype(BF16)
    grad_mixed_ref[:, 2 * PAIR :] = both
    sums_ref[0:1, :] = sum_q
    sums_ref[1:2, :] = jnp.sum(both.astype(F32), axis=0, keepdims=True)


def attend_back(queries, mixed, grad_context, context, key_base, pair, place, grad_mixed):
    length = mixed.shape[0]
    tile = lambda column: pl.BlockSpec((length, PAIR), lambda i: (0, column))
    in_specs = [
        pl.BlockSpec((2, length, PAIR), lambda i: (0, 0, 0)),
        tile(3 * pair + 1),
        tile(3 * pair + 2),
        tile(place),
        tile(place),
        tile(0),
    ]
    operands = (queries, mixed, mixed, grad_context, context, key_base)
    aliases = {}
    if grad_mixed is not None:
        in_specs.append(pl.BlockSpec(memory_space=pl.ANY))
        operands += (grad_mixed,)
        aliases = {6: 0}
    return pl.pallas_call(
        attend_back_kernel,
        grid=(1,),
        in_specs=in_specs,
        out_specs=[
            pl.BlockSpec((length, 3 * PAIR), lambda i: (0, pair)),
            pl.BlockSpec((2, PAIR), lambda i: (0, 0)),
        ],
        out_shape=[
            jax.ShapeDtypeStruct((length, 6 * PAIR), BF16),
            jax.ShapeDtypeStruct((2, PAIR), F32),
        ],
        input_output_aliases=aliases,
        compiler_params=pltpu.CompilerParams(vmem_limit_bytes=VMEM_BYTES),
        cost_estimate=SMALL_COST,
        name="attend_back",
    )(*operands)


def normalize(values):
    center = values - jnp.mean(values, axis=-1, keepdims=True)
    spread = jnp.mean(center * center, axis=-1, keepdims=True)
    scale = lax.rsqrt(spread + EPS)
    return center * scale, scale


def rows_call(kernel, row_inputs, constants, kinds, sum_rows, name):
    rows, width = row_inputs[0].shape
    tile = rows // 7 if rows % 112 == 0 else rows
    block = lambda columns: pl.BlockSpec((tile, columns), lambda i: (i, 0))
    whole = lambda shape: pl.BlockSpec(shape, lambda i: (0, 0))
    out_specs = [block(width)] * len(kinds)
    out_shape = [jax.ShapeDtypeStruct((rows, width), kind) for kind in kinds]
    if sum_rows:
        out_specs.append(whole((sum_rows, width)))
        out_shape.append(jax.ShapeDtypeStruct((sum_rows, width), F32))
    return pl.pallas_call(
        kernel,
        grid=(rows // tile,),
        in_specs=[block(part.shape[1]) for part in row_inputs]
        + [whole(part.shape) for part in constants],
        out_specs=out_specs,
        out_shape=out_shape,
        compiler_params=pltpu.CompilerParams(vmem_limit_bytes=VMEM_BYTES),
        cost_estimate=SMALL_COST,
        name=name,
    )(*row_inputs, *constants)


def add_rows(sums_ref, parts):
    @pl.when(pl.program_id(0) == 0)
    def _():
        sums_ref[...] = jnp.zeros(sums_ref.shape, F32)

    lines = [jnp.sum(part, axis=0, keepdims=True) for part in parts]
    sums_ref[...] += jnp.concatenate(lines, axis=0)


def first_kernel(values_ref, gain_ref, bias_ref, out_ref):
    normal = normalize(values_ref[...].astype(F32))[0]
    out_ref[...] = (normal * gain_ref[...] + bias_ref[...]).astype(BF16)


def middle_kernel(
    own_ref, other_ref, inputs_ref, counted_ref, out_bias_ref, gain_ref, bias_ref, *out_refs
):
    middle_ref, low_ref, sums_ref = out_refs
    branch = own_ref[...] + other_ref[...].astype(F32) + out_bias_ref[...]
    middle = inputs_ref[...].astype(F32) + branch
    middle_ref[...] = middle
    low_ref[...] = (normalize(middle)[0] * gain_ref[...] + bias_ref[...]).astype(BF16)
    counted = counted_ref[...]
    add_rows(sums_ref, [counted * branch * branch, jnp.broadcast_to(counted, branch.shape)])


def end_kernel(own_ref, other_ref, middle_ref, counted_ref, bias_ref, low_ref, sums_ref):
    branch = own_ref[...] + other_ref[...].astype(F32) + bias_ref[...]
    result = middle_ref[...] + branch
    low_ref[...] = result.astype(BF16)
    counted = counted_ref[...]
    add_rows(sums_ref, [counted * result * result, counted * branch * branch])


def norm_back_kernel(own_ref, other_ref, values_ref, residual_ref, gain_ref, *out_refs):
    grad = own_ref[...] + other_ref[...].astype(F32)
    normal, scale = normalize(values_ref[...].astype(F32))
    inner = grad * gain_ref[...]
    first = jnp.mean(inner, axis=-1, keepdims=True)
    second = jnp.mean(inner * normal, axis=-1, keepdims=True)
    total = residual_ref[...].astype(F32) + scale * (inner - first - normal * second)
    low = total.astype(BF16)
    if len(out_refs) == 3:
        out_refs[0][...] = total
    out_refs[-2][...] = low
    add_rows(out_refs[-1], [grad * normal, grad, low.astype(F32)])


def weight_kernel(left_ref, right_ref, kept_ref, sent_ref):
    chip = lax.axis_index("seq") // 2
    left, half = left_ref[...], kept_ref.shape[1]
    for part, out_ref in ((chip, kept_ref), (1 - chip, sent_ref)):
        columns = pl.ds(pl.multiple_of(part * half, half), half)
        out_ref[...] = dot(left, right_ref[:, columns], TN).astype(BF16)


def weight_halves(left, right):
    rows, depth = left.shape
    columns = right.shape[1]
    tile = min(depth, 512)
    half = pl.BlockSpec((tile, columns // 2), lambda i: (i, 0))
    return pl.pallas_call(
        weight_kernel,
        grid=(depth // tile,),
        in_specs=[
            pl.BlockSpec((rows, tile), lambda i: (0, i)),
            pl.BlockSpec((rows, columns), lambda i: (0, 0)),
        ],
        out_specs=[half, half],
        out_shape=[jax.ShapeDtypeStruct((depth, columns // 2), BF16)] * 2,
        compiler_params=pltpu.CompilerParams(vmem_limit_bytes=VMEM_BYTES),
        cost_estimate=SMALL_COST,
        name="weight_halves",
    )(left, right)


def gelu_both(values):
    half = 0.5 * (1.0 + lax.erf(values * (0.5**0.5)))
    density = jnp.exp(-0.5 * values * values) * (0.5 / jnp.pi) ** 0.5
    return values * half, half + values * density


def hidden_kernel(grad_ref, weight_ref, slope_ref, hidden_ref, sums_ref):
    rows = grad_ref.shape[0] // 2
    weight = weight_ref[...]
    total = jnp.zeros((1, weight.shape[0]), F32)
    for span in (slice(0, rows), slice(rows, 2 * rows)):
        hidden = (dot(grad_ref[span, :], weight, NT) * slope_ref[span, :].astype(F32)).astype(BF16)
        hidden_ref[span, :] = hidden
        total = total + jnp.sum(hidden.astype(F32), axis=0, keepdims=True)
    sums_ref[...] = total


def hidden_gradient(grads, weight, slope):
    rows, depth = grads.shape
    columns = weight.shape[0]
    tile = min(columns, 512)
    block = pl.BlockSpec((rows, tile), lambda i: (0, i))
    return pl.pallas_call(
        hidden_kernel,
        grid=(columns // tile,),
        in_specs=[
            pl.BlockSpec((rows, depth), lambda i: (0, 0)),
            pl.BlockSpec((tile, depth), lambda i: (i, 0)),
            block,
        ],
        out_specs=[block, pl.BlockSpec((1, tile), lambda i: (0, i))],
        out_shape=[
            jax.ShapeDtypeStruct((rows, columns), BF16),
            jax.ShapeDtypeStruct((1, columns), F32),
        ],
        compiler_params=pltpu.CompilerParams(vmem_limit_bytes=VMEM_BYTES),
        cost_estimate=SMALL_COST,
        name="hidden_gradient",
    )(grads, weight, slope)


def half_kernel(dims, *refs):
    total = dot(refs[0][...], refs[1][...], dims)
    for n in range(2, len(refs) - 1, 2):
        total = total + dot(refs[n][...], refs[n + 1][...], dims)
    refs[-1][...] = total.astype(refs[-1].dtype)


def half_product(pairs, dims, part, kind):
    rows = pairs[0][0].shape[0] if part is None else pairs[0][0].shape[0] // 2
    part = part or 0
    columns = pairs[0][1].shape[1 if dims is NN else 0]
    tile = min(columns, 512)
    in_specs, operands = [], []
    for left, right in pairs:
        depth = left.shape[1]
        in_specs.append(pl.BlockSpec((rows, depth), lambda i: (part, 0)))
        if dims is NN:
            in_specs.append(pl.BlockSpec((depth, tile), lambda i: (0, i)))
        else:
            in_specs.append(pl.BlockSpec((tile, depth), lambda i: (i, 0)))
        operands += [left, right]
    return pl.pallas_call(
        partial(half_kernel, dims),
        grid=(columns // tile,),
        in_specs=in_specs,
        out_specs=pl.BlockSpec((rows, tile), lambda i: (0, i)),
        out_shape=jax.ShapeDtypeStruct((rows, columns), kind),
        compiler_params=pltpu.CompilerParams(vmem_limit_bytes=VMEM_BYTES),
        cost_estimate=SMALL_COST,
        name="half_product",
    )(*operands)


def both_halves_product(pairs, dims):
    other = half_product(pairs, dims, 1, BF16)
    own = [(after(left, other), right) for left, right in pairs]
    return half_product(own, dims, 0, F32), swap_core(other)


def join_kernel(places, *refs):
    out_ref = refs[-1]
    core = lax.rem(lax.axis_index("seq"), 2)
    for n, (source, start, width, first, second) in enumerate(places):
        for other in range(2):
            target = pl.multiple_of(jnp.where(core == other, first, second), PAIR)
            block = refs[2 * source + other][:, start : start + width]
            out_ref[:, pl.ds(target, width)] = block.astype(F32)


def join_columns(parts, places, columns):
    rows = parts[0].shape[0]
    return pl.pallas_call(
        partial(join_kernel, places),
        in_specs=[pl.BlockSpec(memory_space=pltpu.VMEM)] * len(parts),
        out_specs=pl.BlockSpec(memory_space=pltpu.VMEM),
        out_shape=jax.ShapeDtypeStruct((rows, columns), F32),
        cost_estimate=SMALL_COST,
        name="join_columns",
    )(*parts)


def column_sum(values):
    return jnp.sum(values, axis=0, dtype=F32)


def swap_core(values):
    return lax.ppermute(values, "seq", [(0, 1), (1, 0), (2, 3), (3, 2)])


def swap_chip(values):
    return lax.ppermute(values, "seq", [(0, 2), (2, 0), (1, 3), (3, 1)])


def with_partner(values):
    return jnp.concatenate([values, swap_core(values)], axis=0)


def swap_group(values, bit):
    return lax.ppermute(values, "fsdp", [(i, i ^ bit) for i in range(8)])


def order_kernel(count, *refs):
    pieces, full_ref, held, arrived, sent = refs[:count], refs[count], *refs[-3:]
    group = lax.axis_index("fsdp")
    rows = full_ref.shape[0] // count
    loads = [
        pltpu.make_async_copy(piece, held.at[relative], arrived.at[relative])
        for relative, piece in enumerate(pieces)
    ]
    for load in loads:
        load.start()
    stores = []
    for relative in range(count):
        start = pl.multiple_of((group ^ relative) * rows, rows)
        store = pltpu.make_async_copy(
            held.at[relative, pl.ds(0, rows)], full_ref.at[pl.ds(start, rows)], sent.at[relative]
        )
        loads[relative].wait()
        store.start()
        stores.append(store)
    if len(refs) > count + 4:
        own_width, core = 128, lax.rem(lax.axis_index("seq"), 2)
        wide_ref, bias_ref = refs[count + 1], refs[count + 2]
        for relative in range(count):
            place = group ^ relative
            columns = pl.ds(pl.multiple_of(place * own_width, own_width), own_width)
            extra = held[relative, rows : rows + 8, :].astype(F32)
            lines = [
                extra[k : k + 1, own_width * n : own_width * (n + 1)]
                for k in range(2)
                for n in range(6)
            ]
            for n in range(8):
                wide_ref[n : n + 1, columns] = lines[n]
            for n in range(2):
                start = pl.multiple_of((place * 2 + n) * own_width, own_width)
                bias_ref[:, pl.ds(start, own_width)] = jnp.where(
                    core == 0, lines[8 + n], lines[10 + n]
                )
    for store in stores:
        store.wait()


def in_order(pieces, rows, with_vectors=False):
    count, columns = len(pieces), pieces[0].shape[1]
    out_specs = [pl.BlockSpec(memory_space=pl.ANY)]
    out_shape = [jax.ShapeDtypeStruct((count * rows, columns), pieces[0].dtype)]
    if with_vectors:
        out_specs += [pl.BlockSpec(memory_space=pltpu.VMEM)] * 2
        out_shape += [jax.ShapeDtypeStruct((8, 1024), F32), jax.ShapeDtypeStruct((1, 2048), F32)]
    result = pl.pallas_call(
        partial(order_kernel, count),
        in_specs=[pl.BlockSpec(memory_space=pl.ANY)] * count,
        out_specs=out_specs,
        out_shape=out_shape,
        scratch_shapes=[
            pltpu.VMEM((count,) + pieces[0].shape, pieces[0].dtype),
            pltpu.SemaphoreType.DMA((count,)),
            pltpu.SemaphoreType.DMA((count,)),
        ],
        compiler_params=pltpu.CompilerParams(vmem_limit_bytes=16 * 2**20),
        cost_estimate=SMALL_COST,
        name="in_order",
    )(*pieces)
    return result if with_vectors else result[0]


def own_kernel(qkv_ref, out_ref, *refs):
    vector_refs, (first_ref, second_ref) = refs[:-2], refs[-2:]
    core = lax.rem(lax.axis_index("seq"), 2)
    rows = qkv_ref.shape[0]
    for n in range(3):
        for pair in range(4):
            block_ref = second_ref if pair >= 2 else first_ref
            start = pl.multiple_of((8 * n + pair + 4 * core) * PAIR, PAIR)
            target = (3 * (pair % 2) + n) * PAIR
            block_ref[:rows, target : target + PAIR] = qkv_ref[:, pl.ds(start, PAIR)]
    out_half = out_ref.shape[1] // 2
    start = pl.multiple_of(core * out_half, out_half)
    second_ref[:, 6 * PAIR :] = out_ref[:, pl.ds(start, out_half)]
    lines = []
    for ref in vector_refs:
        vector = ref[...].astype(F32).reshape(ref.shape[0] // PAIR, PAIR)
        lines += [vector[n : n + 1] for n in range(ref.shape[0] // PAIR)]
    row = lax.broadcasted_iota(jnp.int32, (8, PAIR), 0)
    for n in range(6):
        block = jnp.where(row == 0, lines[n], jnp.where(row == 1, lines[n + 6], 0.0))
        first_ref[rows:, PAIR * n : PAIR * (n + 1)] = block.astype(BF16)


def own_qkv_blocks(qkv_weight, out_weight, vectors):
    rows, columns = qkv_weight.shape[0], qkv_weight.shape[1] // 4
    out_half = out_weight.shape[1] // 2
    return pl.pallas_call(
        own_kernel,
        in_specs=[pl.BlockSpec(memory_space=pltpu.VMEM)] * (2 + len(vectors)),
        out_specs=[pl.BlockSpec(memory_space=pltpu.VMEM)] * 2,
        out_shape=[
            jax.ShapeDtypeStruct((rows + 8, columns), BF16),
            jax.ShapeDtypeStruct((rows, columns + out_half), BF16),
        ],
        cost_estimate=SMALL_COST,
        name="own_qkv",
    )(qkv_weight, out_weight, *vectors)


def own_rest_kernel(fc1_ref, fc2_ref, first_ref, second_ref):
    core = lax.rem(lax.axis_index("seq"), 2)
    rows = second_ref.shape[0]
    for n in range(fc1_ref.shape[1] // (2 * rows)):
        start = pl.multiple_of((2 * n + core) * rows, rows)
        first_ref[:, n * rows : (n + 1) * rows] = fc1_ref[:, pl.ds(start, rows)]
    second_ref[...] = fc2_ref[pl.ds(pl.multiple_of(core * rows, rows), rows), :]


def own_rest_blocks(fc1_weight, fc2_weight):
    return pl.pallas_call(
        own_rest_kernel,
        in_specs=[pl.BlockSpec(memory_space=pltpu.VMEM)] * 2,
        out_specs=[pl.BlockSpec(memory_space=pltpu.VMEM)] * 2,
        out_shape=[
            jax.ShapeDtypeStruct((fc1_weight.shape[0], fc1_weight.shape[1] // 2), BF16),
            jax.ShapeDtypeStruct((fc2_weight.shape[0] // 2, fc2_weight.shape[1]), BF16),
        ],
        cost_estimate=SMALL_COST,
        name="own_rest",
    )(fc1_weight, fc2_weight)


def after(values, *others):
    return lax.optimization_barrier((values,) + others)[0] if others else values


class Gather:
    SOURCE = {4: 0, 2: 0, 1: 0, 6: 4, 3: 2, 5: 4, 7: 6}
    STEP = {4: 4, 2: 2, 1: 1, 6: 2, 3: 1, 5: 1, 7: 1}

    def __init__(self, own):
        self.pieces = [own] + [None] * 7
        self.grouped = lax.axis_size("fsdp") == 8

    def send(self, *parts, ready=()):
        if not self.grouped:
            return
        sources = [self.pieces[self.SOURCE[part]] for part in parts]
        if ready:
            sources = lax.optimization_barrier(tuple(sources) + tuple(ready))
        for part, source in zip(parts, sources):
            self.pieces[part] = swap_group(source, self.STEP[part])

    def got(self, *parts):
        return tuple(self.pieces[part] for part in parts) if self.grouped else ()

    def result(self):
        if not self.grouped:
            return lax.all_gather(self.pieces[0], "fsdp", axis=0, tiled=True)
        return in_order(self.pieces, self.pieces[0].shape[0])


def add_low(left, right):
    return (left.astype(F32) + right.astype(F32)).astype(BF16)


def split_kernel(full_ref, *refs):
    sems = refs[2]
    group = lax.axis_index("fsdp")
    rows = full_ref.shape[0] // 8
    copies = []
    for n in range(8):
        far, near, side = n % 2, (n // 2) % 2, n // 4
        start = pl.multiple_of((group ^ (4 * far + 2 * near + side)) * rows, rows)
        target = refs[side].at[pl.ds((n % 4) * rows, rows)]
        copies.append(
            pltpu.make_async_copy(full_ref.at[pl.ds(start, rows)], target, sems.at[n])
        )
    for copy in copies:
        copy.start()
    for copy in copies:
        copy.wait()


def split_blocks(values):
    rows, columns = values.shape
    return pl.pallas_call(
        split_kernel,
        in_specs=[pl.BlockSpec(memory_space=pltpu.VMEM)],
        out_specs=[pl.BlockSpec(memory_space=pl.ANY)] * 2,
        out_shape=[jax.ShapeDtypeStruct((rows // 2, columns), values.dtype)] * 2,
        scratch_shapes=[pltpu.SemaphoreType.DMA((8,))],
        compiler_params=pltpu.CompilerParams(vmem_limit_bytes=16 * 2**20),
        cost_estimate=SMALL_COST,
        name="split_blocks",
    )(values)


def pack_kernel(
    one_ref, two_ref, grads_ref, hidden_ref, end_ref, middle_ref, *refs
):
    sum_refs, packed_ref = refs[:4], refs[4]
    group = lax.axis_index("fsdp")
    core = lax.rem(lax.axis_index("seq"), 2)
    squares = jnp.zeros((4, PAIR), F32)
    for n in range(end_ref.shape[1] // PAIR):
        span = slice(n * PAIR, (n + 1) * PAIR)
        end, middle = end_ref[:, span], middle_ref[:, span]
        squares = squares + jnp.concatenate([end[:1], middle[:1], end[1:], middle[1:]], axis=0)
    for n in range(8):
        far, near, side = n % 2, (n // 2) % 2, n // 4
        target = group ^ (4 * far + 2 * near + side)
        columns = pl.ds(pl.multiple_of(target * PAIR, PAIR), PAIR)
        mine = (target // 4) == core
        pair = lax.rem(target, 4)
        head_sums = jnp.zeros((2, PAIR), F32)
        for k in range(4):
            head_sums = jnp.where(jnp.logical_and(mine, pair == k), sum_refs[k][...], head_sums)
        one, two = one_ref[:, columns], two_ref[:, columns]
        hidden = [
            hidden_ref[:, pl.ds(pl.multiple_of(target * 2 * PAIR + k * PAIR, PAIR), PAIR)]
            for k in range(2)
        ]
        empty = jnp.zeros((1, PAIR), F32)
        rows = [one[:2], head_sums, two[2:3], two[:2], grads_ref[:, columns]]
        rows += [jnp.where(core == 0, part, empty) for part in hidden]
        rows += [jnp.where(core == 0, empty, part) for part in hidden]
        rows.append(squares)
        packed_ref[16 * n : 16 * (n + 1), :] = jnp.concatenate(rows, axis=0).astype(BF16)


def pack_lines(lines, sums):
    return pl.pallas_call(
        pack_kernel,
        in_specs=[pl.BlockSpec(memory_space=pltpu.VMEM)] * 10,
        out_specs=pl.BlockSpec(memory_space=pltpu.VMEM),
        out_shape=jax.ShapeDtypeStruct((128, PAIR), BF16),
        cost_estimate=SMALL_COST,
        name="pack_lines",
    )(*lines, *sums)


class Scatter:
    def __init__(self, values, *ready, halves=None, ordered=False):
        self.grouped = lax.axis_size("fsdp") == 8
        self.halved = halves is not None
        values = values.astype(BF16)
        if self.halved:
            self.kept, self.sent = halves
            self.crossed = swap_chip(self.sent)
        elif self.grouped:
            middle = values.shape[0] // 2
            split = (values[:middle], values[middle:]) if ordered else split_blocks(values)
            self.keep, self.side_send = split
            self.side = swap_group(after(self.side_send, *ready), 1)
        else:
            self.sums = lax.psum_scatter(values, "fsdp", scatter_dimension=0, tiled=True)

    def cross(self, *ready):
        values = add_low(self.kept, after(self.crossed, *ready))
        if self.grouped:
            self.keep, self.side_send = split_blocks(values)
            self.side = swap_group(self.side_send, 1)
        else:
            self.sums = lax.psum_scatter(values, "fsdp", scatter_dimension=0, tiled=True)

    def got(self, *names):
        return tuple(getattr(self, name) for name in names if hasattr(self, name))

    def step(self, name, next_name, bit, ready):
        if self.grouped:
            received = after(getattr(self, name), *ready)
            half = self.keep.shape[0] // 2
            send = add_low(self.keep[half:], received[half:])
            self.keep = add_low(self.keep[:half], received[:half])
            setattr(self, next_name, swap_group(send, bit))

    def near(self, *ready):
        self.step("side", "near_sums", 2, ready)

    def far(self, *ready):
        self.step("near_sums", "far_sums", 4, ready)

    def chips(self, *ready):
        if self.grouped:
            self.sums = add_low(self.keep, after(self.far_sums, *ready))
        self.other_chip = swap_chip(self.sums)

    def cores(self, *ready):
        other_chip = after(self.other_chip, *ready)
        if self.halved:
            chip = lax.axis_index("seq") // 2
            first = jnp.where(chip == 0, self.sums, other_chip)
            second = jnp.where(chip == 0, other_chip, self.sums)
            self.total = jnp.concatenate([first, second], axis=1)
        else:
            self.total = add_low(self.sums, other_chip)
        self.other_core = swap_core(self.total)

    def last(self):
        if not self.grouped:
            return self.sums.astype(F32)
        return self.keep.astype(F32) + self.far_sums.astype(F32)


def take(values, index):
    return lax.dynamic_index_in_dim(values, index, 0, keepdims=False)


def in_core_order(own, other, core, axis):
    first = jnp.where(core == 0, own, other)
    second = jnp.where(core == 0, other, own)
    return first, second


def body(
    inputs,
    cotangent,
    valid,
    ln1_gain,
    ln1_bias,
    qkv_weight,
    q_bias,
    v_bias,
    out_weight,
    out_bias,
    ln2_gain,
    ln2_bias,
    fc1_weight,
    fc1_bias,
    fc2_weight,
    fc2_bias,
):
    clips, rows, width = inputs.shape
    groups = lax.axis_size("fsdp")
    place = lax.axis_index("seq")
    group = lax.axis_index("fsdp")
    chip, core = place // 2, place % 2
    half = width // 2
    hidden_rows = fc2_weight.shape[0]
    half_rows = hidden_rows // 2
    own_rows = clips * rows
    scale_factor = HEAD ** (-0.5)

    def all_clips(values, back):
        mine = values[:rows]
        first = jnp.where(chip == 0, mine, back)
        second = jnp.where(chip == 0, back, mine)
        return jnp.stack([first, second])

    own_width = width // groups
    vectors = (ln1_gain, ln1_bias, q_bias, v_bias, out_bias, ln2_gain, ln2_bias, fc2_bias, fc1_bias)
    quarter = half // 2
    row_width = 3 * quarter
    used = 8 * own_width + fc1_bias.shape[0]
    if groups == 8:
        own_first, own_second = own_qkv_blocks(qkv_weight, out_weight, vectors)
    else:
        by_head = qkv_weight.reshape(own_width, 3, 2, 2, 2, PAIR)
        by_head = lax.dynamic_index_in_dim(by_head, core, 2, keepdims=False)
        by_head = by_head.transpose(0, 2, 3, 1, 4).reshape(own_width, 2, row_width)
        out_columns = lax.dynamic_slice_in_dim(out_weight, core * half, half, 1)
        own_first = by_head[:, 0]
        own_second = jnp.concatenate([by_head[:, 1], out_columns], axis=1)

    qkv_a, qkv_b = Gather(own_first), Gather(own_second)
    qkv_a.send(4, 2, 1)
    other_inputs = swap_chip(take(after(inputs, *qkv_a.got(4, 2, 1)), 1 - chip))
    qkv_a.send(6, 3, 5, ready=qkv_a.got(4, 2, 1))
    qkv_b.send(4, ready=qkv_a.got(4, 2, 1))
    fc1_weight, fc2_weight = after((fc1_weight, fc2_weight), *qkv_a.got(4, 2, 1))
    if groups == 8:
        own_fc1, own_fc2 = own_rest_blocks(fc1_weight, fc2_weight)
    else:
        own_fc1 = lax.dynamic_index_in_dim(
            fc1_weight.reshape(own_width, groups, 2, half_rows), core, 2, keepdims=False
        ).reshape(own_width, groups * half_rows)
        own_fc2 = lax.dynamic_slice_in_dim(fc2_weight, core * half_rows, half_rows, 0)
    fc1_gather, fc2_gather = Gather(own_fc1), Gather(own_fc2)
    qkv_a.send(7, ready=qkv_a.got(6, 3, 5))
    other_inputs = after(other_inputs, own_fc1, *qkv_a.got(6, 3, 5))
    qkv_b.send(2, 1, ready=qkv_a.got(6, 3, 5))
    own_inputs = jnp.concatenate([take(inputs, chip), other_inputs], axis=0)
    all_inputs = with_partner(own_inputs)
    if groups == 8:
        qkv_first, wide, bias_fc1 = in_order(qkv_a.pieces, own_width, True)
    else:
        qkv_first = qkv_a.result()
        packed = lax.all_gather(jnp.concatenate(vectors), "fsdp", axis=0)
        wide = [
            packed[:, i * own_width : (i + 1) * own_width].reshape(width).astype(F32)
            for i in range(8)
        ]
        bias_fc1 = packed[:, 8 * own_width : used].reshape(groups, 2, half_rows)
        bias_fc1 = take(jnp.moveaxis(bias_fc1, 1, 0), core)
        bias_fc1 = bias_fc1.reshape(groups * half_rows).astype(F32)
    gain_one, bias_one, bias_q, bias_v, bias_out, gain_two, bias_two, bias_fc2 = [
        wide[i] for i in range(8)
    ]
    bias_q = take(bias_q.reshape(2, 2, 2, PAIR), core)
    bias_v = take(bias_v.reshape(2, 2, 2, PAIR), core)
    bias_mixed = jnp.stack([bias_q, jnp.zeros_like(bias_q), bias_v], axis=2).reshape(2, row_width)
    scale_mixed = jnp.array([scale_factor, 1.0, 1.0] * 2, F32).repeat(PAIR)
    clip_valid = take(valid, chip).reshape(2 * clips, rows)
    own_valid = jnp.concatenate([take(clip_valid, place), take(clip_valid, place ^ 2)])
    other_valid = jnp.concatenate([take(clip_valid, place ^ 1), take(clip_valid, place ^ 3)])
    key_valid = jnp.concatenate([own_valid, other_valid])
    lane = jnp.arange(PAIR) % HEAD
    key_mask = jnp.where(key_valid > 0, 0.0, MASKED)[:, None]
    key_base = jnp.where(lane == 0, key_mask, jnp.where(lane < 4, 1.0, 0.0)).astype(BF16)


    def project(weight, i):
        return ((dot(h_one, weight) + bias_mixed[i]) * scale_mixed).astype(BF16)

    h_one = rows_call(
        first_kernel, [all_inputs], [gain_one[None], bias_one[None]], [BF16], 0, "first_norm"
    )[0]
    mixed = [project(qkv_first, 0)]
    context, queries = [], []

    def attend_pair(pair, *ready):
        before = context[-1] if context else None
        base = after(key_base, *ready)
        results = attend(mixed[pair // 2], base, pair % 2, before, pair, 4)
        context.append(results[0])
        queries.append(results[1])

    ready = (h_one,) + qkv_b.got(4, 2, 1)
    qkv_b.send(6, 3, 5, ready=ready)
    fc1_gather.send(4, ready=ready)
    attend_pair(0, *ready)
    ready = (queries[0],) + qkv_b.got(6, 3, 5) + fc1_gather.got(4)
    qkv_b.send(7, ready=ready)
    fc1_gather.send(2, 1, 6, 5, ready=ready)
    attend_pair(1, *ready)
    second_columns = qkv_b.result()
    mixed.append(project(second_columns[:, :row_width], 1))
    ready = (queries[1], mixed[1]) + fc1_gather.got(2, 1, 6, 5)
    fc1_gather.send(3, 7, ready=ready)
    fc2_gather.send(4, 2, ready=ready)
    other_grads = swap_chip(after(take(cotangent, 1 - chip), *ready))
    kept = lax.dynamic_slice(second_columns, (core * half, row_width), (half, half))
    received = lax.dynamic_slice(second_columns, ((1 - core) * half, row_width), (half, half))
    received = swap_core(after(received, mixed[1]))
    attend_pair(2, kept, *ready)
    ready = (queries[2], received, other_grads) + fc1_gather.got(3, 7) + fc2_gather.got(4, 2)
    fc2_gather.send(1, ready=ready)
    fc2_gather.send(3, ready=ready)
    attend_pair(3, *ready)
    own_grads = jnp.concatenate([take(cotangent, chip), after(other_grads, queries[3])], axis=0)
    full_out = jnp.concatenate(in_core_order(kept, received, core, 1), axis=1)
    all_context = after(context[3], *fc2_gather.got(1))
    own_part, other_part = both_halves_product([(all_context, full_out)], NN)
    ready = (own_grads, own_part) + fc2_gather.got(3)
    fc2_gather.send(5, 6, ready=ready)
    counted = own_valid.astype(F32)[:, None]
    residual_mid, h_two, middle_sums = rows_call(
        middle_kernel,
        [own_part, after(other_part, *ready), own_inputs, counted],
        [bias_out[None], gain_two[None], bias_two[None]],
        [F32, BF16],
        2,
        "middle",
    )
    h_two = with_partner(after(h_two, *fc2_gather.got(5)))
    all_grads = with_partner(after(own_grads, residual_mid))
    full_fc1 = fc1_gather.result()
    h_two = after(h_two, *fc2_gather.got(6))
    fc2_gather.send(7, ready=(h_two,))
    active, slope = gelu_both(dot(h_two, full_fc1) + bias_fc1)
    active, slope = active.astype(BF16), slope.astype(BF16)
    fc2_product = dot(active, all_grads, TN).astype(BF16)
    fc2_scatter = Scatter(fc2_product)

    full_fc2 = fc2_gather.result()
    late_grads = after(all_grads, *fc2_scatter.got("keep"))
    grad_hidden, hidden_sums = hidden_gradient(late_grads, full_fc2, slope)
    fc1_halves = weight_halves(h_two, grad_hidden)
    fc1_scatter = Scatter(fc1_halves[0], halves=fc1_halves)
    own_part, other_part = both_halves_product(
        [(after(grad_hidden, fc1_scatter.sent), full_fc1)], NT
    )
    grad_residual, own_grad_attn, two_sums = rows_call(
        norm_back_kernel,
        [own_part, other_part, residual_mid, own_grads],
        [gain_two[None]],
        [F32, BF16],
        3,
        "norm_back",
    )
    grad_attn = with_partner(own_grad_attn)
    grad_context = half_product([(grad_attn, full_out)], NT, None, BF16)
    halves, sums = [None, None], []

    def back_pair(pair, *ready):
        grad_mixed, parts = attend_back(
            queries[pair],
            mixed[pair // 2],
            grad_context,
            all_context,
            after(key_base, *ready),
            pair % 2,
            pair,
            halves[pair // 2],
        )
        halves[pair // 2] = grad_mixed
        sums.append(parts)

    grad_sums = column_sum(own_grads)
    back_pair(0, grad_context, grad_sums)
    ready = (sums[0], fc1_scatter.crossed) + fc2_scatter.got("side")
    grad_out = dot(all_context, after(grad_attn, *ready), TN).astype(BF16)
    kept = lax.dynamic_slice_in_dim(grad_out, core * half, half, 1)
    received = swap_core(lax.dynamic_slice_in_dim(grad_out, (1 - core) * half, half, 1))
    fc2_scatter.near(*ready)
    fc1_scatter.cross(*ready)
    back_pair(1, kept, *ready, *fc2_scatter.got("keep"), *fc1_scatter.got("keep"))
    received = after(received, sums[1])
    grad_out = jnp.concatenate(in_core_order(kept, received, core, 0), axis=0)
    early = jnp.concatenate([dot(h_one, halves[0], TN).astype(BF16), grad_out], axis=1)
    ready = (sums[1],) + fc2_scatter.got("near_sums") + fc1_scatter.got("side")
    fc2_scatter.far(*ready)
    fc1_scatter.near(*ready)
    early_scatter = Scatter(early, *ready)
    ready += fc2_scatter.got("keep") + fc1_scatter.got("keep") + early_scatter.got("keep")
    own_mlp, other_mlp = both_halves_product([(after(active, *ready), full_fc2)], NN)
    low_output, end_sums = rows_call(
        end_kernel,
        [own_mlp, other_mlp, residual_mid, counted],
        [bias_fc2[None]],
        [BF16],
        2,
        "end",
    )
    back_pair(2, low_output, *ready)
    ready = (sums[2],) + fc2_scatter.got("far_sums") + fc1_scatter.got("near_sums")
    ready += early_scatter.got("side")
    fc2_scatter.chips(*ready)
    fc1_scatter.far(*ready)
    early_scatter.near(*ready)
    output_back = swap_chip(after(low_output, *ready)[rows:])
    ready += (fc2_scatter.sums,) + fc1_scatter.got("keep") + early_scatter.got("keep")
    back_pair(3, *ready)
    ready = (sums[3], fc2_scatter.other_chip) + fc1_scatter.got("far_sums")
    ready += early_scatter.got("near_sums")
    early_scatter.far(*ready)
    fc1_scatter.chips(*ready)
    fc2_scatter.cores(*ready)
    late_scatter = Scatter(dot(after(h_one, *ready), halves[1], TN))
    gm_first, gm_second = after(tuple(halves), *late_scatter.got("keep"))
    own_one, other_one = both_halves_product(
        [(gm_first, qkv_first), (gm_second, second_columns)], NT
    )
    low_input_grad, one_sums = rows_call(
        norm_back_kernel,
        [own_one, other_one, own_inputs, grad_residual],
        [gain_one[None]],
        [BF16],
        3,
        "norm_back",
    )
    input_back = swap_chip(low_input_grad[rows:])
    ready = late_scatter.got("side") + (fc1_scatter.other_chip, low_input_grad)
    late_scatter.near(*ready)
    fc1_scatter.cores(*ready)
    one_sums = after(one_sums, *ready)

    if groups == 8:
        packed = pack_lines(
            [one_sums, two_sums, grad_sums[None], hidden_sums, end_sums, middle_sums], sums
        )
    else:
        lines = [one_sums[0], one_sums[1], two_sums[2], two_sums[0], two_sums[1], grad_sums]
        lines.append(hidden_sums[0])
        squares = [end_sums[0], middle_sums[0], end_sums[1], middle_sums[1]]
        squares = [jnp.sum(line.reshape(-1, PAIR), axis=0) for line in squares]

        def by_core(values):
            full = jnp.zeros((2, values.shape[0]), F32)
            return lax.dynamic_update_index_in_dim(full, values, core, 0).reshape(-1)

        wide = lines[:2] + [by_core(jnp.concatenate([part[n] for part in sums])) for n in range(2)]
        wide = [line.reshape(groups, own_width) for line in wide + lines[2:6]]
        all_sums = jnp.zeros((groups, 2, half_rows), F32)
        all_sums = lax.dynamic_update_index_in_dim(
            all_sums, lines[6].reshape(groups, half_rows), core, 1
        )
        wide.append(all_sums.reshape(groups, hidden_rows))
        wide.append(jnp.zeros((groups, 12 * PAIR - used)))
        wide.append(jnp.broadcast_to(jnp.concatenate(squares), (groups, 4 * PAIR)))
        packed = jnp.concatenate(wide, axis=1).astype(BF16).reshape(groups * 16, PAIR)
    ready = early_scatter.got("far_sums") + (output_back,)
    packed = add_low(packed, after(swap_chip(packed), *ready))
    early_scatter.chips(packed)
    ready = late_scatter.got("near_sums") + (fc1_scatter.other_core,)
    packed = add_low(packed, after(swap_core(packed), *ready))
    late_scatter.far(packed)
    vector_scatter = Scatter(packed, ordered=True)
    ready = (early_scatter.other_chip, input_back)
    vector_scatter.near(*ready)
    early_scatter.cores(*vector_scatter.got("keep"))
    ready = late_scatter.got("far_sums")
    vector_scatter.far(*ready)
    late_scatter.chips(*vector_scatter.got("keep"))
    late_scatter.cores()
    ready_last = (packed,)
    output = all_clips(low_output, after(output_back, packed))
    input_grad = all_clips(low_input_grad, input_back)

    def in_columns(values, other, blocks):
        size = values.shape[1] // blocks
        parts = in_core_order(values, other, core, 0)
        parts = [part.reshape(own_width, blocks, 1, size) for part in parts]
        return jnp.concatenate(parts, axis=2).reshape(own_width, -1).astype(F32)

    fc2_parts = after((fc2_scatter.total, fc2_scatter.other_core), *ready_last)
    fc2_grad = in_core_order(*fc2_parts, core, 0)
    fc2_grad = jnp.concatenate(fc2_grad, axis=0).astype(F32)
    early_parts = [early_scatter.total, early_scatter.other_core]
    late_parts = [late_scatter.total, late_scatter.other_core]
    fc1_parts = after((fc1_scatter.total, fc1_scatter.other_core), *ready_last)
    if groups == 8:
        fc1_places = [
            (0, n * half_rows, half_rows, 2 * n * half_rows, (2 * n + 1) * half_rows)
            for n in range(groups)
        ]
        fc1_grad = join_columns(fc1_parts, fc1_places, 2 * groups * half_rows)
        out_grad = join_columns(early_parts, [(0, row_width, half, 0, half)], width)
        qkv_places = []
        for n in range(3):
            for pair in range(4):
                target = n * width + pair * PAIR
                start = (3 * (pair % 2) + n) * PAIR
                qkv_places.append((pair // 2, start, PAIR, target, target + half))
        qkv_grad = join_columns(early_parts + late_parts, qkv_places, 3 * width)
    else:
        fc1_grad = in_columns(*fc1_parts, groups)
        out_grad = in_columns(*[part[:, row_width:] for part in early_parts], 1)

        def both_halves(left, right):
            left = left[:, :row_width].reshape(own_width, 1, 2, 3, PAIR)
            right = right.reshape(own_width, 1, 2, 3, PAIR)
            both = jnp.concatenate([left, right], axis=1).transpose(0, 3, 1, 2, 4)
            return both.reshape(own_width, 3 * half)

        qkv_grad = in_columns(*[both_halves(*pair) for pair in zip(early_parts, late_parts)], 3)
    lines = vector_scatter.last()
    flat = lines[:12].reshape(-1)
    own_vectors = [flat[i * own_width : (i + 1) * own_width] for i in range(8)]
    own_hidden = flat[8 * own_width : used]
    totals = jnp.sum(lines[12:], axis=1)
    branch_rms = jnp.sqrt(totals[:3] / totals[3])
    return (
        output,
        input_grad,
        own_vectors[0],
        own_vectors[1],
        qkv_grad,
        own_vectors[2],
        own_vectors[3],
        out_grad,
        own_vectors[4],
        own_vectors[5],
        own_vectors[6],
        fc1_grad,
        own_hidden,
        fc2_grad,
        own_vectors[7],
        branch_rms,
    )


def solution(mesh):
    tokens, rows, vector = P("fsdp", "seq", None), P("fsdp", None), P("fsdp")
    return jax.shard_map(
        body,
        mesh=mesh,
        in_specs=(
            tokens,
            tokens,
            rows,
            vector,
            vector,
            rows,
            vector,
            vector,
            rows,
            vector,
            vector,
            vector,
            rows,
            vector,
            rows,
            vector,
        ),
        out_specs=(
            tokens,
            tokens,
            vector,
            vector,
            rows,
            vector,
            vector,
            rows,
            vector,
            vector,
            vector,
            rows,
            vector,
            rows,
            vector,
            P(),
        ),
        check_vma=False,
    )
```

```python
from functools import partial

import jax
import jax.numpy as jnp
from jax import lax
from jax.experimental import pallas as pl
from jax.experimental.pallas import tpu as pltpu
from jax.sharding import PartitionSpec as P

HEADS = 16
HEAD = 64
PAIR = 2 * HEAD
EPS = 1e-06
MASKED = -1e30
VMEM_BYTES = 28 * 2**20
BF16 = jnp.bfloat16
F32 = jnp.float32
NN = (((1,), (0,)), ((), ()))
NT = (((1,), (1,)), ((), ()))
TN = (((0,), (0,)), ((), ()))
SMALL_COST = pl.CostEstimate(flops=10**7, bytes_accessed=2**20, transcendentals=0)


def dot(left, right, dims=NN):
    return lax.dot_general(left, right, dims, preferred_element_type=F32)


def lanes_of(shape):
    return lax.broadcasted_iota(jnp.int32, shape, len(shape) - 1)


def three_parts(column):
    high = column.astype(BF16).astype(F32)
    rest = column - high
    middle = rest.astype(BF16).astype(F32)
    return high, middle, rest - middle


def block_rows(length, *sizes):
    for rows in sizes + (224, 112, 16):
        if length % rows == 0:
            return rows
    return length


def attend_kernel(q_ref, k_ref, v_ref, key_base_ref, *refs):
    context_ref, query_ref = refs[-2:]
    length = q_ref.shape[0]
    rows = block_rows(length, 392)
    low = lanes_of((length, PAIR)) < HEAD
    keys, values, key_base = k_ref[...], v_ref[...], key_base_ref[...]
    ones = jnp.ones((length, PAIR), BF16)
    keys_of = [jnp.where(low, keys, key_base), jnp.where(low, key_base, keys)]
    values_of = [jnp.where(low, values, ones), jnp.where(low, ones, values)]
    lane = lanes_of((rows, PAIR))
    low_rows = lane < HEAD
    for step in range(length // rows):
        span = slice(step * rows, (step + 1) * rows)
        queries = q_ref[span, :]
        results = []
        for head in range(2):
            base = HEAD * (1 - head)
            own = low_rows if head == 0 else jnp.logical_not(low_rows)
            unit = jnp.where(lane == base, 1.0, 0.0)
            scores = dot(jnp.where(own, queries, unit.astype(BF16)), keys_of[head], NT)
            highest = jnp.max(scores, axis=1, keepdims=True)
            weights = jnp.exp(scores - highest).astype(BF16)
            mixed = dot(weights, values_of[head])
            total = mixed[:, base : base + 1]
            high, middle, rest = three_parts(-(highest + jnp.log(total)))
            extra = jnp.where(lane == base + 3, rest, unit)
            extra = jnp.where(lane == base + 2, middle, extra)
            extra = jnp.where(lane == base + 1, high, extra)
            query_ref[head, span, :] = jnp.where(own, queries, extra.astype(BF16))
            results.append(mixed / total)
        context_ref[span, :] = jnp.where(low_rows, results[0], results[1]).astype(BF16)


def attend(mixed, key_base, pair, context, place, places):
    length = mixed.shape[0]
    tile = lambda column: pl.BlockSpec((length, PAIR), lambda i: (0, column))
    in_specs = [tile(3 * pair), tile(3 * pair + 1), tile(3 * pair + 2), tile(0)]
    operands = (mixed, mixed, mixed, key_base)
    aliases = {}
    if context is not None:
        in_specs.append(pl.BlockSpec(memory_space=pl.ANY))
        operands += (context,)
        aliases = {4: 0}
    return pl.pallas_call(
        attend_kernel,
        grid=(1,),
        in_specs=in_specs,
        out_specs=[tile(place), pl.BlockSpec((2, length, PAIR), lambda i: (0, 0, 0))],
        out_shape=[
            jax.ShapeDtypeStruct((length, places * PAIR), BF16),
            jax.ShapeDtypeStruct((2, length, PAIR), BF16),
        ],
        input_output_aliases=aliases,
        compiler_params=pltpu.CompilerParams(vmem_limit_bytes=VMEM_BYTES),
        cost_estimate=SMALL_COST,
        name="attend",
    )(*operands)


def attend_back_kernel(query_ref, k_ref, v_ref, grad_ref, context_ref, key_base_ref, *refs):
    grad_mixed_ref, sums_ref = refs[-2:]
    length = k_ref.shape[0]
    rows = block_rows(length)
    low = lanes_of((length, PAIR)) < HEAD
    keys, values, key_base = k_ref[...], v_ref[...], key_base_ref[...]
    ones = jnp.ones((length, PAIR), BF16)
    lane = lanes_of((rows, PAIR))
    low_rows = lane < HEAD
    steps = length // rows
    grad_q, grad_k, grad_v = [], [], []
    sum_q = jnp.zeros((1, PAIR), F32)
    for head in range(2):
        base = HEAD * (1 - head)
        own = low if head == 0 else jnp.logical_not(low)
        own_rows = low_rows if head == 0 else jnp.logical_not(low_rows)
        head_keys = jnp.where(own, keys, key_base)
        head_values = jnp.where(own, values, ones)
        sum_k = jnp.zeros((length, PAIR), F32)
        sum_v = jnp.zeros((length, PAIR), F32)
        for step in range(steps):
            span = slice(step * rows, (step + 1) * rows)
            queries = query_ref[head, span, :]
            grads = grad_ref[span, :]
            product = grads.astype(F32) * context_ref[span, :].astype(F32)
            inner = jnp.sum(jnp.where(own_rows, product, 0.0), axis=1, keepdims=True)
            high, middle, rest = three_parts(-inner)
            extra = jnp.where(lane == base + 2, rest, 0.0)
            extra = jnp.where(lane == base + 1, middle, extra)
            extra = jnp.where(lane == base, high, extra)
            head_grads = jnp.where(own_rows, grads, extra.astype(BF16))
            probs = jnp.exp(dot(head_keys, queries, NT))
            grad_scores = (probs * dot(head_values, head_grads, NT)).astype(BF16)
            sum_v = sum_v + dot(probs.astype(BF16), grads)
            sum_k = sum_k + dot(grad_scores, queries)
            part = dot(grad_scores, keys, TN)
            if head == 0:
                grad_q.append(part)
            else:
                both = jnp.where(low_rows, grad_q[step], part).astype(BF16)
                both = both * (HEAD ** (-0.5))
                grad_mixed_ref[span, :PAIR] = both
                sum_q = sum_q + jnp.sum(both.astype(F32), axis=0, keepdims=True)
        grad_k.append(sum_k)
        grad_v.append(sum_v)
    grad_mixed_ref[:, PAIR : 2 * PAIR] = jnp.where(low, grad_k[0], grad_k[1]).astype(BF16)
    both = jnp.where(low, grad_v[0], grad_v[1]).astype(BF16)
    grad_mixed_ref[:, 2 * PAIR :] = both
    sums_ref[0:1, :] = sum_q
    sums_ref[1:2, :] = jnp.sum(both.astype(F32), axis=0, keepdims=True)


def attend_back(queries, mixed, grad_context, context, key_base, pair, place, grad_mixed):
    length = mixed.shape[0]
    tile = lambda column: pl.BlockSpec((length, PAIR), lambda i: (0, column))
    in_specs = [
        pl.BlockSpec((2, length, PAIR), lambda i: (0, 0, 0)),
        tile(3 * pair + 1),
        tile(3 * pair + 2),
        tile(place),
        tile(place),
        tile(0),
    ]
    operands = (queries, mixed, mixed, grad_context, context, key_base)
    aliases = {}
    if grad_mixed is not None:
        in_specs.append(pl.BlockSpec(memory_space=pl.ANY))
        operands += (grad_mixed,)
        aliases = {6: 0}
    return pl.pallas_call(
        attend_back_kernel,
        grid=(1,),
        in_specs=in_specs,
        out_specs=[
            pl.BlockSpec((length, 3 * PAIR), lambda i: (0, pair)),
            pl.BlockSpec((2, PAIR), lambda i: (0, 0)),
        ],
        out_shape=[
            jax.ShapeDtypeStruct((length, 6 * PAIR), BF16),
            jax.ShapeDtypeStruct((2, PAIR), F32),
        ],
        input_output_aliases=aliases,
        compiler_params=pltpu.CompilerParams(vmem_limit_bytes=VMEM_BYTES),
        cost_estimate=SMALL_COST,
        name="attend_back",
    )(*operands)


def normalize(values):
    center = values - jnp.mean(values, axis=-1, keepdims=True)
    spread = jnp.mean(center * center, axis=-1, keepdims=True)
    scale = lax.rsqrt(spread + EPS)
    return center * scale, scale


def rows_call(kernel, row_inputs, constants, kinds, sum_rows, name):
    rows, width = row_inputs[0].shape
    tile = rows // 7 if rows % 112 == 0 else rows
    block = lambda columns: pl.BlockSpec((tile, columns), lambda i: (i, 0))
    whole = lambda shape: pl.BlockSpec(shape, lambda i: (0, 0))
    out_specs = [block(width)] * len(kinds)
    out_shape = [jax.ShapeDtypeStruct((rows, width), kind) for kind in kinds]
    if sum_rows:
        out_specs.append(whole((sum_rows, width)))
        out_shape.append(jax.ShapeDtypeStruct((sum_rows, width), F32))
    return pl.pallas_call(
        kernel,
        grid=(rows // tile,),
        in_specs=[block(part.shape[1]) for part in row_inputs]
        + [whole(part.shape) for part in constants],
        out_specs=out_specs,
        out_shape=out_shape,
        compiler_params=pltpu.CompilerParams(vmem_limit_bytes=VMEM_BYTES),
        cost_estimate=SMALL_COST,
        name=name,
    )(*row_inputs, *constants)


def add_rows(sums_ref, parts):
    @pl.when(pl.program_id(0) == 0)
    def _():
        sums_ref[...] = jnp.zeros(sums_ref.shape, F32)

    lines = [jnp.sum(part, axis=0, keepdims=True) for part in parts]
    sums_ref[...] += jnp.concatenate(lines, axis=0)


def first_kernel(values_ref, gain_ref, bias_ref, out_ref):
    normal = normalize(values_ref[...].astype(F32))[0]
    out_ref[...] = (normal * gain_ref[...] + bias_ref[...]).astype(BF16)


def middle_kernel(
    own_ref, other_ref, inputs_ref, counted_ref, out_bias_ref, gain_ref, bias_ref, *out_refs
):
    middle_ref, low_ref, sums_ref = out_refs
    branch = own_ref[...] + other_ref[...].astype(F32) + out_bias_ref[...]
    middle = inputs_ref[...].astype(F32) + branch
    middle_ref[...] = middle
    low_ref[...] = (normalize(middle)[0] * gain_ref[...] + bias_ref[...]).astype(BF16)
    counted = counted_ref[...]
    add_rows(sums_ref, [counted * branch * branch, jnp.broadcast_to(counted, branch.shape)])


def end_kernel(own_ref, other_ref, middle_ref, counted_ref, bias_ref, low_ref, sums_ref):
    branch = own_ref[...] + other_ref[...].astype(F32) + bias_ref[...]
    result = middle_ref[...] + branch
    low_ref[...] = result.astype(BF16)
    counted = counted_ref[...]
    add_rows(sums_ref, [counted * result * result, counted * branch * branch])


def norm_back_kernel(own_ref, other_ref, values_ref, residual_ref, gain_ref, *out_refs):
    grad = own_ref[...] + other_ref[...].astype(F32)
    normal, scale = normalize(values_ref[...].astype(F32))
    inner = grad * gain_ref[...]
    first = jnp.mean(inner, axis=-1, keepdims=True)
    second = jnp.mean(inner * normal, axis=-1, keepdims=True)
    total = residual_ref[...].astype(F32) + scale * (inner - first - normal * second)
    low = total.astype(BF16)
    if len(out_refs) == 3:
        out_refs[0][...] = total
    out_refs[-2][...] = low
    add_rows(out_refs[-1], [grad * normal, grad, low.astype(F32)])


def weight_kernel(left_ref, right_ref, kept_ref, sent_ref):
    chip = lax.axis_index("seq") // 2
    left, half = left_ref[...], kept_ref.shape[1]
    for part, out_ref in ((chip, kept_ref), (1 - chip, sent_ref)):
        columns = pl.ds(pl.multiple_of(part * half, half), half)
        out_ref[...] = dot(left, right_ref[:, columns], TN).astype(BF16)


def weight_halves(left, right):
    rows, depth = left.shape
    columns = right.shape[1]
    tile = min(depth, 512)
    half = pl.BlockSpec((tile, columns // 2), lambda i: (i, 0))
    return pl.pallas_call(
        weight_kernel,
        grid=(depth // tile,),
        in_specs=[
            pl.BlockSpec((rows, tile), lambda i: (0, i)),
            pl.BlockSpec((rows, columns), lambda i: (0, 0)),
        ],
        out_specs=[half, half],
        out_shape=[jax.ShapeDtypeStruct((depth, columns // 2), BF16)] * 2,
        compiler_params=pltpu.CompilerParams(vmem_limit_bytes=VMEM_BYTES),
        cost_estimate=SMALL_COST,
        name="weight_halves",
    )(left, right)


def gelu_both(values):
    half = 0.5 * (1.0 + lax.erf(values * (0.5**0.5)))
    density = jnp.exp(-0.5 * values * values) * (0.5 / jnp.pi) ** 0.5
    return values * half, half + values * density


def hidden_kernel(grad_ref, weight_ref, slope_ref, hidden_ref, sums_ref):
    rows = grad_ref.shape[0] // 2
    weight = weight_ref[...]
    total = jnp.zeros((1, weight.shape[0]), F32)
    for span in (slice(0, rows), slice(rows, 2 * rows)):
        hidden = (dot(grad_ref[span, :], weight, NT) * slope_ref[span, :].astype(F32)).astype(BF16)
        hidden_ref[span, :] = hidden
        total = total + jnp.sum(hidden.astype(F32), axis=0, keepdims=True)
    sums_ref[...] = total


def hidden_gradient(grads, weight, slope):
    rows, depth = grads.shape
    columns = weight.shape[0]
    tile = min(columns, 512)
    block = pl.BlockSpec((rows, tile), lambda i: (0, i))
    return pl.pallas_call(
        hidden_kernel,
        grid=(columns // tile,),
        in_specs=[
            pl.BlockSpec((rows, depth), lambda i: (0, 0)),
            pl.BlockSpec((tile, depth), lambda i: (i, 0)),
            block,
        ],
        out_specs=[block, pl.BlockSpec((1, tile), lambda i: (0, i))],
        out_shape=[
            jax.ShapeDtypeStruct((rows, columns), BF16),
            jax.ShapeDtypeStruct((1, columns), F32),
        ],
        compiler_params=pltpu.CompilerParams(vmem_limit_bytes=VMEM_BYTES),
        cost_estimate=SMALL_COST,
        name="hidden_gradient",
    )(grads, weight, slope)


def half_kernel(dims, *refs):
    total = dot(refs[0][...], refs[1][...], dims)
    for n in range(2, len(refs) - 1, 2):
        total = total + dot(refs[n][...], refs[n + 1][...], dims)
    refs[-1][...] = total.astype(refs[-1].dtype)


def half_product(pairs, dims, part, kind):
    rows = pairs[0][0].shape[0] if part is None else pairs[0][0].shape[0] // 2
    part = part or 0
    columns = pairs[0][1].shape[1 if dims is NN else 0]
    tile = min(columns, 512)
    in_specs, operands = [], []
    for left, right in pairs:
        depth = left.shape[1]
        in_specs.append(pl.BlockSpec((rows, depth), lambda i: (part, 0)))
        if dims is NN:
            in_specs.append(pl.BlockSpec((depth, tile), lambda i: (0, i)))
        else:
            in_specs.append(pl.BlockSpec((tile, depth), lambda i: (i, 0)))
        operands += [left, right]
    return pl.pallas_call(
        partial(half_kernel, dims),
        grid=(columns // tile,),
        in_specs=in_specs,
        out_specs=pl.BlockSpec((rows, tile), lambda i: (0, i)),
        out_shape=jax.ShapeDtypeStruct((rows, columns), kind),
        compiler_params=pltpu.CompilerParams(vmem_limit_bytes=VMEM_BYTES),
        cost_estimate=SMALL_COST,
        name="half_product",
    )(*operands)


def both_halves_product(pairs, dims):
    other = half_product(pairs, dims, 1, BF16)
    own = [(after(left, other), right) for left, right in pairs]
    return half_product(own, dims, 0, F32), swap_core(other)


def join_kernel(places, *refs):
    out_ref = refs[-1]
    core = lax.rem(lax.axis_index("seq"), 2)
    for n, (source, start, width, first, second) in enumerate(places):
        for other in range(2):
            target = pl.multiple_of(jnp.where(core == other, first, second), PAIR)
            block = refs[2 * source + other][:, start : start + width]
            out_ref[:, pl.ds(target, width)] = block.astype(F32)


def join_columns(parts, places, columns):
    rows = parts[0].shape[0]
    return pl.pallas_call(
        partial(join_kernel, places),
        in_specs=[pl.BlockSpec(memory_space=pltpu.VMEM)] * len(parts),
        out_specs=pl.BlockSpec(memory_space=pltpu.VMEM),
        out_shape=jax.ShapeDtypeStruct((rows, columns), F32),
        cost_estimate=SMALL_COST,
        name="join_columns",
    )(*parts)


def column_sum(values):
    return jnp.sum(values, axis=0, dtype=F32)


def swap_core(values):
    return lax.ppermute(values, "seq", [(0, 1), (1, 0), (2, 3), (3, 2)])


def swap_chip(values):
    return lax.ppermute(values, "seq", [(0, 2), (2, 0), (1, 3), (3, 1)])


def with_partner(values):
    return jnp.concatenate([values, swap_core(values)], axis=0)


def swap_group(values, bit):
    return lax.ppermute(values, "fsdp", [(i, i ^ bit) for i in range(8)])


def order_kernel(count, *refs):
    pieces, full_ref, held, arrived, sent = refs[:count], refs[count], *refs[-3:]
    group = lax.axis_index("fsdp")
    rows = full_ref.shape[0] // count
    loads = [
        pltpu.make_async_copy(piece, held.at[relative], arrived.at[relative])
        for relative, piece in enumerate(pieces)
    ]
    for load in loads:
        load.start()
    stores = []
    for relative in range(count):
        start = pl.multiple_of((group ^ relative) * rows, rows)
        store = pltpu.make_async_copy(
            held.at[relative, pl.ds(0, rows)], full_ref.at[pl.ds(start, rows)], sent.at[relative]
        )
        loads[relative].wait()
        store.start()
        stores.append(store)
    if len(refs) > count + 4:
        own_width, core = 128, lax.rem(lax.axis_index("seq"), 2)
        wide_ref, bias_ref = refs[count + 1], refs[count + 2]
        for relative in range(count):
            place = group ^ relative
            columns = pl.ds(pl.multiple_of(place * own_width, own_width), own_width)
            extra = held[relative, rows : rows + 8, :].astype(F32)
            lines = [
                extra[k : k + 1, own_width * n : own_width * (n + 1)]
                for k in range(2)
                for n in range(6)
            ]
            for n in range(8):
                wide_ref[n : n + 1, columns] = lines[n]
            for n in range(2):
                start = pl.multiple_of((place * 2 + n) * own_width, own_width)
                bias_ref[:, pl.ds(start, own_width)] = jnp.where(
                    core == 0, lines[8 + n], lines[10 + n]
                )
    for store in stores:
        store.wait()


def in_order(pieces, rows, with_vectors=False):
    count, columns = len(pieces), pieces[0].shape[1]
    out_specs = [pl.BlockSpec(memory_space=pl.ANY)]
    out_shape = [jax.ShapeDtypeStruct((count * rows, columns), pieces[0].dtype)]
    if with_vectors:
        out_specs += [pl.BlockSpec(memory_space=pltpu.VMEM)] * 2
        out_shape += [jax.ShapeDtypeStruct((8, 1024), F32), jax.ShapeDtypeStruct((1, 2048), F32)]
    result = pl.pallas_call(
        partial(order_kernel, count),
        in_specs=[pl.BlockSpec(memory_space=pl.ANY)] * count,
        out_specs=out_specs,
        out_shape=out_shape,
        scratch_shapes=[
            pltpu.VMEM((count,) + pieces[0].shape, pieces[0].dtype),
            pltpu.SemaphoreType.DMA((count,)),
            pltpu.SemaphoreType.DMA((count,)),
        ],
        compiler_params=pltpu.CompilerParams(vmem_limit_bytes=16 * 2**20),
        cost_estimate=SMALL_COST,
        name="in_order",
    )(*pieces)
    return result if with_vectors else result[0]


def own_kernel(qkv_ref, out_ref, *refs):
    vector_refs, (first_ref, second_ref) = refs[:-2], refs[-2:]
    core = lax.rem(lax.axis_index("seq"), 2)
    rows = qkv_ref.shape[0]
    for n in range(3):
        for pair in range(4):
            block_ref = second_ref if pair >= 2 else first_ref
            start = pl.multiple_of((8 * n + pair + 4 * core) * PAIR, PAIR)
            target = (3 * (pair % 2) + n) * PAIR
            block_ref[:rows, target : target + PAIR] = qkv_ref[:, pl.ds(start, PAIR)]
    out_half = out_ref.shape[1] // 2
    start = pl.multiple_of(core * out_half, out_half)
    second_ref[:, 6 * PAIR :] = out_ref[:, pl.ds(start, out_half)]
    lines = []
    for ref in vector_refs:
        vector = ref[...].astype(F32).reshape(ref.shape[0] // PAIR, PAIR)
        lines += [vector[n : n + 1] for n in range(ref.shape[0] // PAIR)]
    row = lax.broadcasted_iota(jnp.int32, (8, PAIR), 0)
    for n in range(6):
        block = jnp.where(row == 0, lines[n], jnp.where(row == 1, lines[n + 6], 0.0))
        first_ref[rows:, PAIR * n : PAIR * (n + 1)] = block.astype(BF16)


def own_qkv_blocks(qkv_weight, out_weight, vectors):
    rows, columns = qkv_weight.shape[0], qkv_weight.shape[1] // 4
    out_half = out_weight.shape[1] // 2
    return pl.pallas_call(
        own_kernel,
        in_specs=[pl.BlockSpec(memory_space=pltpu.VMEM)] * (2 + len(vectors)),
        out_specs=[pl.BlockSpec(memory_space=pltpu.VMEM)] * 2,
        out_shape=[
            jax.ShapeDtypeStruct((rows + 8, columns), BF16),
            jax.ShapeDtypeStruct((rows, columns + out_half), BF16),
        ],
        cost_estimate=SMALL_COST,
        name="own_qkv",
    )(qkv_weight, out_weight, *vectors)


def own_rest_kernel(fc1_ref, fc2_ref, first_ref, second_ref):
    core = lax.rem(lax.axis_index("seq"), 2)
    rows = second_ref.shape[0]
    for n in range(fc1_ref.shape[1] // (2 * rows)):
        start = pl.multiple_of((2 * n + core) * rows, rows)
        first_ref[:, n * rows : (n + 1) * rows] = fc1_ref[:, pl.ds(start, rows)]
    second_ref[...] = fc2_ref[pl.ds(pl.multiple_of(core * rows, rows), rows), :]


def own_rest_blocks(fc1_weight, fc2_weight):
    return pl.pallas_call(
        own_rest_kernel,
        in_specs=[pl.BlockSpec(memory_space=pltpu.VMEM)] * 2,
        out_specs=[pl.BlockSpec(memory_space=pltpu.VMEM)] * 2,
        out_shape=[
            jax.ShapeDtypeStruct((fc1_weight.shape[0], fc1_weight.shape[1] // 2), BF16),
            jax.ShapeDtypeStruct((fc2_weight.shape[0] // 2, fc2_weight.shape[1]), BF16),
        ],
        cost_estimate=SMALL_COST,
        name="own_rest",
    )(fc1_weight, fc2_weight)


def after(values, *others):
    return lax.optimization_barrier((values,) + others)[0] if others else values


class Gather:
    SOURCE = {4: 0, 2: 0, 1: 0, 6: 4, 3: 2, 5: 4, 7: 6}
    STEP = {4: 4, 2: 2, 1: 1, 6: 2, 3: 1, 5: 1, 7: 1}

    def __init__(self, own):
        self.pieces = [own] + [None] * 7
        self.grouped = lax.axis_size("fsdp") == 8

    def send(self, *parts, ready=()):
        if not self.grouped:
            return
        sources = [self.pieces[self.SOURCE[part]] for part in parts]
        if ready:
            sources = lax.optimization_barrier(tuple(sources) + tuple(ready))
        for part, source in zip(parts, sources):
            self.pieces[part] = swap_group(source, self.STEP[part])

    def got(self, *parts):
        return tuple(self.pieces[part] for part in parts) if self.grouped else ()

    def result(self):
        if not self.grouped:
            return lax.all_gather(self.pieces[0], "fsdp", axis=0, tiled=True)
        return in_order(self.pieces, self.pieces[0].shape[0])


def add_low(left, right):
    return (left.astype(F32) + right.astype(F32)).astype(BF16)


def split_kernel(full_ref, *refs):
    sems = refs[2]
    group = lax.axis_index("fsdp")
    rows = full_ref.shape[0] // 8
    copies = []
    for n in range(8):
        far, near, side = n % 2, (n // 2) % 2, n // 4
        start = pl.multiple_of((group ^ (4 * far + 2 * near + side)) * rows, rows)
        target = refs[side].at[pl.ds((n % 4) * rows, rows)]
        copies.append(
            pltpu.make_async_copy(full_ref.at[pl.ds(start, rows)], target, sems.at[n])
        )
    for copy in copies:
        copy.start()
    for copy in copies:
        copy.wait()


def split_blocks(values):
    rows, columns = values.shape
    return pl.pallas_call(
        split_kernel,
        in_specs=[pl.BlockSpec(memory_space=pltpu.VMEM)],
        out_specs=[pl.BlockSpec(memory_space=pl.ANY)] * 2,
        out_shape=[jax.ShapeDtypeStruct((rows // 2, columns), values.dtype)] * 2,
        scratch_shapes=[pltpu.SemaphoreType.DMA((8,))],
        compiler_params=pltpu.CompilerParams(vmem_limit_bytes=16 * 2**20),
        cost_estimate=SMALL_COST,
        name="split_blocks",
    )(values)


def pack_kernel(
    one_ref, two_ref, grads_ref, hidden_ref, end_ref, middle_ref, *refs
):
    sum_refs, packed_ref = refs[:4], refs[4]
    group = lax.axis_index("fsdp")
    core = lax.rem(lax.axis_index("seq"), 2)
    squares = jnp.zeros((4, PAIR), F32)
    for n in range(end_ref.shape[1] // PAIR):
        span = slice(n * PAIR, (n + 1) * PAIR)
        end, middle = end_ref[:, span], middle_ref[:, span]
        squares = squares + jnp.concatenate([end[:1], middle[:1], end[1:], middle[1:]], axis=0)
    for n in range(8):
        far, near, side = n % 2, (n // 2) % 2, n // 4
        target = group ^ (4 * far + 2 * near + side)
        columns = pl.ds(pl.multiple_of(target * PAIR, PAIR), PAIR)
        mine = (target // 4) == core
        pair = lax.rem(target, 4)
        head_sums = jnp.zeros((2, PAIR), F32)
        for k in range(4):
            head_sums = jnp.where(jnp.logical_and(mine, pair == k), sum_refs[k][...], head_sums)
        one, two = one_ref[:, columns], two_ref[:, columns]
        hidden = [
            hidden_ref[:, pl.ds(pl.multiple_of(target * 2 * PAIR + k * PAIR, PAIR), PAIR)]
            for k in range(2)
        ]
        empty = jnp.zeros((1, PAIR), F32)
        rows = [one[:2], head_sums, two[2:3], two[:2], grads_ref[:, columns]]
        rows += [jnp.where(core == 0, part, empty) for part in hidden]
        rows += [jnp.where(core == 0, empty, part) for part in hidden]
        rows.append(squares)
        packed_ref[16 * n : 16 * (n + 1), :] = jnp.concatenate(rows, axis=0).astype(BF16)


def pack_lines(lines, sums):
    return pl.pallas_call(
        pack_kernel,
        in_specs=[pl.BlockSpec(memory_space=pltpu.VMEM)] * 10,
        out_specs=pl.BlockSpec(memory_space=pltpu.VMEM),
        out_shape=jax.ShapeDtypeStruct((128, PAIR), BF16),
        cost_estimate=SMALL_COST,
        name="pack_lines",
    )(*lines, *sums)


class Scatter:
    def __init__(self, values, *ready, halves=None, ordered=False):
        self.grouped = lax.axis_size("fsdp") == 8
        self.halved = halves is not None
        values = values.astype(BF16)
        if self.halved:
            self.kept, self.sent = halves
            self.crossed = swap_chip(self.sent)
        elif self.grouped:
            middle = values.shape[0] // 2
            split = (values[:middle], values[middle:]) if ordered else split_blocks(values)
            self.keep, self.side_send = split
            self.side = swap_group(after(self.side_send, *ready), 1)
        else:
            self.sums = lax.psum_scatter(values, "fsdp", scatter_dimension=0, tiled=True)

    def cross(self, *ready):
        values = add_low(self.kept, after(self.crossed, *ready))
        if self.grouped:
            self.keep, self.side_send = split_blocks(values)
            self.side = swap_group(self.side_send, 1)
        else:
            self.sums = lax.psum_scatter(values, "fsdp", scatter_dimension=0, tiled=True)

    def got(self, *names):
        return tuple(getattr(self, name) for name in names if hasattr(self, name))

    def step(self, name, next_name, bit, ready):
        if self.grouped:
            received = after(getattr(self, name), *ready)
            half = self.keep.shape[0] // 2
            send = add_low(self.keep[half:], received[half:])
            self.keep = add_low(self.keep[:half], received[:half])
            setattr(self, next_name, swap_group(send, bit))

    def near(self, *ready):
        self.step("side", "near_sums", 2, ready)

    def far(self, *ready):
        self.step("near_sums", "far_sums", 4, ready)

    def chips(self, *ready):
        if self.grouped:
            self.sums = add_low(self.keep, after(self.far_sums, *ready))
        self.other_chip = swap_chip(self.sums)

    def cores(self, *ready):
        other_chip = after(self.other_chip, *ready)
        if self.halved:
            chip = lax.axis_index("seq") // 2
            first = jnp.where(chip == 0, self.sums, other_chip)
            second = jnp.where(chip == 0, other_chip, self.sums)
            self.total = jnp.concatenate([first, second], axis=1)
        else:
            self.total = add_low(self.sums, other_chip)
        self.other_core = swap_core(self.total)

    def last(self):
        if not self.grouped:
            return self.sums.astype(F32)
        return self.keep.astype(F32) + self.far_sums.astype(F32)


def take(values, index):
    return lax.dynamic_index_in_dim(values, index, 0, keepdims=False)


def in_core_order(own, other, core, axis):
    first = jnp.where(core == 0, own, other)
    second = jnp.where(core == 0, other, own)
    return first, second


def body(
    inputs,
    cotangent,
    valid,
    ln1_gain,
    ln1_bias,
    qkv_weight,
    q_bias,
    v_bias,
    out_weight,
    out_bias,
    ln2_gain,
    ln2_bias,
    fc1_weight,
    fc1_bias,
    fc2_weight,
    fc2_bias,
):
    clips, rows, width = inputs.shape
    groups = lax.axis_size("fsdp")
    place = lax.axis_index("seq")
    group = lax.axis_index("fsdp")
    chip, core = place // 2, place % 2
    half = width // 2
    hidden_rows = fc2_weight.shape[0]
    half_rows = hidden_rows // 2
    own_rows = clips * rows
    scale_factor = HEAD ** (-0.5)

    def all_clips(values, back):
        mine = values[:rows]
        first = jnp.where(chip == 0, mine, back)
        second = jnp.where(chip == 0, back, mine)
        return jnp.stack([first, second])

    own_width = width // groups
    vectors = (ln1_gain, ln1_bias, q_bias, v_bias, out_bias, ln2_gain, ln2_bias, fc2_bias, fc1_bias)
    quarter = half // 2
    row_width = 3 * quarter
    used = 8 * own_width + fc1_bias.shape[0]
    if groups == 8:
        own_first, own_second = own_qkv_blocks(qkv_weight, out_weight, vectors)
    else:
        by_head = qkv_weight.reshape(own_width, 3, 2, 2, 2, PAIR)
        by_head = lax.dynamic_index_in_dim(by_head, core, 2, keepdims=False)
        by_head = by_head.transpose(0, 2, 3, 1, 4).reshape(own_width, 2, row_width)
        out_columns = lax.dynamic_slice_in_dim(out_weight, core * half, half, 1)
        own_first = by_head[:, 0]
        own_second = jnp.concatenate([by_head[:, 1], out_columns], axis=1)

    qkv_a, qkv_b = Gather(own_first), Gather(own_second)
    qkv_a.send(4, 2, 1)
    other_inputs = swap_chip(take(after(inputs, *qkv_a.got(4, 2, 1)), 1 - chip))
    qkv_a.send(6, 3, 5, ready=qkv_a.got(4, 2, 1))
    qkv_b.send(4, ready=qkv_a.got(4, 2, 1))
    fc1_weight, fc2_weight = after((fc1_weight, fc2_weight), own_first)
    if groups == 8:
        own_fc1, own_fc2 = own_rest_blocks(fc1_weight, fc2_weight)
    else:
        own_fc1 = lax.dynamic_index_in_dim(
            fc1_weight.reshape(own_width, groups, 2, half_rows), core, 2, keepdims=False
        ).reshape(own_width, groups * half_rows)
        own_fc2 = lax.dynamic_slice_in_dim(fc2_weight, core * half_rows, half_rows, 0)
    full_fc1 = lax.all_gather(own_fc1, "fsdp", axis=0, tiled=True)
    full_fc2 = lax.all_gather(own_fc2, "fsdp", axis=0, tiled=True)
    qkv_a.send(7, ready=qkv_a.got(6, 3, 5))
    other_inputs = after(other_inputs, own_fc1, *qkv_a.got(6, 3, 5))
    qkv_b.send(2, 1, ready=qkv_a.got(6, 3, 5))
    own_inputs = jnp.concatenate([take(inputs, chip), other_inputs], axis=0)
    all_inputs = with_partner(own_inputs)
    if groups == 8:
        qkv_first, wide, bias_fc1 = in_order(qkv_a.pieces, own_width, True)
    else:
        qkv_first = qkv_a.result()
        packed = lax.all_gather(jnp.concatenate(vectors), "fsdp", axis=0)
        wide = [
            packed[:, i * own_width : (i + 1) * own_width].reshape(width).astype(F32)
            for i in range(8)
        ]
        bias_fc1 = packed[:, 8 * own_width : used].reshape(groups, 2, half_rows)
        bias_fc1 = take(jnp.moveaxis(bias_fc1, 1, 0), core)
        bias_fc1 = bias_fc1.reshape(groups * half_rows).astype(F32)
    gain_one, bias_one, bias_q, bias_v, bias_out, gain_two, bias_two, bias_fc2 = [
        wide[i] for i in range(8)
    ]
    bias_q = take(bias_q.reshape(2, 2, 2, PAIR), core)
    bias_v = take(bias_v.reshape(2, 2, 2, PAIR), core)
    bias_mixed = jnp.stack([bias_q, jnp.zeros_like(bias_q), bias_v], axis=2).reshape(2, row_width)
    scale_mixed = jnp.array([scale_factor, 1.0, 1.0] * 2, F32).repeat(PAIR)
    clip_valid = take(valid, chip).reshape(2 * clips, rows)
    own_valid = jnp.concatenate([take(clip_valid, place), take(clip_valid, place ^ 2)])
    other_valid = jnp.concatenate([take(clip_valid, place ^ 1), take(clip_valid, place ^ 3)])
    key_valid = jnp.concatenate([own_valid, other_valid])
    lane = jnp.arange(PAIR) % HEAD
    key_mask = jnp.where(key_valid > 0, 0.0, MASKED)[:, None]
    key_base = jnp.where(lane == 0, key_mask, jnp.where(lane < 4, 1.0, 0.0)).astype(BF16)


    def project(weight, i):
        return ((dot(h_one, weight) + bias_mixed[i]) * scale_mixed).astype(BF16)

    h_one = rows_call(
        first_kernel, [all_inputs], [gain_one[None], bias_one[None]], [BF16], 0, "first_norm"
    )[0]
    mixed = [project(qkv_first, 0)]
    context, queries = [], []

    def attend_pair(pair, *ready):
        before = context[-1] if context else None
        base = after(key_base, *ready)
        results = attend(mixed[pair // 2], base, pair % 2, before, pair, 4)
        context.append(results[0])
        queries.append(results[1])

    ready = (h_one,) + qkv_b.got(4, 2, 1)
    qkv_b.send(6, 3, 5, ready=ready)
    attend_pair(0, *ready)
    ready = (queries[0],) + qkv_b.got(6, 3, 5)
    qkv_b.send(7, ready=ready)
    other_grads = swap_chip(after(take(cotangent, 1 - chip), *ready))
    attend_pair(1, *ready)
    second_columns = qkv_b.result()
    mixed.append(project(second_columns[:, :row_width], 1))
    ready = (queries[1], mixed[1], other_grads)
    kept = lax.dynamic_slice(second_columns, (core * half, row_width), (half, half))
    received = lax.dynamic_slice(second_columns, ((1 - core) * half, row_width), (half, half))
    received = swap_core(after(received, mixed[1]))
    attend_pair(2, kept, *ready)
    ready = (queries[2], received)
    attend_pair(3, *ready)
    own_grads = jnp.concatenate([take(cotangent, chip), after(other_grads, queries[3])], axis=0)
    full_out = jnp.concatenate(in_core_order(kept, received, core, 1), axis=1)
    all_context = context[3]
    own_part, other_part = both_halves_product([(all_context, full_out)], NN)
    ready = (own_grads, own_part)
    counted = own_valid.astype(F32)[:, None]
    residual_mid, h_two, middle_sums = rows_call(
        middle_kernel,
        [own_part, after(other_part, *ready), own_inputs, counted],
        [bias_out[None], gain_two[None], bias_two[None]],
        [F32, BF16],
        2,
        "middle",
    )
    h_two = with_partner(h_two)
    all_grads = with_partner(after(own_grads, residual_mid))
    active, slope = gelu_both(dot(h_two, full_fc1) + bias_fc1)
    active, slope = active.astype(BF16), slope.astype(BF16)
    active = after(active, full_fc2)
    fc2_product = dot(active, all_grads, TN).astype(BF16)
    fc2_scatter = Scatter(fc2_product)

    late_grads = after(all_grads, *fc2_scatter.got("keep"))
    grad_hidden, hidden_sums = hidden_gradient(late_grads, full_fc2, slope)
    fc1_halves = weight_halves(h_two, grad_hidden)
    fc1_scatter = Scatter(fc1_halves[0], halves=fc1_halves)
    own_part, other_part = both_halves_product(
        [(after(grad_hidden, fc1_scatter.sent), full_fc1)], NT
    )
    grad_residual, own_grad_attn, two_sums = rows_call(
        norm_back_kernel,
        [own_part, other_part, residual_mid, own_grads],
        [gain_two[None]],
        [F32, BF16],
        3,
        "norm_back",
    )
    grad_attn = with_partner(own_grad_attn)
    grad_context = half_product([(grad_attn, full_out)], NT, None, BF16)
    halves, sums = [None, None], []

    def back_pair(pair, *ready):
        grad_mixed, parts = attend_back(
            queries[pair],
            mixed[pair // 2],
            grad_context,
            all_context,
            after(key_base, *ready),
            pair % 2,
            pair,
            halves[pair // 2],
        )
        halves[pair // 2] = grad_mixed
        sums.append(parts)

    grad_sums = column_sum(own_grads)
    back_pair(0, grad_context, grad_sums)
    ready = (sums[0], fc1_scatter.crossed) + fc2_scatter.got("side")
    grad_out = dot(all_context, after(grad_attn, *ready), TN).astype(BF16)
    kept = lax.dynamic_slice_in_dim(grad_out, core * half, half, 1)
    received = swap_core(lax.dynamic_slice_in_dim(grad_out, (1 - core) * half, half, 1))
    fc2_scatter.near(*ready)
    fc1_scatter.cross(*ready)
    back_pair(1, kept, *ready, *fc2_scatter.got("keep"), *fc1_scatter.got("keep"))
    received = after(received, sums[1])
    grad_out = jnp.concatenate(in_core_order(kept, received, core, 0), axis=0)
    early = jnp.concatenate([dot(h_one, halves[0], TN).astype(BF16), grad_out], axis=1)
    ready = (sums[1],) + fc2_scatter.got("near_sums") + fc1_scatter.got("side")
    fc2_scatter.far(*ready)
    fc1_scatter.near(*ready)
    early_scatter = Scatter(early, *ready)
    ready += fc2_scatter.got("keep") + fc1_scatter.got("keep") + early_scatter.got("keep")
    own_mlp, other_mlp = both_halves_product([(after(active, *ready), full_fc2)], NN)
    low_output, end_sums = rows_call(
        end_kernel,
        [own_mlp, other_mlp, residual_mid, counted],
        [bias_fc2[None]],
        [BF16],
        2,
        "end",
    )
    back_pair(2, low_output, *ready)
    ready = (sums[2],) + fc2_scatter.got("far_sums") + fc1_scatter.got("near_sums")
    ready += early_scatter.got("side")
    fc2_scatter.chips(*ready)
    fc1_scatter.far(*ready)
    early_scatter.near(*ready)
    output_back = swap_chip(after(low_output, *ready)[rows:])
    ready += (fc2_scatter.sums,) + fc1_scatter.got("keep") + early_scatter.got("keep")
    back_pair(3, *ready)
    ready = (sums[3], fc2_scatter.other_chip) + fc1_scatter.got("far_sums")
    ready += early_scatter.got("near_sums")
    early_scatter.far(*ready)
    fc1_scatter.chips(*ready)
    fc2_scatter.cores(*ready)
    late_scatter = Scatter(dot(after(h_one, *ready), halves[1], TN))
    gm_first, gm_second = after(tuple(halves), *late_scatter.got("keep"))
    own_one, other_one = both_halves_product(
        [(gm_first, qkv_first), (gm_second, second_columns)], NT
    )
    low_input_grad, one_sums = rows_call(
        norm_back_kernel,
        [own_one, other_one, own_inputs, grad_residual],
        [gain_one[None]],
        [BF16],
        3,
        "norm_back",
    )
    input_back = swap_chip(low_input_grad[rows:])
    ready = late_scatter.got("side") + (fc1_scatter.other_chip, low_input_grad)
    late_scatter.near(*ready)
    fc1_scatter.cores(*ready)
    one_sums = after(one_sums, *ready)

    if groups == 8:
        packed = pack_lines(
            [one_sums, two_sums, grad_sums[None], hidden_sums, end_sums, middle_sums], sums
        )
    else:
        lines = [one_sums[0], one_sums[1], two_sums[2], two_sums[0], two_sums[1], grad_sums]
        lines.append(hidden_sums[0])
        squares = [end_sums[0], middle_sums[0], end_sums[1], middle_sums[1]]
        squares = [jnp.sum(line.reshape(-1, PAIR), axis=0) for line in squares]

        def by_core(values):
            full = jnp.zeros((2, values.shape[0]), F32)
            return lax.dynamic_update_index_in_dim(full, values, core, 0).reshape(-1)

        wide = lines[:2] + [by_core(jnp.concatenate([part[n] for part in sums])) for n in range(2)]
        wide = [line.reshape(groups, own_width) for line in wide + lines[2:6]]
        all_sums = jnp.zeros((groups, 2, half_rows), F32)
        all_sums = lax.dynamic_update_index_in_dim(
            all_sums, lines[6].reshape(groups, half_rows), core, 1
        )
        wide.append(all_sums.reshape(groups, hidden_rows))
        wide.append(jnp.zeros((groups, 12 * PAIR - used)))
        wide.append(jnp.broadcast_to(jnp.concatenate(squares), (groups, 4 * PAIR)))
        packed = jnp.concatenate(wide, axis=1).astype(BF16).reshape(groups * 16, PAIR)
    ready = early_scatter.got("far_sums") + (output_back,)
    packed = add_low(packed, after(swap_chip(packed), *ready))
    early_scatter.chips(packed)
    ready = late_scatter.got("near_sums") + (fc1_scatter.other_core,)
    packed = add_low(packed, after(swap_core(packed), *ready))
    late_scatter.far(packed)
    vector_scatter = Scatter(packed, ordered=True)
    ready = (early_scatter.other_chip, input_back)
    vector_scatter.near(*ready)
    early_scatter.cores(*vector_scatter.got("keep"))
    ready = late_scatter.got("far_sums")
    vector_scatter.far(*ready)
    late_scatter.chips(*vector_scatter.got("keep"))
    late_scatter.cores()
    ready_last = (packed,)
    output = all_clips(low_output, after(output_back, packed))
    input_grad = all_clips(low_input_grad, input_back)

    def in_columns(values, other, blocks):
        size = values.shape[1] // blocks
        parts = in_core_order(values, other, core, 0)
        parts = [part.reshape(own_width, blocks, 1, size) for part in parts]
        return jnp.concatenate(parts, axis=2).reshape(own_width, -1).astype(F32)

    fc2_parts = after((fc2_scatter.total, fc2_scatter.other_core), *ready_last)
    fc2_grad = in_core_order(*fc2_parts, core, 0)
    fc2_grad = jnp.concatenate(fc2_grad, axis=0).astype(F32)
    early_parts = [early_scatter.total, early_scatter.other_core]
    late_parts = [late_scatter.total, late_scatter.other_core]
    fc1_parts = after((fc1_scatter.total, fc1_scatter.other_core), *ready_last)
    if groups == 8:
        fc1_places = [
            (0, n * half_rows, half_rows, 2 * n * half_rows, (2 * n + 1) * half_rows)
            for n in range(groups)
        ]
        fc1_grad = join_columns(fc1_parts, fc1_places, 2 * groups * half_rows)
        out_grad = join_columns(early_parts, [(0, row_width, half, 0, half)], width)
        qkv_places = []
        for n in range(3):
            for pair in range(4):
                target = n * width + pair * PAIR
                start = (3 * (pair % 2) + n) * PAIR
                qkv_places.append((pair // 2, start, PAIR, target, target + half))
        qkv_grad = join_columns(early_parts + late_parts, qkv_places, 3 * width)
    else:
        fc1_grad = in_columns(*fc1_parts, groups)
        out_grad = in_columns(*[part[:, row_width:] for part in early_parts], 1)

        def both_halves(left, right):
            left = left[:, :row_width].reshape(own_width, 1, 2, 3, PAIR)
            right = right.reshape(own_width, 1, 2, 3, PAIR)
            both = jnp.concatenate([left, right], axis=1).transpose(0, 3, 1, 2, 4)
            return both.reshape(own_width, 3 * half)

        qkv_grad = in_columns(*[both_halves(*pair) for pair in zip(early_parts, late_parts)], 3)
    lines = vector_scatter.last()
    flat = lines[:12].reshape(-1)
    own_vectors = [flat[i * own_width : (i + 1) * own_width] for i in range(8)]
    own_hidden = flat[8 * own_width : used]
    totals = jnp.sum(lines[12:], axis=1)
    branch_rms = jnp.sqrt(totals[:3] / totals[3])
    return (
        output,
        input_grad,
        own_vectors[0],
        own_vectors[1],
        qkv_grad,
        own_vectors[2],
        own_vectors[3],
        out_grad,
        own_vectors[4],
        own_vectors[5],
        own_vectors[6],
        fc1_grad,
        own_hidden,
        fc2_grad,
        own_vectors[7],
        branch_rms,
    )


def solution(mesh):
    tokens, rows, vector = P("fsdp", "seq", None), P("fsdp", None), P("fsdp")
    return jax.shard_map(
        body,
        mesh=mesh,
        in_specs=(
            tokens,
            tokens,
            rows,
            vector,
            vector,
            rows,
            vector,
            vector,
            rows,
            vector,
            vector,
            vector,
            rows,
            vector,
            rows,
            vector,
        ),
        out_specs=(
            tokens,
            tokens,
            vector,
            vector,
            rows,
            vector,
            vector,
            rows,
            vector,
            vector,
            vector,
            rows,
            vector,
            rows,
            vector,
            P(),
        ),
        check_vma=False,
    )
```

```python
from functools import partial

import jax
import jax.numpy as jnp
from jax import lax
from jax.experimental import pallas as pl
from jax.experimental.pallas import tpu as pltpu
from jax.sharding import PartitionSpec as P

HEADS = 16
HEAD = 64
PAIR = 2 * HEAD
EPS = 1e-06
MASKED = -1e30
VMEM_BYTES = 28 * 2**20
BF16 = jnp.bfloat16
F32 = jnp.float32
NN = (((1,), (0,)), ((), ()))
NT = (((1,), (1,)), ((), ()))
TN = (((0,), (0,)), ((), ()))
SMALL_COST = pl.CostEstimate(flops=10**7, bytes_accessed=2**20, transcendentals=0)


def dot(left, right, dims=NN):
    return lax.dot_general(left, right, dims, preferred_element_type=F32)


def lanes_of(shape):
    return lax.broadcasted_iota(jnp.int32, shape, len(shape) - 1)


def three_parts(column):
    high = column.astype(BF16).astype(F32)
    rest = column - high
    middle = rest.astype(BF16).astype(F32)
    return high, middle, rest - middle


def block_rows(length, *sizes):
    for rows in sizes + (224, 112, 16):
        if length % rows == 0:
            return rows
    return length


def attend_kernel(q_ref, k_ref, v_ref, key_base_ref, *refs):
    context_ref, query_ref = refs[-2:]
    length = q_ref.shape[0]
    rows = block_rows(length, 392)
    low = lanes_of((length, PAIR)) < HEAD
    keys, values, key_base = k_ref[...], v_ref[...], key_base_ref[...]
    ones = jnp.ones((length, PAIR), BF16)
    keys_of = [jnp.where(low, keys, key_base), jnp.where(low, key_base, keys)]
    values_of = [jnp.where(low, values, ones), jnp.where(low, ones, values)]
    lane = lanes_of((rows, PAIR))
    low_rows = lane < HEAD
    for step in range(length // rows):
        span = slice(step * rows, (step + 1) * rows)
        queries = q_ref[span, :]
        results = []
        for head in range(2):
            base = HEAD * (1 - head)
            own = low_rows if head == 0 else jnp.logical_not(low_rows)
            unit = jnp.where(lane == base, 1.0, 0.0)
            scores = dot(jnp.where(own, queries, unit.astype(BF16)), keys_of[head], NT)
            highest = jnp.max(scores, axis=1, keepdims=True)
            weights = jnp.exp(scores - highest).astype(BF16)
            mixed = dot(weights, values_of[head])
            total = mixed[:, base : base + 1]
            high, middle, rest = three_parts(-(highest + jnp.log(total)))
            extra = jnp.where(lane == base + 3, rest, unit)
            extra = jnp.where(lane == base + 2, middle, extra)
            extra = jnp.where(lane == base + 1, high, extra)
            query_ref[head, span, :] = jnp.where(own, queries, extra.astype(BF16))
            results.append(mixed / total)
        context_ref[span, :] = jnp.where(low_rows, results[0], results[1]).astype(BF16)


def attend(mixed, key_base, pair, context, place, places):
    length = mixed.shape[0]
    tile = lambda column: pl.BlockSpec((length, PAIR), lambda i: (0, column))
    in_specs = [tile(3 * pair), tile(3 * pair + 1), tile(3 * pair + 2), tile(0)]
    operands = (mixed, mixed, mixed, key_base)
    aliases = {}
    if context is not None:
        in_specs.append(pl.BlockSpec(memory_space=pl.ANY))
        operands += (context,)
        aliases = {4: 0}
    return pl.pallas_call(
        attend_kernel,
        grid=(1,),
        in_specs=in_specs,
        out_specs=[tile(place), pl.BlockSpec((2, length, PAIR), lambda i: (0, 0, 0))],
        out_shape=[
            jax.ShapeDtypeStruct((length, places * PAIR), BF16),
            jax.ShapeDtypeStruct((2, length, PAIR), BF16),
        ],
        input_output_aliases=aliases,
        compiler_params=pltpu.CompilerParams(vmem_limit_bytes=VMEM_BYTES),
        cost_estimate=SMALL_COST,
        name="attend",
    )(*operands)


def attend_back_kernel(query_ref, k_ref, v_ref, grad_ref, context_ref, key_base_ref, *refs):
    grad_mixed_ref, sums_ref = refs[-2:]
    length = k_ref.shape[0]
    rows = block_rows(length)
    low = lanes_of((length, PAIR)) < HEAD
    keys, values, key_base = k_ref[...], v_ref[...], key_base_ref[...]
    ones = jnp.ones((length, PAIR), BF16)
    lane = lanes_of((rows, PAIR))
    low_rows = lane < HEAD
    steps = length // rows
    grad_q, grad_k, grad_v = [], [], []
    sum_q = jnp.zeros((1, PAIR), F32)
    for head in range(2):
        base = HEAD * (1 - head)
        own = low if head == 0 else jnp.logical_not(low)
        own_rows = low_rows if head == 0 else jnp.logical_not(low_rows)
        head_keys = jnp.where(own, keys, key_base)
        head_values = jnp.where(own, values, ones)
        sum_k = jnp.zeros((length, PAIR), F32)
        sum_v = jnp.zeros((length, PAIR), F32)
        for step in range(steps):
            span = slice(step * rows, (step + 1) * rows)
            queries = query_ref[head, span, :]
            grads = grad_ref[span, :]
            product = grads.astype(F32) * context_ref[span, :].astype(F32)
            inner = jnp.sum(jnp.where(own_rows, product, 0.0), axis=1, keepdims=True)
            high, middle, rest = three_parts(-inner)
            extra = jnp.where(lane == base + 2, rest, 0.0)
            extra = jnp.where(lane == base + 1, middle, extra)
            extra = jnp.where(lane == base, high, extra)
            head_grads = jnp.where(own_rows, grads, extra.astype(BF16))
            probs = jnp.exp(dot(head_keys, queries, NT))
            grad_scores = (probs * dot(head_values, head_grads, NT)).astype(BF16)
            sum_v = sum_v + dot(probs.astype(BF16), grads)
            sum_k = sum_k + dot(grad_scores, queries)
            part = dot(grad_scores, keys, TN)
            if head == 0:
                grad_q.append(part)
            else:
                both = jnp.where(low_rows, grad_q[step], part).astype(BF16)
                both = both * (HEAD ** (-0.5))
                grad_mixed_ref[span, :PAIR] = both
                sum_q = sum_q + jnp.sum(both.astype(F32), axis=0, keepdims=True)
        grad_k.append(sum_k)
        grad_v.append(sum_v)
    grad_mixed_ref[:, PAIR : 2 * PAIR] = jnp.where(low, grad_k[0], grad_k[1]).astype(BF16)
    both = jnp.where(low, grad_v[0], grad_v[1]).astype(BF16)
    grad_mixed_ref[:, 2 * PAIR :] = both
    sums_ref[0:1, :] = sum_q
    sums_ref[1:2, :] = jnp.sum(both.astype(F32), axis=0, keepdims=True)


def attend_back(queries, mixed, grad_context, context, key_base, pair, place, grad_mixed):
    length = mixed.shape[0]
    tile = lambda column: pl.BlockSpec((length, PAIR), lambda i: (0, column))
    in_specs = [
        pl.BlockSpec((2, length, PAIR), lambda i: (0, 0, 0)),
        tile(3 * pair + 1),
        tile(3 * pair + 2),
        tile(place),
        tile(place),
        tile(0),
    ]
    operands = (queries, mixed, mixed, grad_context, context, key_base)
    aliases = {}
    if grad_mixed is not None:
        in_specs.append(pl.BlockSpec(memory_space=pl.ANY))
        operands += (grad_mixed,)
        aliases = {6: 0}
    return pl.pallas_call(
        attend_back_kernel,
        grid=(1,),
        in_specs=in_specs,
        out_specs=[
            pl.BlockSpec((length, 3 * PAIR), lambda i: (0, pair)),
            pl.BlockSpec((2, PAIR), lambda i: (0, 0)),
        ],
        out_shape=[
            jax.ShapeDtypeStruct((length, 6 * PAIR), BF16),
            jax.ShapeDtypeStruct((2, PAIR), F32),
        ],
        input_output_aliases=aliases,
        compiler_params=pltpu.CompilerParams(vmem_limit_bytes=VMEM_BYTES),
        cost_estimate=SMALL_COST,
        name="attend_back",
    )(*operands)


def normalize(values):
    center = values - jnp.mean(values, axis=-1, keepdims=True)
    spread = jnp.mean(center * center, axis=-1, keepdims=True)
    scale = lax.rsqrt(spread + EPS)
    return center * scale, scale


def rows_call(kernel, row_inputs, constants, kinds, sum_rows, name):
    rows, width = row_inputs[0].shape
    tile = rows // 7 if rows % 112 == 0 else rows
    block = lambda columns: pl.BlockSpec((tile, columns), lambda i: (i, 0))
    whole = lambda shape: pl.BlockSpec(shape, lambda i: (0, 0))
    out_specs = [block(width)] * len(kinds)
    out_shape = [jax.ShapeDtypeStruct((rows, width), kind) for kind in kinds]
    if sum_rows:
        out_specs.append(whole((sum_rows, width)))
        out_shape.append(jax.ShapeDtypeStruct((sum_rows, width), F32))
    return pl.pallas_call(
        kernel,
        grid=(rows // tile,),
        in_specs=[block(part.shape[1]) for part in row_inputs]
        + [whole(part.shape) for part in constants],
        out_specs=out_specs,
        out_shape=out_shape,
        compiler_params=pltpu.CompilerParams(vmem_limit_bytes=VMEM_BYTES),
        cost_estimate=SMALL_COST,
        name=name,
    )(*row_inputs, *constants)


def add_rows(sums_ref, parts):
    @pl.when(pl.program_id(0) == 0)
    def _():
        sums_ref[...] = jnp.zeros(sums_ref.shape, F32)

    lines = [jnp.sum(part, axis=0, keepdims=True) for part in parts]
    sums_ref[...] += jnp.concatenate(lines, axis=0)


def first_kernel(values_ref, gain_ref, bias_ref, out_ref):
    normal = normalize(values_ref[...].astype(F32))[0]
    out_ref[...] = (normal * gain_ref[...] + bias_ref[...]).astype(BF16)


def middle_kernel(
    own_ref, other_ref, inputs_ref, counted_ref, out_bias_ref, gain_ref, bias_ref, *out_refs
):
    middle_ref, low_ref, sums_ref = out_refs
    branch = own_ref[...] + other_ref[...].astype(F32) + out_bias_ref[...]
    middle = inputs_ref[...].astype(F32) + branch
    middle_ref[...] = middle
    low_ref[...] = (normalize(middle)[0] * gain_ref[...] + bias_ref[...]).astype(BF16)
    counted = counted_ref[...]
    add_rows(sums_ref, [counted * branch * branch, jnp.broadcast_to(counted, branch.shape)])


def end_kernel(own_ref, other_ref, middle_ref, counted_ref, bias_ref, low_ref, sums_ref):
    branch = own_ref[...] + other_ref[...].astype(F32) + bias_ref[...]
    result = middle_ref[...] + branch
    low_ref[...] = result.astype(BF16)
    counted = counted_ref[...]
    add_rows(sums_ref, [counted * result * result, counted * branch * branch])


def norm_back_kernel(own_ref, other_ref, values_ref, residual_ref, gain_ref, *out_refs):
    grad = own_ref[...] + other_ref[...].astype(F32)
    normal, scale = normalize(values_ref[...].astype(F32))
    inner = grad * gain_ref[...]
    first = jnp.mean(inner, axis=-1, keepdims=True)
    second = jnp.mean(inner * normal, axis=-1, keepdims=True)
    total = residual_ref[...].astype(F32) + scale * (inner - first - normal * second)
    low = total.astype(BF16)
    if len(out_refs) == 3:
        out_refs[0][...] = total
    out_refs[-2][...] = low
    add_rows(out_refs[-1], [grad * normal, grad, low.astype(F32)])


def weight_kernel(left_ref, right_ref, kept_ref, sent_ref):
    chip = lax.axis_index("seq") // 2
    left, half = left_ref[...], kept_ref.shape[1]
    for part, out_ref in ((chip, kept_ref), (1 - chip, sent_ref)):
        columns = pl.ds(pl.multiple_of(part * half, half), half)
        out_ref[...] = dot(left, right_ref[:, columns], TN).astype(BF16)


def weight_halves(left, right):
    rows, depth = left.shape
    columns = right.shape[1]
    tile = min(depth, 512)
    half = pl.BlockSpec((tile, columns // 2), lambda i: (i, 0))
    return pl.pallas_call(
        weight_kernel,
        grid=(depth // tile,),
        in_specs=[
            pl.BlockSpec((rows, tile), lambda i: (0, i)),
            pl.BlockSpec((rows, columns), lambda i: (0, 0)),
        ],
        out_specs=[half, half],
        out_shape=[jax.ShapeDtypeStruct((depth, columns // 2), BF16)] * 2,
        compiler_params=pltpu.CompilerParams(vmem_limit_bytes=VMEM_BYTES),
        cost_estimate=SMALL_COST,
        name="weight_halves",
    )(left, right)


def gelu_both(values):
    half = 0.5 * (1.0 + lax.erf(values * (0.5**0.5)))
    density = jnp.exp(-0.5 * values * values) * (0.5 / jnp.pi) ** 0.5
    return values * half, half + values * density


def hidden_kernel(grad_ref, weight_ref, slope_ref, hidden_ref, sums_ref):
    rows = grad_ref.shape[0] // 2
    weight = weight_ref[...]
    total = jnp.zeros((1, weight.shape[0]), F32)
    for span in (slice(0, rows), slice(rows, 2 * rows)):
        hidden = (dot(grad_ref[span, :], weight, NT) * slope_ref[span, :].astype(F32)).astype(BF16)
        hidden_ref[span, :] = hidden
        total = total + jnp.sum(hidden.astype(F32), axis=0, keepdims=True)
    sums_ref[...] = total


def hidden_gradient(grads, weight, slope):
    rows, depth = grads.shape
    columns = weight.shape[0]
    tile = min(columns, 512)
    block = pl.BlockSpec((rows, tile), lambda i: (0, i))
    return pl.pallas_call(
        hidden_kernel,
        grid=(columns // tile,),
        in_specs=[
            pl.BlockSpec((rows, depth), lambda i: (0, 0)),
            pl.BlockSpec((tile, depth), lambda i: (i, 0)),
            block,
        ],
        out_specs=[block, pl.BlockSpec((1, tile), lambda i: (0, i))],
        out_shape=[
            jax.ShapeDtypeStruct((rows, columns), BF16),
            jax.ShapeDtypeStruct((1, columns), F32),
        ],
        compiler_params=pltpu.CompilerParams(vmem_limit_bytes=VMEM_BYTES),
        cost_estimate=SMALL_COST,
        name="hidden_gradient",
    )(grads, weight, slope)


def half_kernel(dims, *refs):
    total = dot(refs[0][...], refs[1][...], dims)
    for n in range(2, len(refs) - 1, 2):
        total = total + dot(refs[n][...], refs[n + 1][...], dims)
    refs[-1][...] = total.astype(refs[-1].dtype)


def half_product(pairs, dims, part, kind):
    rows = pairs[0][0].shape[0] if part is None else pairs[0][0].shape[0] // 2
    part = part or 0
    columns = pairs[0][1].shape[1 if dims is NN else 0]
    tile = min(columns, 512)
    in_specs, operands = [], []
    for left, right in pairs:
        depth = left.shape[1]
        in_specs.append(pl.BlockSpec((rows, depth), lambda i: (part, 0)))
        if dims is NN:
            in_specs.append(pl.BlockSpec((depth, tile), lambda i: (0, i)))
        else:
            in_specs.append(pl.BlockSpec((tile, depth), lambda i: (i, 0)))
        operands += [left, right]
    return pl.pallas_call(
        partial(half_kernel, dims),
        grid=(columns // tile,),
        in_specs=in_specs,
        out_specs=pl.BlockSpec((rows, tile), lambda i: (0, i)),
        out_shape=jax.ShapeDtypeStruct((rows, columns), kind),
        compiler_params=pltpu.CompilerParams(vmem_limit_bytes=VMEM_BYTES),
        cost_estimate=SMALL_COST,
        name="half_product",
    )(*operands)


def both_halves_product(pairs, dims):
    other = half_product(pairs, dims, 1, BF16)
    own = [(after(left, other), right) for left, right in pairs]
    return half_product(own, dims, 0, F32), swap_core(other)


def join_kernel(places, *refs):
    out_ref = refs[-1]
    core = lax.rem(lax.axis_index("seq"), 2)
    for n, (source, start, width, first, second) in enumerate(places):
        for other in range(2):
            target = pl.multiple_of(jnp.where(core == other, first, second), PAIR)
            block = refs[2 * source + other][:, start : start + width]
            out_ref[:, pl.ds(target, width)] = block.astype(F32)


def join_columns(parts, places, columns):
    rows = parts[0].shape[0]
    return pl.pallas_call(
        partial(join_kernel, places),
        in_specs=[pl.BlockSpec(memory_space=pltpu.VMEM)] * len(parts),
        out_specs=pl.BlockSpec(memory_space=pltpu.VMEM),
        out_shape=jax.ShapeDtypeStruct((rows, columns), F32),
        cost_estimate=SMALL_COST,
        name="join_columns",
    )(*parts)


def column_sum(values):
    return jnp.sum(values, axis=0, dtype=F32)


def swap_core(values):
    return lax.ppermute(values, "seq", [(0, 1), (1, 0), (2, 3), (3, 2)])


def swap_chip(values):
    return lax.ppermute(values, "seq", [(0, 2), (2, 0), (1, 3), (3, 1)])


def with_partner(values):
    return jnp.concatenate([values, swap_core(values)], axis=0)


def swap_group(values, bit):
    return lax.ppermute(values, "fsdp", [(i, i ^ bit) for i in range(8)])


def order_kernel(count, *refs):
    pieces, full_ref, sent = refs[:count], refs[count], refs[-1]
    group = lax.axis_index("fsdp")
    rows = full_ref.shape[0] // count
    stores = []
    for relative, piece in enumerate(pieces):
        start = pl.multiple_of((group ^ relative) * rows, rows)
        stores.append(
            pltpu.make_async_copy(
                piece.at[pl.ds(0, rows)], full_ref.at[pl.ds(start, rows)], sent.at[relative]
            )
        )
    for store in stores:
        store.start()
    if len(refs) > count + 2:
        own_width, core = 128, lax.rem(lax.axis_index("seq"), 2)
        wide_ref, bias_ref = refs[count + 1], refs[count + 2]
        for relative in range(count):
            place = group ^ relative
            columns = pl.ds(pl.multiple_of(place * own_width, own_width), own_width)
            extra = pieces[relative][rows : rows + 8, :].astype(F32)
            lines = [
                extra[k : k + 1, own_width * n : own_width * (n + 1)]
                for k in range(2)
                for n in range(6)
            ]
            for n in range(8):
                wide_ref[n : n + 1, columns] = lines[n]
            for n in range(2):
                start = pl.multiple_of((place * 2 + n) * own_width, own_width)
                bias_ref[:, pl.ds(start, own_width)] = jnp.where(
                    core == 0, lines[8 + n], lines[10 + n]
                )
    for store in stores:
        store.wait()


def in_order(pieces, rows, with_vectors=False):
    count, columns = len(pieces), pieces[0].shape[1]
    out_specs = [pl.BlockSpec(memory_space=pl.ANY)]
    out_shape = [jax.ShapeDtypeStruct((count * rows, columns), pieces[0].dtype)]
    if with_vectors:
        out_specs += [pl.BlockSpec(memory_space=pltpu.VMEM)] * 2
        out_shape += [jax.ShapeDtypeStruct((8, 1024), F32), jax.ShapeDtypeStruct((1, 2048), F32)]
    result = pl.pallas_call(
        partial(order_kernel, count),
        in_specs=[pl.BlockSpec(memory_space=pltpu.VMEM)] * count,
        out_specs=out_specs,
        out_shape=out_shape,
        scratch_shapes=[pltpu.SemaphoreType.DMA((count,))],
        compiler_params=pltpu.CompilerParams(vmem_limit_bytes=16 * 2**20),
        cost_estimate=SMALL_COST,
        name="in_order",
    )(*pieces)
    return result if with_vectors else result[0]


def own_kernel(qkv_ref, out_ref, *refs):
    vector_refs, (first_ref, second_ref) = refs[:-2], refs[-2:]
    core = lax.rem(lax.axis_index("seq"), 2)
    rows = qkv_ref.shape[0]
    for n in range(3):
        for pair in range(4):
            block_ref = second_ref if pair >= 2 else first_ref
            start = pl.multiple_of((8 * n + pair + 4 * core) * PAIR, PAIR)
            target = (3 * (pair % 2) + n) * PAIR
            block_ref[:rows, target : target + PAIR] = qkv_ref[:, pl.ds(start, PAIR)]
    out_half = out_ref.shape[1] // 2
    start = pl.multiple_of(core * out_half, out_half)
    second_ref[:, 6 * PAIR :] = out_ref[:, pl.ds(start, out_half)]
    lines = []
    for ref in vector_refs:
        vector = ref[...].astype(F32).reshape(ref.shape[0] // PAIR, PAIR)
        lines += [vector[n : n + 1] for n in range(ref.shape[0] // PAIR)]
    row = lax.broadcasted_iota(jnp.int32, (8, PAIR), 0)
    for n in range(6):
        block = jnp.where(row == 0, lines[n], jnp.where(row == 1, lines[n + 6], 0.0))
        first_ref[rows:, PAIR * n : PAIR * (n + 1)] = block.astype(BF16)


def own_qkv_blocks(qkv_weight, out_weight, vectors):
    rows, columns = qkv_weight.shape[0], qkv_weight.shape[1] // 4
    out_half = out_weight.shape[1] // 2
    return pl.pallas_call(
        own_kernel,
        in_specs=[pl.BlockSpec(memory_space=pltpu.VMEM)] * (2 + len(vectors)),
        out_specs=[pl.BlockSpec(memory_space=pltpu.VMEM)] * 2,
        out_shape=[
            jax.ShapeDtypeStruct((rows + 8, columns), BF16),
            jax.ShapeDtypeStruct((rows, columns + out_half), BF16),
        ],
        cost_estimate=SMALL_COST,
        name="own_qkv",
    )(qkv_weight, out_weight, *vectors)


def own_rest_kernel(fc1_ref, fc2_ref, first_ref, second_ref):
    core = lax.rem(lax.axis_index("seq"), 2)
    rows = second_ref.shape[0]
    for n in range(fc1_ref.shape[1] // (2 * rows)):
        start = pl.multiple_of((2 * n + core) * rows, rows)
        first_ref[:, n * rows : (n + 1) * rows] = fc1_ref[:, pl.ds(start, rows)]
    second_ref[...] = fc2_ref[pl.ds(pl.multiple_of(core * rows, rows), rows), :]


def own_rest_blocks(fc1_weight, fc2_weight):
    return pl.pallas_call(
        own_rest_kernel,
        in_specs=[pl.BlockSpec(memory_space=pltpu.VMEM)] * 2,
        out_specs=[pl.BlockSpec(memory_space=pltpu.VMEM)] * 2,
        out_shape=[
            jax.ShapeDtypeStruct((fc1_weight.shape[0], fc1_weight.shape[1] // 2), BF16),
            jax.ShapeDtypeStruct((fc2_weight.shape[0] // 2, fc2_weight.shape[1]), BF16),
        ],
        cost_estimate=SMALL_COST,
        name="own_rest",
    )(fc1_weight, fc2_weight)


def after(values, *others):
    return lax.optimization_barrier((values,) + others)[0] if others else values


class Gather:
    SOURCE = {4: 0, 2: 0, 1: 0, 6: 4, 3: 2, 5: 4, 7: 6}
    STEP = {4: 4, 2: 2, 1: 1, 6: 2, 3: 1, 5: 1, 7: 1}

    def __init__(self, own):
        self.pieces = [own] + [None] * 7
        self.grouped = lax.axis_size("fsdp") == 8

    def send(self, *parts, ready=()):
        if not self.grouped:
            return
        sources = [self.pieces[self.SOURCE[part]] for part in parts]
        if ready:
            sources = lax.optimization_barrier(tuple(sources) + tuple(ready))
        for part, source in zip(parts, sources):
            self.pieces[part] = swap_group(source, self.STEP[part])

    def got(self, *parts):
        return tuple(self.pieces[part] for part in parts) if self.grouped else ()

    def result(self):
        if not self.grouped:
            return lax.all_gather(self.pieces[0], "fsdp", axis=0, tiled=True)
        return in_order(self.pieces, self.pieces[0].shape[0])


def add_low(left, right):
    return (left.astype(F32) + right.astype(F32)).astype(BF16)


def split_kernel(full_ref, *refs):
    sems = refs[2]
    group = lax.axis_index("fsdp")
    rows = full_ref.shape[0] // 8
    copies = []
    for n in range(8):
        far, near, side = n % 2, (n // 2) % 2, n // 4
        start = pl.multiple_of((group ^ (4 * far + 2 * near + side)) * rows, rows)
        target = refs[side].at[pl.ds((n % 4) * rows, rows)]
        copies.append(
            pltpu.make_async_copy(full_ref.at[pl.ds(start, rows)], target, sems.at[n])
        )
    for copy in copies:
        copy.start()
    for copy in copies:
        copy.wait()


def split_blocks(values):
    rows, columns = values.shape
    return pl.pallas_call(
        split_kernel,
        in_specs=[pl.BlockSpec(memory_space=pltpu.VMEM)],
        out_specs=[pl.BlockSpec(memory_space=pl.ANY)] * 2,
        out_shape=[jax.ShapeDtypeStruct((rows // 2, columns), values.dtype)] * 2,
        scratch_shapes=[pltpu.SemaphoreType.DMA((8,))],
        compiler_params=pltpu.CompilerParams(vmem_limit_bytes=16 * 2**20),
        cost_estimate=SMALL_COST,
        name="split_blocks",
    )(values)


def pack_kernel(
    one_ref, two_ref, grads_ref, hidden_ref, end_ref, middle_ref, *refs
):
    sum_refs, packed_ref = refs[:4], refs[4]
    group = lax.axis_index("fsdp")
    core = lax.rem(lax.axis_index("seq"), 2)
    squares = jnp.zeros((4, PAIR), F32)
    for n in range(end_ref.shape[1] // PAIR):
        span = slice(n * PAIR, (n + 1) * PAIR)
        end, middle = end_ref[:, span], middle_ref[:, span]
        squares = squares + jnp.concatenate([end[:1], middle[:1], end[1:], middle[1:]], axis=0)
    for n in range(8):
        far, near, side = n % 2, (n // 2) % 2, n // 4
        target = group ^ (4 * far + 2 * near + side)
        columns = pl.ds(pl.multiple_of(target * PAIR, PAIR), PAIR)
        mine = (target // 4) == core
        pair = lax.rem(target, 4)
        head_sums = jnp.zeros((2, PAIR), F32)
        for k in range(4):
            head_sums = jnp.where(jnp.logical_and(mine, pair == k), sum_refs[k][...], head_sums)
        one, two = one_ref[:, columns], two_ref[:, columns]
        hidden = [
            hidden_ref[:, pl.ds(pl.multiple_of(target * 2 * PAIR + k * PAIR, PAIR), PAIR)]
            for k in range(2)
        ]
        empty = jnp.zeros((1, PAIR), F32)
        rows = [one[:2], head_sums, two[2:3], two[:2], grads_ref[:, columns]]
        rows += [jnp.where(core == 0, part, empty) for part in hidden]
        rows += [jnp.where(core == 0, empty, part) for part in hidden]
        rows.append(squares)
        packed_ref[16 * n : 16 * (n + 1), :] = jnp.concatenate(rows, axis=0).astype(BF16)


def pack_lines(lines, sums):
    return pl.pallas_call(
        pack_kernel,
        in_specs=[pl.BlockSpec(memory_space=pltpu.VMEM)] * 10,
        out_specs=pl.BlockSpec(memory_space=pltpu.VMEM),
        out_shape=jax.ShapeDtypeStruct((128, PAIR), BF16),
        cost_estimate=SMALL_COST,
        name="pack_lines",
    )(*lines, *sums)


class Scatter:
    def __init__(self, values, *ready, halves=None, ordered=False):
        self.grouped = lax.axis_size("fsdp") == 8
        self.halved = halves is not None
        values = values.astype(BF16)
        if self.halved:
            self.kept, self.sent = halves
            self.crossed = swap_chip(self.sent)
        elif self.grouped:
            middle = values.shape[0] // 2
            split = (values[:middle], values[middle:]) if ordered else split_blocks(values)
            self.keep, self.side_send = split
            self.side = swap_group(after(self.side_send, *ready), 1)
        else:
            self.sums = lax.psum_scatter(values, "fsdp", scatter_dimension=0, tiled=True)

    def cross(self, *ready):
        values = add_low(self.kept, after(self.crossed, *ready))
        if self.grouped:
            self.keep, self.side_send = split_blocks(values)
            self.side = swap_group(self.side_send, 1)
        else:
            self.sums = lax.psum_scatter(values, "fsdp", scatter_dimension=0, tiled=True)

    def got(self, *names):
        return tuple(getattr(self, name) for name in names if hasattr(self, name))

    def step(self, name, next_name, bit, ready):
        if self.grouped:
            received = after(getattr(self, name), *ready)
            half = self.keep.shape[0] // 2
            send = add_low(self.keep[half:], received[half:])
            self.keep = add_low(self.keep[:half], received[:half])
            setattr(self, next_name, swap_group(send, bit))

    def near(self, *ready):
        self.step("side", "near_sums", 2, ready)

    def far(self, *ready):
        self.step("near_sums", "far_sums", 4, ready)

    def chips(self, *ready):
        if self.grouped:
            self.sums = add_low(self.keep, after(self.far_sums, *ready))
        self.other_chip = swap_chip(self.sums)

    def cores(self, *ready):
        other_chip = after(self.other_chip, *ready)
        if self.halved:
            chip = lax.axis_index("seq") // 2
            first = jnp.where(chip == 0, self.sums, other_chip)
            second = jnp.where(chip == 0, other_chip, self.sums)
            self.total = jnp.concatenate([first, second], axis=1)
        else:
            self.total = add_low(self.sums, other_chip)
        self.other_core = swap_core(self.total)

    def last(self):
        if not self.grouped:
            return self.sums.astype(F32)
        return self.keep.astype(F32) + self.far_sums.astype(F32)


def take(values, index):
    return lax.dynamic_index_in_dim(values, index, 0, keepdims=False)


def in_core_order(own, other, core, axis):
    first = jnp.where(core == 0, own, other)
    second = jnp.where(core == 0, other, own)
    return first, second


def body(
    inputs,
    cotangent,
    valid,
    ln1_gain,
    ln1_bias,
    qkv_weight,
    q_bias,
    v_bias,
    out_weight,
    out_bias,
    ln2_gain,
    ln2_bias,
    fc1_weight,
    fc1_bias,
    fc2_weight,
    fc2_bias,
):
    clips, rows, width = inputs.shape
    groups = lax.axis_size("fsdp")
    place = lax.axis_index("seq")
    group = lax.axis_index("fsdp")
    chip, core = place // 2, place % 2
    half = width // 2
    hidden_rows = fc2_weight.shape[0]
    half_rows = hidden_rows // 2
    own_rows = clips * rows
    scale_factor = HEAD ** (-0.5)

    def all_clips(values, back):
        mine = values[:rows]
        first = jnp.where(chip == 0, mine, back)
        second = jnp.where(chip == 0, back, mine)
        return jnp.stack([first, second])

    own_width = width // groups
    vectors = (ln1_gain, ln1_bias, q_bias, v_bias, out_bias, ln2_gain, ln2_bias, fc2_bias, fc1_bias)
    quarter = half // 2
    row_width = 3 * quarter
    used = 8 * own_width + fc1_bias.shape[0]
    if groups == 8:
        own_first, own_second = own_qkv_blocks(qkv_weight, out_weight, vectors)
    else:
        by_head = qkv_weight.reshape(own_width, 3, 2, 2, 2, PAIR)
        by_head = lax.dynamic_index_in_dim(by_head, core, 2, keepdims=False)
        by_head = by_head.transpose(0, 2, 3, 1, 4).reshape(own_width, 2, row_width)
        out_columns = lax.dynamic_slice_in_dim(out_weight, core * half, half, 1)
        own_first = by_head[:, 0]
        own_second = jnp.concatenate([by_head[:, 1], out_columns], axis=1)

    qkv_a, qkv_b = Gather(own_first), Gather(own_second)
    qkv_a.send(4, 2, 1)
    other_inputs = swap_chip(take(after(inputs, *qkv_a.got(4, 2, 1)), 1 - chip))
    qkv_a.send(6, 3, 5, ready=qkv_a.got(4, 2, 1))
    qkv_b.send(4, ready=qkv_a.got(4, 2, 1))
    fc1_weight, fc2_weight = after((fc1_weight, fc2_weight), own_first)
    if groups == 8:
        own_fc1, own_fc2 = own_rest_blocks(fc1_weight, fc2_weight)
    else:
        own_fc1 = lax.dynamic_index_in_dim(
            fc1_weight.reshape(own_width, groups, 2, half_rows), core, 2, keepdims=False
        ).reshape(own_width, groups * half_rows)
        own_fc2 = lax.dynamic_slice_in_dim(fc2_weight, core * half_rows, half_rows, 0)
    full_fc1 = lax.all_gather(own_fc1, "fsdp", axis=0, tiled=True)
    full_fc2 = lax.all_gather(own_fc2, "fsdp", axis=0, tiled=True)
    qkv_a.send(7, ready=qkv_a.got(6, 3, 5))
    other_inputs = after(other_inputs, own_fc1, *qkv_a.got(6, 3, 5))
    qkv_b.send(2, 1, ready=qkv_a.got(6, 3, 5))
    own_inputs = jnp.concatenate([take(inputs, chip), other_inputs], axis=0)
    all_inputs = with_partner(own_inputs)
    if groups == 8:
        qkv_first, wide, bias_fc1 = in_order(qkv_a.pieces, own_width, True)
    else:
        qkv_first = qkv_a.result()
        packed = lax.all_gather(jnp.concatenate(vectors), "fsdp", axis=0)
        wide = [
            packed[:, i * own_width : (i + 1) * own_width].reshape(width).astype(F32)
            for i in range(8)
        ]
        bias_fc1 = packed[:, 8 * own_width : used].reshape(groups, 2, half_rows)
        bias_fc1 = take(jnp.moveaxis(bias_fc1, 1, 0), core)
        bias_fc1 = bias_fc1.reshape(groups * half_rows).astype(F32)
    gain_one, bias_one, bias_q, bias_v, bias_out, gain_two, bias_two, bias_fc2 = [
        wide[i] for i in range(8)
    ]
    bias_q = take(bias_q.reshape(2, 2, 2, PAIR), core)
    bias_v = take(bias_v.reshape(2, 2, 2, PAIR), core)
    bias_mixed = jnp.stack([bias_q, jnp.zeros_like(bias_q), bias_v], axis=2).reshape(2, row_width)
    scale_mixed = jnp.array([scale_factor, 1.0, 1.0] * 2, F32).repeat(PAIR)
    clip_valid = take(valid, chip).reshape(2 * clips, rows)
    own_valid = jnp.concatenate([take(clip_valid, place), take(clip_valid, place ^ 2)])
    other_valid = jnp.concatenate([take(clip_valid, place ^ 1), take(clip_valid, place ^ 3)])
    key_valid = jnp.concatenate([own_valid, other_valid])
    lane = jnp.arange(PAIR) % HEAD
    key_mask = jnp.where(key_valid > 0, 0.0, MASKED)[:, None]
    key_base = jnp.where(lane == 0, key_mask, jnp.where(lane < 4, 1.0, 0.0)).astype(BF16)


    def project(weight, i):
        return ((dot(h_one, weight) + bias_mixed[i]) * scale_mixed).astype(BF16)

    h_one = rows_call(
        first_kernel, [all_inputs], [gain_one[None], bias_one[None]], [BF16], 0, "first_norm"
    )[0]
    mixed = [project(qkv_first, 0)]
    context, queries = [], []

    def attend_pair(pair, *ready):
        before = context[-1] if context else None
        base = after(key_base, *ready)
        results = attend(mixed[pair // 2], base, pair % 2, before, pair, 4)
        context.append(results[0])
        queries.append(results[1])

    ready = (h_one,) + qkv_b.got(4, 2, 1)
    qkv_b.send(6, 3, 5, ready=ready)
    attend_pair(0, *ready)
    ready = (queries[0],) + qkv_b.got(6, 3, 5)
    qkv_b.send(7, ready=ready)
    other_grads = swap_chip(after(take(cotangent, 1 - chip), *ready))
    attend_pair(1, *ready)
    second_columns = qkv_b.result()
    mixed.append(project(second_columns[:, :row_width], 1))
    ready = (queries[1], mixed[1], other_grads)
    kept = lax.dynamic_slice(second_columns, (core * half, row_width), (half, half))
    received = lax.dynamic_slice(second_columns, ((1 - core) * half, row_width), (half, half))
    received = swap_core(after(received, mixed[1]))
    attend_pair(2, kept, *ready)
    ready = (queries[2], received)
    attend_pair(3, *ready)
    own_grads = jnp.concatenate([take(cotangent, chip), after(other_grads, queries[3])], axis=0)
    full_out = jnp.concatenate(in_core_order(kept, received, core, 1), axis=1)
    all_context = context[3]
    own_part, other_part = both_halves_product([(all_context, full_out)], NN)
    ready = (own_grads, own_part)
    counted = own_valid.astype(F32)[:, None]
    residual_mid, h_two, middle_sums = rows_call(
        middle_kernel,
        [own_part, after(other_part, *ready), own_inputs, counted],
        [bias_out[None], gain_two[None], bias_two[None]],
        [F32, BF16],
        2,
        "middle",
    )
    h_two = with_partner(h_two)
    all_grads = with_partner(after(own_grads, residual_mid))
    grad_sums = column_sum(own_grads)
    h_two = after(h_two, grad_sums)
    active, slope = gelu_both(dot(h_two, full_fc1) + bias_fc1)
    active, slope = active.astype(BF16), slope.astype(BF16)
    active = after(active, full_fc2)
    fc2_product = dot(active, all_grads, TN).astype(BF16)
    fc2_scatter = Scatter(fc2_product)

    late_grads = after(all_grads, *fc2_scatter.got("keep"))
    grad_hidden, hidden_sums = hidden_gradient(late_grads, full_fc2, slope)
    fc1_halves = weight_halves(h_two, grad_hidden)
    fc1_scatter = Scatter(fc1_halves[0], halves=fc1_halves)
    own_part, other_part = both_halves_product(
        [(after(grad_hidden, fc1_scatter.sent), full_fc1)], NT
    )
    grad_residual, own_grad_attn, two_sums = rows_call(
        norm_back_kernel,
        [own_part, other_part, residual_mid, own_grads],
        [gain_two[None]],
        [F32, BF16],
        3,
        "norm_back",
    )
    grad_attn = with_partner(own_grad_attn)
    grad_context = half_product([(grad_attn, full_out)], NT, None, BF16)
    halves, sums = [None, None], []

    def back_pair(pair, *ready):
        grad_mixed, parts = attend_back(
            queries[pair],
            mixed[pair // 2],
            grad_context,
            all_context,
            after(key_base, *ready),
            pair % 2,
            pair,
            halves[pair // 2],
        )
        halves[pair // 2] = grad_mixed
        sums.append(parts)

    back_pair(0, grad_context)
    ready = (sums[0],) + fc2_scatter.got("side")
    grad_out = dot(all_context, after(grad_attn, *ready), TN).astype(BF16)
    kept = lax.dynamic_slice_in_dim(grad_out, core * half, half, 1)
    received = swap_core(lax.dynamic_slice_in_dim(grad_out, (1 - core) * half, half, 1))
    fc2_scatter.near(*ready)
    back_pair(1, kept, *ready, *fc2_scatter.got("keep"))
    received = after(received, sums[1])
    grad_out = jnp.concatenate(in_core_order(kept, received, core, 0), axis=0)
    early = jnp.concatenate([dot(h_one, halves[0], TN).astype(BF16), grad_out], axis=1)
    ready = (sums[1], fc1_scatter.crossed) + fc2_scatter.got("near_sums")
    fc2_scatter.far(*ready)
    fc1_scatter.cross(*ready)
    early_scatter = Scatter(early, *ready)
    ready += fc2_scatter.got("keep") + fc1_scatter.got("keep") + early_scatter.got("keep")
    own_mlp, other_mlp = both_halves_product([(after(active, *ready), full_fc2)], NN)
    low_output, end_sums = rows_call(
        end_kernel,
        [own_mlp, other_mlp, residual_mid, counted],
        [bias_fc2[None]],
        [BF16],
        2,
        "end",
    )
    back_pair(2, low_output, *ready)
    output_back = swap_chip(low_output[rows:])
    ready = (sums[2], output_back) + fc2_scatter.got("far_sums") + fc1_scatter.got("side")
    ready += early_scatter.got("side")
    fc2_scatter.chips(*ready)
    fc1_scatter.near(*ready)
    early_scatter.near(*ready)
    ready += (fc2_scatter.sums,) + fc1_scatter.got("keep") + early_scatter.got("keep")
    back_pair(3, *ready)
    ready = (sums[3], fc2_scatter.other_chip) + fc1_scatter.got("near_sums")
    ready += early_scatter.got("near_sums")
    early_scatter.far(*ready)
    fc1_scatter.far(*ready)
    fc2_scatter.cores(*ready)
    late_scatter = Scatter(dot(after(h_one, *ready), halves[1], TN))
    gm_first, gm_second = after(tuple(halves), *late_scatter.got("keep"))
    own_one, other_one = both_halves_product(
        [(gm_first, qkv_first), (gm_second, second_columns)], NT
    )
    low_input_grad, one_sums = rows_call(
        norm_back_kernel,
        [own_one, other_one, own_inputs, grad_residual],
        [gain_one[None]],
        [BF16],
        3,
        "norm_back",
    )
    input_back = swap_chip(low_input_grad[rows:])
    ready = late_scatter.got("side") + (low_input_grad,)
    late_scatter.near(*ready)
    one_sums = after(one_sums, *ready)

    if groups == 8:
        packed = pack_lines(
            [one_sums, two_sums, grad_sums[None], hidden_sums, end_sums, middle_sums], sums
        )
    else:
        lines = [one_sums[0], one_sums[1], two_sums[2], two_sums[0], two_sums[1], grad_sums]
        lines.append(hidden_sums[0])
        squares = [end_sums[0], middle_sums[0], end_sums[1], middle_sums[1]]
        squares = [jnp.sum(line.reshape(-1, PAIR), axis=0) for line in squares]

        def by_core(values):
            full = jnp.zeros((2, values.shape[0]), F32)
            return lax.dynamic_update_index_in_dim(full, values, core, 0).reshape(-1)

        wide = lines[:2] + [by_core(jnp.concatenate([part[n] for part in sums])) for n in range(2)]
        wide = [line.reshape(groups, own_width) for line in wide + lines[2:6]]
        all_sums = jnp.zeros((groups, 2, half_rows), F32)
        all_sums = lax.dynamic_update_index_in_dim(
            all_sums, lines[6].reshape(groups, half_rows), core, 1
        )
        wide.append(all_sums.reshape(groups, hidden_rows))
        wide.append(jnp.zeros((groups, 12 * PAIR - used)))
        wide.append(jnp.broadcast_to(jnp.concatenate(squares), (groups, 4 * PAIR)))
        packed = jnp.concatenate(wide, axis=1).astype(BF16).reshape(groups * 16, PAIR)
    ready = early_scatter.got("far_sums")
    packed = add_low(packed, after(swap_chip(packed), *ready))
    fc1_scatter.chips(packed)
    early_scatter.chips(packed)
    ready = late_scatter.got("near_sums")
    packed = add_low(packed, after(swap_core(packed), *ready))
    late_scatter.far(packed)
    vector_scatter = Scatter(packed, ordered=True)
    vector_scatter.near(early_scatter.other_chip, fc1_scatter.other_chip)
    fc1_scatter.cores(*vector_scatter.got("keep"))
    early_scatter.cores(*vector_scatter.got("keep"))
    ready = late_scatter.got("far_sums") + (input_back,)
    vector_scatter.far(*ready)
    late_scatter.chips(*vector_scatter.got("keep"))
    late_scatter.cores()
    ready_last = (packed,)
    output = all_clips(low_output, after(output_back, packed))
    input_grad = all_clips(low_input_grad, input_back)

    def in_columns(values, other, blocks):
        size = values.shape[1] // blocks
        parts = in_core_order(values, other, core, 0)
        parts = [part.reshape(own_width, blocks, 1, size) for part in parts]
        return jnp.concatenate(parts, axis=2).reshape(own_width, -1).astype(F32)

    fc2_parts = after((fc2_scatter.total, fc2_scatter.other_core), *ready_last)
    fc2_grad = in_core_order(*fc2_parts, core, 0)
    fc2_grad = jnp.concatenate(fc2_grad, axis=0).astype(F32)
    early_parts = [early_scatter.total, early_scatter.other_core]
    late_parts = [late_scatter.total, late_scatter.other_core]
    fc1_parts = after((fc1_scatter.total, fc1_scatter.other_core), *ready_last)
    if groups == 8:
        fc1_places = [
            (0, n * half_rows, half_rows, 2 * n * half_rows, (2 * n + 1) * half_rows)
            for n in range(groups)
        ]
        fc1_grad = join_columns(fc1_parts, fc1_places, 2 * groups * half_rows)
        out_grad = join_columns(early_parts, [(0, row_width, half, 0, half)], width)
        qkv_places = []
        for n in range(3):
            for pair in range(4):
                target = n * width + pair * PAIR
                start = (3 * (pair % 2) + n) * PAIR
                qkv_places.append((pair // 2, start, PAIR, target, target + half))
        qkv_grad = join_columns(early_parts + late_parts, qkv_places, 3 * width)
    else:
        fc1_grad = in_columns(*fc1_parts, groups)
        out_grad = in_columns(*[part[:, row_width:] for part in early_parts], 1)

        def both_halves(left, right):
            left = left[:, :row_width].reshape(own_width, 1, 2, 3, PAIR)
            right = right.reshape(own_width, 1, 2, 3, PAIR)
            both = jnp.concatenate([left, right], axis=1).transpose(0, 3, 1, 2, 4)
            return both.reshape(own_width, 3 * half)

        qkv_grad = in_columns(*[both_halves(*pair) for pair in zip(early_parts, late_parts)], 3)
    lines = vector_scatter.last()
    flat = lines[:12].reshape(-1)
    own_vectors = [flat[i * own_width : (i + 1) * own_width] for i in range(8)]
    own_hidden = flat[8 * own_width : used]
    totals = jnp.sum(lines[12:], axis=1)
    branch_rms = jnp.sqrt(totals[:3] / totals[3])
    return (
        output,
        input_grad,
        own_vectors[0],
        own_vectors[1],
        qkv_grad,
        own_vectors[2],
        own_vectors[3],
        out_grad,
        own_vectors[4],
        own_vectors[5],
        own_vectors[6],
        fc1_grad,
        own_hidden,
        fc2_grad,
        own_vectors[7],
        branch_rms,
    )


def solution(mesh):
    tokens, rows, vector = P("fsdp", "seq", None), P("fsdp", None), P("fsdp")
    return jax.shard_map(
        body,
        mesh=mesh,
        in_specs=(
            tokens,
            tokens,
            rows,
            vector,
            vector,
            rows,
            vector,
            vector,
            rows,
            vector,
            vector,
            vector,
            rows,
            vector,
            rows,
            vector,
        ),
        out_specs=(
            tokens,
            tokens,
            vector,
            vector,
            rows,
            vector,
            vector,
            rows,
            vector,
            vector,
            vector,
            rows,
            vector,
            rows,
            vector,
            P(),
        ),
        check_vma=False,
    )
```

```python
from functools import partial

import jax
import jax.numpy as jnp
from jax import lax
from jax.experimental import pallas as pl
from jax.experimental.pallas import tpu as pltpu
from jax.sharding import PartitionSpec as P

HEADS = 16
HEAD = 64
PAIR = 2 * HEAD
EPS = 1e-06
MASKED = -1e30
VMEM_BYTES = 28 * 2**20
BF16 = jnp.bfloat16
F32 = jnp.float32
NN = (((1,), (0,)), ((), ()))
NT = (((1,), (1,)), ((), ()))
TN = (((0,), (0,)), ((), ()))
SMALL_COST = pl.CostEstimate(flops=10**7, bytes_accessed=2**20, transcendentals=0)


def dot(left, right, dims=NN):
    return lax.dot_general(left, right, dims, preferred_element_type=F32)


def lanes_of(shape):
    return lax.broadcasted_iota(jnp.int32, shape, len(shape) - 1)


def three_parts(column):
    high = column.astype(BF16).astype(F32)
    rest = column - high
    middle = rest.astype(BF16).astype(F32)
    return high, middle, rest - middle


def block_rows(length, *sizes):
    for rows in sizes + (224, 112, 16):
        if length % rows == 0:
            return rows
    return length


def attend_kernel(q_ref, k_ref, v_ref, key_base_ref, *refs):
    context_ref, query_ref = refs[-2:]
    length = q_ref.shape[0]
    rows = block_rows(length, 392)
    low = lanes_of((length, PAIR)) < HEAD
    keys, values, key_base = k_ref[...], v_ref[...], key_base_ref[...]
    ones = jnp.ones((length, PAIR), BF16)
    keys_of = [jnp.where(low, keys, key_base), jnp.where(low, key_base, keys)]
    values_of = [jnp.where(low, values, ones), jnp.where(low, ones, values)]
    lane = lanes_of((rows, PAIR))
    low_rows = lane < HEAD
    for step in range(length // rows):
        span = slice(step * rows, (step + 1) * rows)
        queries = q_ref[span, :]
        results = []
        for head in range(2):
            base = HEAD * (1 - head)
            own = low_rows if head == 0 else jnp.logical_not(low_rows)
            unit = jnp.where(lane == base, 1.0, 0.0)
            scores = dot(jnp.where(own, queries, unit.astype(BF16)), keys_of[head], NT)
            highest = jnp.max(scores, axis=1, keepdims=True)
            weights = jnp.exp(scores - highest).astype(BF16)
            mixed = dot(weights, values_of[head])
            total = mixed[:, base : base + 1]
            high, middle, rest = three_parts(-(highest + jnp.log(total)))
            extra = jnp.where(lane == base + 3, rest, unit)
            extra = jnp.where(lane == base + 2, middle, extra)
            extra = jnp.where(lane == base + 1, high, extra)
            query_ref[head, span, :] = jnp.where(own, queries, extra.astype(BF16))
            results.append(mixed / total)
        context_ref[span, :] = jnp.where(low_rows, results[0], results[1]).astype(BF16)


def attend(mixed, key_base, pair, context, place, places):
    length = mixed.shape[0]
    tile = lambda column: pl.BlockSpec((length, PAIR), lambda i: (0, column))
    in_specs = [tile(3 * pair), tile(3 * pair + 1), tile(3 * pair + 2), tile(0)]
    operands = (mixed, mixed, mixed, key_base)
    aliases = {}
    if context is not None:
        in_specs.append(pl.BlockSpec(memory_space=pl.ANY))
        operands += (context,)
        aliases = {4: 0}
    return pl.pallas_call(
        attend_kernel,
        grid=(1,),
        in_specs=in_specs,
        out_specs=[tile(place), pl.BlockSpec((2, length, PAIR), lambda i: (0, 0, 0))],
        out_shape=[
            jax.ShapeDtypeStruct((length, places * PAIR), BF16),
            jax.ShapeDtypeStruct((2, length, PAIR), BF16),
        ],
        input_output_aliases=aliases,
        compiler_params=pltpu.CompilerParams(vmem_limit_bytes=VMEM_BYTES),
        cost_estimate=SMALL_COST,
        name="attend",
    )(*operands)


def attend_back_kernel(query_ref, k_ref, v_ref, grad_ref, context_ref, key_base_ref, *refs):
    grad_mixed_ref, sums_ref = refs[-2:]
    length = k_ref.shape[0]
    rows = block_rows(length)
    low = lanes_of((length, PAIR)) < HEAD
    keys, values, key_base = k_ref[...], v_ref[...], key_base_ref[...]
    ones = jnp.ones((length, PAIR), BF16)
    lane = lanes_of((rows, PAIR))
    low_rows = lane < HEAD
    steps = length // rows
    grad_q, grad_k, grad_v = [], [], []
    sum_q = jnp.zeros((1, PAIR), F32)
    for head in range(2):
        base = HEAD * (1 - head)
        own = low if head == 0 else jnp.logical_not(low)
        own_rows = low_rows if head == 0 else jnp.logical_not(low_rows)
        head_keys = jnp.where(own, keys, key_base)
        head_values = jnp.where(own, values, ones)
        sum_k = jnp.zeros((length, PAIR), F32)
        sum_v = jnp.zeros((length, PAIR), F32)
        for step in range(steps):
            span = slice(step * rows, (step + 1) * rows)
            queries = query_ref[head, span, :]
            grads = grad_ref[span, :]
            product = grads.astype(F32) * context_ref[span, :].astype(F32)
            inner = jnp.sum(jnp.where(own_rows, product, 0.0), axis=1, keepdims=True)
            high, middle, rest = three_parts(-inner)
            extra = jnp.where(lane == base + 2, rest, 0.0)
            extra = jnp.where(lane == base + 1, middle, extra)
            extra = jnp.where(lane == base, high, extra)
            head_grads = jnp.where(own_rows, grads, extra.astype(BF16))
            probs = jnp.exp(dot(head_keys, queries, NT))
            grad_scores = (probs * dot(head_values, head_grads, NT)).astype(BF16)
            sum_v = sum_v + dot(probs.astype(BF16), grads)
            sum_k = sum_k + dot(grad_scores, queries)
            part = dot(grad_scores, keys, TN)
            if head == 0:
                grad_q.append(part)
            else:
                both = jnp.where(low_rows, grad_q[step], part).astype(BF16)
                both = both * (HEAD ** (-0.5))
                grad_mixed_ref[span, :PAIR] = both
                sum_q = sum_q + jnp.sum(both.astype(F32), axis=0, keepdims=True)
        grad_k.append(sum_k)
        grad_v.append(sum_v)
    grad_mixed_ref[:, PAIR : 2 * PAIR] = jnp.where(low, grad_k[0], grad_k[1]).astype(BF16)
    both = jnp.where(low, grad_v[0], grad_v[1]).astype(BF16)
    grad_mixed_ref[:, 2 * PAIR :] = both
    sums_ref[0:1, :] = sum_q
    sums_ref[1:2, :] = jnp.sum(both.astype(F32), axis=0, keepdims=True)


def attend_back(queries, mixed, grad_context, context, key_base, pair, place, grad_mixed):
    length = mixed.shape[0]
    tile = lambda column: pl.BlockSpec((length, PAIR), lambda i: (0, column))
    in_specs = [
        pl.BlockSpec((2, length, PAIR), lambda i: (0, 0, 0)),
        tile(3 * pair + 1),
        tile(3 * pair + 2),
        tile(place),
        tile(place),
        tile(0),
    ]
    operands = (queries, mixed, mixed, grad_context, context, key_base)
    aliases = {}
    if grad_mixed is not None:
        in_specs.append(pl.BlockSpec(memory_space=pl.ANY))
        operands += (grad_mixed,)
        aliases = {6: 0}
    return pl.pallas_call(
        attend_back_kernel,
        grid=(1,),
        in_specs=in_specs,
        out_specs=[
            pl.BlockSpec((length, 3 * PAIR), lambda i: (0, pair)),
            pl.BlockSpec((2, PAIR), lambda i: (0, 0)),
        ],
        out_shape=[
            jax.ShapeDtypeStruct((length, 6 * PAIR), BF16),
            jax.ShapeDtypeStruct((2, PAIR), F32),
        ],
        input_output_aliases=aliases,
        compiler_params=pltpu.CompilerParams(vmem_limit_bytes=VMEM_BYTES),
        cost_estimate=SMALL_COST,
        name="attend_back",
    )(*operands)


def normalize(values):
    center = values - jnp.mean(values, axis=-1, keepdims=True)
    spread = jnp.mean(center * center, axis=-1, keepdims=True)
    scale = lax.rsqrt(spread + EPS)
    return center * scale, scale


def rows_call(kernel, row_inputs, constants, kinds, sum_rows, name):
    rows, width = row_inputs[0].shape
    tile = rows // 7 if rows % 112 == 0 else rows
    block = lambda columns: pl.BlockSpec((tile, columns), lambda i: (i, 0))
    whole = lambda shape: pl.BlockSpec(shape, lambda i: (0, 0))
    out_specs = [block(width)] * len(kinds)
    out_shape = [jax.ShapeDtypeStruct((rows, width), kind) for kind in kinds]
    if sum_rows:
        out_specs.append(whole((sum_rows, width)))
        out_shape.append(jax.ShapeDtypeStruct((sum_rows, width), F32))
    return pl.pallas_call(
        kernel,
        grid=(rows // tile,),
        in_specs=[block(part.shape[1]) for part in row_inputs]
        + [whole(part.shape) for part in constants],
        out_specs=out_specs,
        out_shape=out_shape,
        compiler_params=pltpu.CompilerParams(vmem_limit_bytes=VMEM_BYTES),
        cost_estimate=SMALL_COST,
        name=name,
    )(*row_inputs, *constants)


def add_rows(sums_ref, parts):
    @pl.when(pl.program_id(0) == 0)
    def _():
        sums_ref[...] = jnp.zeros(sums_ref.shape, F32)

    lines = [jnp.sum(part, axis=0, keepdims=True) for part in parts]
    sums_ref[...] += jnp.concatenate(lines, axis=0)


def first_kernel(values_ref, gain_ref, bias_ref, out_ref):
    normal = normalize(values_ref[...].astype(F32))[0]
    out_ref[...] = (normal * gain_ref[...] + bias_ref[...]).astype(BF16)


def middle_kernel(
    own_ref, other_ref, inputs_ref, counted_ref, out_bias_ref, gain_ref, bias_ref, *out_refs
):
    middle_ref, low_ref, sums_ref = out_refs
    branch = own_ref[...] + other_ref[...].astype(F32) + out_bias_ref[...]
    middle = inputs_ref[...].astype(F32) + branch
    middle_ref[...] = middle
    low_ref[...] = (normalize(middle)[0] * gain_ref[...] + bias_ref[...]).astype(BF16)
    counted = counted_ref[...]
    add_rows(sums_ref, [counted * branch * branch, jnp.broadcast_to(counted, branch.shape)])


def end_kernel(own_ref, other_ref, middle_ref, counted_ref, bias_ref, low_ref, sums_ref):
    branch = own_ref[...] + other_ref[...].astype(F32) + bias_ref[...]
    result = middle_ref[...] + branch
    low_ref[...] = result.astype(BF16)
    counted = counted_ref[...]
    add_rows(sums_ref, [counted * result * result, counted * branch * branch])


def norm_back_kernel(own_ref, other_ref, values_ref, residual_ref, gain_ref, *out_refs):
    grad = own_ref[...] + other_ref[...].astype(F32)
    normal, scale = normalize(values_ref[...].astype(F32))
    inner = grad * gain_ref[...]
    first = jnp.mean(inner, axis=-1, keepdims=True)
    second = jnp.mean(inner * normal, axis=-1, keepdims=True)
    total = residual_ref[...].astype(F32) + scale * (inner - first - normal * second)
    low = total.astype(BF16)
    if len(out_refs) == 3:
        out_refs[0][...] = total
    out_refs[-2][...] = low
    add_rows(out_refs[-1], [grad * normal, grad, low.astype(F32)])


def weight_kernel(left_ref, right_ref, kept_ref, sent_ref):
    chip = lax.axis_index("seq") // 2
    left, half = left_ref[...], kept_ref.shape[1]
    for part, out_ref in ((chip, kept_ref), (1 - chip, sent_ref)):
        columns = pl.ds(pl.multiple_of(part * half, half), half)
        out_ref[...] = dot(left, right_ref[:, columns], TN).astype(BF16)


def weight_halves(left, right):
    rows, depth = left.shape
    columns = right.shape[1]
    tile = min(depth, 512)
    half = pl.BlockSpec((tile, columns // 2), lambda i: (i, 0))
    return pl.pallas_call(
        weight_kernel,
        grid=(depth // tile,),
        in_specs=[
            pl.BlockSpec((rows, tile), lambda i: (0, i)),
            pl.BlockSpec((rows, columns), lambda i: (0, 0)),
        ],
        out_specs=[half, half],
        out_shape=[jax.ShapeDtypeStruct((depth, columns // 2), BF16)] * 2,
        compiler_params=pltpu.CompilerParams(vmem_limit_bytes=VMEM_BYTES),
        cost_estimate=SMALL_COST,
        name="weight_halves",
    )(left, right)


def gelu_both(values):
    half = 0.5 * (1.0 + lax.erf(values * (0.5**0.5)))
    density = jnp.exp(-0.5 * values * values) * (0.5 / jnp.pi) ** 0.5
    return values * half, half + values * density


def hidden_kernel(grad_ref, weight_ref, slope_ref, hidden_ref, sums_ref):
    rows = grad_ref.shape[0] // 2
    weight = weight_ref[...]
    total = jnp.zeros((1, weight.shape[0]), F32)
    for span in (slice(0, rows), slice(rows, 2 * rows)):
        hidden = (dot(grad_ref[span, :], weight, NT) * slope_ref[span, :].astype(F32)).astype(BF16)
        hidden_ref[span, :] = hidden
        total = total + jnp.sum(hidden.astype(F32), axis=0, keepdims=True)
    sums_ref[...] = total


def hidden_gradient(grads, weight, slope):
    rows, depth = grads.shape
    columns = weight.shape[0]
    tile = min(columns, 512)
    block = pl.BlockSpec((rows, tile), lambda i: (0, i))
    return pl.pallas_call(
        hidden_kernel,
        grid=(columns // tile,),
        in_specs=[
            pl.BlockSpec((rows, depth), lambda i: (0, 0)),
            pl.BlockSpec((tile, depth), lambda i: (i, 0)),
            block,
        ],
        out_specs=[block, pl.BlockSpec((1, tile), lambda i: (0, i))],
        out_shape=[
            jax.ShapeDtypeStruct((rows, columns), BF16),
            jax.ShapeDtypeStruct((1, columns), F32),
        ],
        compiler_params=pltpu.CompilerParams(vmem_limit_bytes=VMEM_BYTES),
        cost_estimate=SMALL_COST,
        name="hidden_gradient",
    )(grads, weight, slope)


def half_kernel(dims, *refs):
    total = dot(refs[0][...], refs[1][...], dims)
    for n in range(2, len(refs) - 1, 2):
        total = total + dot(refs[n][...], refs[n + 1][...], dims)
    refs[-1][...] = total.astype(refs[-1].dtype)


def half_product(pairs, dims, part, kind):
    rows = pairs[0][0].shape[0] if part is None else pairs[0][0].shape[0] // 2
    part = part or 0
    columns = pairs[0][1].shape[1 if dims is NN else 0]
    tile = min(columns, 512)
    in_specs, operands = [], []
    for left, right in pairs:
        depth = left.shape[1]
        in_specs.append(pl.BlockSpec((rows, depth), lambda i: (part, 0)))
        if dims is NN:
            in_specs.append(pl.BlockSpec((depth, tile), lambda i: (0, i)))
        else:
            in_specs.append(pl.BlockSpec((tile, depth), lambda i: (i, 0)))
        operands += [left, right]
    return pl.pallas_call(
        partial(half_kernel, dims),
        grid=(columns // tile,),
        in_specs=in_specs,
        out_specs=pl.BlockSpec((rows, tile), lambda i: (0, i)),
        out_shape=jax.ShapeDtypeStruct((rows, columns), kind),
        compiler_params=pltpu.CompilerParams(vmem_limit_bytes=VMEM_BYTES),
        cost_estimate=SMALL_COST,
        name="half_product",
    )(*operands)


def both_halves_product(pairs, dims):
    other = half_product(pairs, dims, 1, BF16)
    own = [(after(left, other), right) for left, right in pairs]
    return half_product(own, dims, 0, F32), swap_core(other)


def join_kernel(places, *refs):
    out_ref = refs[-1]
    core = lax.rem(lax.axis_index("seq"), 2)
    for n, (source, start, width, first, second) in enumerate(places):
        for other in range(2):
            target = pl.multiple_of(jnp.where(core == other, first, second), PAIR)
            block = refs[2 * source + other][:, start : start + width]
            out_ref[:, pl.ds(target, width)] = block.astype(F32)


def join_columns(parts, places, columns):
    rows = parts[0].shape[0]
    return pl.pallas_call(
        partial(join_kernel, places),
        in_specs=[pl.BlockSpec(memory_space=pltpu.VMEM)] * len(parts),
        out_specs=pl.BlockSpec(memory_space=pltpu.VMEM),
        out_shape=jax.ShapeDtypeStruct((rows, columns), F32),
        cost_estimate=SMALL_COST,
        name="join_columns",
    )(*parts)


def column_sum(values):
    return jnp.sum(values, axis=0, dtype=F32)


def swap_core(values):
    return lax.ppermute(values, "seq", [(0, 1), (1, 0), (2, 3), (3, 2)])


def swap_chip(values):
    return lax.ppermute(values, "seq", [(0, 2), (2, 0), (1, 3), (3, 1)])


def stack_kernel(own_ref, other_ref, out_ref, sems):
    rows = own_ref.shape[0]
    copies = [
        pltpu.make_async_copy(ref, out_ref.at[pl.ds(n * rows, rows)], sems.at[n])
        for n, ref in enumerate((own_ref, other_ref))
    ]
    for copy in copies:
        copy.start()
    for copy in copies:
        copy.wait()


def with_partner(values):
    rows, columns = values.shape
    return pl.pallas_call(
        stack_kernel,
        in_specs=[pl.BlockSpec(memory_space=pltpu.VMEM)] * 2,
        out_specs=pl.BlockSpec(memory_space=pl.ANY),
        out_shape=jax.ShapeDtypeStruct((2 * rows, columns), values.dtype),
        scratch_shapes=[pltpu.SemaphoreType.DMA((2,))],
        compiler_params=pltpu.CompilerParams(vmem_limit_bytes=16 * 2**20),
        cost_estimate=SMALL_COST,
        name="stack_rows",
    )(values, swap_core(values))


def swap_group(values, bit):
    return lax.ppermute(values, "fsdp", [(i, i ^ bit) for i in range(8)])


def order_kernel(count, *refs):
    pieces, full_ref, held, arrived, sent = refs[:count], refs[count], *refs[-3:]
    group = lax.axis_index("fsdp")
    rows = full_ref.shape[0] // count
    loads = [
        pltpu.make_async_copy(piece, held.at[relative], arrived.at[relative])
        for relative, piece in enumerate(pieces)
    ]
    for load in loads:
        load.start()
    stores = []
    for relative in range(count):
        start = pl.multiple_of((group ^ relative) * rows, rows)
        store = pltpu.make_async_copy(
            held.at[relative, pl.ds(0, rows)], full_ref.at[pl.ds(start, rows)], sent.at[relative]
        )
        loads[relative].wait()
        store.start()
        stores.append(store)
    if len(refs) > count + 4:
        own_width, core = 128, lax.rem(lax.axis_index("seq"), 2)
        wide_ref, bias_ref = refs[count + 1], refs[count + 2]
        for relative in range(count):
            place = group ^ relative
            columns = pl.ds(pl.multiple_of(place * own_width, own_width), own_width)
            extra = held[relative, rows : rows + 8, :].astype(F32)
            lines = [
                extra[k : k + 1, own_width * n : own_width * (n + 1)]
                for k in range(2)
                for n in range(6)
            ]
            for n in range(8):
                wide_ref[n : n + 1, columns] = lines[n]
            for n in range(2):
                start = pl.multiple_of((place * 2 + n) * own_width, own_width)
                bias_ref[:, pl.ds(start, own_width)] = jnp.where(
                    core == 0, lines[8 + n], lines[10 + n]
                )
    for store in stores:
        store.wait()


def in_order(pieces, rows, with_vectors=False):
    count, columns = len(pieces), pieces[0].shape[1]
    out_specs = [pl.BlockSpec(memory_space=pl.ANY)]
    out_shape = [jax.ShapeDtypeStruct((count * rows, columns), pieces[0].dtype)]
    if with_vectors:
        out_specs += [pl.BlockSpec(memory_space=pltpu.VMEM)] * 2
        out_shape += [jax.ShapeDtypeStruct((8, 1024), F32), jax.ShapeDtypeStruct((1, 2048), F32)]
    result = pl.pallas_call(
        partial(order_kernel, count),
        in_specs=[pl.BlockSpec(memory_space=pl.ANY)] * count,
        out_specs=out_specs,
        out_shape=out_shape,
        scratch_shapes=[
            pltpu.VMEM((count,) + pieces[0].shape, pieces[0].dtype),
            pltpu.SemaphoreType.DMA((count,)),
            pltpu.SemaphoreType.DMA((count,)),
        ],
        compiler_params=pltpu.CompilerParams(vmem_limit_bytes=16 * 2**20),
        cost_estimate=SMALL_COST,
        name="in_order",
    )(*pieces)
    return result if with_vectors else result[0]


def own_kernel(qkv_ref, out_ref, *refs):
    vector_refs, (first_ref, second_ref) = refs[:-2], refs[-2:]
    core = lax.rem(lax.axis_index("seq"), 2)
    rows = qkv_ref.shape[0]
    for n in range(3):
        for pair in range(4):
            block_ref = second_ref if pair >= 2 else first_ref
            start = pl.multiple_of((8 * n + pair + 4 * core) * PAIR, PAIR)
            target = (3 * (pair % 2) + n) * PAIR
            block_ref[:rows, target : target + PAIR] = qkv_ref[:, pl.ds(start, PAIR)]
    out_half = out_ref.shape[1] // 2
    start = pl.multiple_of(core * out_half, out_half)
    second_ref[:, 6 * PAIR :] = out_ref[:, pl.ds(start, out_half)]
    lines = []
    for ref in vector_refs:
        vector = ref[...].astype(F32).reshape(ref.shape[0] // PAIR, PAIR)
        lines += [vector[n : n + 1] for n in range(ref.shape[0] // PAIR)]
    row = lax.broadcasted_iota(jnp.int32, (8, PAIR), 0)
    for n in range(6):
        block = jnp.where(row == 0, lines[n], jnp.where(row == 1, lines[n + 6], 0.0))
        first_ref[rows:, PAIR * n : PAIR * (n + 1)] = block.astype(BF16)


def own_qkv_blocks(qkv_weight, out_weight, vectors):
    rows, columns = qkv_weight.shape[0], qkv_weight.shape[1] // 4
    out_half = out_weight.shape[1] // 2
    return pl.pallas_call(
        own_kernel,
        in_specs=[pl.BlockSpec(memory_space=pltpu.VMEM)] * (2 + len(vectors)),
        out_specs=[pl.BlockSpec(memory_space=pltpu.VMEM)] * 2,
        out_shape=[
            jax.ShapeDtypeStruct((rows + 8, columns), BF16),
            jax.ShapeDtypeStruct((rows, columns + out_half), BF16),
        ],
        cost_estimate=SMALL_COST,
        name="own_qkv",
    )(qkv_weight, out_weight, *vectors)


def own_rest_kernel(fc1_ref, fc2_ref, first_ref, second_ref):
    core = lax.rem(lax.axis_index("seq"), 2)
    rows = second_ref.shape[0]
    for n in range(fc1_ref.shape[1] // (2 * rows)):
        start = pl.multiple_of((2 * n + core) * rows, rows)
        first_ref[:, n * rows : (n + 1) * rows] = fc1_ref[:, pl.ds(start, rows)]
    second_ref[...] = fc2_ref[pl.ds(pl.multiple_of(core * rows, rows), rows), :]


def own_rest_blocks(fc1_weight, fc2_weight):
    return pl.pallas_call(
        own_rest_kernel,
        in_specs=[pl.BlockSpec(memory_space=pltpu.VMEM)] * 2,
        out_specs=[pl.BlockSpec(memory_space=pltpu.VMEM)] * 2,
        out_shape=[
            jax.ShapeDtypeStruct((fc1_weight.shape[0], fc1_weight.shape[1] // 2), BF16),
            jax.ShapeDtypeStruct((fc2_weight.shape[0] // 2, fc2_weight.shape[1]), BF16),
        ],
        cost_estimate=SMALL_COST,
        name="own_rest",
    )(fc1_weight, fc2_weight)


def after(values, *others):
    return lax.optimization_barrier((values,) + others)[0] if others else values


class Gather:
    SOURCE = {4: 0, 2: 0, 1: 0, 6: 4, 3: 2, 5: 4, 7: 6}
    STEP = {4: 4, 2: 2, 1: 1, 6: 2, 3: 1, 5: 1, 7: 1}

    def __init__(self, own):
        self.pieces = [own] + [None] * 7
        self.grouped = lax.axis_size("fsdp") == 8

    def send(self, *parts, ready=()):
        if not self.grouped:
            return
        sources = [self.pieces[self.SOURCE[part]] for part in parts]
        if ready:
            sources = lax.optimization_barrier(tuple(sources) + tuple(ready))
        for part, source in zip(parts, sources):
            self.pieces[part] = swap_group(source, self.STEP[part])

    def got(self, *parts):
        return tuple(self.pieces[part] for part in parts) if self.grouped else ()

    def result(self):
        if not self.grouped:
            return lax.all_gather(self.pieces[0], "fsdp", axis=0, tiled=True)
        return in_order(self.pieces, self.pieces[0].shape[0])


def add_low(left, right):
    return (left.astype(F32) + right.astype(F32)).astype(BF16)


def split_kernel(full_ref, *refs):
    sems = refs[2]
    group = lax.axis_index("fsdp")
    rows = full_ref.shape[0] // 8
    copies = []
    for n in range(8):
        far, near, side = n % 2, (n // 2) % 2, n // 4
        start = pl.multiple_of((group ^ (4 * far + 2 * near + side)) * rows, rows)
        target = refs[side].at[pl.ds((n % 4) * rows, rows)]
        copies.append(
            pltpu.make_async_copy(full_ref.at[pl.ds(start, rows)], target, sems.at[n])
        )
    for copy in copies:
        copy.start()
    for copy in copies:
        copy.wait()


def split_blocks(values):
    rows, columns = values.shape
    return pl.pallas_call(
        split_kernel,
        in_specs=[pl.BlockSpec(memory_space=pltpu.VMEM)],
        out_specs=[pl.BlockSpec(memory_space=pl.ANY)] * 2,
        out_shape=[jax.ShapeDtypeStruct((rows // 2, columns), values.dtype)] * 2,
        scratch_shapes=[pltpu.SemaphoreType.DMA((8,))],
        compiler_params=pltpu.CompilerParams(vmem_limit_bytes=16 * 2**20),
        cost_estimate=SMALL_COST,
        name="split_blocks",
    )(values)


def pack_kernel(
    one_ref, two_ref, grads_ref, hidden_ref, end_ref, middle_ref, *refs
):
    sum_refs, packed_ref = refs[:4], refs[4]
    group = lax.axis_index("fsdp")
    core = lax.rem(lax.axis_index("seq"), 2)
    squares = jnp.zeros((4, PAIR), F32)
    for n in range(end_ref.shape[1] // PAIR):
        span = slice(n * PAIR, (n + 1) * PAIR)
        end, middle = end_ref[:, span], middle_ref[:, span]
        squares = squares + jnp.concatenate([end[:1], middle[:1], end[1:], middle[1:]], axis=0)
    for n in range(8):
        far, near, side = n % 2, (n // 2) % 2, n // 4
        target = group ^ (4 * far + 2 * near + side)
        columns = pl.ds(pl.multiple_of(target * PAIR, PAIR), PAIR)
        mine = (target // 4) == core
        pair = lax.rem(target, 4)
        head_sums = jnp.zeros((2, PAIR), F32)
        for k in range(4):
            head_sums = jnp.where(jnp.logical_and(mine, pair == k), sum_refs[k][...], head_sums)
        one, two = one_ref[:, columns], two_ref[:, columns]
        hidden = [
            hidden_ref[:, pl.ds(pl.multiple_of(target * 2 * PAIR + k * PAIR, PAIR), PAIR)]
            for k in range(2)
        ]
        empty = jnp.zeros((1, PAIR), F32)
        rows = [one[:2], head_sums, two[2:3], two[:2], grads_ref[:, columns]]
        rows += [jnp.where(core == 0, part, empty) for part in hidden]
        rows += [jnp.where(core == 0, empty, part) for part in hidden]
        rows.append(squares)
        packed_ref[16 * n : 16 * (n + 1), :] = jnp.concatenate(rows, axis=0).astype(BF16)


def pack_lines(lines, sums):
    return pl.pallas_call(
        pack_kernel,
        in_specs=[pl.BlockSpec(memory_space=pltpu.VMEM)] * 10,
        out_specs=pl.BlockSpec(memory_space=pltpu.VMEM),
        out_shape=jax.ShapeDtypeStruct((128, PAIR), BF16),
        cost_estimate=SMALL_COST,
        name="pack_lines",
    )(*lines, *sums)


class Scatter:
    def __init__(self, values, *ready, halves=None, ordered=False):
        self.grouped = lax.axis_size("fsdp") == 8
        self.halved = halves is not None
        values = values.astype(BF16)
        if self.halved:
            self.kept, self.sent = halves
            self.crossed = swap_chip(self.sent)
        elif self.grouped:
            middle = values.shape[0] // 2
            split = (values[:middle], values[middle:]) if ordered else split_blocks(values)
            self.keep, self.side_send = split
            self.side = swap_group(after(self.side_send, *ready), 1)
        else:
            self.sums = lax.psum_scatter(values, "fsdp", scatter_dimension=0, tiled=True)

    def cross(self, *ready):
        values = add_low(self.kept, after(self.crossed, *ready))
        if self.grouped:
            self.keep, self.side_send = split_blocks(values)
            self.side = swap_group(self.side_send, 1)
        else:
            self.sums = lax.psum_scatter(values, "fsdp", scatter_dimension=0, tiled=True)

    def got(self, *names):
        return tuple(getattr(self, name) for name in names if hasattr(self, name))

    def step(self, name, next_name, bit, ready):
        if self.grouped:
            received = after(getattr(self, name), *ready)
            half = self.keep.shape[0] // 2
            send = add_low(self.keep[half:], received[half:])
            self.keep = add_low(self.keep[:half], received[:half])
            setattr(self, next_name, swap_group(send, bit))

    def near(self, *ready):
        self.step("side", "near_sums", 2, ready)

    def far(self, *ready):
        self.step("near_sums", "far_sums", 4, ready)

    def chips(self, *ready, beside=None):
        if self.grouped:
            self.sums = add_low(self.keep, after(self.far_sums, *ready))
        if beside is not None:
            self.sums = jnp.concatenate([self.sums, beside], axis=1)
        self.other_chip = swap_chip(self.sums)

    def cores(self, *ready):
        other_chip = after(self.other_chip, *ready)
        if self.halved:
            chip = lax.axis_index("seq") // 2
            first = jnp.where(chip == 0, self.sums, other_chip)
            second = jnp.where(chip == 0, other_chip, self.sums)
            self.total = jnp.concatenate([first, second], axis=1)
        else:
            self.total = add_low(self.sums, other_chip)
        self.other_core = swap_core(self.total)

    def last(self):
        if not self.grouped:
            return self.sums.astype(F32)
        return self.keep.astype(F32) + self.far_sums.astype(F32)


def take(values, index):
    return lax.dynamic_index_in_dim(values, index, 0, keepdims=False)


def in_core_order(own, other, core, axis):
    first = jnp.where(core == 0, own, other)
    second = jnp.where(core == 0, other, own)
    return first, second


def body(
    inputs,
    cotangent,
    valid,
    ln1_gain,
    ln1_bias,
    qkv_weight,
    q_bias,
    v_bias,
    out_weight,
    out_bias,
    ln2_gain,
    ln2_bias,
    fc1_weight,
    fc1_bias,
    fc2_weight,
    fc2_bias,
):
    clips, rows, width = inputs.shape
    groups = lax.axis_size("fsdp")
    place = lax.axis_index("seq")
    group = lax.axis_index("fsdp")
    chip, core = place // 2, place % 2
    half = width // 2
    hidden_rows = fc2_weight.shape[0]
    half_rows = hidden_rows // 2
    own_rows = clips * rows
    scale_factor = HEAD ** (-0.5)

    def all_clips(values, back):
        mine = values[:rows]
        first = jnp.where(chip == 0, mine, back)
        second = jnp.where(chip == 0, back, mine)
        return jnp.stack([first, second])

    own_width = width // groups
    vectors = (ln1_gain, ln1_bias, q_bias, v_bias, out_bias, ln2_gain, ln2_bias, fc2_bias, fc1_bias)
    quarter = half // 2
    row_width = 3 * quarter
    used = 8 * own_width + fc1_bias.shape[0]
    if groups == 8:
        own_first, own_second = own_qkv_blocks(qkv_weight, out_weight, vectors)
    else:
        by_head = qkv_weight.reshape(own_width, 3, 2, 2, 2, PAIR)
        by_head = lax.dynamic_index_in_dim(by_head, core, 2, keepdims=False)
        by_head = by_head.transpose(0, 2, 3, 1, 4).reshape(own_width, 2, row_width)
        out_columns = lax.dynamic_slice_in_dim(out_weight, core * half, half, 1)
        own_first = by_head[:, 0]
        own_second = jnp.concatenate([by_head[:, 1], out_columns], axis=1)

    qkv_a, qkv_b = Gather(own_first), Gather(own_second)
    qkv_a.send(4, 2, 1)
    other_inputs = swap_chip(take(after(inputs, *qkv_a.got(4, 2, 1)), 1 - chip))
    qkv_a.send(6, 3, 5, ready=qkv_a.got(4, 2, 1))
    qkv_b.send(4, ready=qkv_a.got(4, 2, 1))
    fc1_weight, fc2_weight = after((fc1_weight, fc2_weight), own_first)
    if groups == 8:
        own_fc1, own_fc2 = own_rest_blocks(fc1_weight, fc2_weight)
    else:
        own_fc1 = lax.dynamic_index_in_dim(
            fc1_weight.reshape(own_width, groups, 2, half_rows), core, 2, keepdims=False
        ).reshape(own_width, groups * half_rows)
        own_fc2 = lax.dynamic_slice_in_dim(fc2_weight, core * half_rows, half_rows, 0)
    full_fc1 = lax.all_gather(own_fc1, "fsdp", axis=0, tiled=True)
    full_fc2 = lax.all_gather(own_fc2, "fsdp", axis=0, tiled=True)
    qkv_a.send(7, ready=qkv_a.got(6, 3, 5))
    other_inputs = after(other_inputs, own_fc1, *qkv_a.got(6, 3, 5))
    qkv_b.send(2, 1, ready=qkv_a.got(6, 3, 5))
    own_inputs = jnp.concatenate([take(inputs, chip), other_inputs], axis=0)
    all_inputs = with_partner(own_inputs)
    if groups == 8:
        qkv_first, wide, bias_fc1 = in_order(qkv_a.pieces, own_width, True)
    else:
        qkv_first = qkv_a.result()
        packed = lax.all_gather(jnp.concatenate(vectors), "fsdp", axis=0)
        wide = [
            packed[:, i * own_width : (i + 1) * own_width].reshape(width).astype(F32)
            for i in range(8)
        ]
        bias_fc1 = packed[:, 8 * own_width : used].reshape(groups, 2, half_rows)
        bias_fc1 = take(jnp.moveaxis(bias_fc1, 1, 0), core)
        bias_fc1 = bias_fc1.reshape(groups * half_rows).astype(F32)
    gain_one, bias_one, bias_q, bias_v, bias_out, gain_two, bias_two, bias_fc2 = [
        wide[i] for i in range(8)
    ]
    bias_q = take(bias_q.reshape(2, 2, 2, PAIR), core)
    bias_v = take(bias_v.reshape(2, 2, 2, PAIR), core)
    bias_mixed = jnp.stack([bias_q, jnp.zeros_like(bias_q), bias_v], axis=2).reshape(2, row_width)
    scale_mixed = jnp.array([scale_factor, 1.0, 1.0] * 2, F32).repeat(PAIR)
    clip_valid = take(valid, chip).reshape(2 * clips, rows)
    own_valid = jnp.concatenate([take(clip_valid, place), take(clip_valid, place ^ 2)])
    other_valid = jnp.concatenate([take(clip_valid, place ^ 1), take(clip_valid, place ^ 3)])
    key_valid = jnp.concatenate([own_valid, other_valid])
    lane = jnp.arange(PAIR) % HEAD
    key_mask = jnp.where(key_valid > 0, 0.0, MASKED)[:, None]
    key_base = jnp.where(lane == 0, key_mask, jnp.where(lane < 4, 1.0, 0.0)).astype(BF16)


    def project(weight, i):
        return ((dot(h_one, weight) + bias_mixed[i]) * scale_mixed).astype(BF16)

    h_one = rows_call(
        first_kernel, [all_inputs], [gain_one[None], bias_one[None]], [BF16], 0, "first_norm"
    )[0]
    mixed = [project(qkv_first, 0)]
    context, queries = [], []

    def attend_pair(pair, *ready):
        before = context[-1] if context else None
        base = after(key_base, *ready)
        results = attend(mixed[pair // 2], base, pair % 2, before, pair, 4)
        context.append(results[0])
        queries.append(results[1])

    ready = (h_one,) + qkv_b.got(4, 2, 1)
    qkv_b.send(6, 3, 5, ready=ready)
    attend_pair(0, *ready)
    ready = (queries[0],) + qkv_b.got(6, 3, 5)
    qkv_b.send(7, ready=ready)
    other_grads = swap_chip(after(take(cotangent, 1 - chip), *ready))
    attend_pair(1, *ready)
    second_columns = qkv_b.result()
    mixed.append(project(second_columns[:, :row_width], 1))
    ready = (queries[1], mixed[1], other_grads)
    kept = lax.dynamic_slice(second_columns, (core * half, row_width), (half, half))
    received = lax.dynamic_slice(second_columns, ((1 - core) * half, row_width), (half, half))
    received = swap_core(after(received, mixed[1]))
    attend_pair(2, kept, *ready)
    ready = (queries[2], received)
    attend_pair(3, *ready)
    own_grads = jnp.concatenate([take(cotangent, chip), after(other_grads, queries[3])], axis=0)
    full_out = jnp.concatenate(in_core_order(kept, received, core, 1), axis=1)
    all_context = context[3]
    own_part, other_part = both_halves_product([(all_context, full_out)], NN)
    ready = (own_grads, own_part)
    counted = own_valid.astype(F32)[:, None]
    residual_mid, h_two, middle_sums = rows_call(
        middle_kernel,
        [own_part, after(other_part, *ready), own_inputs, counted],
        [bias_out[None], gain_two[None], bias_two[None]],
        [F32, BF16],
        2,
        "middle",
    )
    h_two = with_partner(h_two)
    all_grads = with_partner(after(own_grads, residual_mid))
    grad_sums = column_sum(own_grads)
    h_two = after(h_two, grad_sums)
    active, slope = gelu_both(dot(h_two, full_fc1) + bias_fc1)
    active, slope = active.astype(BF16), slope.astype(BF16)
    active = after(active, full_fc2)
    fc2_product = dot(active, all_grads, TN).astype(BF16)
    fc2_scatter = Scatter(fc2_product)

    late_grads = after(all_grads, *fc2_scatter.got("keep"))
    grad_hidden, hidden_sums = hidden_gradient(late_grads, full_fc2, slope)
    fc1_halves = weight_halves(h_two, grad_hidden)
    fc1_scatter = Scatter(fc1_halves[0], halves=fc1_halves)
    own_part, other_part = both_halves_product(
        [(after(grad_hidden, fc1_scatter.sent), full_fc1)], NT
    )
    grad_residual, own_grad_attn, two_sums = rows_call(
        norm_back_kernel,
        [own_part, other_part, residual_mid, own_grads],
        [gain_two[None]],
        [F32, BF16],
        3,
        "norm_back",
    )
    grad_attn = with_partner(own_grad_attn)
    grad_context = half_product([(grad_attn, full_out)], NT, None, BF16)
    halves, sums = [None, None], []

    def back_pair(pair, *ready):
        grad_mixed, parts = attend_back(
            queries[pair],
            mixed[pair // 2],
            grad_context,
            all_context,
            after(key_base, *ready),
            pair % 2,
            pair,
            halves[pair // 2],
        )
        halves[pair // 2] = grad_mixed
        sums.append(parts)

    back_pair(0, grad_context)
    ready = (sums[0], fc1_scatter.crossed) + fc2_scatter.got("side")
    grad_out = dot(all_context, after(grad_attn, *ready), TN).astype(BF16)
    kept = lax.dynamic_slice_in_dim(grad_out, core * half, half, 1)
    received = swap_core(lax.dynamic_slice_in_dim(grad_out, (1 - core) * half, half, 1))
    fc2_scatter.near(*ready)
    fc1_scatter.cross(*ready)
    grad_out = jnp.concatenate(in_core_order(kept, received, core, 0), axis=0)
    out_sums = lax.psum_scatter(grad_out, "fsdp", scatter_dimension=0, tiled=True)
    back_pair(1, grad_out, *ready, *fc2_scatter.got("keep"), *fc1_scatter.got("keep"))
    early = dot(h_one, halves[0], TN).astype(BF16)
    ready = (sums[1],) + fc2_scatter.got("near_sums") + fc1_scatter.got("side")
    fc2_scatter.far(*ready)
    fc1_scatter.near(*ready)
    early_scatter = Scatter(early, *ready)
    ready += fc2_scatter.got("keep") + fc1_scatter.got("keep") + early_scatter.got("keep")
    own_mlp, other_mlp = both_halves_product([(after(active, *ready), full_fc2)], NN)
    low_output, end_sums = rows_call(
        end_kernel,
        [own_mlp, other_mlp, residual_mid, counted],
        [bias_fc2[None]],
        [BF16],
        2,
        "end",
    )
    back_pair(2, low_output, *ready)
    output_back = swap_chip(low_output[rows:])
    ready = (sums[2], output_back) + fc2_scatter.got("far_sums") + fc1_scatter.got("near_sums")
    ready += early_scatter.got("side")
    fc2_scatter.chips(*ready)
    fc1_scatter.far(*ready)
    early_scatter.near(*ready)
    ready += (fc2_scatter.sums,) + fc1_scatter.got("keep") + early_scatter.got("keep")
    back_pair(3, *ready)
    ready = (sums[3], fc2_scatter.other_chip) + fc1_scatter.got("far_sums")
    ready += early_scatter.got("near_sums")
    early_scatter.far(*ready)
    fc1_scatter.chips(*ready)
    fc2_scatter.cores(*ready)
    late_scatter = Scatter(dot(after(h_one, *ready), halves[1], TN))
    gm_first, gm_second = after(tuple(halves), *late_scatter.got("keep"))
    own_one, other_one = both_halves_product(
        [(gm_first, qkv_first), (gm_second, second_columns)], NT
    )
    low_input_grad, one_sums = rows_call(
        norm_back_kernel,
        [own_one, other_one, own_inputs, grad_residual],
        [gain_one[None]],
        [BF16],
        3,
        "norm_back",
    )
    input_back = swap_chip(low_input_grad[rows:])
    ready = late_scatter.got("side") + (low_input_grad,)
    late_scatter.near(*ready)
    one_sums = after(one_sums, *ready)

    if groups == 8:
        packed = pack_lines(
            [one_sums, two_sums, grad_sums[None], hidden_sums, end_sums, middle_sums], sums
        )
    else:
        lines = [one_sums[0], one_sums[1], two_sums[2], two_sums[0], two_sums[1], grad_sums]
        lines.append(hidden_sums[0])
        squares = [end_sums[0], middle_sums[0], end_sums[1], middle_sums[1]]
        squares = [jnp.sum(line.reshape(-1, PAIR), axis=0) for line in squares]

        def by_core(values):
            full = jnp.zeros((2, values.shape[0]), F32)
            return lax.dynamic_update_index_in_dim(full, values, core, 0).reshape(-1)

        wide = lines[:2] + [by_core(jnp.concatenate([part[n] for part in sums])) for n in range(2)]
        wide = [line.reshape(groups, own_width) for line in wide + lines[2:6]]
        all_sums = jnp.zeros((groups, 2, half_rows), F32)
        all_sums = lax.dynamic_update_index_in_dim(
            all_sums, lines[6].reshape(groups, half_rows), core, 1
        )
        wide.append(all_sums.reshape(groups, hidden_rows))
        wide.append(jnp.zeros((groups, 12 * PAIR - used)))
        wide.append(jnp.broadcast_to(jnp.concatenate(squares), (groups, 4 * PAIR)))
        packed = jnp.concatenate(wide, axis=1).astype(BF16).reshape(groups * 16, PAIR)
    ready = early_scatter.got("far_sums") + (fc1_scatter.other_chip,)
    packed = add_low(packed, after(swap_chip(packed), *ready))
    early_scatter.chips(packed, beside=out_sums)
    fc1_scatter.cores(packed)
    ready = late_scatter.got("near_sums")
    packed = add_low(packed, after(swap_core(packed), *ready))
    late_scatter.far(packed)
    vector_scatter = Scatter(packed, ordered=True)
    vector_scatter.near(early_scatter.other_chip)
    early_scatter.cores(*vector_scatter.got("keep"))
    ready = late_scatter.got("far_sums") + (input_back,)
    vector_scatter.far(*ready)
    late_scatter.chips(*vector_scatter.got("keep"))
    late_scatter.cores()
    ready_last = (packed,)
    output = all_clips(low_output, after(output_back, packed))
    input_grad = all_clips(low_input_grad, input_back)

    def in_columns(values, other, blocks):
        size = values.shape[1] // blocks
        parts = in_core_order(values, other, core, 0)
        parts = [part.reshape(own_width, blocks, 1, size) for part in parts]
        return jnp.concatenate(parts, axis=2).reshape(own_width, -1).astype(F32)

    fc2_parts = after((fc2_scatter.total, fc2_scatter.other_core), *ready_last)
    fc2_grad = in_core_order(*fc2_parts, core, 0)
    fc2_grad = jnp.concatenate(fc2_grad, axis=0).astype(F32)
    early_parts = [early_scatter.total, early_scatter.other_core]
    late_parts = [late_scatter.total, late_scatter.other_core]
    fc1_parts = after((fc1_scatter.total, fc1_scatter.other_core), *ready_last)
    if groups == 8:
        fc1_places = [
            (0, n * half_rows, half_rows, 2 * n * half_rows, (2 * n + 1) * half_rows)
            for n in range(groups)
        ]
        fc1_grad = join_columns(fc1_parts, fc1_places, 2 * groups * half_rows)
        out_grad = join_columns(early_parts, [(0, row_width, half, 0, half)], width)
        qkv_places = []
        for n in range(3):
            for pair in range(4):
                target = n * width + pair * PAIR
                start = (3 * (pair % 2) + n) * PAIR
                qkv_places.append((pair // 2, start, PAIR, target, target + half))
        qkv_grad = join_columns(early_parts + late_parts, qkv_places, 3 * width)
    else:
        fc1_grad = in_columns(*fc1_parts, groups)
        out_grad = in_columns(*[part[:, row_width:] for part in early_parts], 1)

        def both_halves(left, right):
            left = left[:, :row_width].reshape(own_width, 1, 2, 3, PAIR)
            right = right.reshape(own_width, 1, 2, 3, PAIR)
            both = jnp.concatenate([left, right], axis=1).transpose(0, 3, 1, 2, 4)
            return both.reshape(own_width, 3 * half)

        qkv_grad = in_columns(*[both_halves(*pair) for pair in zip(early_parts, late_parts)], 3)
    lines = vector_scatter.last()
    flat = lines[:12].reshape(-1)
    own_vectors = [flat[i * own_width : (i + 1) * own_width] for i in range(8)]
    own_hidden = flat[8 * own_width : used]
    totals = jnp.sum(lines[12:], axis=1)
    branch_rms = jnp.sqrt(totals[:3] / totals[3])
    return (
        output,
        input_grad,
        own_vectors[0],
        own_vectors[1],
        qkv_grad,
        own_vectors[2],
        own_vectors[3],
        out_grad,
        own_vectors[4],
        own_vectors[5],
        own_vectors[6],
        fc1_grad,
        own_hidden,
        fc2_grad,
        own_vectors[7],
        branch_rms,
    )


def solution(mesh):
    tokens, rows, vector = P("fsdp", "seq", None), P("fsdp", None), P("fsdp")
    return jax.shard_map(
        body,
        mesh=mesh,
        in_specs=(
            tokens,
            tokens,
            rows,
            vector,
            vector,
            rows,
            vector,
            vector,
            rows,
            vector,
            vector,
            vector,
            rows,
            vector,
            rows,
            vector,
        ),
        out_specs=(
            tokens,
            tokens,
            vector,
            vector,
            rows,
            vector,
            vector,
            rows,
            vector,
            vector,
            vector,
            rows,
            vector,
            rows,
            vector,
            P(),
        ),
        check_vma=False,
    )
```

```python
from functools import partial

import jax
import jax.numpy as jnp
from jax import lax
from jax.experimental import pallas as pl
from jax.experimental.pallas import tpu as pltpu
from jax.sharding import PartitionSpec as P

HEADS = 16
HEAD = 64
PAIR = 2 * HEAD
EPS = 1e-06
MASKED = -1e30
VMEM_BYTES = 28 * 2**20
BF16 = jnp.bfloat16
F32 = jnp.float32
NN = (((1,), (0,)), ((), ()))
NT = (((1,), (1,)), ((), ()))
TN = (((0,), (0,)), ((), ()))
SMALL_COST = pl.CostEstimate(flops=10**7, bytes_accessed=2**20, transcendentals=0)


def dot(left, right, dims=NN):
    return lax.dot_general(left, right, dims, preferred_element_type=F32)


def lanes_of(shape):
    return lax.broadcasted_iota(jnp.int32, shape, len(shape) - 1)


def three_parts(column):
    high = column.astype(BF16).astype(F32)
    rest = column - high
    middle = rest.astype(BF16).astype(F32)
    return high, middle, rest - middle


def block_rows(length, *sizes):
    for rows in sizes + (224, 112, 16):
        if length % rows == 0:
            return rows
    return length


def attend_kernel(q_ref, k_ref, v_ref, key_base_ref, *refs):
    context_ref, query_ref = refs[-2:]
    length = q_ref.shape[0]
    rows = block_rows(length, 392)
    low = lanes_of((length, PAIR)) < HEAD
    keys, values, key_base = k_ref[...], v_ref[...], key_base_ref[...]
    ones = jnp.ones((length, PAIR), BF16)
    keys_of = [jnp.where(low, keys, key_base), jnp.where(low, key_base, keys)]
    values_of = [jnp.where(low, values, ones), jnp.where(low, ones, values)]
    lane = lanes_of((rows, PAIR))
    low_rows = lane < HEAD
    for step in range(length // rows):
        span = slice(step * rows, (step + 1) * rows)
        queries = q_ref[span, :]
        results = []
        for head in range(2):
            base = HEAD * (1 - head)
            own = low_rows if head == 0 else jnp.logical_not(low_rows)
            unit = jnp.where(lane == base, 1.0, 0.0)
            scores = dot(jnp.where(own, queries, unit.astype(BF16)), keys_of[head], NT)
            highest = jnp.max(scores, axis=1, keepdims=True)
            weights = jnp.exp(scores - highest).astype(BF16)
            mixed = dot(weights, values_of[head])
            total = mixed[:, base : base + 1]
            high, middle, rest = three_parts(-(highest + jnp.log(total)))
            extra = jnp.where(lane == base + 3, rest, unit)
            extra = jnp.where(lane == base + 2, middle, extra)
            extra = jnp.where(lane == base + 1, high, extra)
            query_ref[head, span, :] = jnp.where(own, queries, extra.astype(BF16))
            results.append(mixed / total)
        context_ref[span, :] = jnp.where(low_rows, results[0], results[1]).astype(BF16)


def attend(mixed, key_base, pair, context, place, places):
    length = mixed.shape[0]
    tile = lambda column: pl.BlockSpec((length, PAIR), lambda i: (0, column))
    in_specs = [tile(3 * pair), tile(3 * pair + 1), tile(3 * pair + 2), tile(0)]
    operands = (mixed, mixed, mixed, key_base)
    aliases = {}
    if context is not None:
        in_specs.append(pl.BlockSpec(memory_space=pl.ANY))
        operands += (context,)
        aliases = {4: 0}
    return pl.pallas_call(
        attend_kernel,
        grid=(1,),
        in_specs=in_specs,
        out_specs=[tile(place), pl.BlockSpec((2, length, PAIR), lambda i: (0, 0, 0))],
        out_shape=[
            jax.ShapeDtypeStruct((length, places * PAIR), BF16),
            jax.ShapeDtypeStruct((2, length, PAIR), BF16),
        ],
        input_output_aliases=aliases,
        compiler_params=pltpu.CompilerParams(vmem_limit_bytes=VMEM_BYTES),
        cost_estimate=SMALL_COST,
        name="attend",
    )(*operands)


def attend_back_kernel(query_ref, k_ref, v_ref, grad_ref, context_ref, key_base_ref, *refs):
    grad_mixed_ref, sums_ref = refs[-2:]
    length = k_ref.shape[0]
    rows = block_rows(length)
    low = lanes_of((length, PAIR)) < HEAD
    keys, values, key_base = k_ref[...], v_ref[...], key_base_ref[...]
    ones = jnp.ones((length, PAIR), BF16)
    lane = lanes_of((rows, PAIR))
    low_rows = lane < HEAD
    steps = length // rows
    grad_q, grad_k, grad_v = [], [], []
    sum_q = jnp.zeros((1, PAIR), F32)
    for head in range(2):
        base = HEAD * (1 - head)
        own = low if head == 0 else jnp.logical_not(low)
        own_rows = low_rows if head == 0 else jnp.logical_not(low_rows)
        head_keys = jnp.where(own, keys, key_base)
        head_values = jnp.where(own, values, ones)
        sum_k = jnp.zeros((length, PAIR), F32)
        sum_v = jnp.zeros((length, PAIR), F32)
        for step in range(steps):
            span = slice(step * rows, (step + 1) * rows)
            queries = query_ref[head, span, :]
            grads = grad_ref[span, :]
            product = grads.astype(F32) * context_ref[span, :].astype(F32)
            inner = jnp.sum(jnp.where(own_rows, product, 0.0), axis=1, keepdims=True)
            high, middle, rest = three_parts(-inner)
            extra = jnp.where(lane == base + 2, rest, 0.0)
            extra = jnp.where(lane == base + 1, middle, extra)
            extra = jnp.where(lane == base, high, extra)
            head_grads = jnp.where(own_rows, grads, extra.astype(BF16))
            probs = jnp.exp(dot(head_keys, queries, NT))
            grad_scores = (probs * dot(head_values, head_grads, NT)).astype(BF16)
            sum_v = sum_v + dot(probs.astype(BF16), grads)
            sum_k = sum_k + dot(grad_scores, queries)
            part = dot(grad_scores, keys, TN)
            if head == 0:
                grad_q.append(part)
            else:
                both = jnp.where(low_rows, grad_q[step], part).astype(BF16)
                both = both * (HEAD ** (-0.5))
                grad_mixed_ref[span, :PAIR] = both
                sum_q = sum_q + jnp.sum(both.astype(F32), axis=0, keepdims=True)
        grad_k.append(sum_k)
        grad_v.append(sum_v)
    grad_mixed_ref[:, PAIR : 2 * PAIR] = jnp.where(low, grad_k[0], grad_k[1]).astype(BF16)
    both = jnp.where(low, grad_v[0], grad_v[1]).astype(BF16)
    grad_mixed_ref[:, 2 * PAIR :] = both
    sums_ref[0:1, :] = sum_q
    sums_ref[1:2, :] = jnp.sum(both.astype(F32), axis=0, keepdims=True)


def attend_back(queries, mixed, grad_context, context, key_base, pair, place, grad_mixed):
    length = mixed.shape[0]
    tile = lambda column: pl.BlockSpec((length, PAIR), lambda i: (0, column))
    in_specs = [
        pl.BlockSpec((2, length, PAIR), lambda i: (0, 0, 0)),
        tile(3 * pair + 1),
        tile(3 * pair + 2),
        tile(place),
        tile(place),
        tile(0),
    ]
    operands = (queries, mixed, mixed, grad_context, context, key_base)
    aliases = {}
    if grad_mixed is not None:
        in_specs.append(pl.BlockSpec(memory_space=pl.ANY))
        operands += (grad_mixed,)
        aliases = {6: 0}
    return pl.pallas_call(
        attend_back_kernel,
        grid=(1,),
        in_specs=in_specs,
        out_specs=[
            pl.BlockSpec((length, 3 * PAIR), lambda i: (0, pair)),
            pl.BlockSpec((2, PAIR), lambda i: (0, 0)),
        ],
        out_shape=[
            jax.ShapeDtypeStruct((length, 6 * PAIR), BF16),
            jax.ShapeDtypeStruct((2, PAIR), F32),
        ],
        input_output_aliases=aliases,
        compiler_params=pltpu.CompilerParams(vmem_limit_bytes=VMEM_BYTES),
        cost_estimate=SMALL_COST,
        name="attend_back",
    )(*operands)


def normalize(values):
    center = values - jnp.mean(values, axis=-1, keepdims=True)
    spread = jnp.mean(center * center, axis=-1, keepdims=True)
    scale = lax.rsqrt(spread + EPS)
    return center * scale, scale


def rows_call(kernel, row_inputs, constants, kinds, sum_rows, name):
    rows, width = row_inputs[0].shape
    tile = rows // 7 if rows % 112 == 0 else rows
    block = lambda columns: pl.BlockSpec((tile, columns), lambda i: (i, 0))
    whole = lambda shape: pl.BlockSpec(shape, lambda i: (0, 0))
    out_specs = [block(width)] * len(kinds)
    out_shape = [jax.ShapeDtypeStruct((rows, width), kind) for kind in kinds]
    if sum_rows:
        out_specs.append(whole((sum_rows, width)))
        out_shape.append(jax.ShapeDtypeStruct((sum_rows, width), F32))
    return pl.pallas_call(
        kernel,
        grid=(rows // tile,),
        in_specs=[block(part.shape[1]) for part in row_inputs]
        + [whole(part.shape) for part in constants],
        out_specs=out_specs,
        out_shape=out_shape,
        compiler_params=pltpu.CompilerParams(vmem_limit_bytes=VMEM_BYTES),
        cost_estimate=SMALL_COST,
        name=name,
    )(*row_inputs, *constants)


def add_rows(sums_ref, parts):
    @pl.when(pl.program_id(0) == 0)
    def _():
        sums_ref[...] = jnp.zeros(sums_ref.shape, F32)

    lines = [jnp.sum(part, axis=0, keepdims=True) for part in parts]
    sums_ref[...] += jnp.concatenate(lines, axis=0)


def first_kernel(values_ref, gain_ref, bias_ref, out_ref):
    normal = normalize(values_ref[...].astype(F32))[0]
    out_ref[...] = (normal * gain_ref[...] + bias_ref[...]).astype(BF16)


def middle_kernel(
    own_ref, other_ref, inputs_ref, counted_ref, out_bias_ref, gain_ref, bias_ref, *out_refs
):
    middle_ref, low_ref, sums_ref = out_refs
    branch = own_ref[...] + other_ref[...].astype(F32) + out_bias_ref[...]
    middle = inputs_ref[...].astype(F32) + branch
    middle_ref[...] = middle
    low_ref[...] = (normalize(middle)[0] * gain_ref[...] + bias_ref[...]).astype(BF16)
    counted = counted_ref[...]
    add_rows(sums_ref, [counted * branch * branch, jnp.broadcast_to(counted, branch.shape)])


def end_kernel(own_ref, other_ref, middle_ref, counted_ref, bias_ref, low_ref, sums_ref):
    branch = own_ref[...] + other_ref[...].astype(F32) + bias_ref[...]
    result = middle_ref[...] + branch
    low_ref[...] = result.astype(BF16)
    counted = counted_ref[...]
    add_rows(sums_ref, [counted * result * result, counted * branch * branch])


def norm_back_kernel(own_ref, other_ref, values_ref, residual_ref, gain_ref, *out_refs):
    grad = own_ref[...] + other_ref[...].astype(F32)
    normal, scale = normalize(values_ref[...].astype(F32))
    inner = grad * gain_ref[...]
    first = jnp.mean(inner, axis=-1, keepdims=True)
    second = jnp.mean(inner * normal, axis=-1, keepdims=True)
    total = residual_ref[...].astype(F32) + scale * (inner - first - normal * second)
    low = total.astype(BF16)
    if len(out_refs) == 3:
        out_refs[0][...] = total
    out_refs[-2][...] = low
    add_rows(out_refs[-1], [grad * normal, grad, low.astype(F32)])


def weight_kernel(left_ref, right_ref, kept_ref, sent_ref):
    chip = lax.axis_index("seq") // 2
    left, half = left_ref[...], kept_ref.shape[1]
    for part, out_ref in ((chip, kept_ref), (1 - chip, sent_ref)):
        columns = pl.ds(pl.multiple_of(part * half, half), half)
        out_ref[...] = dot(left, right_ref[:, columns], TN).astype(BF16)


def weight_halves(left, right):
    rows, depth = left.shape
    columns = right.shape[1]
    tile = min(depth, 512)
    half = pl.BlockSpec((tile, columns // 2), lambda i: (i, 0))
    return pl.pallas_call(
        weight_kernel,
        grid=(depth // tile,),
        in_specs=[
            pl.BlockSpec((rows, tile), lambda i: (0, i)),
            pl.BlockSpec((rows, columns), lambda i: (0, 0)),
        ],
        out_specs=[half, half],
        out_shape=[jax.ShapeDtypeStruct((depth, columns // 2), BF16)] * 2,
        compiler_params=pltpu.CompilerParams(vmem_limit_bytes=VMEM_BYTES),
        cost_estimate=SMALL_COST,
        name="weight_halves",
    )(left, right)


def gelu_both(values):
    half = 0.5 * (1.0 + lax.erf(values * (0.5**0.5)))
    density = jnp.exp(-0.5 * values * values) * (0.5 / jnp.pi) ** 0.5
    return values * half, half + values * density


def hidden_kernel(grad_ref, weight_ref, slope_ref, hidden_ref, sums_ref):
    rows = grad_ref.shape[0] // 2
    weight = weight_ref[...]
    total = jnp.zeros((1, weight.shape[0]), F32)
    for span in (slice(0, rows), slice(rows, 2 * rows)):
        hidden = (dot(grad_ref[span, :], weight, NT) * slope_ref[span, :].astype(F32)).astype(BF16)
        hidden_ref[span, :] = hidden
        total = total + jnp.sum(hidden.astype(F32), axis=0, keepdims=True)
    sums_ref[...] = total


def hidden_gradient(grads, weight, slope):
    rows, depth = grads.shape
    columns = weight.shape[0]
    tile = min(columns, 512)
    block = pl.BlockSpec((rows, tile), lambda i: (0, i))
    return pl.pallas_call(
        hidden_kernel,
        grid=(columns // tile,),
        in_specs=[
            pl.BlockSpec((rows, depth), lambda i: (0, 0)),
            pl.BlockSpec((tile, depth), lambda i: (i, 0)),
            block,
        ],
        out_specs=[block, pl.BlockSpec((1, tile), lambda i: (0, i))],
        out_shape=[
            jax.ShapeDtypeStruct((rows, columns), BF16),
            jax.ShapeDtypeStruct((1, columns), F32),
        ],
        compiler_params=pltpu.CompilerParams(vmem_limit_bytes=VMEM_BYTES),
        cost_estimate=SMALL_COST,
        name="hidden_gradient",
    )(grads, weight, slope)


def half_kernel(dims, *refs):
    total = dot(refs[0][...], refs[1][...], dims)
    for n in range(2, len(refs) - 1, 2):
        total = total + dot(refs[n][...], refs[n + 1][...], dims)
    refs[-1][...] = total.astype(refs[-1].dtype)


def half_product(pairs, dims, part, kind):
    rows = pairs[0][0].shape[0] if part is None else pairs[0][0].shape[0] // 2
    part = part or 0
    columns = pairs[0][1].shape[1 if dims is NN else 0]
    tile = min(columns, 512)
    in_specs, operands = [], []
    for left, right in pairs:
        depth = left.shape[1]
        in_specs.append(pl.BlockSpec((rows, depth), lambda i: (part, 0)))
        if dims is NN:
            in_specs.append(pl.BlockSpec((depth, tile), lambda i: (0, i)))
        else:
            in_specs.append(pl.BlockSpec((tile, depth), lambda i: (i, 0)))
        operands += [left, right]
    return pl.pallas_call(
        partial(half_kernel, dims),
        grid=(columns // tile,),
        in_specs=in_specs,
        out_specs=pl.BlockSpec((rows, tile), lambda i: (0, i)),
        out_shape=jax.ShapeDtypeStruct((rows, columns), kind),
        compiler_params=pltpu.CompilerParams(vmem_limit_bytes=VMEM_BYTES),
        cost_estimate=SMALL_COST,
        name="half_product",
    )(*operands)


def both_halves_product(pairs, dims):
    other = half_product(pairs, dims, 1, BF16)
    own = [(after(left, other), right) for left, right in pairs]
    return half_product(own, dims, 0, F32), swap_core(other)


def join_kernel(places, *refs):
    out_ref = refs[-1]
    core = lax.rem(lax.axis_index("seq"), 2)
    for n, (source, start, width, first, second) in enumerate(places):
        for other in range(2):
            target = pl.multiple_of(jnp.where(core == other, first, second), PAIR)
            block = refs[2 * source + other][:, start : start + width]
            out_ref[:, pl.ds(target, width)] = block.astype(F32)


def join_columns(parts, places, columns):
    rows = parts[0].shape[0]
    return pl.pallas_call(
        partial(join_kernel, places),
        in_specs=[pl.BlockSpec(memory_space=pltpu.VMEM)] * len(parts),
        out_specs=pl.BlockSpec(memory_space=pltpu.VMEM),
        out_shape=jax.ShapeDtypeStruct((rows, columns), F32),
        cost_estimate=SMALL_COST,
        name="join_columns",
    )(*parts)


def column_sum(values):
    return jnp.sum(values, axis=0, dtype=F32)


def swap_core(values):
    return lax.ppermute(values, "seq", [(0, 1), (1, 0), (2, 3), (3, 2)])


def swap_chip(values):
    return lax.ppermute(values, "seq", [(0, 2), (2, 0), (1, 3), (3, 1)])


def stack_kernel(own_ref, other_ref, out_ref, sems):
    rows = own_ref.shape[0]
    copies = [
        pltpu.make_async_copy(ref, out_ref.at[pl.ds(n * rows, rows)], sems.at[n])
        for n, ref in enumerate((own_ref, other_ref))
    ]
    for copy in copies:
        copy.start()
    for copy in copies:
        copy.wait()


def with_partner(values):
    rows, columns = values.shape
    return pl.pallas_call(
        stack_kernel,
        in_specs=[pl.BlockSpec(memory_space=pltpu.VMEM)] * 2,
        out_specs=pl.BlockSpec(memory_space=pl.ANY),
        out_shape=jax.ShapeDtypeStruct((2 * rows, columns), values.dtype),
        scratch_shapes=[pltpu.SemaphoreType.DMA((2,))],
        compiler_params=pltpu.CompilerParams(vmem_limit_bytes=16 * 2**20),
        cost_estimate=SMALL_COST,
        name="stack_rows",
    )(values, swap_core(values))


def swap_group(values, bit):
    return lax.ppermute(values, "fsdp", [(i, i ^ bit) for i in range(8)])


def order_kernel(count, *refs):
    pieces, full_ref, held, arrived, sent = refs[:count], refs[count], *refs[-3:]
    group = lax.axis_index("fsdp")
    rows = full_ref.shape[0] // count
    loads = [
        pltpu.make_async_copy(piece, held.at[relative], arrived.at[relative])
        for relative, piece in enumerate(pieces)
    ]
    for load in loads:
        load.start()
    stores = []
    for relative in range(count):
        start = pl.multiple_of((group ^ relative) * rows, rows)
        store = pltpu.make_async_copy(
            held.at[relative, pl.ds(0, rows)], full_ref.at[pl.ds(start, rows)], sent.at[relative]
        )
        loads[relative].wait()
        store.start()
        stores.append(store)
    if len(refs) > count + 4:
        own_width, core = 128, lax.rem(lax.axis_index("seq"), 2)
        wide_ref, bias_ref = refs[count + 1], refs[count + 2]
        for relative in range(count):
            place = group ^ relative
            columns = pl.ds(pl.multiple_of(place * own_width, own_width), own_width)
            extra = held[relative, rows : rows + 8, :].astype(F32)
            lines = [
                extra[k : k + 1, own_width * n : own_width * (n + 1)]
                for k in range(2)
                for n in range(6)
            ]
            for n in range(8):
                wide_ref[n : n + 1, columns] = lines[n]
            for n in range(2):
                start = pl.multiple_of((place * 2 + n) * own_width, own_width)
                bias_ref[:, pl.ds(start, own_width)] = jnp.where(
                    core == 0, lines[8 + n], lines[10 + n]
                )
    for store in stores:
        store.wait()


def in_order(pieces, rows, with_vectors=False):
    count, columns = len(pieces), pieces[0].shape[1]
    out_specs = [pl.BlockSpec(memory_space=pl.ANY)]
    out_shape = [jax.ShapeDtypeStruct((count * rows, columns), pieces[0].dtype)]
    if with_vectors:
        out_specs += [pl.BlockSpec(memory_space=pltpu.VMEM)] * 2
        out_shape += [jax.ShapeDtypeStruct((8, 1024), F32), jax.ShapeDtypeStruct((1, 2048), F32)]
    result = pl.pallas_call(
        partial(order_kernel, count),
        in_specs=[pl.BlockSpec(memory_space=pl.ANY)] * count,
        out_specs=out_specs,
        out_shape=out_shape,
        scratch_shapes=[
            pltpu.VMEM((count,) + pieces[0].shape, pieces[0].dtype),
            pltpu.SemaphoreType.DMA((count,)),
            pltpu.SemaphoreType.DMA((count,)),
        ],
        compiler_params=pltpu.CompilerParams(vmem_limit_bytes=16 * 2**20),
        cost_estimate=SMALL_COST,
        name="in_order",
    )(*pieces)
    return result if with_vectors else result[0]


def own_kernel(qkv_ref, out_ref, *refs):
    vector_refs, (first_ref, second_ref) = refs[:-2], refs[-2:]
    core = lax.rem(lax.axis_index("seq"), 2)
    rows = qkv_ref.shape[0]
    for n in range(3):
        for pair in range(4):
            block_ref = second_ref if pair >= 2 else first_ref
            start = pl.multiple_of((8 * n + pair + 4 * core) * PAIR, PAIR)
            target = (3 * (pair % 2) + n) * PAIR
            block_ref[:rows, target : target + PAIR] = qkv_ref[:, pl.ds(start, PAIR)]
    out_half = out_ref.shape[1] // 2
    start = pl.multiple_of(core * out_half, out_half)
    second_ref[:, 6 * PAIR :] = out_ref[:, pl.ds(start, out_half)]
    lines = []
    for ref in vector_refs:
        vector = ref[...].astype(F32).reshape(ref.shape[0] // PAIR, PAIR)
        lines += [vector[n : n + 1] for n in range(ref.shape[0] // PAIR)]
    row = lax.broadcasted_iota(jnp.int32, (8, PAIR), 0)
    for n in range(6):
        block = jnp.where(row == 0, lines[n], jnp.where(row == 1, lines[n + 6], 0.0))
        first_ref[rows:, PAIR * n : PAIR * (n + 1)] = block.astype(BF16)


def own_qkv_blocks(qkv_weight, out_weight, vectors):
    rows, columns = qkv_weight.shape[0], qkv_weight.shape[1] // 4
    out_half = out_weight.shape[1] // 2
    return pl.pallas_call(
        own_kernel,
        in_specs=[pl.BlockSpec(memory_space=pltpu.VMEM)] * (2 + len(vectors)),
        out_specs=[pl.BlockSpec(memory_space=pltpu.VMEM)] * 2,
        out_shape=[
            jax.ShapeDtypeStruct((rows + 8, columns), BF16),
            jax.ShapeDtypeStruct((rows, columns + out_half), BF16),
        ],
        cost_estimate=SMALL_COST,
        name="own_qkv",
    )(qkv_weight, out_weight, *vectors)


def own_rest_kernel(fc1_ref, fc2_ref, first_ref, second_ref):
    core = lax.rem(lax.axis_index("seq"), 2)
    rows = second_ref.shape[0]
    for n in range(fc1_ref.shape[1] // (2 * rows)):
        start = pl.multiple_of((2 * n + core) * rows, rows)
        first_ref[:, n * rows : (n + 1) * rows] = fc1_ref[:, pl.ds(start, rows)]
    second_ref[...] = fc2_ref[pl.ds(pl.multiple_of(core * rows, rows), rows), :]


def own_rest_blocks(fc1_weight, fc2_weight):
    return pl.pallas_call(
        own_rest_kernel,
        in_specs=[pl.BlockSpec(memory_space=pltpu.VMEM)] * 2,
        out_specs=[pl.BlockSpec(memory_space=pltpu.VMEM)] * 2,
        out_shape=[
            jax.ShapeDtypeStruct((fc1_weight.shape[0], fc1_weight.shape[1] // 2), BF16),
            jax.ShapeDtypeStruct((fc2_weight.shape[0] // 2, fc2_weight.shape[1]), BF16),
        ],
        cost_estimate=SMALL_COST,
        name="own_rest",
    )(fc1_weight, fc2_weight)


def after(values, *others):
    return lax.optimization_barrier((values,) + others)[0] if others else values


class Gather:
    SOURCE = {4: 0, 2: 0, 1: 0, 6: 4, 3: 2, 5: 4, 7: 6}
    STEP = {4: 4, 2: 2, 1: 1, 6: 2, 3: 1, 5: 1, 7: 1}

    def __init__(self, own):
        self.pieces = [own] + [None] * 7
        self.grouped = lax.axis_size("fsdp") == 8

    def send(self, *parts, ready=()):
        if not self.grouped:
            return
        sources = [self.pieces[self.SOURCE[part]] for part in parts]
        if ready:
            sources = lax.optimization_barrier(tuple(sources) + tuple(ready))
        for part, source in zip(parts, sources):
            self.pieces[part] = swap_group(source, self.STEP[part])

    def got(self, *parts):
        return tuple(self.pieces[part] for part in parts) if self.grouped else ()

    def result(self):
        if not self.grouped:
            return lax.all_gather(self.pieces[0], "fsdp", axis=0, tiled=True)
        return in_order(self.pieces, self.pieces[0].shape[0])


def add_low(left, right):
    return (left.astype(F32) + right.astype(F32)).astype(BF16)


def split_kernel(full_ref, *refs):
    sems = refs[2]
    group = lax.axis_index("fsdp")
    rows = full_ref.shape[0] // 8
    copies = []
    for n in range(8):
        far, near, side = n % 2, (n // 2) % 2, n // 4
        start = pl.multiple_of((group ^ (4 * far + 2 * near + side)) * rows, rows)
        target = refs[side].at[pl.ds((n % 4) * rows, rows)]
        copies.append(
            pltpu.make_async_copy(full_ref.at[pl.ds(start, rows)], target, sems.at[n])
        )
    for copy in copies:
        copy.start()
    for copy in copies:
        copy.wait()


def split_blocks(values):
    rows, columns = values.shape
    return pl.pallas_call(
        split_kernel,
        in_specs=[pl.BlockSpec(memory_space=pltpu.VMEM)],
        out_specs=[pl.BlockSpec(memory_space=pl.ANY)] * 2,
        out_shape=[jax.ShapeDtypeStruct((rows // 2, columns), values.dtype)] * 2,
        scratch_shapes=[pltpu.SemaphoreType.DMA((8,))],
        compiler_params=pltpu.CompilerParams(vmem_limit_bytes=16 * 2**20),
        cost_estimate=SMALL_COST,
        name="split_blocks",
    )(values)


def pack_kernel(
    one_ref, two_ref, grads_ref, hidden_ref, end_ref, middle_ref, *refs
):
    sum_refs, packed_ref = refs[:4], refs[4]
    group = lax.axis_index("fsdp")
    core = lax.rem(lax.axis_index("seq"), 2)
    squares = jnp.zeros((4, PAIR), F32)
    for n in range(end_ref.shape[1] // PAIR):
        span = slice(n * PAIR, (n + 1) * PAIR)
        end, middle = end_ref[:, span], middle_ref[:, span]
        squares = squares + jnp.concatenate([end[:1], middle[:1], end[1:], middle[1:]], axis=0)
    for n in range(8):
        far, near, side = n % 2, (n // 2) % 2, n // 4
        target = group ^ (4 * far + 2 * near + side)
        columns = pl.ds(pl.multiple_of(target * PAIR, PAIR), PAIR)
        mine = (target // 4) == core
        pair = lax.rem(target, 4)
        head_sums = jnp.zeros((2, PAIR), F32)
        for k in range(4):
            head_sums = jnp.where(jnp.logical_and(mine, pair == k), sum_refs[k][...], head_sums)
        one, two = one_ref[:, columns], two_ref[:, columns]
        hidden = [
            hidden_ref[:, pl.ds(pl.multiple_of(target * 2 * PAIR + k * PAIR, PAIR), PAIR)]
            for k in range(2)
        ]
        empty = jnp.zeros((1, PAIR), F32)
        rows = [one[:2], head_sums, two[2:3], two[:2], grads_ref[:, columns]]
        rows += [jnp.where(core == 0, part, empty) for part in hidden]
        rows += [jnp.where(core == 0, empty, part) for part in hidden]
        rows.append(squares)
        packed_ref[16 * n : 16 * (n + 1), :] = jnp.concatenate(rows, axis=0).astype(BF16)


def pack_lines(lines, sums):
    return pl.pallas_call(
        pack_kernel,
        in_specs=[pl.BlockSpec(memory_space=pltpu.VMEM)] * 10,
        out_specs=pl.BlockSpec(memory_space=pltpu.VMEM),
        out_shape=jax.ShapeDtypeStruct((128, PAIR), BF16),
        cost_estimate=SMALL_COST,
        name="pack_lines",
    )(*lines, *sums)


class Scatter:
    def __init__(self, values, *ready, halves=None, ordered=False):
        self.grouped = lax.axis_size("fsdp") == 8
        self.halved = halves is not None
        values = values.astype(BF16)
        if self.halved:
            self.kept, self.sent = halves
            self.crossed = swap_chip(self.sent)
        elif self.grouped:
            middle = values.shape[0] // 2
            split = (values[:middle], values[middle:]) if ordered else split_blocks(values)
            self.keep, self.side_send = split
            self.side = swap_group(after(self.side_send, *ready), 1)
        else:
            self.sums = lax.psum_scatter(values, "fsdp", scatter_dimension=0, tiled=True)

    def cross(self, *ready):
        values = add_low(self.kept, after(self.crossed, *ready))
        if self.grouped:
            self.keep, self.side_send = split_blocks(values)
            self.side = swap_group(self.side_send, 1)
        else:
            self.sums = lax.psum_scatter(values, "fsdp", scatter_dimension=0, tiled=True)

    def got(self, *names):
        return tuple(getattr(self, name) for name in names if hasattr(self, name))

    def step(self, name, next_name, bit, ready):
        if self.grouped:
            received = after(getattr(self, name), *ready)
            half = self.keep.shape[0] // 2
            send = add_low(self.keep[half:], received[half:])
            self.keep = add_low(self.keep[:half], received[:half])
            setattr(self, next_name, swap_group(send, bit))

    def near(self, *ready):
        self.step("side", "near_sums", 2, ready)

    def far(self, *ready):
        self.step("near_sums", "far_sums", 4, ready)

    def chips(self, *ready, beside=None):
        if self.grouped:
            self.sums = add_low(self.keep, after(self.far_sums, *ready))
        if beside is not None:
            self.sums = jnp.concatenate([self.sums, beside], axis=1)
        self.other_chip = swap_chip(self.sums)

    def cores(self, *ready):
        other_chip = after(self.other_chip, *ready)
        if self.halved:
            chip = lax.axis_index("seq") // 2
            first = jnp.where(chip == 0, self.sums, other_chip)
            second = jnp.where(chip == 0, other_chip, self.sums)
            self.total = jnp.concatenate([first, second], axis=1)
        else:
            self.total = add_low(self.sums, other_chip)
        self.other_core = swap_core(self.total)

    def last(self):
        if not self.grouped:
            return self.sums.astype(F32)
        return self.keep.astype(F32) + self.far_sums.astype(F32)


def take(values, index):
    return lax.dynamic_index_in_dim(values, index, 0, keepdims=False)


def in_core_order(own, other, core, axis):
    first = jnp.where(core == 0, own, other)
    second = jnp.where(core == 0, other, own)
    return first, second


def body(
    inputs,
    cotangent,
    valid,
    ln1_gain,
    ln1_bias,
    qkv_weight,
    q_bias,
    v_bias,
    out_weight,
    out_bias,
    ln2_gain,
    ln2_bias,
    fc1_weight,
    fc1_bias,
    fc2_weight,
    fc2_bias,
):
    clips, rows, width = inputs.shape
    groups = lax.axis_size("fsdp")
    place = lax.axis_index("seq")
    group = lax.axis_index("fsdp")
    chip, core = place // 2, place % 2
    half = width // 2
    hidden_rows = fc2_weight.shape[0]
    half_rows = hidden_rows // 2
    own_rows = clips * rows
    scale_factor = HEAD ** (-0.5)

    def all_clips(values, back):
        mine = values[:rows]
        first = jnp.where(chip == 0, mine, back)
        second = jnp.where(chip == 0, back, mine)
        return jnp.stack([first, second])

    own_width = width // groups
    vectors = (ln1_gain, ln1_bias, q_bias, v_bias, out_bias, ln2_gain, ln2_bias, fc2_bias, fc1_bias)
    quarter = half // 2
    row_width = 3 * quarter
    used = 8 * own_width + fc1_bias.shape[0]
    if groups == 8:
        own_first, own_second = own_qkv_blocks(qkv_weight, out_weight, vectors)
    else:
        by_head = qkv_weight.reshape(own_width, 3, 2, 2, 2, PAIR)
        by_head = lax.dynamic_index_in_dim(by_head, core, 2, keepdims=False)
        by_head = by_head.transpose(0, 2, 3, 1, 4).reshape(own_width, 2, row_width)
        out_columns = lax.dynamic_slice_in_dim(out_weight, core * half, half, 1)
        own_first = by_head[:, 0]
        own_second = jnp.concatenate([by_head[:, 1], out_columns], axis=1)

    qkv_a, qkv_b = Gather(own_first), Gather(own_second)
    qkv_a.send(4, 2, 1)
    other_inputs = swap_chip(take(after(inputs, *qkv_a.got(4, 2, 1)), 1 - chip))
    qkv_a.send(6, 3, 5, ready=qkv_a.got(4, 2, 1))
    qkv_b.send(4, ready=qkv_a.got(4, 2, 1))
    fc1_weight, fc2_weight = after((fc1_weight, fc2_weight), own_first)
    if groups == 8:
        own_fc1, own_fc2 = own_rest_blocks(fc1_weight, fc2_weight)
    else:
        own_fc1 = lax.dynamic_index_in_dim(
            fc1_weight.reshape(own_width, groups, 2, half_rows), core, 2, keepdims=False
        ).reshape(own_width, groups * half_rows)
        own_fc2 = lax.dynamic_slice_in_dim(fc2_weight, core * half_rows, half_rows, 0)
    full_fc1 = lax.all_gather(own_fc1, "fsdp", axis=0, tiled=True)
    full_fc2 = lax.all_gather(own_fc2, "fsdp", axis=0, tiled=True)
    qkv_a.send(7, ready=qkv_a.got(6, 3, 5))
    other_inputs = after(other_inputs, own_fc1, *qkv_a.got(6, 3, 5))
    qkv_b.send(2, 1, ready=qkv_a.got(6, 3, 5))
    own_inputs = jnp.concatenate([take(inputs, chip), other_inputs], axis=0)
    all_inputs = with_partner(own_inputs)
    if groups == 8:
        qkv_first, wide, bias_fc1 = in_order(qkv_a.pieces, own_width, True)
    else:
        qkv_first = qkv_a.result()
        packed = lax.all_gather(jnp.concatenate(vectors), "fsdp", axis=0)
        wide = [
            packed[:, i * own_width : (i + 1) * own_width].reshape(width).astype(F32)
            for i in range(8)
        ]
        bias_fc1 = packed[:, 8 * own_width : used].reshape(groups, 2, half_rows)
        bias_fc1 = take(jnp.moveaxis(bias_fc1, 1, 0), core)
        bias_fc1 = bias_fc1.reshape(groups * half_rows).astype(F32)
    gain_one, bias_one, bias_q, bias_v, bias_out, gain_two, bias_two, bias_fc2 = [
        wide[i] for i in range(8)
    ]
    bias_q = take(bias_q.reshape(2, 2, 2, PAIR), core)
    bias_v = take(bias_v.reshape(2, 2, 2, PAIR), core)
    bias_mixed = jnp.stack([bias_q, jnp.zeros_like(bias_q), bias_v], axis=2).reshape(2, row_width)
    scale_mixed = jnp.array([scale_factor, 1.0, 1.0] * 2, F32).repeat(PAIR)
    clip_valid = take(valid, chip).reshape(2 * clips, rows)
    own_valid = jnp.concatenate([take(clip_valid, place), take(clip_valid, place ^ 2)])
    other_valid = jnp.concatenate([take(clip_valid, place ^ 1), take(clip_valid, place ^ 3)])
    key_valid = jnp.concatenate([own_valid, other_valid])
    lane = jnp.arange(PAIR) % HEAD
    key_mask = jnp.where(key_valid > 0, 0.0, MASKED)[:, None]
    key_base = jnp.where(lane == 0, key_mask, jnp.where(lane < 4, 1.0, 0.0)).astype(BF16)


    def project(weight, i):
        return ((dot(h_one, weight) + bias_mixed[i]) * scale_mixed).astype(BF16)

    h_one = rows_call(
        first_kernel, [all_inputs], [gain_one[None], bias_one[None]], [BF16], 0, "first_norm"
    )[0]
    mixed = [project(qkv_first, 0)]
    context, queries = [], []

    def attend_pair(pair, *ready):
        before = context[-1] if context else None
        base = after(key_base, *ready)
        results = attend(mixed[pair // 2], base, pair % 2, before, pair, 4)
        context.append(results[0])
        queries.append(results[1])

    ready = (h_one,) + qkv_b.got(4, 2, 1)
    qkv_b.send(6, 3, 5, ready=ready)
    attend_pair(0, *ready)
    ready = (queries[0],) + qkv_b.got(6, 3, 5)
    qkv_b.send(7, ready=ready)
    other_grads = swap_chip(after(take(cotangent, 1 - chip), *ready))
    attend_pair(1, *ready)
    second_columns = qkv_b.result()
    mixed.append(project(second_columns[:, :row_width], 1))
    ready = (queries[1], mixed[1], other_grads)
    kept = lax.dynamic_slice(second_columns, (core * half, row_width), (half, half))
    received = lax.dynamic_slice(second_columns, ((1 - core) * half, row_width), (half, half))
    received = swap_core(after(received, mixed[1]))
    attend_pair(2, kept, *ready)
    ready = (queries[2], received)
    attend_pair(3, *ready)
    own_grads = jnp.concatenate([take(cotangent, chip), after(other_grads, queries[3])], axis=0)
    full_out = jnp.concatenate(in_core_order(kept, received, core, 1), axis=1)
    all_context = context[3]
    own_part, other_part = both_halves_product([(all_context, full_out)], NN)
    ready = (own_grads, own_part)
    counted = own_valid.astype(F32)[:, None]
    residual_mid, h_two, middle_sums = rows_call(
        middle_kernel,
        [own_part, after(other_part, *ready), own_inputs, counted],
        [bias_out[None], gain_two[None], bias_two[None]],
        [F32, BF16],
        2,
        "middle",
    )
    h_two = with_partner(h_two)
    all_grads = with_partner(after(own_grads, residual_mid))
    grad_sums = column_sum(own_grads)
    h_two = after(h_two, grad_sums)
    active, slope = gelu_both(dot(h_two, full_fc1) + bias_fc1)
    active, slope = active.astype(BF16), slope.astype(BF16)
    active = after(active, full_fc2)
    fc2_product = dot(active, all_grads, TN).astype(BF16)
    fc2_scatter = Scatter(fc2_product)

    late_grads = after(all_grads, *fc2_scatter.got("keep"))
    grad_hidden, hidden_sums = hidden_gradient(late_grads, full_fc2, slope)
    fc1_halves = weight_halves(h_two, grad_hidden)
    fc1_scatter = Scatter(fc1_halves[0], halves=fc1_halves)
    own_part, other_part = both_halves_product(
        [(after(grad_hidden, fc1_scatter.sent), full_fc1)], NT
    )
    grad_residual, own_grad_attn, two_sums = rows_call(
        norm_back_kernel,
        [own_part, other_part, residual_mid, own_grads],
        [gain_two[None]],
        [F32, BF16],
        3,
        "norm_back",
    )
    grad_attn = with_partner(own_grad_attn)
    grad_context = half_product([(grad_attn, full_out)], NT, None, BF16)
    halves, sums = [None, None], []

    def back_pair(pair, *ready):
        grad_mixed, parts = attend_back(
            queries[pair],
            mixed[pair // 2],
            grad_context,
            all_context,
            after(key_base, *ready),
            pair % 2,
            pair,
            halves[pair // 2],
        )
        halves[pair // 2] = grad_mixed
        sums.append(parts)

    back_pair(0, grad_context)
    ready = (sums[0], fc1_scatter.crossed) + fc2_scatter.got("side")
    grad_out = dot(all_context, after(grad_attn, *ready), TN).astype(BF16)
    kept = lax.dynamic_slice_in_dim(grad_out, core * half, half, 1)
    received = swap_core(lax.dynamic_slice_in_dim(grad_out, (1 - core) * half, half, 1))
    fc2_scatter.near(*ready)
    fc1_scatter.cross(*ready)
    grad_out = jnp.concatenate(in_core_order(kept, received, core, 0), axis=0)
    out_sums = lax.psum_scatter(grad_out, "fsdp", scatter_dimension=0, tiled=True)
    back_pair(1, grad_out, *ready, *fc2_scatter.got("keep"), *fc1_scatter.got("keep"))
    early = dot(h_one, halves[0], TN).astype(BF16)
    ready = (sums[1],) + fc2_scatter.got("near_sums") + fc1_scatter.got("side")
    fc2_scatter.far(*ready)
    fc1_scatter.near(*ready)
    early_scatter = Scatter(early, *ready)
    ready += fc2_scatter.got("keep") + fc1_scatter.got("keep") + early_scatter.got("keep")
    own_mlp, other_mlp = both_halves_product([(after(active, *ready), full_fc2)], NN)
    low_output, end_sums = rows_call(
        end_kernel,
        [own_mlp, other_mlp, residual_mid, counted],
        [bias_fc2[None]],
        [BF16],
        2,
        "end",
    )
    back_pair(2, low_output, *ready)
    output_back = swap_chip(low_output[rows:])
    ready = (sums[2], output_back) + fc2_scatter.got("far_sums") + fc1_scatter.got("near_sums")
    ready += early_scatter.got("side")
    fc2_scatter.chips(*ready)
    fc1_scatter.far(*ready)
    early_scatter.near(*ready)
    ready += (fc2_scatter.sums,) + fc1_scatter.got("keep") + early_scatter.got("keep")
    back_pair(3, *ready)
    ready = (sums[3], fc2_scatter.other_chip) + fc1_scatter.got("far_sums")
    ready += early_scatter.got("near_sums") + (out_sums,)
    early_scatter.far(*ready)
    fc1_scatter.chips(*ready)
    fc2_scatter.cores(*ready)
    late_scatter = Scatter(dot(after(h_one, *ready), halves[1], TN))
    gm_first, gm_second = after(tuple(halves), *late_scatter.got("keep"))
    own_one, other_one = both_halves_product(
        [(gm_first, qkv_first), (gm_second, second_columns)], NT
    )
    low_input_grad, one_sums = rows_call(
        norm_back_kernel,
        [own_one, other_one, own_inputs, grad_residual],
        [gain_one[None]],
        [BF16],
        3,
        "norm_back",
    )
    input_back = swap_chip(low_input_grad[rows:])
    ready = late_scatter.got("side") + (low_input_grad,)
    late_scatter.near(*ready)
    one_sums = after(one_sums, *ready)

    if groups == 8:
        packed = pack_lines(
            [one_sums, two_sums, grad_sums[None], hidden_sums, end_sums, middle_sums], sums
        )
    else:
        lines = [one_sums[0], one_sums[1], two_sums[2], two_sums[0], two_sums[1], grad_sums]
        lines.append(hidden_sums[0])
        squares = [end_sums[0], middle_sums[0], end_sums[1], middle_sums[1]]
        squares = [jnp.sum(line.reshape(-1, PAIR), axis=0) for line in squares]

        def by_core(values):
            full = jnp.zeros((2, values.shape[0]), F32)
            return lax.dynamic_update_index_in_dim(full, values, core, 0).reshape(-1)

        wide = lines[:2] + [by_core(jnp.concatenate([part[n] for part in sums])) for n in range(2)]
        wide = [line.reshape(groups, own_width) for line in wide + lines[2:6]]
        all_sums = jnp.zeros((groups, 2, half_rows), F32)
        all_sums = lax.dynamic_update_index_in_dim(
            all_sums, lines[6].reshape(groups, half_rows), core, 1
        )
        wide.append(all_sums.reshape(groups, hidden_rows))
        wide.append(jnp.zeros((groups, 12 * PAIR - used)))
        wide.append(jnp.broadcast_to(jnp.concatenate(squares), (groups, 4 * PAIR)))
        packed = jnp.concatenate(wide, axis=1).astype(BF16).reshape(groups * 16, PAIR)
    ready = early_scatter.got("far_sums") + (fc1_scatter.other_chip,)
    packed = add_low(packed, after(swap_chip(packed), *ready))
    early_scatter.chips(packed, beside=out_sums)
    fc1_scatter.cores(packed)
    ready = late_scatter.got("near_sums")
    packed = add_low(packed, after(swap_core(packed), *ready))
    late_scatter.far(packed)
    vector_scatter = Scatter(packed, ordered=True)
    vector_scatter.near(early_scatter.other_chip)
    early_scatter.cores(*vector_scatter.got("keep"))
    ready = late_scatter.got("far_sums") + (input_back,)
    vector_scatter.far(*ready)
    late_scatter.chips(*vector_scatter.got("keep"))
    late_scatter.cores()
    ready_last = (packed,)
    output = all_clips(low_output, after(output_back, packed))
    input_grad = all_clips(low_input_grad, input_back)

    def in_columns(values, other, blocks):
        size = values.shape[1] // blocks
        parts = in_core_order(values, other, core, 0)
        parts = [part.reshape(own_width, blocks, 1, size) for part in parts]
        return jnp.concatenate(parts, axis=2).reshape(own_width, -1).astype(F32)

    fc2_parts = after((fc2_scatter.total, fc2_scatter.other_core), *ready_last)
    fc2_grad = in_core_order(*fc2_parts, core, 0)
    fc2_grad = jnp.concatenate(fc2_grad, axis=0).astype(F32)
    early_parts = [early_scatter.total, early_scatter.other_core]
    late_parts = [late_scatter.total, late_scatter.other_core]
    fc1_parts = after((fc1_scatter.total, fc1_scatter.other_core), *ready_last)
    if groups == 8:
        fc1_places = [
            (0, n * half_rows, half_rows, 2 * n * half_rows, (2 * n + 1) * half_rows)
            for n in range(groups)
        ]
        fc1_grad = join_columns(fc1_parts, fc1_places, 2 * groups * half_rows)
        out_grad = join_columns(early_parts, [(0, row_width, half, 0, half)], width)
        qkv_places = []
        for n in range(3):
            for pair in range(4):
                target = n * width + pair * PAIR
                start = (3 * (pair % 2) + n) * PAIR
                qkv_places.append((pair // 2, start, PAIR, target, target + half))
        qkv_grad = join_columns(early_parts + late_parts, qkv_places, 3 * width)
    else:
        fc1_grad = in_columns(*fc1_parts, groups)
        out_grad = in_columns(*[part[:, row_width:] for part in early_parts], 1)

        def both_halves(left, right):
            left = left[:, :row_width].reshape(own_width, 1, 2, 3, PAIR)
            right = right.reshape(own_width, 1, 2, 3, PAIR)
            both = jnp.concatenate([left, right], axis=1).transpose(0, 3, 1, 2, 4)
            return both.reshape(own_width, 3 * half)

        qkv_grad = in_columns(*[both_halves(*pair) for pair in zip(early_parts, late_parts)], 3)
    lines = vector_scatter.last()
    flat = lines[:12].reshape(-1)
    own_vectors = [flat[i * own_width : (i + 1) * own_width] for i in range(8)]
    own_hidden = flat[8 * own_width : used]
    totals = jnp.sum(lines[12:], axis=1)
    branch_rms = jnp.sqrt(totals[:3] / totals[3])
    return (
        output,
        input_grad,
        own_vectors[0],
        own_vectors[1],
        qkv_grad,
        own_vectors[2],
        own_vectors[3],
        out_grad,
        own_vectors[4],
        own_vectors[5],
        own_vectors[6],
        fc1_grad,
        own_hidden,
        fc2_grad,
        own_vectors[7],
        branch_rms,
    )


def solution(mesh):
    tokens, rows, vector = P("fsdp", "seq", None), P("fsdp", None), P("fsdp")
    return jax.shard_map(
        body,
        mesh=mesh,
        in_specs=(
            tokens,
            tokens,
            rows,
            vector,
            vector,
            rows,
            vector,
            vector,
            rows,
            vector,
            vector,
            vector,
            rows,
            vector,
            rows,
            vector,
        ),
        out_specs=(
            tokens,
            tokens,
            vector,
            vector,
            rows,
            vector,
            vector,
            rows,
            vector,
            vector,
            vector,
            rows,
            vector,
            rows,
            vector,
            P(),
        ),
        check_vma=False,
    )
```

```python
from functools import partial

import jax
import jax.numpy as jnp
from jax import lax
from jax.experimental import pallas as pl
from jax.experimental.pallas import tpu as pltpu
from jax.sharding import PartitionSpec as P

HEADS = 16
HEAD = 64
PAIR = 2 * HEAD
EPS = 1e-06
MASKED = -1e30
VMEM_BYTES = 28 * 2**20
BF16 = jnp.bfloat16
F32 = jnp.float32
NN = (((1,), (0,)), ((), ()))
NT = (((1,), (1,)), ((), ()))
TN = (((0,), (0,)), ((), ()))
SMALL_COST = pl.CostEstimate(flops=10**7, bytes_accessed=2**20, transcendentals=0)


def dot(left, right, dims=NN):
    return lax.dot_general(left, right, dims, preferred_element_type=F32)


def lanes_of(shape):
    return lax.broadcasted_iota(jnp.int32, shape, len(shape) - 1)


def three_parts(column):
    high = column.astype(BF16).astype(F32)
    rest = column - high
    middle = rest.astype(BF16).astype(F32)
    return high, middle, rest - middle


def block_rows(length, *sizes):
    for rows in sizes + (224, 112, 16):
        if length % rows == 0:
            return rows
    return length


def attend_kernel(q_ref, k_ref, v_ref, key_base_ref, *refs):
    context_ref, query_ref = refs[-2:]
    length = q_ref.shape[0]
    rows = block_rows(length, 392)
    low = lanes_of((length, PAIR)) < HEAD
    keys, values, key_base = k_ref[...], v_ref[...], key_base_ref[...]
    ones = jnp.ones((length, PAIR), BF16)
    keys_of = [jnp.where(low, keys, key_base), jnp.where(low, key_base, keys)]
    values_of = [jnp.where(low, values, ones), jnp.where(low, ones, values)]
    lane = lanes_of((rows, PAIR))
    low_rows = lane < HEAD
    for step in range(length // rows):
        span = slice(step * rows, (step + 1) * rows)
        queries = q_ref[span, :]
        results = []
        for head in range(2):
            base = HEAD * (1 - head)
            own = low_rows if head == 0 else jnp.logical_not(low_rows)
            unit = jnp.where(lane == base, 1.0, 0.0)
            scores = dot(jnp.where(own, queries, unit.astype(BF16)), keys_of[head], NT)
            highest = jnp.max(scores, axis=1, keepdims=True)
            weights = jnp.exp(scores - highest).astype(BF16)
            mixed = dot(weights, values_of[head])
            total = mixed[:, base : base + 1]
            high, middle, rest = three_parts(-(highest + jnp.log(total)))
            extra = jnp.where(lane == base + 3, rest, unit)
            extra = jnp.where(lane == base + 2, middle, extra)
            extra = jnp.where(lane == base + 1, high, extra)
            query_ref[head, span, :] = jnp.where(own, queries, extra.astype(BF16))
            results.append(mixed / total)
        context_ref[span, :] = jnp.where(low_rows, results[0], results[1]).astype(BF16)


def attend(mixed, key_base, pair, context, place, places):
    length = mixed.shape[0]
    tile = lambda column: pl.BlockSpec((length, PAIR), lambda i: (0, column))
    in_specs = [tile(3 * pair), tile(3 * pair + 1), tile(3 * pair + 2), tile(0)]
    operands = (mixed, mixed, mixed, key_base)
    aliases = {}
    if context is not None:
        in_specs.append(pl.BlockSpec(memory_space=pl.ANY))
        operands += (context,)
        aliases = {4: 0}
    return pl.pallas_call(
        attend_kernel,
        grid=(1,),
        in_specs=in_specs,
        out_specs=[tile(place), pl.BlockSpec((2, length, PAIR), lambda i: (0, 0, 0))],
        out_shape=[
            jax.ShapeDtypeStruct((length, places * PAIR), BF16),
            jax.ShapeDtypeStruct((2, length, PAIR), BF16),
        ],
        input_output_aliases=aliases,
        compiler_params=pltpu.CompilerParams(vmem_limit_bytes=VMEM_BYTES),
        cost_estimate=SMALL_COST,
        name="attend",
    )(*operands)


def attend_back_kernel(query_ref, k_ref, v_ref, grad_ref, context_ref, key_base_ref, *refs):
    grad_mixed_ref, sums_ref = refs[-2:]
    length = k_ref.shape[0]
    rows = block_rows(length)
    low = lanes_of((length, PAIR)) < HEAD
    keys, values, key_base = k_ref[...], v_ref[...], key_base_ref[...]
    ones = jnp.ones((length, PAIR), BF16)
    lane = lanes_of((rows, PAIR))
    low_rows = lane < HEAD
    steps = length // rows
    grad_q, grad_k, grad_v = [], [], []
    sum_q = jnp.zeros((1, PAIR), F32)
    for head in range(2):
        base = HEAD * (1 - head)
        own = low if head == 0 else jnp.logical_not(low)
        own_rows = low_rows if head == 0 else jnp.logical_not(low_rows)
        head_keys = jnp.where(own, keys, key_base)
        head_values = jnp.where(own, values, ones)
        sum_k = jnp.zeros((length, PAIR), F32)
        sum_v = jnp.zeros((length, PAIR), F32)
        for step in range(steps):
            span = slice(step * rows, (step + 1) * rows)
            queries = query_ref[head, span, :]
            grads = grad_ref[span, :]
            product = grads.astype(F32) * context_ref[span, :].astype(F32)
            inner = jnp.sum(jnp.where(own_rows, product, 0.0), axis=1, keepdims=True)
            high, middle, rest = three_parts(-inner)
            extra = jnp.where(lane == base + 2, rest, 0.0)
            extra = jnp.where(lane == base + 1, middle, extra)
            extra = jnp.where(lane == base, high, extra)
            head_grads = jnp.where(own_rows, grads, extra.astype(BF16))
            probs = jnp.exp(dot(head_keys, queries, NT))
            grad_scores = (probs * dot(head_values, head_grads, NT)).astype(BF16)
            sum_v = sum_v + dot(probs.astype(BF16), grads)
            sum_k = sum_k + dot(grad_scores, queries)
            part = dot(grad_scores, keys, TN)
            if head == 0:
                grad_q.append(part)
            else:
                both = jnp.where(low_rows, grad_q[step], part).astype(BF16)
                both = both * (HEAD ** (-0.5))
                grad_mixed_ref[span, :PAIR] = both
                sum_q = sum_q + jnp.sum(both.astype(F32), axis=0, keepdims=True)
        grad_k.append(sum_k)
        grad_v.append(sum_v)
    grad_mixed_ref[:, PAIR : 2 * PAIR] = jnp.where(low, grad_k[0], grad_k[1]).astype(BF16)
    both = jnp.where(low, grad_v[0], grad_v[1]).astype(BF16)
    grad_mixed_ref[:, 2 * PAIR :] = both
    sums_ref[0:1, :] = sum_q
    sums_ref[1:2, :] = jnp.sum(both.astype(F32), axis=0, keepdims=True)


def attend_back(queries, mixed, grad_context, context, key_base, pair, place, grad_mixed):
    length = mixed.shape[0]
    tile = lambda column: pl.BlockSpec((length, PAIR), lambda i: (0, column))
    in_specs = [
        pl.BlockSpec((2, length, PAIR), lambda i: (0, 0, 0)),
        tile(3 * pair + 1),
        tile(3 * pair + 2),
        tile(place),
        tile(place),
        tile(0),
    ]
    operands = (queries, mixed, mixed, grad_context, context, key_base)
    aliases = {}
    if grad_mixed is not None:
        in_specs.append(pl.BlockSpec(memory_space=pl.ANY))
        operands += (grad_mixed,)
        aliases = {6: 0}
    return pl.pallas_call(
        attend_back_kernel,
        grid=(1,),
        in_specs=in_specs,
        out_specs=[
            pl.BlockSpec((length, 3 * PAIR), lambda i: (0, pair)),
            pl.BlockSpec((2, PAIR), lambda i: (0, 0)),
        ],
        out_shape=[
            jax.ShapeDtypeStruct((length, 6 * PAIR), BF16),
            jax.ShapeDtypeStruct((2, PAIR), F32),
        ],
        input_output_aliases=aliases,
        compiler_params=pltpu.CompilerParams(vmem_limit_bytes=VMEM_BYTES),
        cost_estimate=SMALL_COST,
        name="attend_back",
    )(*operands)


def normalize(values):
    center = values - jnp.mean(values, axis=-1, keepdims=True)
    spread = jnp.mean(center * center, axis=-1, keepdims=True)
    scale = lax.rsqrt(spread + EPS)
    return center * scale, scale


def rows_call(kernel, row_inputs, constants, kinds, sum_rows, name):
    rows, width = row_inputs[0].shape
    tile = rows // 7 if rows % 112 == 0 else rows
    block = lambda columns: pl.BlockSpec((tile, columns), lambda i: (i, 0))
    whole = lambda shape: pl.BlockSpec(shape, lambda i: (0, 0))
    out_specs = [block(width)] * len(kinds)
    out_shape = [jax.ShapeDtypeStruct((rows, width), kind) for kind in kinds]
    if sum_rows:
        out_specs.append(whole((sum_rows, width)))
        out_shape.append(jax.ShapeDtypeStruct((sum_rows, width), F32))
    return pl.pallas_call(
        kernel,
        grid=(rows // tile,),
        in_specs=[block(part.shape[1]) for part in row_inputs]
        + [whole(part.shape) for part in constants],
        out_specs=out_specs,
        out_shape=out_shape,
        compiler_params=pltpu.CompilerParams(vmem_limit_bytes=VMEM_BYTES),
        cost_estimate=SMALL_COST,
        name=name,
    )(*row_inputs, *constants)


def add_rows(sums_ref, parts):
    @pl.when(pl.program_id(0) == 0)
    def _():
        sums_ref[...] = jnp.zeros(sums_ref.shape, F32)

    lines = [jnp.sum(part, axis=0, keepdims=True) for part in parts]
    sums_ref[...] += jnp.concatenate(lines, axis=0)


def first_kernel(values_ref, gain_ref, bias_ref, out_ref):
    normal = normalize(values_ref[...].astype(F32))[0]
    out_ref[...] = (normal * gain_ref[...] + bias_ref[...]).astype(BF16)


def middle_kernel(
    own_ref, other_ref, inputs_ref, counted_ref, out_bias_ref, gain_ref, bias_ref, *out_refs
):
    middle_ref, low_ref, sums_ref = out_refs
    branch = own_ref[...] + other_ref[...].astype(F32) + out_bias_ref[...]
    middle = inputs_ref[...].astype(F32) + branch
    middle_ref[...] = middle
    low_ref[...] = (normalize(middle)[0] * gain_ref[...] + bias_ref[...]).astype(BF16)
    counted = counted_ref[...]
    add_rows(sums_ref, [counted * branch * branch, jnp.broadcast_to(counted, branch.shape)])


def end_kernel(own_ref, other_ref, middle_ref, counted_ref, bias_ref, low_ref, sums_ref):
    branch = own_ref[...] + other_ref[...].astype(F32) + bias_ref[...]
    result = middle_ref[...] + branch
    low_ref[...] = result.astype(BF16)
    counted = counted_ref[...]
    add_rows(sums_ref, [counted * result * result, counted * branch * branch])


def norm_back_kernel(own_ref, other_ref, values_ref, residual_ref, gain_ref, *out_refs):
    grad = own_ref[...] + other_ref[...].astype(F32)
    normal, scale = normalize(values_ref[...].astype(F32))
    inner = grad * gain_ref[...]
    first = jnp.mean(inner, axis=-1, keepdims=True)
    second = jnp.mean(inner * normal, axis=-1, keepdims=True)
    total = residual_ref[...].astype(F32) + scale * (inner - first - normal * second)
    low = total.astype(BF16)
    if len(out_refs) == 3:
        out_refs[0][...] = total
    out_refs[-2][...] = low
    add_rows(out_refs[-1], [grad * normal, grad, low.astype(F32)])


def weight_kernel(left_ref, right_ref, kept_ref, sent_ref):
    chip = lax.axis_index("seq") // 2
    left, half = left_ref[...], kept_ref.shape[1]
    for part, out_ref in ((chip, kept_ref), (1 - chip, sent_ref)):
        columns = pl.ds(pl.multiple_of(part * half, half), half)
        out_ref[...] = dot(left, right_ref[:, columns], TN).astype(BF16)


def weight_halves(left, right):
    rows, depth = left.shape
    columns = right.shape[1]
    tile = min(depth, 512)
    half = pl.BlockSpec((tile, columns // 2), lambda i: (i, 0))
    return pl.pallas_call(
        weight_kernel,
        grid=(depth // tile,),
        in_specs=[
            pl.BlockSpec((rows, tile), lambda i: (0, i)),
            pl.BlockSpec((rows, columns), lambda i: (0, 0)),
        ],
        out_specs=[half, half],
        out_shape=[jax.ShapeDtypeStruct((depth, columns // 2), BF16)] * 2,
        compiler_params=pltpu.CompilerParams(vmem_limit_bytes=VMEM_BYTES),
        cost_estimate=SMALL_COST,
        name="weight_halves",
    )(left, right)


def gelu_both(values):
    half = 0.5 * (1.0 + lax.erf(values * (0.5**0.5)))
    density = jnp.exp(-0.5 * values * values) * (0.5 / jnp.pi) ** 0.5
    return values * half, half + values * density


def hidden_kernel(grad_ref, weight_ref, slope_ref, hidden_ref, sums_ref):
    rows = grad_ref.shape[0] // 2
    weight = weight_ref[...]
    total = jnp.zeros((1, weight.shape[0]), F32)
    for span in (slice(0, rows), slice(rows, 2 * rows)):
        hidden = (dot(grad_ref[span, :], weight, NT) * slope_ref[span, :].astype(F32)).astype(BF16)
        hidden_ref[span, :] = hidden
        total = total + jnp.sum(hidden.astype(F32), axis=0, keepdims=True)
    sums_ref[...] = total


def hidden_gradient(grads, weight, slope):
    rows, depth = grads.shape
    columns = weight.shape[0]
    tile = min(columns, 512)
    block = pl.BlockSpec((rows, tile), lambda i: (0, i))
    return pl.pallas_call(
        hidden_kernel,
        grid=(columns // tile,),
        in_specs=[
            pl.BlockSpec((rows, depth), lambda i: (0, 0)),
            pl.BlockSpec((tile, depth), lambda i: (i, 0)),
            block,
        ],
        out_specs=[block, pl.BlockSpec((1, tile), lambda i: (0, i))],
        out_shape=[
            jax.ShapeDtypeStruct((rows, columns), BF16),
            jax.ShapeDtypeStruct((1, columns), F32),
        ],
        compiler_params=pltpu.CompilerParams(vmem_limit_bytes=VMEM_BYTES),
        cost_estimate=SMALL_COST,
        name="hidden_gradient",
    )(grads, weight, slope)


def half_kernel(dims, *refs):
    total = dot(refs[0][...], refs[1][...], dims)
    for n in range(2, len(refs) - 1, 2):
        total = total + dot(refs[n][...], refs[n + 1][...], dims)
    refs[-1][...] = total.astype(refs[-1].dtype)


def half_product(pairs, dims, part, kind):
    rows = pairs[0][0].shape[0] if part is None else pairs[0][0].shape[0] // 2
    part = part or 0
    columns = pairs[0][1].shape[1 if dims is NN else 0]
    tile = min(columns, 512)
    in_specs, operands = [], []
    for left, right in pairs:
        depth = left.shape[1]
        in_specs.append(pl.BlockSpec((rows, depth), lambda i: (part, 0)))
        if dims is NN:
            in_specs.append(pl.BlockSpec((depth, tile), lambda i: (0, i)))
        else:
            in_specs.append(pl.BlockSpec((tile, depth), lambda i: (i, 0)))
        operands += [left, right]
    return pl.pallas_call(
        partial(half_kernel, dims),
        grid=(columns // tile,),
        in_specs=in_specs,
        out_specs=pl.BlockSpec((rows, tile), lambda i: (0, i)),
        out_shape=jax.ShapeDtypeStruct((rows, columns), kind),
        compiler_params=pltpu.CompilerParams(vmem_limit_bytes=VMEM_BYTES),
        cost_estimate=SMALL_COST,
        name="half_product",
    )(*operands)


def both_halves_product(pairs, dims):
    other = half_product(pairs, dims, 1, BF16)
    own = [(after(left, other), right) for left, right in pairs]
    return half_product(own, dims, 0, F32), swap_core(other)


def join_kernel(places, *refs):
    out_ref = refs[-1]
    core = lax.rem(lax.axis_index("seq"), 2)
    for n, (source, start, width, first, second) in enumerate(places):
        for other in range(2):
            target = pl.multiple_of(jnp.where(core == other, first, second), PAIR)
            block = refs[2 * source + other][:, start : start + width]
            out_ref[:, pl.ds(target, width)] = block.astype(F32)


def join_columns(parts, places, columns):
    rows = parts[0].shape[0]
    return pl.pallas_call(
        partial(join_kernel, places),
        in_specs=[pl.BlockSpec(memory_space=pltpu.VMEM)] * len(parts),
        out_specs=pl.BlockSpec(memory_space=pltpu.VMEM),
        out_shape=jax.ShapeDtypeStruct((rows, columns), F32),
        cost_estimate=SMALL_COST,
        name="join_columns",
    )(*parts)


def column_sum(values):
    return jnp.sum(values, axis=0, dtype=F32)


def swap_core(values):
    return lax.ppermute(values, "seq", [(0, 1), (1, 0), (2, 3), (3, 2)])


def swap_chip(values):
    return lax.ppermute(values, "seq", [(0, 2), (2, 0), (1, 3), (3, 1)])


def stack_kernel(own_ref, other_ref, out_ref, sems):
    rows = own_ref.shape[0]
    copies = [
        pltpu.make_async_copy(ref, out_ref.at[pl.ds(n * rows, rows)], sems.at[n])
        for n, ref in enumerate((own_ref, other_ref))
    ]
    for copy in copies:
        copy.start()
    for copy in copies:
        copy.wait()


def with_partner(values):
    rows, columns = values.shape
    return pl.pallas_call(
        stack_kernel,
        in_specs=[pl.BlockSpec(memory_space=pltpu.VMEM)] * 2,
        out_specs=pl.BlockSpec(memory_space=pl.ANY),
        out_shape=jax.ShapeDtypeStruct((2 * rows, columns), values.dtype),
        scratch_shapes=[pltpu.SemaphoreType.DMA((2,))],
        compiler_params=pltpu.CompilerParams(vmem_limit_bytes=16 * 2**20),
        cost_estimate=SMALL_COST,
        name="stack_rows",
    )(values, swap_core(values))


def swap_group(values, bit):
    return lax.ppermute(values, "fsdp", [(i, i ^ bit) for i in range(8)])


def order_kernel(count, *refs):
    pieces, full_ref, held, arrived, sent = refs[:count], refs[count], *refs[-3:]
    group = lax.axis_index("fsdp")
    rows = full_ref.shape[0] // count
    loads = [
        pltpu.make_async_copy(piece, held.at[relative], arrived.at[relative])
        for relative, piece in enumerate(pieces)
    ]
    for load in loads:
        load.start()
    stores = []
    for relative in range(count):
        start = pl.multiple_of((group ^ relative) * rows, rows)
        store = pltpu.make_async_copy(
            held.at[relative, pl.ds(0, rows)], full_ref.at[pl.ds(start, rows)], sent.at[relative]
        )
        loads[relative].wait()
        store.start()
        stores.append(store)
    if len(refs) > count + 4:
        own_width, core = 128, lax.rem(lax.axis_index("seq"), 2)
        wide_ref, bias_ref = refs[count + 1], refs[count + 2]
        for relative in range(count):
            place = group ^ relative
            columns = pl.ds(pl.multiple_of(place * own_width, own_width), own_width)
            extra = held[relative, rows : rows + 8, :].astype(F32)
            lines = [
                extra[k : k + 1, own_width * n : own_width * (n + 1)]
                for k in range(2)
                for n in range(6)
            ]
            for n in range(8):
                wide_ref[n : n + 1, columns] = lines[n]
            for n in range(2):
                start = pl.multiple_of((place * 2 + n) * own_width, own_width)
                bias_ref[:, pl.ds(start, own_width)] = jnp.where(
                    core == 0, lines[8 + n], lines[10 + n]
                )
    for store in stores:
        store.wait()


def in_order(pieces, rows, with_vectors=False):
    count, columns = len(pieces), pieces[0].shape[1]
    out_specs = [pl.BlockSpec(memory_space=pl.ANY)]
    out_shape = [jax.ShapeDtypeStruct((count * rows, columns), pieces[0].dtype)]
    if with_vectors:
        out_specs += [pl.BlockSpec(memory_space=pltpu.VMEM)] * 2
        out_shape += [jax.ShapeDtypeStruct((8, 1024), F32), jax.ShapeDtypeStruct((1, 2048), F32)]
    result = pl.pallas_call(
        partial(order_kernel, count),
        in_specs=[pl.BlockSpec(memory_space=pl.ANY)] * count,
        out_specs=out_specs,
        out_shape=out_shape,
        scratch_shapes=[
            pltpu.VMEM((count,) + pieces[0].shape, pieces[0].dtype),
            pltpu.SemaphoreType.DMA((count,)),
            pltpu.SemaphoreType.DMA((count,)),
        ],
        compiler_params=pltpu.CompilerParams(vmem_limit_bytes=16 * 2**20),
        cost_estimate=SMALL_COST,
        name="in_order",
    )(*pieces)
    return result if with_vectors else result[0]


def own_kernel(qkv_ref, out_ref, *refs):
    vector_refs, (first_ref, second_ref) = refs[:-2], refs[-2:]
    core = lax.rem(lax.axis_index("seq"), 2)
    rows = qkv_ref.shape[0]
    for n in range(3):
        for pair in range(4):
            block_ref = second_ref if pair >= 2 else first_ref
            start = pl.multiple_of((8 * n + pair + 4 * core) * PAIR, PAIR)
            target = (3 * (pair % 2) + n) * PAIR
            block_ref[:rows, target : target + PAIR] = qkv_ref[:, pl.ds(start, PAIR)]
    out_half = out_ref.shape[1] // 2
    start = pl.multiple_of(core * out_half, out_half)
    second_ref[:, 6 * PAIR :] = out_ref[:, pl.ds(start, out_half)]
    lines = []
    for ref in vector_refs:
        vector = ref[...].astype(F32).reshape(ref.shape[0] // PAIR, PAIR)
        lines += [vector[n : n + 1] for n in range(ref.shape[0] // PAIR)]
    row = lax.broadcasted_iota(jnp.int32, (8, PAIR), 0)
    for n in range(6):
        block = jnp.where(row == 0, lines[n], jnp.where(row == 1, lines[n + 6], 0.0))
        first_ref[rows:, PAIR * n : PAIR * (n + 1)] = block.astype(BF16)


def own_qkv_blocks(qkv_weight, out_weight, vectors):
    rows, columns = qkv_weight.shape[0], qkv_weight.shape[1] // 4
    out_half = out_weight.shape[1] // 2
    return pl.pallas_call(
        own_kernel,
        in_specs=[pl.BlockSpec(memory_space=pltpu.VMEM)] * (2 + len(vectors)),
        out_specs=[pl.BlockSpec(memory_space=pltpu.VMEM)] * 2,
        out_shape=[
            jax.ShapeDtypeStruct((rows + 8, columns), BF16),
            jax.ShapeDtypeStruct((rows, columns + out_half), BF16),
        ],
        cost_estimate=SMALL_COST,
        name="own_qkv",
    )(qkv_weight, out_weight, *vectors)


def own_rest_kernel(fc1_ref, fc2_ref, first_ref, second_ref):
    core = lax.rem(lax.axis_index("seq"), 2)
    rows = second_ref.shape[0]
    for n in range(fc1_ref.shape[1] // (2 * rows)):
        start = pl.multiple_of((2 * n + core) * rows, rows)
        first_ref[:, n * rows : (n + 1) * rows] = fc1_ref[:, pl.ds(start, rows)]
    second_ref[...] = fc2_ref[pl.ds(pl.multiple_of(core * rows, rows), rows), :]


def own_rest_blocks(fc1_weight, fc2_weight):
    return pl.pallas_call(
        own_rest_kernel,
        in_specs=[pl.BlockSpec(memory_space=pltpu.VMEM)] * 2,
        out_specs=[pl.BlockSpec(memory_space=pltpu.VMEM)] * 2,
        out_shape=[
            jax.ShapeDtypeStruct((fc1_weight.shape[0], fc1_weight.shape[1] // 2), BF16),
            jax.ShapeDtypeStruct((fc2_weight.shape[0] // 2, fc2_weight.shape[1]), BF16),
        ],
        cost_estimate=SMALL_COST,
        name="own_rest",
    )(fc1_weight, fc2_weight)


def after(values, *others):
    return lax.optimization_barrier((values,) + others)[0] if others else values


class Gather:
    SOURCE = {4: 0, 2: 0, 1: 0, 6: 4, 3: 2, 5: 4, 7: 6}
    STEP = {4: 4, 2: 2, 1: 1, 6: 2, 3: 1, 5: 1, 7: 1}

    def __init__(self, own):
        self.pieces = [own] + [None] * 7
        self.grouped = lax.axis_size("fsdp") == 8

    def send(self, *parts, ready=()):
        if not self.grouped:
            return
        sources = [self.pieces[self.SOURCE[part]] for part in parts]
        if ready:
            sources = lax.optimization_barrier(tuple(sources) + tuple(ready))
        for part, source in zip(parts, sources):
            self.pieces[part] = swap_group(source, self.STEP[part])

    def got(self, *parts):
        return tuple(self.pieces[part] for part in parts) if self.grouped else ()

    def result(self):
        if not self.grouped:
            return lax.all_gather(self.pieces[0], "fsdp", axis=0, tiled=True)
        return in_order(self.pieces, self.pieces[0].shape[0])


def add_low(left, right):
    return (left.astype(F32) + right.astype(F32)).astype(BF16)


def split_kernel(full_ref, *refs):
    sems = refs[2]
    group = lax.axis_index("fsdp")
    rows = full_ref.shape[0] // 8
    copies = []
    for n in range(8):
        far, near, side = n % 2, (n // 2) % 2, n // 4
        start = pl.multiple_of((group ^ (4 * far + 2 * near + side)) * rows, rows)
        target = refs[side].at[pl.ds((n % 4) * rows, rows)]
        copies.append(
            pltpu.make_async_copy(full_ref.at[pl.ds(start, rows)], target, sems.at[n])
        )
    for copy in copies:
        copy.start()
    for copy in copies:
        copy.wait()


def split_blocks(values):
    rows, columns = values.shape
    return pl.pallas_call(
        split_kernel,
        in_specs=[pl.BlockSpec(memory_space=pltpu.VMEM)],
        out_specs=[pl.BlockSpec(memory_space=pl.ANY)] * 2,
        out_shape=[jax.ShapeDtypeStruct((rows // 2, columns), values.dtype)] * 2,
        scratch_shapes=[pltpu.SemaphoreType.DMA((8,))],
        compiler_params=pltpu.CompilerParams(vmem_limit_bytes=16 * 2**20),
        cost_estimate=SMALL_COST,
        name="split_blocks",
    )(values)


def pack_kernel(
    one_ref, two_ref, grads_ref, hidden_ref, end_ref, middle_ref, *refs
):
    sum_refs, packed_ref = refs[:4], refs[4]
    group = lax.axis_index("fsdp")
    core = lax.rem(lax.axis_index("seq"), 2)
    squares = jnp.zeros((4, PAIR), F32)
    for n in range(end_ref.shape[1] // PAIR):
        span = slice(n * PAIR, (n + 1) * PAIR)
        end, middle = end_ref[:, span], middle_ref[:, span]
        squares = squares + jnp.concatenate([end[:1], middle[:1], end[1:], middle[1:]], axis=0)
    for n in range(8):
        far, near, side = n % 2, (n // 2) % 2, n // 4
        target = group ^ (4 * far + 2 * near + side)
        columns = pl.ds(pl.multiple_of(target * PAIR, PAIR), PAIR)
        mine = (target // 4) == core
        pair = lax.rem(target, 4)
        head_sums = jnp.zeros((2, PAIR), F32)
        for k in range(4):
            head_sums = jnp.where(jnp.logical_and(mine, pair == k), sum_refs[k][...], head_sums)
        one, two = one_ref[:, columns], two_ref[:, columns]
        hidden = [
            hidden_ref[:, pl.ds(pl.multiple_of(target * 2 * PAIR + k * PAIR, PAIR), PAIR)]
            for k in range(2)
        ]
        empty = jnp.zeros((1, PAIR), F32)
        rows = [one[:2], head_sums, two[2:3], two[:2], grads_ref[:, columns]]
        rows += [jnp.where(core == 0, part, empty) for part in hidden]
        rows += [jnp.where(core == 0, empty, part) for part in hidden]
        rows.append(squares)
        packed_ref[16 * n : 16 * (n + 1), :] = jnp.concatenate(rows, axis=0).astype(BF16)


def pack_lines(lines, sums):
    return pl.pallas_call(
        pack_kernel,
        in_specs=[pl.BlockSpec(memory_space=pltpu.VMEM)] * 10,
        out_specs=pl.BlockSpec(memory_space=pltpu.VMEM),
        out_shape=jax.ShapeDtypeStruct((128, PAIR), BF16),
        cost_estimate=SMALL_COST,
        name="pack_lines",
    )(*lines, *sums)


class Scatter:
    def __init__(self, values, *ready, halves=None, ordered=False):
        self.grouped = lax.axis_size("fsdp") == 8
        self.halved = halves is not None
        values = values.astype(BF16)
        if self.halved:
            self.kept, self.sent = halves
            self.crossed = swap_chip(self.sent)
        elif self.grouped:
            middle = values.shape[0] // 2
            split = (values[:middle], values[middle:]) if ordered else split_blocks(values)
            self.keep, self.side_send = split
            self.side = swap_group(after(self.side_send, *ready), 1)
        else:
            self.sums = lax.psum_scatter(values, "fsdp", scatter_dimension=0, tiled=True)

    def cross(self, *ready):
        values = add_low(self.kept, after(self.crossed, *ready))
        if self.grouped:
            self.keep, self.side_send = split_blocks(values)
            self.side = swap_group(self.side_send, 1)
        else:
            self.sums = lax.psum_scatter(values, "fsdp", scatter_dimension=0, tiled=True)

    def got(self, *names):
        return tuple(getattr(self, name) for name in names if hasattr(self, name))

    def step(self, name, next_name, bit, ready):
        if self.grouped:
            received = after(getattr(self, name), *ready)
            half = self.keep.shape[0] // 2
            send = add_low(self.keep[half:], received[half:])
            self.keep = add_low(self.keep[:half], received[:half])
            setattr(self, next_name, swap_group(send, bit))

    def near(self, *ready):
        self.step("side", "near_sums", 2, ready)

    def far(self, *ready):
        self.step("near_sums", "far_sums", 4, ready)

    def chips(self, *ready):
        if self.grouped:
            self.sums = add_low(self.keep, after(self.far_sums, *ready))
        self.other_chip = swap_chip(self.sums)

    def cores(self, *ready):
        other_chip = after(self.other_chip, *ready)
        if self.halved:
            chip = lax.axis_index("seq") // 2
            first = jnp.where(chip == 0, self.sums, other_chip)
            second = jnp.where(chip == 0, other_chip, self.sums)
            self.total = jnp.concatenate([first, second], axis=1)
        else:
            self.total = add_low(self.sums, other_chip)
        self.other_core = swap_core(self.total)

    def last(self):
        if not self.grouped:
            return self.sums.astype(F32)
        return self.keep.astype(F32) + self.far_sums.astype(F32)


def take(values, index):
    return lax.dynamic_index_in_dim(values, index, 0, keepdims=False)


def in_core_order(own, other, core, axis):
    first = jnp.where(core == 0, own, other)
    second = jnp.where(core == 0, other, own)
    return first, second


def body(
    inputs,
    cotangent,
    valid,
    ln1_gain,
    ln1_bias,
    qkv_weight,
    q_bias,
    v_bias,
    out_weight,
    out_bias,
    ln2_gain,
    ln2_bias,
    fc1_weight,
    fc1_bias,
    fc2_weight,
    fc2_bias,
):
    clips, rows, width = inputs.shape
    groups = lax.axis_size("fsdp")
    place = lax.axis_index("seq")
    group = lax.axis_index("fsdp")
    chip, core = place // 2, place % 2
    half = width // 2
    hidden_rows = fc2_weight.shape[0]
    half_rows = hidden_rows // 2
    own_rows = clips * rows
    scale_factor = HEAD ** (-0.5)

    def all_clips(values, back):
        mine = values[:rows]
        first = jnp.where(chip == 0, mine, back)
        second = jnp.where(chip == 0, back, mine)
        return jnp.stack([first, second])

    own_width = width // groups
    vectors = (ln1_gain, ln1_bias, q_bias, v_bias, out_bias, ln2_gain, ln2_bias, fc2_bias, fc1_bias)
    quarter = half // 2
    row_width = 3 * quarter
    used = 8 * own_width + fc1_bias.shape[0]
    if groups == 8:
        own_first, own_second = own_qkv_blocks(qkv_weight, out_weight, vectors)
    else:
        by_head = qkv_weight.reshape(own_width, 3, 2, 2, 2, PAIR)
        by_head = lax.dynamic_index_in_dim(by_head, core, 2, keepdims=False)
        by_head = by_head.transpose(0, 2, 3, 1, 4).reshape(own_width, 2, row_width)
        out_columns = lax.dynamic_slice_in_dim(out_weight, core * half, half, 1)
        own_first = by_head[:, 0]
        own_second = jnp.concatenate([by_head[:, 1], out_columns], axis=1)

    qkv_a, qkv_b = Gather(own_first), Gather(own_second)
    qkv_a.send(4, 2, 1)
    other_inputs = swap_chip(take(after(inputs, *qkv_a.got(4, 2, 1)), 1 - chip))
    qkv_a.send(6, 3, 5, ready=qkv_a.got(4, 2, 1))
    qkv_b.send(4, ready=qkv_a.got(4, 2, 1))
    fc1_weight, fc2_weight = after((fc1_weight, fc2_weight), own_first)
    if groups == 8:
        own_fc1, own_fc2 = own_rest_blocks(fc1_weight, fc2_weight)
    else:
        own_fc1 = lax.dynamic_index_in_dim(
            fc1_weight.reshape(own_width, groups, 2, half_rows), core, 2, keepdims=False
        ).reshape(own_width, groups * half_rows)
        own_fc2 = lax.dynamic_slice_in_dim(fc2_weight, core * half_rows, half_rows, 0)
    full_fc1 = lax.all_gather(own_fc1, "fsdp", axis=0, tiled=True)
    full_fc2 = lax.all_gather(own_fc2, "fsdp", axis=0, tiled=True)
    qkv_a.send(7, ready=qkv_a.got(6, 3, 5))
    other_inputs = after(other_inputs, own_fc1, *qkv_a.got(6, 3, 5))
    qkv_b.send(2, 1, ready=qkv_a.got(6, 3, 5))
    own_inputs = jnp.concatenate([take(inputs, chip), other_inputs], axis=0)
    all_inputs = with_partner(own_inputs)
    if groups == 8:
        qkv_first, wide, bias_fc1 = in_order(qkv_a.pieces, own_width, True)
    else:
        qkv_first = qkv_a.result()
        packed = lax.all_gather(jnp.concatenate(vectors), "fsdp", axis=0)
        wide = [
            packed[:, i * own_width : (i + 1) * own_width].reshape(width).astype(F32)
            for i in range(8)
        ]
        bias_fc1 = packed[:, 8 * own_width : used].reshape(groups, 2, half_rows)
        bias_fc1 = take(jnp.moveaxis(bias_fc1, 1, 0), core)
        bias_fc1 = bias_fc1.reshape(groups * half_rows).astype(F32)
    gain_one, bias_one, bias_q, bias_v, bias_out, gain_two, bias_two, bias_fc2 = [
        wide[i] for i in range(8)
    ]
    bias_q = take(bias_q.reshape(2, 2, 2, PAIR), core)
    bias_v = take(bias_v.reshape(2, 2, 2, PAIR), core)
    bias_mixed = jnp.stack([bias_q, jnp.zeros_like(bias_q), bias_v], axis=2).reshape(2, row_width)
    scale_mixed = jnp.array([scale_factor, 1.0, 1.0] * 2, F32).repeat(PAIR)
    clip_valid = take(valid, chip).reshape(2 * clips, rows)
    own_valid = jnp.concatenate([take(clip_valid, place), take(clip_valid, place ^ 2)])
    other_valid = jnp.concatenate([take(clip_valid, place ^ 1), take(clip_valid, place ^ 3)])
    key_valid = jnp.concatenate([own_valid, other_valid])
    lane = jnp.arange(PAIR) % HEAD
    key_mask = jnp.where(key_valid > 0, 0.0, MASKED)[:, None]
    key_base = jnp.where(lane == 0, key_mask, jnp.where(lane < 4, 1.0, 0.0)).astype(BF16)


    def project(weight, i):
        return ((dot(h_one, weight) + bias_mixed[i]) * scale_mixed).astype(BF16)

    h_one = rows_call(
        first_kernel, [all_inputs], [gain_one[None], bias_one[None]], [BF16], 0, "first_norm"
    )[0]
    mixed = [project(qkv_first, 0)]
    context, queries = [], []

    def attend_pair(pair, *ready):
        before = context[-1] if context else None
        base = after(key_base, *ready)
        results = attend(mixed[pair // 2], base, pair % 2, before, pair, 4)
        context.append(results[0])
        queries.append(results[1])

    ready = (h_one,) + qkv_b.got(4, 2, 1)
    qkv_b.send(6, 3, 5, ready=ready)
    attend_pair(0, *ready)
    ready = (queries[0],) + qkv_b.got(6, 3, 5)
    qkv_b.send(7, ready=ready)
    other_grads = swap_chip(after(take(cotangent, 1 - chip), *ready))
    attend_pair(1, *ready)
    second_columns = qkv_b.result()
    mixed.append(project(second_columns[:, :row_width], 1))
    ready = (queries[1], mixed[1], other_grads)
    kept = lax.dynamic_slice(second_columns, (core * half, row_width), (half, half))
    received = lax.dynamic_slice(second_columns, ((1 - core) * half, row_width), (half, half))
    received = swap_core(after(received, mixed[1]))
    attend_pair(2, kept, *ready)
    ready = (queries[2], received)
    attend_pair(3, *ready)
    own_grads = jnp.concatenate([take(cotangent, chip), after(other_grads, queries[3])], axis=0)
    full_out = jnp.concatenate(in_core_order(kept, received, core, 1), axis=1)
    all_context = context[3]
    own_part, other_part = both_halves_product([(all_context, full_out)], NN)
    ready = (own_grads, own_part)
    counted = own_valid.astype(F32)[:, None]
    residual_mid, h_two, middle_sums = rows_call(
        middle_kernel,
        [own_part, after(other_part, *ready), own_inputs, counted],
        [bias_out[None], gain_two[None], bias_two[None]],
        [F32, BF16],
        2,
        "middle",
    )
    h_two = with_partner(h_two)
    all_grads = with_partner(after(own_grads, residual_mid))
    grad_sums = column_sum(own_grads)
    h_two = after(h_two, grad_sums)
    active, slope = gelu_both(dot(h_two, full_fc1) + bias_fc1)
    active, slope = active.astype(BF16), slope.astype(BF16)
    active = after(active, full_fc2)
    fc2_product = dot(active, all_grads, TN).astype(BF16)
    fc2_scatter = Scatter(fc2_product)

    late_grads = after(all_grads, *fc2_scatter.got("keep"))
    grad_hidden, hidden_sums = hidden_gradient(late_grads, full_fc2, slope)
    fc1_halves = weight_halves(h_two, grad_hidden)
    fc1_scatter = Scatter(fc1_halves[0], halves=fc1_halves)
    own_part, other_part = both_halves_product(
        [(after(grad_hidden, fc1_scatter.sent), full_fc1)], NT
    )
    grad_residual, own_grad_attn, two_sums = rows_call(
        norm_back_kernel,
        [own_part, other_part, residual_mid, own_grads],
        [gain_two[None]],
        [F32, BF16],
        3,
        "norm_back",
    )
    grad_attn = with_partner(own_grad_attn)
    grad_context = half_product([(grad_attn, full_out)], NT, None, BF16)
    halves, sums = [None, None], []

    def back_pair(pair, *ready):
        grad_mixed, parts = attend_back(
            queries[pair],
            mixed[pair // 2],
            grad_context,
            all_context,
            after(key_base, *ready),
            pair % 2,
            pair,
            halves[pair // 2],
        )
        halves[pair // 2] = grad_mixed
        sums.append(parts)

    back_pair(0, grad_context)
    ready = (sums[0], fc1_scatter.crossed) + fc2_scatter.got("side")
    grad_out = dot(all_context, after(grad_attn, *ready), TN).astype(BF16)
    kept = lax.dynamic_slice_in_dim(grad_out, core * half, half, 1)
    received = swap_core(lax.dynamic_slice_in_dim(grad_out, (1 - core) * half, half, 1))
    fc2_scatter.near(*ready)
    fc1_scatter.cross(*ready)
    back_pair(1, kept, *ready, *fc2_scatter.got("keep"), *fc1_scatter.got("keep"))
    received = after(received, sums[1])
    grad_out = jnp.concatenate(in_core_order(kept, received, core, 0), axis=0)
    early = jnp.concatenate([dot(h_one, halves[0], TN).astype(BF16), grad_out], axis=1)
    ready = (sums[1],) + fc2_scatter.got("near_sums") + fc1_scatter.got("side")
    fc2_scatter.far(*ready)
    fc1_scatter.near(*ready)
    early_scatter = Scatter(early, *ready)
    ready += fc2_scatter.got("keep") + fc1_scatter.got("keep") + early_scatter.got("keep")
    own_mlp, other_mlp = both_halves_product([(after(active, *ready), full_fc2)], NN)
    low_output, end_sums = rows_call(
        end_kernel,
        [own_mlp, other_mlp, residual_mid, counted],
        [bias_fc2[None]],
        [BF16],
        2,
        "end",
    )
    back_pair(2, low_output, *ready)
    output_back = swap_chip(low_output[rows:])
    ready = (sums[2], output_back) + fc2_scatter.got("far_sums") + fc1_scatter.got("near_sums")
    ready += early_scatter.got("side")
    fc2_scatter.chips(*ready)
    fc1_scatter.far(*ready)
    early_scatter.near(*ready)
    ready += (fc2_scatter.sums,) + fc1_scatter.got("keep") + early_scatter.got("keep")
    back_pair(3, *ready)
    ready = (sums[3], fc2_scatter.other_chip) + fc1_scatter.got("far_sums")
    ready += early_scatter.got("near_sums")
    early_scatter.far(*ready)
    fc1_scatter.chips(*ready)
    fc2_scatter.cores(*ready)
    late_scatter = Scatter(dot(after(h_one, *ready), halves[1], TN))
    gm_first, gm_second = after(tuple(halves), *late_scatter.got("keep"))
    own_one, other_one = both_halves_product(
        [(gm_first, qkv_first), (gm_second, second_columns)], NT
    )
    low_input_grad, one_sums = rows_call(
        norm_back_kernel,
        [own_one, other_one, own_inputs, grad_residual],
        [gain_one[None]],
        [BF16],
        3,
        "norm_back",
    )
    input_back = swap_chip(low_input_grad[rows:])
    ready = late_scatter.got("side") + (low_input_grad,)
    late_scatter.near(*ready)
    one_sums = after(one_sums, *ready)

    if groups == 8:
        packed = pack_lines(
            [one_sums, two_sums, grad_sums[None], hidden_sums, end_sums, middle_sums], sums
        )
    else:
        lines = [one_sums[0], one_sums[1], two_sums[2], two_sums[0], two_sums[1], grad_sums]
        lines.append(hidden_sums[0])
        squares = [end_sums[0], middle_sums[0], end_sums[1], middle_sums[1]]
        squares = [jnp.sum(line.reshape(-1, PAIR), axis=0) for line in squares]

        def by_core(values):
            full = jnp.zeros((2, values.shape[0]), F32)
            return lax.dynamic_update_index_in_dim(full, values, core, 0).reshape(-1)

        wide = lines[:2] + [by_core(jnp.concatenate([part[n] for part in sums])) for n in range(2)]
        wide = [line.reshape(groups, own_width) for line in wide + lines[2:6]]
        all_sums = jnp.zeros((groups, 2, half_rows), F32)
        all_sums = lax.dynamic_update_index_in_dim(
            all_sums, lines[6].reshape(groups, half_rows), core, 1
        )
        wide.append(all_sums.reshape(groups, hidden_rows))
        wide.append(jnp.zeros((groups, 12 * PAIR - used)))
        wide.append(jnp.broadcast_to(jnp.concatenate(squares), (groups, 4 * PAIR)))
        packed = jnp.concatenate(wide, axis=1).astype(BF16).reshape(groups * 16, PAIR)
    ready = early_scatter.got("far_sums") + (fc1_scatter.other_chip,)
    packed = add_low(packed, after(swap_chip(packed), *ready))
    early_scatter.chips(packed)
    fc1_scatter.cores(packed)
    ready = late_scatter.got("near_sums")
    packed = add_low(packed, after(swap_core(packed), *ready))
    late_scatter.far(packed)
    vector_scatter = Scatter(packed, ordered=True)
    vector_scatter.near(early_scatter.other_chip)
    early_scatter.cores(*vector_scatter.got("keep"))
    ready = late_scatter.got("far_sums") + (input_back,)
    vector_scatter.far(*ready)
    late_scatter.chips(*vector_scatter.got("keep"))
    late_scatter.cores()
    ready_last = (packed,)
    output = all_clips(low_output, after(output_back, packed))
    input_grad = all_clips(low_input_grad, input_back)

    def in_columns(values, other, blocks):
        size = values.shape[1] // blocks
        parts = in_core_order(values, other, core, 0)
        parts = [part.reshape(own_width, blocks, 1, size) for part in parts]
        return jnp.concatenate(parts, axis=2).reshape(own_width, -1).astype(F32)

    fc2_parts = after((fc2_scatter.total, fc2_scatter.other_core), *ready_last)
    fc2_grad = in_core_order(*fc2_parts, core, 0)
    fc2_grad = jnp.concatenate(fc2_grad, axis=0).astype(F32)
    early_parts = [early_scatter.total, early_scatter.other_core]
    late_parts = [late_scatter.total, late_scatter.other_core]
    fc1_parts = after((fc1_scatter.total, fc1_scatter.other_core), *ready_last)
    if groups == 8:
        fc1_places = [
            (0, n * half_rows, half_rows, 2 * n * half_rows, (2 * n + 1) * half_rows)
            for n in range(groups)
        ]
        fc1_grad = join_columns(fc1_parts, fc1_places, 2 * groups * half_rows)
        out_grad = join_columns(early_parts, [(0, row_width, half, 0, half)], width)
        qkv_places = []
        for n in range(3):
            for pair in range(4):
                target = n * width + pair * PAIR
                start = (3 * (pair % 2) + n) * PAIR
                qkv_places.append((pair // 2, start, PAIR, target, target + half))
        qkv_grad = join_columns(early_parts + late_parts, qkv_places, 3 * width)
    else:
        fc1_grad = in_columns(*fc1_parts, groups)
        out_grad = in_columns(*[part[:, row_width:] for part in early_parts], 1)

        def both_halves(left, right):
            left = left[:, :row_width].reshape(own_width, 1, 2, 3, PAIR)
            right = right.reshape(own_width, 1, 2, 3, PAIR)
            both = jnp.concatenate([left, right], axis=1).transpose(0, 3, 1, 2, 4)
            return both.reshape(own_width, 3 * half)

        qkv_grad = in_columns(*[both_halves(*pair) for pair in zip(early_parts, late_parts)], 3)
    lines = vector_scatter.last()
    flat = lines[:12].reshape(-1)
    own_vectors = [flat[i * own_width : (i + 1) * own_width] for i in range(8)]
    own_hidden = flat[8 * own_width : used]
    totals = jnp.sum(lines[12:], axis=1)
    branch_rms = jnp.sqrt(totals[:3] / totals[3])
    return (
        output,
        input_grad,
        own_vectors[0],
        own_vectors[1],
        qkv_grad,
        own_vectors[2],
        own_vectors[3],
        out_grad,
        own_vectors[4],
        own_vectors[5],
        own_vectors[6],
        fc1_grad,
        own_hidden,
        fc2_grad,
        own_vectors[7],
        branch_rms,
    )


def solution(mesh):
    tokens, rows, vector = P("fsdp", "seq", None), P("fsdp", None), P("fsdp")
    return jax.shard_map(
        body,
        mesh=mesh,
        in_specs=(
            tokens,
            tokens,
            rows,
            vector,
            vector,
            rows,
            vector,
            vector,
            rows,
            vector,
            vector,
            vector,
            rows,
            vector,
            rows,
            vector,
        ),
        out_specs=(
            tokens,
            tokens,
            vector,
            vector,
            rows,
            vector,
            vector,
            rows,
            vector,
            vector,
            vector,
            rows,
            vector,
            rows,
            vector,
            P(),
        ),
        check_vma=False,
    )
```

```python
from functools import partial

import jax
import jax.numpy as jnp
from jax import lax
from jax.experimental import pallas as pl
from jax.experimental.pallas import tpu as pltpu
from jax.sharding import PartitionSpec as P

HEADS = 16
HEAD = 64
PAIR = 2 * HEAD
EPS = 1e-06
MASKED = -1e30
VMEM_BYTES = 28 * 2**20
BF16 = jnp.bfloat16
F32 = jnp.float32
NN = (((1,), (0,)), ((), ()))
NT = (((1,), (1,)), ((), ()))
TN = (((0,), (0,)), ((), ()))
SMALL_COST = pl.CostEstimate(flops=10**7, bytes_accessed=2**20, transcendentals=0)


def dot(left, right, dims=NN):
    return lax.dot_general(left, right, dims, preferred_element_type=F32)


def lanes_of(shape):
    return lax.broadcasted_iota(jnp.int32, shape, len(shape) - 1)


def three_parts(column):
    high = column.astype(BF16).astype(F32)
    rest = column - high
    middle = rest.astype(BF16).astype(F32)
    return high, middle, rest - middle


def block_rows(length, *sizes):
    for rows in sizes + (224, 112, 16):
        if length % rows == 0:
            return rows
    return length


def attend_kernel(q_ref, k_ref, v_ref, key_base_ref, *refs):
    context_ref, query_ref = refs[-2:]
    length = q_ref.shape[0]
    rows = block_rows(length, 392)
    low = lanes_of((length, PAIR)) < HEAD
    keys, values, key_base = k_ref[...], v_ref[...], key_base_ref[...]
    ones = jnp.ones((length, PAIR), BF16)
    keys_of = [jnp.where(low, keys, key_base), jnp.where(low, key_base, keys)]
    values_of = [jnp.where(low, values, ones), jnp.where(low, ones, values)]
    lane = lanes_of((rows, PAIR))
    low_rows = lane < HEAD
    for step in range(length // rows):
        span = slice(step * rows, (step + 1) * rows)
        queries = q_ref[span, :]
        results = []
        for head in range(2):
            base = HEAD * (1 - head)
            own = low_rows if head == 0 else jnp.logical_not(low_rows)
            unit = jnp.where(lane == base, 1.0, 0.0)
            scores = dot(jnp.where(own, queries, unit.astype(BF16)), keys_of[head], NT)
            highest = jnp.max(scores, axis=1, keepdims=True)
            weights = jnp.exp(scores - highest).astype(BF16)
            mixed = dot(weights, values_of[head])
            total = mixed[:, base : base + 1]
            high, middle, rest = three_parts(-(highest + jnp.log(total)))
            extra = jnp.where(lane == base + 3, rest, unit)
            extra = jnp.where(lane == base + 2, middle, extra)
            extra = jnp.where(lane == base + 1, high, extra)
            query_ref[head, span, :] = jnp.where(own, queries, extra.astype(BF16))
            results.append(mixed / total)
        context_ref[span, :] = jnp.where(low_rows, results[0], results[1]).astype(BF16)


def attend(mixed, key_base, pair, context, place, places):
    length = mixed.shape[0]
    tile = lambda column: pl.BlockSpec((length, PAIR), lambda i: (0, column))
    in_specs = [tile(3 * pair), tile(3 * pair + 1), tile(3 * pair + 2), tile(0)]
    operands = (mixed, mixed, mixed, key_base)
    aliases = {}
    if context is not None:
        in_specs.append(pl.BlockSpec(memory_space=pl.ANY))
        operands += (context,)
        aliases = {4: 0}
    return pl.pallas_call(
        attend_kernel,
        grid=(1,),
        in_specs=in_specs,
        out_specs=[tile(place), pl.BlockSpec((2, length, PAIR), lambda i: (0, 0, 0))],
        out_shape=[
            jax.ShapeDtypeStruct((length, places * PAIR), BF16),
            jax.ShapeDtypeStruct((2, length, PAIR), BF16),
        ],
        input_output_aliases=aliases,
        compiler_params=pltpu.CompilerParams(vmem_limit_bytes=VMEM_BYTES),
        cost_estimate=SMALL_COST,
        name="attend",
    )(*operands)


def attend_back_kernel(query_ref, k_ref, v_ref, grad_ref, context_ref, key_base_ref, *refs):
    grad_mixed_ref, sums_ref = refs[-2:]
    length = k_ref.shape[0]
    rows = block_rows(length)
    low = lanes_of((length, PAIR)) < HEAD
    keys, values, key_base = k_ref[...], v_ref[...], key_base_ref[...]
    ones = jnp.ones((length, PAIR), BF16)
    lane = lanes_of((rows, PAIR))
    low_rows = lane < HEAD
    steps = length // rows
    grad_q, grad_k, grad_v = [], [], []
    sum_q = jnp.zeros((1, PAIR), F32)
    for head in range(2):
        base = HEAD * (1 - head)
        own = low if head == 0 else jnp.logical_not(low)
        own_rows = low_rows if head == 0 else jnp.logical_not(low_rows)
        head_keys = jnp.where(own, keys, key_base)
        head_values = jnp.where(own, values, ones)
        sum_k = jnp.zeros((length, PAIR), F32)
        sum_v = jnp.zeros((length, PAIR), F32)
        for step in range(steps):
            span = slice(step * rows, (step + 1) * rows)
            queries = query_ref[head, span, :]
            grads = grad_ref[span, :]
            product = grads.astype(F32) * context_ref[span, :].astype(F32)
            inner = jnp.sum(jnp.where(own_rows, product, 0.0), axis=1, keepdims=True)
            high, middle, rest = three_parts(-inner)
            extra = jnp.where(lane == base + 2, rest, 0.0)
            extra = jnp.where(lane == base + 1, middle, extra)
            extra = jnp.where(lane == base, high, extra)
            head_grads = jnp.where(own_rows, grads, extra.astype(BF16))
            probs = jnp.exp(dot(head_keys, queries, NT))
            grad_scores = (probs * dot(head_values, head_grads, NT)).astype(BF16)
            sum_v = sum_v + dot(probs.astype(BF16), grads)
            sum_k = sum_k + dot(grad_scores, queries)
            part = dot(grad_scores, keys, TN)
            if head == 0:
                grad_q.append(part)
            else:
                both = jnp.where(low_rows, grad_q[step], part).astype(BF16)
                both = both * (HEAD ** (-0.5))
                grad_mixed_ref[span, :PAIR] = both
                sum_q = sum_q + jnp.sum(both.astype(F32), axis=0, keepdims=True)
        grad_k.append(sum_k)
        grad_v.append(sum_v)
    grad_mixed_ref[:, PAIR : 2 * PAIR] = jnp.where(low, grad_k[0], grad_k[1]).astype(BF16)
    both = jnp.where(low, grad_v[0], grad_v[1]).astype(BF16)
    grad_mixed_ref[:, 2 * PAIR :] = both
    sums_ref[0:1, :] = sum_q
    sums_ref[1:2, :] = jnp.sum(both.astype(F32), axis=0, keepdims=True)


def attend_back(queries, mixed, grad_context, context, key_base, pair, place, grad_mixed):
    length = mixed.shape[0]
    tile = lambda column: pl.BlockSpec((length, PAIR), lambda i: (0, column))
    in_specs = [
        pl.BlockSpec((2, length, PAIR), lambda i: (0, 0, 0)),
        tile(3 * pair + 1),
        tile(3 * pair + 2),
        tile(place),
        tile(place),
        tile(0),
    ]
    operands = (queries, mixed, mixed, grad_context, context, key_base)
    aliases = {}
    if grad_mixed is not None:
        in_specs.append(pl.BlockSpec(memory_space=pl.ANY))
        operands += (grad_mixed,)
        aliases = {6: 0}
    return pl.pallas_call(
        attend_back_kernel,
        grid=(1,),
        in_specs=in_specs,
        out_specs=[
            pl.BlockSpec((length, 3 * PAIR), lambda i: (0, pair)),
            pl.BlockSpec((2, PAIR), lambda i: (0, 0)),
        ],
        out_shape=[
            jax.ShapeDtypeStruct((length, 6 * PAIR), BF16),
            jax.ShapeDtypeStruct((2, PAIR), F32),
        ],
        input_output_aliases=aliases,
        compiler_params=pltpu.CompilerParams(vmem_limit_bytes=VMEM_BYTES),
        cost_estimate=SMALL_COST,
        name="attend_back",
    )(*operands)


def normalize(values):
    center = values - jnp.mean(values, axis=-1, keepdims=True)
    spread = jnp.mean(center * center, axis=-1, keepdims=True)
    scale = lax.rsqrt(spread + EPS)
    return center * scale, scale


def rows_call(kernel, row_inputs, constants, kinds, sum_rows, name):
    rows, width = row_inputs[0].shape
    tile = rows // 7 if rows % 112 == 0 else rows
    block = lambda columns: pl.BlockSpec((tile, columns), lambda i: (i, 0))
    whole = lambda shape: pl.BlockSpec(shape, lambda i: (0, 0))
    out_specs = [block(width)] * len(kinds)
    out_shape = [jax.ShapeDtypeStruct((rows, width), kind) for kind in kinds]
    if sum_rows:
        out_specs.append(whole((sum_rows, width)))
        out_shape.append(jax.ShapeDtypeStruct((sum_rows, width), F32))
    return pl.pallas_call(
        kernel,
        grid=(rows // tile,),
        in_specs=[block(part.shape[1]) for part in row_inputs]
        + [whole(part.shape) for part in constants],
        out_specs=out_specs,
        out_shape=out_shape,
        compiler_params=pltpu.CompilerParams(vmem_limit_bytes=VMEM_BYTES),
        cost_estimate=SMALL_COST,
        name=name,
    )(*row_inputs, *constants)


def add_rows(sums_ref, parts):
    @pl.when(pl.program_id(0) == 0)
    def _():
        sums_ref[...] = jnp.zeros(sums_ref.shape, F32)

    lines = [jnp.sum(part, axis=0, keepdims=True) for part in parts]
    sums_ref[...] += jnp.concatenate(lines, axis=0)


def first_kernel(values_ref, gain_ref, bias_ref, out_ref):
    normal = normalize(values_ref[...].astype(F32))[0]
    out_ref[...] = (normal * gain_ref[...] + bias_ref[...]).astype(BF16)


def middle_kernel(
    own_ref, other_ref, inputs_ref, counted_ref, out_bias_ref, gain_ref, bias_ref, *out_refs
):
    middle_ref, low_ref, sums_ref = out_refs
    branch = own_ref[...] + other_ref[...].astype(F32) + out_bias_ref[...]
    middle = inputs_ref[...].astype(F32) + branch
    middle_ref[...] = middle
    low_ref[...] = (normalize(middle)[0] * gain_ref[...] + bias_ref[...]).astype(BF16)
    counted = counted_ref[...]
    add_rows(sums_ref, [counted * branch * branch, jnp.broadcast_to(counted, branch.shape)])


def end_kernel(own_ref, other_ref, middle_ref, counted_ref, bias_ref, low_ref, sums_ref):
    branch = own_ref[...] + other_ref[...].astype(F32) + bias_ref[...]
    result = middle_ref[...] + branch
    low_ref[...] = result.astype(BF16)
    counted = counted_ref[...]
    add_rows(sums_ref, [counted * result * result, counted * branch * branch])


def norm_back_kernel(own_ref, other_ref, values_ref, residual_ref, gain_ref, *out_refs):
    grad = own_ref[...] + other_ref[...].astype(F32)
    normal, scale = normalize(values_ref[...].astype(F32))
    inner = grad * gain_ref[...]
    first = jnp.mean(inner, axis=-1, keepdims=True)
    second = jnp.mean(inner * normal, axis=-1, keepdims=True)
    total = residual_ref[...].astype(F32) + scale * (inner - first - normal * second)
    low = total.astype(BF16)
    if len(out_refs) == 3:
        out_refs[0][...] = total
    out_refs[-2][...] = low
    add_rows(out_refs[-1], [grad * normal, grad, low.astype(F32)])


def weight_kernel(left_ref, right_ref, kept_ref, sent_ref):
    chip = lax.axis_index("seq") // 2
    left, half = left_ref[...], kept_ref.shape[1]
    for part, out_ref in ((chip, kept_ref), (1 - chip, sent_ref)):
        columns = pl.ds(pl.multiple_of(part * half, half), half)
        out_ref[...] = dot(left, right_ref[:, columns], TN).astype(BF16)


def weight_halves(left, right):
    rows, depth = left.shape
    columns = right.shape[1]
    tile = min(depth, 512)
    half = pl.BlockSpec((tile, columns // 2), lambda i: (i, 0))
    return pl.pallas_call(
        weight_kernel,
        grid=(depth // tile,),
        in_specs=[
            pl.BlockSpec((rows, tile), lambda i: (0, i)),
            pl.BlockSpec((rows, columns), lambda i: (0, 0)),
        ],
        out_specs=[half, half],
        out_shape=[jax.ShapeDtypeStruct((depth, columns // 2), BF16)] * 2,
        compiler_params=pltpu.CompilerParams(vmem_limit_bytes=VMEM_BYTES),
        cost_estimate=SMALL_COST,
        name="weight_halves",
    )(left, right)


def gelu_both(values):
    half = 0.5 * (1.0 + lax.erf(values * (0.5**0.5)))
    density = jnp.exp(-0.5 * values * values) * (0.5 / jnp.pi) ** 0.5
    return values * half, half + values * density


def hidden_kernel(grad_ref, weight_ref, slope_ref, hidden_ref, sums_ref):
    rows = grad_ref.shape[0] // 2
    weight = weight_ref[...]
    total = jnp.zeros((1, weight.shape[0]), F32)
    for span in (slice(0, rows), slice(rows, 2 * rows)):
        hidden = (dot(grad_ref[span, :], weight, NT) * slope_ref[span, :].astype(F32)).astype(BF16)
        hidden_ref[span, :] = hidden
        total = total + jnp.sum(hidden.astype(F32), axis=0, keepdims=True)
    sums_ref[...] = total


def hidden_gradient(grads, weight, slope):
    rows, depth = grads.shape
    columns = weight.shape[0]
    tile = min(columns, 512)
    block = pl.BlockSpec((rows, tile), lambda i: (0, i))
    return pl.pallas_call(
        hidden_kernel,
        grid=(columns // tile,),
        in_specs=[
            pl.BlockSpec((rows, depth), lambda i: (0, 0)),
            pl.BlockSpec((tile, depth), lambda i: (i, 0)),
            block,
        ],
        out_specs=[block, pl.BlockSpec((1, tile), lambda i: (0, i))],
        out_shape=[
            jax.ShapeDtypeStruct((rows, columns), BF16),
            jax.ShapeDtypeStruct((1, columns), F32),
        ],
        compiler_params=pltpu.CompilerParams(vmem_limit_bytes=VMEM_BYTES),
        cost_estimate=SMALL_COST,
        name="hidden_gradient",
    )(grads, weight, slope)


def half_kernel(dims, *refs):
    total = dot(refs[0][...], refs[1][...], dims)
    for n in range(2, len(refs) - 1, 2):
        total = total + dot(refs[n][...], refs[n + 1][...], dims)
    refs[-1][...] = total.astype(refs[-1].dtype)


def half_product(pairs, dims, part, kind):
    rows = pairs[0][0].shape[0] if part is None else pairs[0][0].shape[0] // 2
    part = part or 0
    columns = pairs[0][1].shape[1 if dims is NN else 0]
    tile = min(columns, 512)
    in_specs, operands = [], []
    for left, right in pairs:
        depth = left.shape[1]
        in_specs.append(pl.BlockSpec((rows, depth), lambda i: (part, 0)))
        if dims is NN:
            in_specs.append(pl.BlockSpec((depth, tile), lambda i: (0, i)))
        else:
            in_specs.append(pl.BlockSpec((tile, depth), lambda i: (i, 0)))
        operands += [left, right]
    return pl.pallas_call(
        partial(half_kernel, dims),
        grid=(columns // tile,),
        in_specs=in_specs,
        out_specs=pl.BlockSpec((rows, tile), lambda i: (0, i)),
        out_shape=jax.ShapeDtypeStruct((rows, columns), kind),
        compiler_params=pltpu.CompilerParams(vmem_limit_bytes=VMEM_BYTES),
        cost_estimate=SMALL_COST,
        name="half_product",
    )(*operands)


def both_halves_product(pairs, dims):
    other = half_product(pairs, dims, 1, BF16)
    own = [(after(left, other), right) for left, right in pairs]
    return half_product(own, dims, 0, F32), swap_core(other)


def join_kernel(places, *refs):
    out_ref = refs[-1]
    core = lax.rem(lax.axis_index("seq"), 2)
    for n, (source, start, width, first, second) in enumerate(places):
        for other in range(2):
            target = pl.multiple_of(jnp.where(core == other, first, second), PAIR)
            block = refs[2 * source + other][:, start : start + width]
            out_ref[:, pl.ds(target, width)] = block.astype(F32)


def join_columns(parts, places, columns):
    rows = parts[0].shape[0]
    return pl.pallas_call(
        partial(join_kernel, places),
        in_specs=[pl.BlockSpec(memory_space=pltpu.VMEM)] * len(parts),
        out_specs=pl.BlockSpec(memory_space=pltpu.VMEM),
        out_shape=jax.ShapeDtypeStruct((rows, columns), F32),
        cost_estimate=SMALL_COST,
        name="join_columns",
    )(*parts)


def column_sum(values):
    return jnp.sum(values, axis=0, dtype=F32)


def swap_core(values):
    return lax.ppermute(values, "seq", [(0, 1), (1, 0), (2, 3), (3, 2)])


def swap_chip(values):
    return lax.ppermute(values, "seq", [(0, 2), (2, 0), (1, 3), (3, 1)])


def stack_kernel(own_ref, other_ref, out_ref, sems):
    rows = own_ref.shape[0]
    copies = [
        pltpu.make_async_copy(ref, out_ref.at[pl.ds(n * rows, rows)], sems.at[n])
        for n, ref in enumerate((own_ref, other_ref))
    ]
    for copy in copies:
        copy.start()
    for copy in copies:
        copy.wait()


def with_partner(values):
    rows, columns = values.shape
    return pl.pallas_call(
        stack_kernel,
        in_specs=[pl.BlockSpec(memory_space=pltpu.VMEM)] * 2,
        out_specs=pl.BlockSpec(memory_space=pl.ANY),
        out_shape=jax.ShapeDtypeStruct((2 * rows, columns), values.dtype),
        scratch_shapes=[pltpu.SemaphoreType.DMA((2,))],
        compiler_params=pltpu.CompilerParams(vmem_limit_bytes=16 * 2**20),
        cost_estimate=SMALL_COST,
        name="stack_rows",
    )(values, swap_core(values))


def swap_group(values, bit):
    return lax.ppermute(values, "fsdp", [(i, i ^ bit) for i in range(8)])


def order_kernel(count, *refs):
    pieces, full_ref, held, arrived, sent = refs[:count], refs[count], *refs[-3:]
    group = lax.axis_index("fsdp")
    rows = full_ref.shape[0] // count
    loads = [
        pltpu.make_async_copy(piece, held.at[relative], arrived.at[relative])
        for relative, piece in enumerate(pieces)
    ]
    for load in loads:
        load.start()
    stores = []
    for relative in range(count):
        start = pl.multiple_of((group ^ relative) * rows, rows)
        store = pltpu.make_async_copy(
            held.at[relative, pl.ds(0, rows)], full_ref.at[pl.ds(start, rows)], sent.at[relative]
        )
        loads[relative].wait()
        store.start()
        stores.append(store)
    if len(refs) > count + 4:
        own_width, core = 128, lax.rem(lax.axis_index("seq"), 2)
        wide_ref, bias_ref = refs[count + 1], refs[count + 2]
        for relative in range(count):
            place = group ^ relative
            columns = pl.ds(pl.multiple_of(place * own_width, own_width), own_width)
            extra = held[relative, rows : rows + 8, :].astype(F32)
            lines = [
                extra[k : k + 1, own_width * n : own_width * (n + 1)]
                for k in range(2)
                for n in range(6)
            ]
            for n in range(8):
                wide_ref[n : n + 1, columns] = lines[n]
            for n in range(2):
                start = pl.multiple_of((place * 2 + n) * own_width, own_width)
                bias_ref[:, pl.ds(start, own_width)] = jnp.where(
                    core == 0, lines[8 + n], lines[10 + n]
                )
    for store in stores:
        store.wait()


def in_order(pieces, rows, with_vectors=False):
    count, columns = len(pieces), pieces[0].shape[1]
    out_specs = [pl.BlockSpec(memory_space=pl.ANY)]
    out_shape = [jax.ShapeDtypeStruct((count * rows, columns), pieces[0].dtype)]
    if with_vectors:
        out_specs += [pl.BlockSpec(memory_space=pltpu.VMEM)] * 2
        out_shape += [jax.ShapeDtypeStruct((8, 1024), F32), jax.ShapeDtypeStruct((1, 2048), F32)]
    result = pl.pallas_call(
        partial(order_kernel, count),
        in_specs=[pl.BlockSpec(memory_space=pl.ANY)] * count,
        out_specs=out_specs,
        out_shape=out_shape,
        scratch_shapes=[
            pltpu.VMEM((count,) + pieces[0].shape, pieces[0].dtype),
            pltpu.SemaphoreType.DMA((count,)),
            pltpu.SemaphoreType.DMA((count,)),
        ],
        compiler_params=pltpu.CompilerParams(vmem_limit_bytes=16 * 2**20),
        cost_estimate=SMALL_COST,
        name="in_order",
    )(*pieces)
    return result if with_vectors else result[0]


def own_kernel(qkv_ref, out_ref, *refs):
    vector_refs, (first_ref, second_ref) = refs[:-2], refs[-2:]
    core = lax.rem(lax.axis_index("seq"), 2)
    rows = qkv_ref.shape[0]
    for n in range(3):
        for pair in range(4):
            block_ref = second_ref if pair >= 2 else first_ref
            start = pl.multiple_of((8 * n + pair + 4 * core) * PAIR, PAIR)
            target = (3 * (pair % 2) + n) * PAIR
            block_ref[:rows, target : target + PAIR] = qkv_ref[:, pl.ds(start, PAIR)]
    out_half = out_ref.shape[1] // 2
    start = pl.multiple_of(core * out_half, out_half)
    second_ref[:, 6 * PAIR :] = out_ref[:, pl.ds(start, out_half)]
    lines = []
    for ref in vector_refs:
        vector = ref[...].astype(F32).reshape(ref.shape[0] // PAIR, PAIR)
        lines += [vector[n : n + 1] for n in range(ref.shape[0] // PAIR)]
    row = lax.broadcasted_iota(jnp.int32, (8, PAIR), 0)
    for n in range(6):
        block = jnp.where(row == 0, lines[n], jnp.where(row == 1, lines[n + 6], 0.0))
        first_ref[rows:, PAIR * n : PAIR * (n + 1)] = block.astype(BF16)


def own_qkv_blocks(qkv_weight, out_weight, vectors):
    rows, columns = qkv_weight.shape[0], qkv_weight.shape[1] // 4
    out_half = out_weight.shape[1] // 2
    return pl.pallas_call(
        own_kernel,
        in_specs=[pl.BlockSpec(memory_space=pltpu.VMEM)] * (2 + len(vectors)),
        out_specs=[pl.BlockSpec(memory_space=pltpu.VMEM)] * 2,
        out_shape=[
            jax.ShapeDtypeStruct((rows + 8, columns), BF16),
            jax.ShapeDtypeStruct((rows, columns + out_half), BF16),
        ],
        cost_estimate=SMALL_COST,
        name="own_qkv",
    )(qkv_weight, out_weight, *vectors)


def own_rest_kernel(fc1_ref, fc2_ref, first_ref, second_ref):
    core = lax.rem(lax.axis_index("seq"), 2)
    rows = second_ref.shape[0]
    for n in range(fc1_ref.shape[1] // (2 * rows)):
        start = pl.multiple_of((2 * n + core) * rows, rows)
        first_ref[:, n * rows : (n + 1) * rows] = fc1_ref[:, pl.ds(start, rows)]
    second_ref[...] = fc2_ref[pl.ds(pl.multiple_of(core * rows, rows), rows), :]


def own_rest_blocks(fc1_weight, fc2_weight):
    return pl.pallas_call(
        own_rest_kernel,
        in_specs=[pl.BlockSpec(memory_space=pltpu.VMEM)] * 2,
        out_specs=[pl.BlockSpec(memory_space=pltpu.VMEM)] * 2,
        out_shape=[
            jax.ShapeDtypeStruct((fc1_weight.shape[0], fc1_weight.shape[1] // 2), BF16),
            jax.ShapeDtypeStruct((fc2_weight.shape[0] // 2, fc2_weight.shape[1]), BF16),
        ],
        cost_estimate=SMALL_COST,
        name="own_rest",
    )(fc1_weight, fc2_weight)


def after(values, *others):
    return lax.optimization_barrier((values,) + others)[0] if others else values


class Gather:
    SOURCE = {4: 0, 2: 0, 1: 0, 6: 4, 3: 2, 5: 4, 7: 6}
    STEP = {4: 4, 2: 2, 1: 1, 6: 2, 3: 1, 5: 1, 7: 1}

    def __init__(self, own):
        self.pieces = [own] + [None] * 7
        self.grouped = lax.axis_size("fsdp") == 8

    def send(self, *parts, ready=()):
        if not self.grouped:
            return
        sources = [self.pieces[self.SOURCE[part]] for part in parts]
        if ready:
            sources = lax.optimization_barrier(tuple(sources) + tuple(ready))
        for part, source in zip(parts, sources):
            self.pieces[part] = swap_group(source, self.STEP[part])

    def got(self, *parts):
        return tuple(self.pieces[part] for part in parts) if self.grouped else ()

    def result(self):
        if not self.grouped:
            return lax.all_gather(self.pieces[0], "fsdp", axis=0, tiled=True)
        return in_order(self.pieces, self.pieces[0].shape[0])


def add_low(left, right):
    return (left.astype(F32) + right.astype(F32)).astype(BF16)


def split_kernel(full_ref, *refs):
    sems = refs[2]
    group = lax.axis_index("fsdp")
    rows = full_ref.shape[0] // 8
    copies = []
    for n in range(8):
        far, near, side = n % 2, (n // 2) % 2, n // 4
        start = pl.multiple_of((group ^ (4 * far + 2 * near + side)) * rows, rows)
        target = refs[side].at[pl.ds((n % 4) * rows, rows)]
        copies.append(
            pltpu.make_async_copy(full_ref.at[pl.ds(start, rows)], target, sems.at[n])
        )
    for copy in copies:
        copy.start()
    for copy in copies:
        copy.wait()


def split_blocks(values):
    rows, columns = values.shape
    return pl.pallas_call(
        split_kernel,
        in_specs=[pl.BlockSpec(memory_space=pltpu.VMEM)],
        out_specs=[pl.BlockSpec(memory_space=pl.ANY)] * 2,
        out_shape=[jax.ShapeDtypeStruct((rows // 2, columns), values.dtype)] * 2,
        scratch_shapes=[pltpu.SemaphoreType.DMA((8,))],
        compiler_params=pltpu.CompilerParams(vmem_limit_bytes=16 * 2**20),
        cost_estimate=SMALL_COST,
        name="split_blocks",
    )(values)


def pack_kernel(
    one_ref, two_ref, grads_ref, hidden_ref, end_ref, middle_ref, *refs
):
    sum_refs, packed_ref = refs[:4], refs[4]
    group = lax.axis_index("fsdp")
    core = lax.rem(lax.axis_index("seq"), 2)
    squares = jnp.zeros((4, PAIR), F32)
    for n in range(end_ref.shape[1] // PAIR):
        span = slice(n * PAIR, (n + 1) * PAIR)
        end, middle = end_ref[:, span], middle_ref[:, span]
        squares = squares + jnp.concatenate([end[:1], middle[:1], end[1:], middle[1:]], axis=0)
    for n in range(8):
        far, near, side = n % 2, (n // 2) % 2, n // 4
        target = group ^ (4 * far + 2 * near + side)
        columns = pl.ds(pl.multiple_of(target * PAIR, PAIR), PAIR)
        mine = (target // 4) == core
        pair = lax.rem(target, 4)
        head_sums = jnp.zeros((2, PAIR), F32)
        for k in range(4):
            head_sums = jnp.where(jnp.logical_and(mine, pair == k), sum_refs[k][...], head_sums)
        one, two = one_ref[:, columns], two_ref[:, columns]
        hidden = [
            hidden_ref[:, pl.ds(pl.multiple_of(target * 2 * PAIR + k * PAIR, PAIR), PAIR)]
            for k in range(2)
        ]
        empty = jnp.zeros((1, PAIR), F32)
        rows = [one[:2], head_sums, two[2:3], two[:2], grads_ref[:, columns]]
        rows += [jnp.where(core == 0, part, empty) for part in hidden]
        rows += [jnp.where(core == 0, empty, part) for part in hidden]
        rows.append(squares)
        packed_ref[16 * n : 16 * (n + 1), :] = jnp.concatenate(rows, axis=0).astype(BF16)


def pack_lines(lines, sums):
    return pl.pallas_call(
        pack_kernel,
        in_specs=[pl.BlockSpec(memory_space=pltpu.VMEM)] * 10,
        out_specs=pl.BlockSpec(memory_space=pltpu.VMEM),
        out_shape=jax.ShapeDtypeStruct((128, PAIR), BF16),
        cost_estimate=SMALL_COST,
        name="pack_lines",
    )(*lines, *sums)


class Scatter:
    def __init__(self, values, *ready, halves=None, ordered=False):
        self.grouped = lax.axis_size("fsdp") == 8
        self.halved = halves is not None
        values = values.astype(BF16)
        if self.halved:
            self.kept, self.sent = halves
            self.crossed = swap_chip(self.sent)
        elif self.grouped:
            middle = values.shape[0] // 2
            split = (values[:middle], values[middle:]) if ordered else split_blocks(values)
            self.keep, self.side_send = split
            self.side = swap_group(after(self.side_send, *ready), 1)
        else:
            self.sums = lax.psum_scatter(values, "fsdp", scatter_dimension=0, tiled=True)

    def cross(self, *ready):
        values = add_low(self.kept, after(self.crossed, *ready))
        if self.grouped:
            self.keep, self.side_send = split_blocks(values)
            self.side = swap_group(self.side_send, 1)
        else:
            self.sums = lax.psum_scatter(values, "fsdp", scatter_dimension=0, tiled=True)

    def got(self, *names):
        return tuple(getattr(self, name) for name in names if hasattr(self, name))

    def step(self, name, next_name, bit, ready):
        if self.grouped:
            received = after(getattr(self, name), *ready)
            half = self.keep.shape[0] // 2
            send = add_low(self.keep[half:], received[half:])
            self.keep = add_low(self.keep[:half], received[:half])
            setattr(self, next_name, swap_group(send, bit))

    def near(self, *ready):
        self.step("side", "near_sums", 2, ready)

    def far(self, *ready):
        self.step("near_sums", "far_sums", 4, ready)

    def chips(self, *ready):
        if self.grouped:
            self.sums = add_low(self.keep, after(self.far_sums, *ready))
        self.other_chip = swap_chip(self.sums)

    def cores(self, *ready):
        other_chip = after(self.other_chip, *ready)
        if self.halved:
            chip = lax.axis_index("seq") // 2
            first = jnp.where(chip == 0, self.sums, other_chip)
            second = jnp.where(chip == 0, other_chip, self.sums)
            self.total = jnp.concatenate([first, second], axis=1)
        else:
            self.total = add_low(self.sums, other_chip)
        self.other_core = swap_core(self.total)

    def last(self):
        if not self.grouped:
            return self.sums.astype(F32)
        return self.keep.astype(F32) + self.far_sums.astype(F32)


def take(values, index):
    return lax.dynamic_index_in_dim(values, index, 0, keepdims=False)


def in_core_order(own, other, core, axis):
    first = jnp.where(core == 0, own, other)
    second = jnp.where(core == 0, other, own)
    return first, second


def body(
    inputs,
    cotangent,
    valid,
    ln1_gain,
    ln1_bias,
    qkv_weight,
    q_bias,
    v_bias,
    out_weight,
    out_bias,
    ln2_gain,
    ln2_bias,
    fc1_weight,
    fc1_bias,
    fc2_weight,
    fc2_bias,
):
    clips, rows, width = inputs.shape
    groups = lax.axis_size("fsdp")
    place = lax.axis_index("seq")
    group = lax.axis_index("fsdp")
    chip, core = place // 2, place % 2
    half = width // 2
    hidden_rows = fc2_weight.shape[0]
    half_rows = hidden_rows // 2
    own_rows = clips * rows
    scale_factor = HEAD ** (-0.5)

    def all_clips(values, back):
        mine = values[:rows]
        first = jnp.where(chip == 0, mine, back)
        second = jnp.where(chip == 0, back, mine)
        return jnp.stack([first, second])

    own_width = width // groups
    vectors = (ln1_gain, ln1_bias, q_bias, v_bias, out_bias, ln2_gain, ln2_bias, fc2_bias, fc1_bias)
    quarter = half // 2
    row_width = 3 * quarter
    used = 8 * own_width + fc1_bias.shape[0]
    if groups == 8:
        own_first, own_second = own_qkv_blocks(qkv_weight, out_weight, vectors)
    else:
        by_head = qkv_weight.reshape(own_width, 3, 2, 2, 2, PAIR)
        by_head = lax.dynamic_index_in_dim(by_head, core, 2, keepdims=False)
        by_head = by_head.transpose(0, 2, 3, 1, 4).reshape(own_width, 2, row_width)
        out_columns = lax.dynamic_slice_in_dim(out_weight, core * half, half, 1)
        own_first = by_head[:, 0]
        own_second = jnp.concatenate([by_head[:, 1], out_columns], axis=1)

    qkv_a, qkv_b = Gather(own_first), Gather(own_second)
    qkv_a.send(4, 2, 1)
    other_inputs = swap_chip(take(after(inputs, *qkv_a.got(4, 2, 1)), 1 - chip))
    qkv_a.send(6, 3, 5, ready=qkv_a.got(4, 2, 1))
    qkv_b.send(4, ready=qkv_a.got(4, 2, 1))
    fc1_weight, fc2_weight = after((fc1_weight, fc2_weight), own_first)
    if groups == 8:
        own_fc1, own_fc2 = own_rest_blocks(fc1_weight, fc2_weight)
    else:
        own_fc1 = lax.dynamic_index_in_dim(
            fc1_weight.reshape(own_width, groups, 2, half_rows), core, 2, keepdims=False
        ).reshape(own_width, groups * half_rows)
        own_fc2 = lax.dynamic_slice_in_dim(fc2_weight, core * half_rows, half_rows, 0)
    full_fc1 = lax.all_gather(own_fc1, "fsdp", axis=0, tiled=True)
    full_fc2 = lax.all_gather(own_fc2, "fsdp", axis=0, tiled=True)
    qkv_a.send(7, ready=qkv_a.got(6, 3, 5))
    other_inputs = after(other_inputs, own_fc1, *qkv_a.got(6, 3, 5))
    qkv_b.send(2, 1, ready=qkv_a.got(6, 3, 5))
    own_inputs = jnp.concatenate([take(inputs, chip), other_inputs], axis=0)
    all_inputs = with_partner(own_inputs)
    if groups == 8:
        qkv_first, wide, bias_fc1 = in_order(qkv_a.pieces, own_width, True)
    else:
        qkv_first = qkv_a.result()
        packed = lax.all_gather(jnp.concatenate(vectors), "fsdp", axis=0)
        wide = [
            packed[:, i * own_width : (i + 1) * own_width].reshape(width).astype(F32)
            for i in range(8)
        ]
        bias_fc1 = packed[:, 8 * own_width : used].reshape(groups, 2, half_rows)
        bias_fc1 = take(jnp.moveaxis(bias_fc1, 1, 0), core)
        bias_fc1 = bias_fc1.reshape(groups * half_rows).astype(F32)
    gain_one, bias_one, bias_q, bias_v, bias_out, gain_two, bias_two, bias_fc2 = [
        wide[i] for i in range(8)
    ]
    bias_q = take(bias_q.reshape(2, 2, 2, PAIR), core)
    bias_v = take(bias_v.reshape(2, 2, 2, PAIR), core)
    bias_mixed = jnp.stack([bias_q, jnp.zeros_like(bias_q), bias_v], axis=2).reshape(2, row_width)
    scale_mixed = jnp.array([scale_factor, 1.0, 1.0] * 2, F32).repeat(PAIR)
    clip_valid = take(valid, chip).reshape(2 * clips, rows)
    own_valid = jnp.concatenate([take(clip_valid, place), take(clip_valid, place ^ 2)])
    other_valid = jnp.concatenate([take(clip_valid, place ^ 1), take(clip_valid, place ^ 3)])
    key_valid = jnp.concatenate([own_valid, other_valid])
    lane = jnp.arange(PAIR) % HEAD
    key_mask = jnp.where(key_valid > 0, 0.0, MASKED)[:, None]
    key_base = jnp.where(lane == 0, key_mask, jnp.where(lane < 4, 1.0, 0.0)).astype(BF16)


    def project(weight, i):
        return ((dot(h_one, weight) + bias_mixed[i]) * scale_mixed).astype(BF16)

    h_one = rows_call(
        first_kernel, [all_inputs], [gain_one[None], bias_one[None]], [BF16], 0, "first_norm"
    )[0]
    mixed = [project(qkv_first, 0)]
    context, queries = [], []

    def attend_pair(pair, *ready):
        before = context[-1] if context else None
        base = after(key_base, *ready)
        results = attend(mixed[pair // 2], base, pair % 2, before, pair, 4)
        context.append(results[0])
        queries.append(results[1])

    ready = (h_one,) + qkv_b.got(4, 2, 1)
    qkv_b.send(6, 3, 5, ready=ready)
    attend_pair(0, *ready)
    ready = (queries[0],) + qkv_b.got(6, 3, 5)
    qkv_b.send(7, ready=ready)
    other_grads = swap_chip(after(take(cotangent, 1 - chip), *ready))
    attend_pair(1, *ready)
    second_columns = qkv_b.result()
    mixed.append(project(second_columns[:, :row_width], 1))
    ready = (queries[1], mixed[1], other_grads)
    kept = lax.dynamic_slice(second_columns, (core * half, row_width), (half, half))
    received = lax.dynamic_slice(second_columns, ((1 - core) * half, row_width), (half, half))
    received = swap_core(after(received, mixed[1]))
    attend_pair(2, kept, *ready)
    ready = (queries[2], received)
    attend_pair(3, *ready)
    own_grads = jnp.concatenate([take(cotangent, chip), after(other_grads, queries[3])], axis=0)
    full_out = jnp.concatenate(in_core_order(kept, received, core, 1), axis=1)
    all_context = context[3]
    own_part, other_part = both_halves_product([(all_context, full_out)], NN)
    ready = (own_grads, own_part)
    counted = own_valid.astype(F32)[:, None]
    residual_mid, h_two, middle_sums = rows_call(
        middle_kernel,
        [own_part, after(other_part, *ready), own_inputs, counted],
        [bias_out[None], gain_two[None], bias_two[None]],
        [F32, BF16],
        2,
        "middle",
    )
    h_two = with_partner(h_two)
    all_grads = with_partner(after(own_grads, residual_mid))
    grad_sums = column_sum(own_grads)
    h_two = after(h_two, grad_sums)
    active, slope = gelu_both(dot(h_two, full_fc1) + bias_fc1)
    active, slope = active.astype(BF16), slope.astype(BF16)
    active = after(active, full_fc2)
    fc2_product = dot(active, all_grads, TN).astype(BF16)
    fc2_scatter = Scatter(fc2_product)

    late_grads = after(all_grads, *fc2_scatter.got("keep"))
    grad_hidden, hidden_sums = hidden_gradient(late_grads, full_fc2, slope)
    fc1_halves = weight_halves(h_two, grad_hidden)
    fc1_scatter = Scatter(fc1_halves[0], halves=fc1_halves)
    own_part, other_part = both_halves_product(
        [(after(grad_hidden, fc1_scatter.sent), full_fc1)], NT
    )
    grad_residual, own_grad_attn, two_sums = rows_call(
        norm_back_kernel,
        [own_part, other_part, residual_mid, own_grads],
        [gain_two[None]],
        [F32, BF16],
        3,
        "norm_back",
    )
    grad_attn = with_partner(own_grad_attn)
    grad_context = half_product([(grad_attn, full_out)], NT, None, BF16)
    halves, sums = [None, None], []

    def back_pair(pair, *ready):
        grad_mixed, parts = attend_back(
            queries[pair],
            mixed[pair // 2],
            grad_context,
            all_context,
            after(key_base, *ready),
            pair % 2,
            pair,
            halves[pair // 2],
        )
        halves[pair // 2] = grad_mixed
        sums.append(parts)

    back_pair(0, grad_context)
    own_mlp, other_mlp = both_halves_product([(after(active, sums[0]), full_fc2)], NN)
    low_output, end_sums = rows_call(
        end_kernel,
        [own_mlp, other_mlp, residual_mid, counted],
        [bias_fc2[None]],
        [BF16],
        2,
        "end",
    )
    ready = (low_output, fc1_scatter.crossed) + fc2_scatter.got("side")
    output_back = swap_chip(after(low_output, *ready)[rows:])
    grad_out = dot(all_context, after(grad_attn, *ready), TN).astype(BF16)
    kept = lax.dynamic_slice_in_dim(grad_out, core * half, half, 1)
    received = swap_core(lax.dynamic_slice_in_dim(grad_out, (1 - core) * half, half, 1))
    fc2_scatter.near(*ready)
    fc1_scatter.cross(*ready)
    back_pair(1, kept, *ready, *fc2_scatter.got("keep"), *fc1_scatter.got("keep"))
    received = after(received, sums[1])
    grad_out = jnp.concatenate(in_core_order(kept, received, core, 0), axis=0)
    early = jnp.concatenate([dot(h_one, halves[0], TN).astype(BF16), grad_out], axis=1)
    ready = (sums[1], output_back) + fc2_scatter.got("near_sums") + fc1_scatter.got("side")
    fc2_scatter.far(*ready)
    fc1_scatter.near(*ready)
    early_scatter = Scatter(early, *ready)
    ready += fc2_scatter.got("keep") + fc1_scatter.got("keep") + early_scatter.got("keep")
    back_pair(2, *ready)
    ready = (sums[2],) + fc1_scatter.got("near_sums") + fc2_scatter.got("far_sums")
    ready += early_scatter.got("side")
    fc1_scatter.far(*ready)
    early_scatter.near(*ready)
    ready += fc1_scatter.got("keep") + early_scatter.got("keep")
    back_pair(3, *ready)
    ready = (sums[3],) + fc1_scatter.got("far_sums")
    ready += early_scatter.got("near_sums")
    early_scatter.far(*ready)
    fc2_scatter.chips(*ready)
    fc1_scatter.chips(*ready)
    late_scatter = Scatter(dot(after(h_one, *ready), halves[1], TN))
    gm_first, gm_second = after(tuple(halves), *late_scatter.got("keep"))
    own_one, other_one = both_halves_product(
        [(gm_first, qkv_first), (gm_second, second_columns)], NT
    )
    low_input_grad, one_sums = rows_call(
        norm_back_kernel,
        [own_one, other_one, own_inputs, grad_residual],
        [gain_one[None]],
        [BF16],
        3,
        "norm_back",
    )
    ready = late_scatter.got("side") + (low_input_grad,)
    late_scatter.near(*ready)
    one_sums = after(one_sums, *ready)

    if groups == 8:
        packed = pack_lines(
            [one_sums, two_sums, grad_sums[None], hidden_sums, end_sums, middle_sums], sums
        )
    else:
        lines = [one_sums[0], one_sums[1], two_sums[2], two_sums[0], two_sums[1], grad_sums]
        lines.append(hidden_sums[0])
        squares = [end_sums[0], middle_sums[0], end_sums[1], middle_sums[1]]
        squares = [jnp.sum(line.reshape(-1, PAIR), axis=0) for line in squares]

        def by_core(values):
            full = jnp.zeros((2, values.shape[0]), F32)
            return lax.dynamic_update_index_in_dim(full, values, core, 0).reshape(-1)

        wide = lines[:2] + [by_core(jnp.concatenate([part[n] for part in sums])) for n in range(2)]
        wide = [line.reshape(groups, own_width) for line in wide + lines[2:6]]
        all_sums = jnp.zeros((groups, 2, half_rows), F32)
        all_sums = lax.dynamic_update_index_in_dim(
            all_sums, lines[6].reshape(groups, half_rows), core, 1
        )
        wide.append(all_sums.reshape(groups, hidden_rows))
        wide.append(jnp.zeros((groups, 12 * PAIR - used)))
        wide.append(jnp.broadcast_to(jnp.concatenate(squares), (groups, 4 * PAIR)))
        packed = jnp.concatenate(wide, axis=1).astype(BF16).reshape(groups * 16, PAIR)
    ready = early_scatter.got("far_sums") + (fc1_scatter.other_chip, fc2_scatter.other_chip)
    packed = add_low(packed, after(swap_chip(packed), *ready))
    early_scatter.chips(packed)
    input_back = swap_chip(after(low_input_grad, early_scatter.sums)[rows:])
    fc1_scatter.cores(packed)
    fc2_scatter.cores(packed)
    ready = late_scatter.got("near_sums")
    packed = add_low(packed, after(swap_core(packed), *ready))
    late_scatter.far(packed)
    vector_scatter = Scatter(packed, ordered=True)
    vector_scatter.near(early_scatter.other_chip)
    early_scatter.cores(*vector_scatter.got("keep"))
    ready = late_scatter.got("far_sums") + (input_back,)
    vector_scatter.far(*ready)
    late_scatter.chips(*vector_scatter.got("keep"))
    late_scatter.cores()
    ready_last = (packed,)
    output = all_clips(low_output, after(output_back, packed))
    input_grad = all_clips(low_input_grad, input_back)

    def in_columns(values, other, blocks):
        size = values.shape[1] // blocks
        parts = in_core_order(values, other, core, 0)
        parts = [part.reshape(own_width, blocks, 1, size) for part in parts]
        return jnp.concatenate(parts, axis=2).reshape(own_width, -1).astype(F32)

    fc2_parts = after((fc2_scatter.total, fc2_scatter.other_core), *ready_last)
    fc2_grad = in_core_order(*fc2_parts, core, 0)
    fc2_grad = jnp.concatenate(fc2_grad, axis=0).astype(F32)
    early_parts = [early_scatter.total, early_scatter.other_core]
    late_parts = [late_scatter.total, late_scatter.other_core]
    fc1_parts = after((fc1_scatter.total, fc1_scatter.other_core), *ready_last)
    if groups == 8:
        fc1_places = [
            (0, n * half_rows, half_rows, 2 * n * half_rows, (2 * n + 1) * half_rows)
            for n in range(groups)
        ]
        fc1_grad = join_columns(fc1_parts, fc1_places, 2 * groups * half_rows)
        out_grad = join_columns(early_parts, [(0, row_width, half, 0, half)], width)
        qkv_places = []
        for n in range(3):
            for pair in range(4):
                target = n * width + pair * PAIR
                start = (3 * (pair % 2) + n) * PAIR
                qkv_places.append((pair // 2, start, PAIR, target, target + half))
        qkv_grad = join_columns(early_parts + late_parts, qkv_places, 3 * width)
    else:
        fc1_grad = in_columns(*fc1_parts, groups)
        out_grad = in_columns(*[part[:, row_width:] for part in early_parts], 1)

        def both_halves(left, right):
            left = left[:, :row_width].reshape(own_width, 1, 2, 3, PAIR)
            right = right.reshape(own_width, 1, 2, 3, PAIR)
            both = jnp.concatenate([left, right], axis=1).transpose(0, 3, 1, 2, 4)
            return both.reshape(own_width, 3 * half)

        qkv_grad = in_columns(*[both_halves(*pair) for pair in zip(early_parts, late_parts)], 3)
    lines = vector_scatter.last()
    flat = lines[:12].reshape(-1)
    own_vectors = [flat[i * own_width : (i + 1) * own_width] for i in range(8)]
    own_hidden = flat[8 * own_width : used]
    totals = jnp.sum(lines[12:], axis=1)
    branch_rms = jnp.sqrt(totals[:3] / totals[3])
    return (
        output,
        input_grad,
        own_vectors[0],
        own_vectors[1],
        qkv_grad,
        own_vectors[2],
        own_vectors[3],
        out_grad,
        own_vectors[4],
        own_vectors[5],
        own_vectors[6],
        fc1_grad,
        own_hidden,
        fc2_grad,
        own_vectors[7],
        branch_rms,
    )


def solution(mesh):
    tokens, rows, vector = P("fsdp", "seq", None), P("fsdp", None), P("fsdp")
    return jax.shard_map(
        body,
        mesh=mesh,
        in_specs=(
            tokens,
            tokens,
            rows,
            vector,
            vector,
            rows,
            vector,
            vector,
            rows,
            vector,
            vector,
            vector,
            rows,
            vector,
            rows,
            vector,
        ),
        out_specs=(
            tokens,
            tokens,
            vector,
            vector,
            rows,
            vector,
            vector,
            rows,
            vector,
            vector,
            vector,
            rows,
            vector,
            rows,
            vector,
            P(),
        ),
        check_vma=False,
    )
```

```python
from functools import partial

import jax
import jax.numpy as jnp
from jax import lax
from jax.experimental import pallas as pl
from jax.experimental.pallas import tpu as pltpu
from jax.sharding import PartitionSpec as P

HEADS = 16
HEAD = 64
PAIR = 2 * HEAD
EPS = 1e-06
MASKED = -1e30
VMEM_BYTES = 28 * 2**20
BF16 = jnp.bfloat16
F32 = jnp.float32
NN = (((1,), (0,)), ((), ()))
NT = (((1,), (1,)), ((), ()))
TN = (((0,), (0,)), ((), ()))
SMALL_COST = pl.CostEstimate(flops=10**7, bytes_accessed=2**20, transcendentals=0)


def dot(left, right, dims=NN):
    return lax.dot_general(left, right, dims, preferred_element_type=F32)


def lanes_of(shape):
    return lax.broadcasted_iota(jnp.int32, shape, len(shape) - 1)


def three_parts(column):
    high = column.astype(BF16).astype(F32)
    rest = column - high
    middle = rest.astype(BF16).astype(F32)
    return high, middle, rest - middle


def block_rows(length, *sizes):
    for rows in sizes + (224, 112, 16):
        if length % rows == 0:
            return rows
    return length


def attend_kernel(q_ref, k_ref, v_ref, key_base_ref, *refs):
    context_ref, query_ref = refs[-2:]
    length = q_ref.shape[0]
    rows = block_rows(length, 392)
    low = lanes_of((length, PAIR)) < HEAD
    keys, values, key_base = k_ref[...], v_ref[...], key_base_ref[...]
    ones = jnp.ones((length, PAIR), BF16)
    keys_of = [jnp.where(low, keys, key_base), jnp.where(low, key_base, keys)]
    values_of = [jnp.where(low, values, ones), jnp.where(low, ones, values)]
    lane = lanes_of((rows, PAIR))
    low_rows = lane < HEAD
    for step in range(length // rows):
        span = slice(step * rows, (step + 1) * rows)
        queries = q_ref[span, :]
        results = []
        for head in range(2):
            base = HEAD * (1 - head)
            own = low_rows if head == 0 else jnp.logical_not(low_rows)
            unit = jnp.where(lane == base, 1.0, 0.0)
            scores = dot(jnp.where(own, queries, unit.astype(BF16)), keys_of[head], NT)
            highest = jnp.max(scores, axis=1, keepdims=True)
            weights = jnp.exp(scores - highest).astype(BF16)
            mixed = dot(weights, values_of[head])
            total = mixed[:, base : base + 1]
            high, middle, rest = three_parts(-(highest + jnp.log(total)))
            extra = jnp.where(lane == base + 3, rest, unit)
            extra = jnp.where(lane == base + 2, middle, extra)
            extra = jnp.where(lane == base + 1, high, extra)
            query_ref[head, span, :] = jnp.where(own, queries, extra.astype(BF16))
            results.append(mixed / total)
        context_ref[span, :] = jnp.where(low_rows, results[0], results[1]).astype(BF16)


def attend(mixed, key_base, pair, context, place, places):
    length = mixed.shape[0]
    tile = lambda column: pl.BlockSpec((length, PAIR), lambda i: (0, column))
    in_specs = [tile(3 * pair), tile(3 * pair + 1), tile(3 * pair + 2), tile(0)]
    operands = (mixed, mixed, mixed, key_base)
    aliases = {}
    if context is not None:
        in_specs.append(pl.BlockSpec(memory_space=pl.ANY))
        operands += (context,)
        aliases = {4: 0}
    return pl.pallas_call(
        attend_kernel,
        grid=(1,),
        in_specs=in_specs,
        out_specs=[tile(place), pl.BlockSpec((2, length, PAIR), lambda i: (0, 0, 0))],
        out_shape=[
            jax.ShapeDtypeStruct((length, places * PAIR), BF16),
            jax.ShapeDtypeStruct((2, length, PAIR), BF16),
        ],
        input_output_aliases=aliases,
        compiler_params=pltpu.CompilerParams(vmem_limit_bytes=VMEM_BYTES),
        cost_estimate=SMALL_COST,
        name="attend",
    )(*operands)


def attend_back_kernel(query_ref, k_ref, v_ref, grad_ref, context_ref, key_base_ref, *refs):
    grad_mixed_ref, sums_ref = refs[-2:]
    length = k_ref.shape[0]
    rows = block_rows(length)
    low = lanes_of((length, PAIR)) < HEAD
    keys, values, key_base = k_ref[...], v_ref[...], key_base_ref[...]
    ones = jnp.ones((length, PAIR), BF16)
    lane = lanes_of((rows, PAIR))
    low_rows = lane < HEAD
    steps = length // rows
    grad_q, grad_k, grad_v = [], [], []
    sum_q = jnp.zeros((1, PAIR), F32)
    for head in range(2):
        base = HEAD * (1 - head)
        own = low if head == 0 else jnp.logical_not(low)
        own_rows = low_rows if head == 0 else jnp.logical_not(low_rows)
        head_keys = jnp.where(own, keys, key_base)
        head_values = jnp.where(own, values, ones)
        sum_k = jnp.zeros((length, PAIR), F32)
        sum_v = jnp.zeros((length, PAIR), F32)
        for step in range(steps):
            span = slice(step * rows, (step + 1) * rows)
            queries = query_ref[head, span, :]
            grads = grad_ref[span, :]
            product = grads.astype(F32) * context_ref[span, :].astype(F32)
            inner = jnp.sum(jnp.where(own_rows, product, 0.0), axis=1, keepdims=True)
            high, middle, rest = three_parts(-inner)
            extra = jnp.where(lane == base + 2, rest, 0.0)
            extra = jnp.where(lane == base + 1, middle, extra)
            extra = jnp.where(lane == base, high, extra)
            head_grads = jnp.where(own_rows, grads, extra.astype(BF16))
            probs = jnp.exp(dot(head_keys, queries, NT))
            grad_scores = (probs * dot(head_values, head_grads, NT)).astype(BF16)
            sum_v = sum_v + dot(probs.astype(BF16), grads)
            sum_k = sum_k + dot(grad_scores, queries)
            part = dot(grad_scores, keys, TN)
            if head == 0:
                grad_q.append(part)
            else:
                both = jnp.where(low_rows, grad_q[step], part).astype(BF16)
                both = both * (HEAD ** (-0.5))
                grad_mixed_ref[span, :PAIR] = both
                sum_q = sum_q + jnp.sum(both.astype(F32), axis=0, keepdims=True)
        grad_k.append(sum_k)
        grad_v.append(sum_v)
    grad_mixed_ref[:, PAIR : 2 * PAIR] = jnp.where(low, grad_k[0], grad_k[1]).astype(BF16)
    both = jnp.where(low, grad_v[0], grad_v[1]).astype(BF16)
    grad_mixed_ref[:, 2 * PAIR :] = both
    sums_ref[0:1, :] = sum_q
    sums_ref[1:2, :] = jnp.sum(both.astype(F32), axis=0, keepdims=True)


def attend_back(queries, mixed, grad_context, context, key_base, pair, place, grad_mixed):
    length = mixed.shape[0]
    tile = lambda column: pl.BlockSpec((length, PAIR), lambda i: (0, column))
    in_specs = [
        pl.BlockSpec((2, length, PAIR), lambda i: (0, 0, 0)),
        tile(3 * pair + 1),
        tile(3 * pair + 2),
        tile(place),
        tile(place),
        tile(0),
    ]
    operands = (queries, mixed, mixed, grad_context, context, key_base)
    aliases = {}
    if grad_mixed is not None:
        in_specs.append(pl.BlockSpec(memory_space=pl.ANY))
        operands += (grad_mixed,)
        aliases = {6: 0}
    return pl.pallas_call(
        attend_back_kernel,
        grid=(1,),
        in_specs=in_specs,
        out_specs=[
            pl.BlockSpec((length, 3 * PAIR), lambda i: (0, pair)),
            pl.BlockSpec((2, PAIR), lambda i: (0, 0)),
        ],
        out_shape=[
            jax.ShapeDtypeStruct((length, 6 * PAIR), BF16),
            jax.ShapeDtypeStruct((2, PAIR), F32),
        ],
        input_output_aliases=aliases,
        compiler_params=pltpu.CompilerParams(vmem_limit_bytes=VMEM_BYTES),
        cost_estimate=SMALL_COST,
        name="attend_back",
    )(*operands)


def normalize(values):
    center = values - jnp.mean(values, axis=-1, keepdims=True)
    spread = jnp.mean(center * center, axis=-1, keepdims=True)
    scale = lax.rsqrt(spread + EPS)
    return center * scale, scale


def rows_call(kernel, row_inputs, constants, kinds, sum_rows, name):
    rows, width = row_inputs[0].shape
    tile = rows // 7 if rows % 112 == 0 else rows
    block = lambda columns: pl.BlockSpec((tile, columns), lambda i: (i, 0))
    whole = lambda shape: pl.BlockSpec(shape, lambda i: (0, 0))
    out_specs = [block(width)] * len(kinds)
    out_shape = [jax.ShapeDtypeStruct((rows, width), kind) for kind in kinds]
    if sum_rows:
        out_specs.append(whole((sum_rows, width)))
        out_shape.append(jax.ShapeDtypeStruct((sum_rows, width), F32))
    return pl.pallas_call(
        kernel,
        grid=(rows // tile,),
        in_specs=[block(part.shape[1]) for part in row_inputs]
        + [whole(part.shape) for part in constants],
        out_specs=out_specs,
        out_shape=out_shape,
        compiler_params=pltpu.CompilerParams(vmem_limit_bytes=VMEM_BYTES),
        cost_estimate=SMALL_COST,
        name=name,
    )(*row_inputs, *constants)


def add_rows(sums_ref, parts):
    @pl.when(pl.program_id(0) == 0)
    def _():
        sums_ref[...] = jnp.zeros(sums_ref.shape, F32)

    lines = [jnp.sum(part, axis=0, keepdims=True) for part in parts]
    sums_ref[...] += jnp.concatenate(lines, axis=0)


def first_kernel(values_ref, gain_ref, bias_ref, out_ref):
    normal = normalize(values_ref[...].astype(F32))[0]
    out_ref[...] = (normal * gain_ref[...] + bias_ref[...]).astype(BF16)


def middle_kernel(
    own_ref, other_ref, inputs_ref, counted_ref, out_bias_ref, gain_ref, bias_ref, *out_refs
):
    middle_ref, low_ref, sums_ref = out_refs
    branch = own_ref[...] + other_ref[...].astype(F32) + out_bias_ref[...]
    middle = inputs_ref[...].astype(F32) + branch
    middle_ref[...] = middle
    low_ref[...] = (normalize(middle)[0] * gain_ref[...] + bias_ref[...]).astype(BF16)
    counted = counted_ref[...]
    add_rows(sums_ref, [counted * branch * branch, jnp.broadcast_to(counted, branch.shape)])


def end_kernel(own_ref, other_ref, middle_ref, counted_ref, bias_ref, low_ref, sums_ref):
    branch = own_ref[...] + other_ref[...].astype(F32) + bias_ref[...]
    result = middle_ref[...] + branch
    low_ref[...] = result.astype(BF16)
    counted = counted_ref[...]
    add_rows(sums_ref, [counted * result * result, counted * branch * branch])


def norm_back_kernel(own_ref, other_ref, values_ref, residual_ref, gain_ref, *out_refs):
    grad = own_ref[...] + other_ref[...].astype(F32)
    normal, scale = normalize(values_ref[...].astype(F32))
    inner = grad * gain_ref[...]
    first = jnp.mean(inner, axis=-1, keepdims=True)
    second = jnp.mean(inner * normal, axis=-1, keepdims=True)
    total = residual_ref[...].astype(F32) + scale * (inner - first - normal * second)
    low = total.astype(BF16)
    if len(out_refs) == 3:
        out_refs[0][...] = total
    out_refs[-2][...] = low
    add_rows(out_refs[-1], [grad * normal, grad, low.astype(F32)])


def weight_kernel(left_ref, right_ref, kept_ref, sent_ref):
    chip = lax.axis_index("seq") // 2
    left, half = left_ref[...], kept_ref.shape[1]
    for part, out_ref in ((chip, kept_ref), (1 - chip, sent_ref)):
        columns = pl.ds(pl.multiple_of(part * half, half), half)
        out_ref[...] = dot(left, right_ref[:, columns], TN).astype(BF16)


def weight_halves(left, right):
    rows, depth = left.shape
    columns = right.shape[1]
    tile = min(depth, 512)
    half = pl.BlockSpec((tile, columns // 2), lambda i: (i, 0))
    return pl.pallas_call(
        weight_kernel,
        grid=(depth // tile,),
        in_specs=[
            pl.BlockSpec((rows, tile), lambda i: (0, i)),
            pl.BlockSpec((rows, columns), lambda i: (0, 0)),
        ],
        out_specs=[half, half],
        out_shape=[jax.ShapeDtypeStruct((depth, columns // 2), BF16)] * 2,
        compiler_params=pltpu.CompilerParams(vmem_limit_bytes=VMEM_BYTES),
        cost_estimate=SMALL_COST,
        name="weight_halves",
    )(left, right)


def gelu_both(values):
    half = 0.5 * (1.0 + lax.erf(values * (0.5**0.5)))
    density = jnp.exp(-0.5 * values * values) * (0.5 / jnp.pi) ** 0.5
    return values * half, half + values * density


def hidden_kernel(grad_ref, weight_ref, slope_ref, hidden_ref, sums_ref):
    rows = grad_ref.shape[0] // 2
    weight = weight_ref[...]
    total = jnp.zeros((1, weight.shape[0]), F32)
    for span in (slice(0, rows), slice(rows, 2 * rows)):
        hidden = (dot(grad_ref[span, :], weight, NT) * slope_ref[span, :].astype(F32)).astype(BF16)
        hidden_ref[span, :] = hidden
        total = total + jnp.sum(hidden.astype(F32), axis=0, keepdims=True)
    sums_ref[...] = total


def hidden_gradient(grads, weight, slope):
    rows, depth = grads.shape
    columns = weight.shape[0]
    tile = min(columns, 512)
    block = pl.BlockSpec((rows, tile), lambda i: (0, i))
    return pl.pallas_call(
        hidden_kernel,
        grid=(columns // tile,),
        in_specs=[
            pl.BlockSpec((rows, depth), lambda i: (0, 0)),
            pl.BlockSpec((tile, depth), lambda i: (i, 0)),
            block,
        ],
        out_specs=[block, pl.BlockSpec((1, tile), lambda i: (0, i))],
        out_shape=[
            jax.ShapeDtypeStruct((rows, columns), BF16),
            jax.ShapeDtypeStruct((1, columns), F32),
        ],
        compiler_params=pltpu.CompilerParams(vmem_limit_bytes=VMEM_BYTES),
        cost_estimate=SMALL_COST,
        name="hidden_gradient",
    )(grads, weight, slope)


def half_kernel(dims, *refs):
    total = dot(refs[0][...], refs[1][...], dims)
    for n in range(2, len(refs) - 1, 2):
        total = total + dot(refs[n][...], refs[n + 1][...], dims)
    refs[-1][...] = total.astype(refs[-1].dtype)


def half_product(pairs, dims, part, kind):
    rows = pairs[0][0].shape[0] if part is None else pairs[0][0].shape[0] // 2
    part = part or 0
    columns = pairs[0][1].shape[1 if dims is NN else 0]
    tile = min(columns, 512)
    in_specs, operands = [], []
    for left, right in pairs:
        depth = left.shape[1]
        in_specs.append(pl.BlockSpec((rows, depth), lambda i: (part, 0)))
        if dims is NN:
            in_specs.append(pl.BlockSpec((depth, tile), lambda i: (0, i)))
        else:
            in_specs.append(pl.BlockSpec((tile, depth), lambda i: (i, 0)))
        operands += [left, right]
    return pl.pallas_call(
        partial(half_kernel, dims),
        grid=(columns // tile,),
        in_specs=in_specs,
        out_specs=pl.BlockSpec((rows, tile), lambda i: (0, i)),
        out_shape=jax.ShapeDtypeStruct((rows, columns), kind),
        compiler_params=pltpu.CompilerParams(vmem_limit_bytes=VMEM_BYTES),
        cost_estimate=SMALL_COST,
        name="half_product",
    )(*operands)


def both_halves_product(pairs, dims):
    other = half_product(pairs, dims, 1, BF16)
    own = [(after(left, other), right) for left, right in pairs]
    return half_product(own, dims, 0, F32), swap_core(other)


def join_kernel(places, *refs):
    out_ref = refs[-1]
    core = lax.rem(lax.axis_index("seq"), 2)
    for n, (source, start, width, first, second) in enumerate(places):
        for other in range(2):
            target = pl.multiple_of(jnp.where(core == other, first, second), PAIR)
            block = refs[2 * source + other][:, start : start + width]
            out_ref[:, pl.ds(target, width)] = block.astype(F32)


def join_columns(parts, places, columns):
    rows = parts[0].shape[0]
    return pl.pallas_call(
        partial(join_kernel, places),
        in_specs=[pl.BlockSpec(memory_space=pltpu.VMEM)] * len(parts),
        out_specs=pl.BlockSpec(memory_space=pltpu.VMEM),
        out_shape=jax.ShapeDtypeStruct((rows, columns), F32),
        cost_estimate=SMALL_COST,
        name="join_columns",
    )(*parts)


def column_sum(values):
    return jnp.sum(values, axis=0, dtype=F32)


def swap_core(values):
    return lax.ppermute(values, "seq", [(0, 1), (1, 0), (2, 3), (3, 2)])


def swap_chip(values):
    return lax.ppermute(values, "seq", [(0, 2), (2, 0), (1, 3), (3, 1)])


def stack_kernel(own_ref, other_ref, out_ref, sems):
    rows = own_ref.shape[0]
    copies = [
        pltpu.make_async_copy(ref, out_ref.at[pl.ds(n * rows, rows)], sems.at[n])
        for n, ref in enumerate((own_ref, other_ref))
    ]
    for copy in copies:
        copy.start()
    for copy in copies:
        copy.wait()


def with_partner(values):
    rows, columns = values.shape
    return pl.pallas_call(
        stack_kernel,
        in_specs=[pl.BlockSpec(memory_space=pltpu.VMEM)] * 2,
        out_specs=pl.BlockSpec(memory_space=pl.ANY),
        out_shape=jax.ShapeDtypeStruct((2 * rows, columns), values.dtype),
        scratch_shapes=[pltpu.SemaphoreType.DMA((2,))],
        compiler_params=pltpu.CompilerParams(vmem_limit_bytes=16 * 2**20),
        cost_estimate=SMALL_COST,
        name="stack_rows",
    )(values, swap_core(values))


def swap_group(values, bit):
    return lax.ppermute(values, "fsdp", [(i, i ^ bit) for i in range(8)])


def order_kernel(count, *refs):
    pieces, full_ref, held, arrived, sent = refs[:count], refs[count], *refs[-3:]
    group = lax.axis_index("fsdp")
    rows = full_ref.shape[0] // count
    loads = [
        pltpu.make_async_copy(piece, held.at[relative], arrived.at[relative])
        for relative, piece in enumerate(pieces)
    ]
    for load in loads:
        load.start()
    stores = []
    for relative in range(count):
        start = pl.multiple_of((group ^ relative) * rows, rows)
        store = pltpu.make_async_copy(
            held.at[relative, pl.ds(0, rows)], full_ref.at[pl.ds(start, rows)], sent.at[relative]
        )
        loads[relative].wait()
        store.start()
        stores.append(store)
    if len(refs) > count + 4:
        own_width, core = 128, lax.rem(lax.axis_index("seq"), 2)
        wide_ref, bias_ref = refs[count + 1], refs[count + 2]
        for relative in range(count):
            place = group ^ relative
            columns = pl.ds(pl.multiple_of(place * own_width, own_width), own_width)
            extra = held[relative, rows : rows + 8, :].astype(F32)
            lines = [
                extra[k : k + 1, own_width * n : own_width * (n + 1)]
                for k in range(2)
                for n in range(6)
            ]
            for n in range(8):
                wide_ref[n : n + 1, columns] = lines[n]
            for n in range(2):
                start = pl.multiple_of((place * 2 + n) * own_width, own_width)
                bias_ref[:, pl.ds(start, own_width)] = jnp.where(
                    core == 0, lines[8 + n], lines[10 + n]
                )
    for store in stores:
        store.wait()


def in_order(pieces, rows, with_vectors=False):
    count, columns = len(pieces), pieces[0].shape[1]
    out_specs = [pl.BlockSpec(memory_space=pl.ANY)]
    out_shape = [jax.ShapeDtypeStruct((count * rows, columns), pieces[0].dtype)]
    if with_vectors:
        out_specs += [pl.BlockSpec(memory_space=pltpu.VMEM)] * 2
        out_shape += [jax.ShapeDtypeStruct((8, 1024), F32), jax.ShapeDtypeStruct((1, 2048), F32)]
    result = pl.pallas_call(
        partial(order_kernel, count),
        in_specs=[pl.BlockSpec(memory_space=pl.ANY)] * count,
        out_specs=out_specs,
        out_shape=out_shape,
        scratch_shapes=[
            pltpu.VMEM((count,) + pieces[0].shape, pieces[0].dtype),
            pltpu.SemaphoreType.DMA((count,)),
            pltpu.SemaphoreType.DMA((count,)),
        ],
        compiler_params=pltpu.CompilerParams(vmem_limit_bytes=16 * 2**20),
        cost_estimate=SMALL_COST,
        name="in_order",
    )(*pieces)
    return result if with_vectors else result[0]


def own_kernel(qkv_ref, out_ref, *refs):
    vector_refs, (first_ref, second_ref) = refs[:-2], refs[-2:]
    core = lax.rem(lax.axis_index("seq"), 2)
    rows = qkv_ref.shape[0]
    for n in range(3):
        for pair in range(4):
            block_ref = second_ref if pair >= 2 else first_ref
            start = pl.multiple_of((8 * n + pair + 4 * core) * PAIR, PAIR)
            target = (3 * (pair % 2) + n) * PAIR
            block_ref[:rows, target : target + PAIR] = qkv_ref[:, pl.ds(start, PAIR)]
    out_half = out_ref.shape[1] // 2
    start = pl.multiple_of(core * out_half, out_half)
    second_ref[:, 6 * PAIR :] = out_ref[:, pl.ds(start, out_half)]
    lines = []
    for ref in vector_refs:
        vector = ref[...].astype(F32).reshape(ref.shape[0] // PAIR, PAIR)
        lines += [vector[n : n + 1] for n in range(ref.shape[0] // PAIR)]
    row = lax.broadcasted_iota(jnp.int32, (8, PAIR), 0)
    for n in range(6):
        block = jnp.where(row == 0, lines[n], jnp.where(row == 1, lines[n + 6], 0.0))
        first_ref[rows:, PAIR * n : PAIR * (n + 1)] = block.astype(BF16)


def own_qkv_blocks(qkv_weight, out_weight, vectors):
    rows, columns = qkv_weight.shape[0], qkv_weight.shape[1] // 4
    out_half = out_weight.shape[1] // 2
    return pl.pallas_call(
        own_kernel,
        in_specs=[pl.BlockSpec(memory_space=pltpu.VMEM)] * (2 + len(vectors)),
        out_specs=[pl.BlockSpec(memory_space=pltpu.VMEM)] * 2,
        out_shape=[
            jax.ShapeDtypeStruct((rows + 8, columns), BF16),
            jax.ShapeDtypeStruct((rows, columns + out_half), BF16),
        ],
        cost_estimate=SMALL_COST,
        name="own_qkv",
    )(qkv_weight, out_weight, *vectors)


def own_rest_kernel(fc1_ref, fc2_ref, first_ref, second_ref):
    core = lax.rem(lax.axis_index("seq"), 2)
    rows = second_ref.shape[0]
    for n in range(fc1_ref.shape[1] // (2 * rows)):
        start = pl.multiple_of((2 * n + core) * rows, rows)
        first_ref[:, n * rows : (n + 1) * rows] = fc1_ref[:, pl.ds(start, rows)]
    second_ref[...] = fc2_ref[pl.ds(pl.multiple_of(core * rows, rows), rows), :]


def own_rest_blocks(fc1_weight, fc2_weight):
    return pl.pallas_call(
        own_rest_kernel,
        in_specs=[pl.BlockSpec(memory_space=pltpu.VMEM)] * 2,
        out_specs=[pl.BlockSpec(memory_space=pltpu.VMEM)] * 2,
        out_shape=[
            jax.ShapeDtypeStruct((fc1_weight.shape[0], fc1_weight.shape[1] // 2), BF16),
            jax.ShapeDtypeStruct((fc2_weight.shape[0] // 2, fc2_weight.shape[1]), BF16),
        ],
        cost_estimate=SMALL_COST,
        name="own_rest",
    )(fc1_weight, fc2_weight)


def after(values, *others):
    return lax.optimization_barrier((values,) + others)[0] if others else values


class Gather:
    SOURCE = {4: 0, 2: 0, 1: 0, 6: 4, 3: 2, 5: 4, 7: 6}
    STEP = {4: 4, 2: 2, 1: 1, 6: 2, 3: 1, 5: 1, 7: 1}

    def __init__(self, own):
        self.pieces = [own] + [None] * 7
        self.grouped = lax.axis_size("fsdp") == 8

    def send(self, *parts, ready=()):
        if not self.grouped:
            return
        sources = [self.pieces[self.SOURCE[part]] for part in parts]
        if ready:
            sources = lax.optimization_barrier(tuple(sources) + tuple(ready))
        for part, source in zip(parts, sources):
            self.pieces[part] = swap_group(source, self.STEP[part])

    def got(self, *parts):
        return tuple(self.pieces[part] for part in parts) if self.grouped else ()

    def result(self):
        if not self.grouped:
            return lax.all_gather(self.pieces[0], "fsdp", axis=0, tiled=True)
        return in_order(self.pieces, self.pieces[0].shape[0])


def add_low(left, right):
    return (left.astype(F32) + right.astype(F32)).astype(BF16)


def split_kernel(full_ref, *refs):
    sems = refs[2]
    group = lax.axis_index("fsdp")
    rows = full_ref.shape[0] // 8
    copies = []
    for n in range(8):
        far, near, side = n % 2, (n // 2) % 2, n // 4
        start = pl.multiple_of((group ^ (4 * far + 2 * near + side)) * rows, rows)
        target = refs[side].at[pl.ds((n % 4) * rows, rows)]
        copies.append(
            pltpu.make_async_copy(full_ref.at[pl.ds(start, rows)], target, sems.at[n])
        )
    for copy in copies:
        copy.start()
    for copy in copies:
        copy.wait()


def split_blocks(values):
    rows, columns = values.shape
    return pl.pallas_call(
        split_kernel,
        in_specs=[pl.BlockSpec(memory_space=pltpu.VMEM)],
        out_specs=[pl.BlockSpec(memory_space=pl.ANY)] * 2,
        out_shape=[jax.ShapeDtypeStruct((rows // 2, columns), values.dtype)] * 2,
        scratch_shapes=[pltpu.SemaphoreType.DMA((8,))],
        compiler_params=pltpu.CompilerParams(vmem_limit_bytes=16 * 2**20),
        cost_estimate=SMALL_COST,
        name="split_blocks",
    )(values)


def pack_kernel(
    one_ref, two_ref, grads_ref, hidden_ref, end_ref, middle_ref, *refs
):
    sum_refs, packed_ref = refs[:4], refs[4]
    group = lax.axis_index("fsdp")
    core = lax.rem(lax.axis_index("seq"), 2)
    squares = jnp.zeros((4, PAIR), F32)
    for n in range(end_ref.shape[1] // PAIR):
        span = slice(n * PAIR, (n + 1) * PAIR)
        end, middle = end_ref[:, span], middle_ref[:, span]
        squares = squares + jnp.concatenate([end[:1], middle[:1], end[1:], middle[1:]], axis=0)
    for n in range(8):
        far, near, side = n % 2, (n // 2) % 2, n // 4
        target = group ^ (4 * far + 2 * near + side)
        columns = pl.ds(pl.multiple_of(target * PAIR, PAIR), PAIR)
        mine = (target // 4) == core
        pair = lax.rem(target, 4)
        head_sums = jnp.zeros((2, PAIR), F32)
        for k in range(4):
            head_sums = jnp.where(jnp.logical_and(mine, pair == k), sum_refs[k][...], head_sums)
        one, two = one_ref[:, columns], two_ref[:, columns]
        hidden = [
            hidden_ref[:, pl.ds(pl.multiple_of(target * 2 * PAIR + k * PAIR, PAIR), PAIR)]
            for k in range(2)
        ]
        empty = jnp.zeros((1, PAIR), F32)
        rows = [one[:2], head_sums, two[2:3], two[:2], grads_ref[:, columns]]
        rows += [jnp.where(core == 0, part, empty) for part in hidden]
        rows += [jnp.where(core == 0, empty, part) for part in hidden]
        rows.append(squares)
        packed_ref[16 * n : 16 * (n + 1), :] = jnp.concatenate(rows, axis=0).astype(BF16)


def pack_lines(lines, sums):
    return pl.pallas_call(
        pack_kernel,
        in_specs=[pl.BlockSpec(memory_space=pltpu.VMEM)] * 10,
        out_specs=pl.BlockSpec(memory_space=pltpu.VMEM),
        out_shape=jax.ShapeDtypeStruct((128, PAIR), BF16),
        cost_estimate=SMALL_COST,
        name="pack_lines",
    )(*lines, *sums)


class Scatter:
    def __init__(self, values, *ready, halves=None, ordered=False):
        self.grouped = lax.axis_size("fsdp") == 8
        self.halved = halves is not None
        values = values.astype(BF16)
        if self.halved:
            self.kept, self.sent = halves
            self.crossed = swap_chip(self.sent)
        elif self.grouped:
            middle = values.shape[0] // 2
            split = (values[:middle], values[middle:]) if ordered else split_blocks(values)
            self.keep, self.side_send = split
            self.side = swap_group(after(self.side_send, *ready), 1)
        else:
            self.sums = lax.psum_scatter(values, "fsdp", scatter_dimension=0, tiled=True)

    def cross(self, *ready):
        values = add_low(self.kept, after(self.crossed, *ready))
        if self.grouped:
            self.keep, self.side_send = split_blocks(values)
            self.side = swap_group(self.side_send, 1)
        else:
            self.sums = lax.psum_scatter(values, "fsdp", scatter_dimension=0, tiled=True)

    def got(self, *names):
        return tuple(getattr(self, name) for name in names if hasattr(self, name))

    def step(self, name, next_name, bit, ready):
        if self.grouped:
            received = after(getattr(self, name), *ready)
            half = self.keep.shape[0] // 2
            send = add_low(self.keep[half:], received[half:])
            self.keep = add_low(self.keep[:half], received[:half])
            setattr(self, next_name, swap_group(send, bit))

    def near(self, *ready):
        self.step("side", "near_sums", 2, ready)

    def far(self, *ready):
        self.step("near_sums", "far_sums", 4, ready)

    def chips(self, *ready):
        if self.grouped:
            self.sums = add_low(self.keep, after(self.far_sums, *ready))
        self.other_chip = swap_chip(self.sums)

    def cores(self, *ready):
        other_chip = after(self.other_chip, *ready)
        if self.halved:
            chip = lax.axis_index("seq") // 2
            first = jnp.where(chip == 0, self.sums, other_chip)
            second = jnp.where(chip == 0, other_chip, self.sums)
            self.total = jnp.concatenate([first, second], axis=1)
        else:
            self.total = add_low(self.sums, other_chip)
        self.other_core = swap_core(self.total)

    def last(self):
        if not self.grouped:
            return self.sums.astype(F32)
        return self.keep.astype(F32) + self.far_sums.astype(F32)


def take(values, index):
    return lax.dynamic_index_in_dim(values, index, 0, keepdims=False)


def in_core_order(own, other, core, axis):
    first = jnp.where(core == 0, own, other)
    second = jnp.where(core == 0, other, own)
    return first, second


def body(
    inputs,
    cotangent,
    valid,
    ln1_gain,
    ln1_bias,
    qkv_weight,
    q_bias,
    v_bias,
    out_weight,
    out_bias,
    ln2_gain,
    ln2_bias,
    fc1_weight,
    fc1_bias,
    fc2_weight,
    fc2_bias,
):
    clips, rows, width = inputs.shape
    groups = lax.axis_size("fsdp")
    place = lax.axis_index("seq")
    group = lax.axis_index("fsdp")
    chip, core = place // 2, place % 2
    half = width // 2
    hidden_rows = fc2_weight.shape[0]
    half_rows = hidden_rows // 2
    own_rows = clips * rows
    scale_factor = HEAD ** (-0.5)

    def all_clips(values, back):
        mine = values[:rows]
        first = jnp.where(chip == 0, mine, back)
        second = jnp.where(chip == 0, back, mine)
        return jnp.stack([first, second])

    own_width = width // groups
    vectors = (ln1_gain, ln1_bias, q_bias, v_bias, out_bias, ln2_gain, ln2_bias, fc2_bias, fc1_bias)
    quarter = half // 2
    row_width = 3 * quarter
    used = 8 * own_width + fc1_bias.shape[0]
    if groups == 8:
        own_first, own_second = own_qkv_blocks(qkv_weight, out_weight, vectors)
    else:
        by_head = qkv_weight.reshape(own_width, 3, 2, 2, 2, PAIR)
        by_head = lax.dynamic_index_in_dim(by_head, core, 2, keepdims=False)
        by_head = by_head.transpose(0, 2, 3, 1, 4).reshape(own_width, 2, row_width)
        out_columns = lax.dynamic_slice_in_dim(out_weight, core * half, half, 1)
        own_first = by_head[:, 0]
        own_second = jnp.concatenate([by_head[:, 1], out_columns], axis=1)

    qkv_a, qkv_b = Gather(own_first), Gather(own_second)
    qkv_a.send(4, 2, 1)
    other_inputs = swap_chip(take(after(inputs, *qkv_a.got(4, 2, 1)), 1 - chip))
    qkv_a.send(6, 3, 5, ready=qkv_a.got(4, 2, 1))
    qkv_b.send(4, ready=qkv_a.got(4, 2, 1))
    fc1_weight, fc2_weight = after((fc1_weight, fc2_weight), own_first)
    if groups == 8:
        own_fc1, own_fc2 = own_rest_blocks(fc1_weight, fc2_weight)
    else:
        own_fc1 = lax.dynamic_index_in_dim(
            fc1_weight.reshape(own_width, groups, 2, half_rows), core, 2, keepdims=False
        ).reshape(own_width, groups * half_rows)
        own_fc2 = lax.dynamic_slice_in_dim(fc2_weight, core * half_rows, half_rows, 0)
    full_fc1 = lax.all_gather(own_fc1, "fsdp", axis=0, tiled=True)
    full_fc2 = lax.all_gather(own_fc2, "fsdp", axis=0, tiled=True)
    qkv_a.send(7, ready=qkv_a.got(6, 3, 5))
    other_inputs = after(other_inputs, own_fc1, *qkv_a.got(6, 3, 5))
    qkv_b.send(2, 1, ready=qkv_a.got(6, 3, 5))
    own_inputs = jnp.concatenate([take(inputs, chip), other_inputs], axis=0)
    all_inputs = with_partner(own_inputs)
    if groups == 8:
        qkv_first, wide, bias_fc1 = in_order(qkv_a.pieces, own_width, True)
    else:
        qkv_first = qkv_a.result()
        packed = lax.all_gather(jnp.concatenate(vectors), "fsdp", axis=0)
        wide = [
            packed[:, i * own_width : (i + 1) * own_width].reshape(width).astype(F32)
            for i in range(8)
        ]
        bias_fc1 = packed[:, 8 * own_width : used].reshape(groups, 2, half_rows)
        bias_fc1 = take(jnp.moveaxis(bias_fc1, 1, 0), core)
        bias_fc1 = bias_fc1.reshape(groups * half_rows).astype(F32)
    gain_one, bias_one, bias_q, bias_v, bias_out, gain_two, bias_two, bias_fc2 = [
        wide[i] for i in range(8)
    ]
    bias_q = take(bias_q.reshape(2, 2, 2, PAIR), core)
    bias_v = take(bias_v.reshape(2, 2, 2, PAIR), core)
    bias_mixed = jnp.stack([bias_q, jnp.zeros_like(bias_q), bias_v], axis=2).reshape(2, row_width)
    scale_mixed = jnp.array([scale_factor, 1.0, 1.0] * 2, F32).repeat(PAIR)
    clip_valid = take(valid, chip).reshape(2 * clips, rows)
    own_valid = jnp.concatenate([take(clip_valid, place), take(clip_valid, place ^ 2)])
    other_valid = jnp.concatenate([take(clip_valid, place ^ 1), take(clip_valid, place ^ 3)])
    key_valid = jnp.concatenate([own_valid, other_valid])
    lane = jnp.arange(PAIR) % HEAD
    key_mask = jnp.where(key_valid > 0, 0.0, MASKED)[:, None]
    key_base = jnp.where(lane == 0, key_mask, jnp.where(lane < 4, 1.0, 0.0)).astype(BF16)


    def project(weight, i):
        return ((dot(h_one, weight) + bias_mixed[i]) * scale_mixed).astype(BF16)

    h_one = rows_call(
        first_kernel, [all_inputs], [gain_one[None], bias_one[None]], [BF16], 0, "first_norm"
    )[0]
    mixed = [project(qkv_first, 0)]
    context, queries = [], []

    def attend_pair(pair, *ready):
        before = context[-1] if context else None
        base = after(key_base, *ready)
        results = attend(mixed[pair // 2], base, pair % 2, before, pair, 4)
        context.append(results[0])
        queries.append(results[1])

    ready = (h_one,) + qkv_b.got(4, 2, 1)
    qkv_b.send(6, 3, 5, ready=ready)
    attend_pair(0, *ready)
    ready = (queries[0],) + qkv_b.got(6, 3, 5)
    qkv_b.send(7, ready=ready)
    other_grads = swap_chip(after(take(cotangent, 1 - chip), *ready))
    attend_pair(1, *ready)
    second_columns = qkv_b.result()
    mixed.append(project(second_columns[:, :row_width], 1))
    ready = (queries[1], mixed[1], other_grads)
    kept = lax.dynamic_slice(second_columns, (core * half, row_width), (half, half))
    received = lax.dynamic_slice(second_columns, ((1 - core) * half, row_width), (half, half))
    received = swap_core(after(received, mixed[1]))
    attend_pair(2, kept, *ready)
    ready = (queries[2], received)
    attend_pair(3, *ready)
    own_grads = jnp.concatenate([take(cotangent, chip), after(other_grads, queries[3])], axis=0)
    full_out = jnp.concatenate(in_core_order(kept, received, core, 1), axis=1)
    all_context = context[3]
    own_part, other_part = both_halves_product([(all_context, full_out)], NN)
    ready = (own_grads, own_part)
    counted = own_valid.astype(F32)[:, None]
    residual_mid, h_two, middle_sums = rows_call(
        middle_kernel,
        [own_part, after(other_part, *ready), own_inputs, counted],
        [bias_out[None], gain_two[None], bias_two[None]],
        [F32, BF16],
        2,
        "middle",
    )
    h_two = with_partner(h_two)
    all_grads = with_partner(after(own_grads, residual_mid))
    grad_sums = column_sum(own_grads)
    h_two = after(h_two, grad_sums)
    active, slope = gelu_both(dot(h_two, full_fc1) + bias_fc1)
    active, slope = active.astype(BF16), slope.astype(BF16)
    active = after(active, full_fc2)
    fc2_product = dot(active, all_grads, TN).astype(BF16)
    fc2_scatter = Scatter(fc2_product)

    late_grads = after(all_grads, *fc2_scatter.got("keep"))
    grad_hidden, hidden_sums = hidden_gradient(late_grads, full_fc2, slope)
    fc1_halves = weight_halves(h_two, grad_hidden)
    fc1_scatter = Scatter(fc1_halves[0], halves=fc1_halves)
    own_part, other_part = both_halves_product(
        [(after(grad_hidden, fc1_scatter.sent), full_fc1)], NT
    )
    grad_residual, own_grad_attn, two_sums = rows_call(
        norm_back_kernel,
        [own_part, other_part, residual_mid, own_grads],
        [gain_two[None]],
        [F32, BF16],
        3,
        "norm_back",
    )
    grad_attn = with_partner(own_grad_attn)
    grad_context = half_product([(grad_attn, full_out)], NT, None, BF16)
    halves, sums = [None, None], []

    def back_pair(pair, *ready):
        grad_mixed, parts = attend_back(
            queries[pair],
            mixed[pair // 2],
            grad_context,
            all_context,
            after(key_base, *ready),
            pair % 2,
            pair,
            halves[pair // 2],
        )
        halves[pair // 2] = grad_mixed
        sums.append(parts)

    back_pair(0, grad_context)
    own_mlp, other_mlp = both_halves_product([(after(active, sums[0]), full_fc2)], NN)
    low_output, end_sums = rows_call(
        end_kernel,
        [own_mlp, other_mlp, residual_mid, counted],
        [bias_fc2[None]],
        [BF16],
        2,
        "end",
    )
    ready = (low_output, fc1_scatter.crossed) + fc2_scatter.got("side")
    output_back = swap_chip(after(low_output, *ready)[rows:])
    grad_out = dot(all_context, after(grad_attn, *ready), TN).astype(BF16)
    kept = lax.dynamic_slice_in_dim(grad_out, core * half, half, 1)
    received = swap_core(lax.dynamic_slice_in_dim(grad_out, (1 - core) * half, half, 1))
    fc2_scatter.near(*ready)
    fc1_scatter.cross(*ready)
    back_pair(1, kept, *ready, *fc2_scatter.got("keep"), *fc1_scatter.got("keep"))
    received = after(received, sums[1])
    grad_out = jnp.concatenate(in_core_order(kept, received, core, 0), axis=0)
    early = jnp.concatenate([dot(h_one, halves[0], TN).astype(BF16), grad_out], axis=1)
    ready = (sums[1], output_back) + fc2_scatter.got("near_sums") + fc1_scatter.got("side")
    fc2_scatter.far(*ready)
    fc1_scatter.near(*ready)
    early_scatter = Scatter(early, *ready)
    ready += fc2_scatter.got("keep") + fc1_scatter.got("keep") + early_scatter.got("keep")
    back_pair(2, *ready)
    ready = (sums[2],) + fc1_scatter.got("near_sums") + fc2_scatter.got("far_sums")
    ready += early_scatter.got("side")
    fc1_scatter.far(*ready)
    early_scatter.near(*ready)
    ready += fc1_scatter.got("keep") + early_scatter.got("keep")
    back_pair(3, *ready)
    ready = (sums[3],) + fc1_scatter.got("far_sums")
    ready += early_scatter.got("near_sums")
    early_scatter.far(*ready)
    fc2_scatter.chips(*ready)
    fc1_scatter.chips(*ready)
    late_scatter = Scatter(dot(after(h_one, *ready), halves[1], TN))
    gm_first, gm_second = after(tuple(halves), *late_scatter.got("keep"))
    own_one, other_one = both_halves_product(
        [(gm_first, qkv_first), (gm_second, second_columns)], NT
    )
    low_input_grad, one_sums = rows_call(
        norm_back_kernel,
        [own_one, other_one, own_inputs, grad_residual],
        [gain_one[None]],
        [BF16],
        3,
        "norm_back",
    )
    ready = late_scatter.got("side") + (low_input_grad,)
    late_scatter.near(*ready)
    one_sums = after(one_sums, *ready)

    if groups == 8:
        packed = pack_lines(
            [one_sums, two_sums, grad_sums[None], hidden_sums, end_sums, middle_sums], sums
        )
    else:
        lines = [one_sums[0], one_sums[1], two_sums[2], two_sums[0], two_sums[1], grad_sums]
        lines.append(hidden_sums[0])
        squares = [end_sums[0], middle_sums[0], end_sums[1], middle_sums[1]]
        squares = [jnp.sum(line.reshape(-1, PAIR), axis=0) for line in squares]

        def by_core(values):
            full = jnp.zeros((2, values.shape[0]), F32)
            return lax.dynamic_update_index_in_dim(full, values, core, 0).reshape(-1)

        wide = lines[:2] + [by_core(jnp.concatenate([part[n] for part in sums])) for n in range(2)]
        wide = [line.reshape(groups, own_width) for line in wide + lines[2:6]]
        all_sums = jnp.zeros((groups, 2, half_rows), F32)
        all_sums = lax.dynamic_update_index_in_dim(
            all_sums, lines[6].reshape(groups, half_rows), core, 1
        )
        wide.append(all_sums.reshape(groups, hidden_rows))
        wide.append(jnp.zeros((groups, 12 * PAIR - used)))
        wide.append(jnp.broadcast_to(jnp.concatenate(squares), (groups, 4 * PAIR)))
        packed = jnp.concatenate(wide, axis=1).astype(BF16).reshape(groups * 16, PAIR)
    input_back = swap_chip(low_input_grad[rows:])
    ready = early_scatter.got("far_sums") + (fc1_scatter.other_chip, fc2_scatter.other_chip)
    packed = add_low(packed, after(swap_chip(packed), *ready))
    early_scatter.chips(packed)
    fc1_scatter.cores(packed)
    fc2_scatter.cores(packed)
    ready = late_scatter.got("near_sums")
    packed = add_low(packed, after(swap_core(packed), *ready))
    late_scatter.far(packed)
    vector_scatter = Scatter(packed, ordered=True)
    vector_scatter.near(early_scatter.other_chip, input_back)
    early_scatter.cores(*vector_scatter.got("keep"))
    ready = late_scatter.got("far_sums")
    vector_scatter.far(*ready)
    late_scatter.chips(*vector_scatter.got("keep"))
    late_scatter.cores()
    ready_last = (packed,)
    output = all_clips(low_output, after(output_back, packed))
    input_grad = all_clips(low_input_grad, input_back)

    def in_columns(values, other, blocks):
        size = values.shape[1] // blocks
        parts = in_core_order(values, other, core, 0)
        parts = [part.reshape(own_width, blocks, 1, size) for part in parts]
        return jnp.concatenate(parts, axis=2).reshape(own_width, -1).astype(F32)

    fc2_parts = after((fc2_scatter.total, fc2_scatter.other_core), *ready_last)
    fc2_grad = in_core_order(*fc2_parts, core, 0)
    fc2_grad = jnp.concatenate(fc2_grad, axis=0).astype(F32)
    early_parts = [early_scatter.total, early_scatter.other_core]
    late_parts = [late_scatter.total, late_scatter.other_core]
    fc1_parts = after((fc1_scatter.total, fc1_scatter.other_core), *ready_last)
    if groups == 8:
        fc1_places = [
            (0, n * half_rows, half_rows, 2 * n * half_rows, (2 * n + 1) * half_rows)
            for n in range(groups)
        ]
        fc1_grad = join_columns(fc1_parts, fc1_places, 2 * groups * half_rows)
        out_grad = join_columns(early_parts, [(0, row_width, half, 0, half)], width)
        qkv_places = []
        for n in range(3):
            for pair in range(4):
                target = n * width + pair * PAIR
                start = (3 * (pair % 2) + n) * PAIR
                qkv_places.append((pair // 2, start, PAIR, target, target + half))
        qkv_grad = join_columns(early_parts + late_parts, qkv_places, 3 * width)
    else:
        fc1_grad = in_columns(*fc1_parts, groups)
        out_grad = in_columns(*[part[:, row_width:] for part in early_parts], 1)

        def both_halves(left, right):
            left = left[:, :row_width].reshape(own_width, 1, 2, 3, PAIR)
            right = right.reshape(own_width, 1, 2, 3, PAIR)
            both = jnp.concatenate([left, right], axis=1).transpose(0, 3, 1, 2, 4)
            return both.reshape(own_width, 3 * half)

        qkv_grad = in_columns(*[both_halves(*pair) for pair in zip(early_parts, late_parts)], 3)
    lines = vector_scatter.last()
    flat = lines[:12].reshape(-1)
    own_vectors = [flat[i * own_width : (i + 1) * own_width] for i in range(8)]
    own_hidden = flat[8 * own_width : used]
    totals = jnp.sum(lines[12:], axis=1)
    branch_rms = jnp.sqrt(totals[:3] / totals[3])
    return (
        output,
        input_grad,
        own_vectors[0],
        own_vectors[1],
        qkv_grad,
        own_vectors[2],
        own_vectors[3],
        out_grad,
        own_vectors[4],
        own_vectors[5],
        own_vectors[6],
        fc1_grad,
        own_hidden,
        fc2_grad,
        own_vectors[7],
        branch_rms,
    )


def solution(mesh):
    tokens, rows, vector = P("fsdp", "seq", None), P("fsdp", None), P("fsdp")
    return jax.shard_map(
        body,
        mesh=mesh,
        in_specs=(
            tokens,
            tokens,
            rows,
            vector,
            vector,
            rows,
            vector,
            vector,
            rows,
            vector,
            vector,
            vector,
            rows,
            vector,
            rows,
            vector,
        ),
        out_specs=(
            tokens,
            tokens,
            vector,
            vector,
            rows,
            vector,
            vector,
            rows,
            vector,
            vector,
            vector,
            rows,
            vector,
            rows,
            vector,
            P(),
        ),
        check_vma=False,
    )
```

```python
from functools import partial

import jax
import jax.numpy as jnp
from jax import lax
from jax.experimental import pallas as pl
from jax.experimental.pallas import tpu as pltpu
from jax.sharding import PartitionSpec as P

HEADS = 16
HEAD = 64
PAIR = 2 * HEAD
EPS = 1e-06
MASKED = -1e30
VMEM_BYTES = 28 * 2**20
BF16 = jnp.bfloat16
F32 = jnp.float32
NN = (((1,), (0,)), ((), ()))
NT = (((1,), (1,)), ((), ()))
TN = (((0,), (0,)), ((), ()))
SMALL_COST = pl.CostEstimate(flops=10**7, bytes_accessed=2**20, transcendentals=0)


def dot(left, right, dims=NN):
    return lax.dot_general(left, right, dims, preferred_element_type=F32)


def lanes_of(shape):
    return lax.broadcasted_iota(jnp.int32, shape, len(shape) - 1)


def three_parts(column):
    high = column.astype(BF16).astype(F32)
    rest = column - high
    middle = rest.astype(BF16).astype(F32)
    return high, middle, rest - middle


def block_rows(length, *sizes):
    for rows in sizes + (224, 112, 16):
        if length % rows == 0:
            return rows
    return length


def attend_kernel(q_ref, k_ref, v_ref, key_base_ref, *refs):
    context_ref, query_ref = refs[-2:]
    length = q_ref.shape[0]
    rows = block_rows(length, 392)
    low = lanes_of((length, PAIR)) < HEAD
    keys, values, key_base = k_ref[...], v_ref[...], key_base_ref[...]
    ones = jnp.ones((length, PAIR), BF16)
    keys_of = [jnp.where(low, keys, key_base), jnp.where(low, key_base, keys)]
    values_of = [jnp.where(low, values, ones), jnp.where(low, ones, values)]
    lane = lanes_of((rows, PAIR))
    low_rows = lane < HEAD
    for step in range(length // rows):
        span = slice(step * rows, (step + 1) * rows)
        queries = q_ref[span, :]
        results = []
        for head in range(2):
            base = HEAD * (1 - head)
            own = low_rows if head == 0 else jnp.logical_not(low_rows)
            unit = jnp.where(lane == base, 1.0, 0.0)
            scores = dot(jnp.where(own, queries, unit.astype(BF16)), keys_of[head], NT)
            highest = jnp.max(scores, axis=1, keepdims=True)
            weights = jnp.exp(scores - highest).astype(BF16)
            mixed = dot(weights, values_of[head])
            total = mixed[:, base : base + 1]
            high, middle, rest = three_parts(-(highest + jnp.log(total)))
            extra = jnp.where(lane == base + 3, rest, unit)
            extra = jnp.where(lane == base + 2, middle, extra)
            extra = jnp.where(lane == base + 1, high, extra)
            query_ref[head, span, :] = jnp.where(own, queries, extra.astype(BF16))
            results.append(mixed / total)
        context_ref[span, :] = jnp.where(low_rows, results[0], results[1]).astype(BF16)


def attend(mixed, key_base, pair, context, place, places):
    length = mixed.shape[0]
    tile = lambda column: pl.BlockSpec((length, PAIR), lambda i: (0, column))
    in_specs = [tile(3 * pair), tile(3 * pair + 1), tile(3 * pair + 2), tile(0)]
    operands = (mixed, mixed, mixed, key_base)
    aliases = {}
    if context is not None:
        in_specs.append(pl.BlockSpec(memory_space=pl.ANY))
        operands += (context,)
        aliases = {4: 0}
    return pl.pallas_call(
        attend_kernel,
        grid=(1,),
        in_specs=in_specs,
        out_specs=[tile(place), pl.BlockSpec((2, length, PAIR), lambda i: (0, 0, 0))],
        out_shape=[
            jax.ShapeDtypeStruct((length, places * PAIR), BF16),
            jax.ShapeDtypeStruct((2, length, PAIR), BF16),
        ],
        input_output_aliases=aliases,
        compiler_params=pltpu.CompilerParams(vmem_limit_bytes=VMEM_BYTES),
        cost_estimate=SMALL_COST,
        name="attend",
    )(*operands)


def attend_back_kernel(query_ref, k_ref, v_ref, grad_ref, context_ref, key_base_ref, *refs):
    grad_mixed_ref, sums_ref = refs[-2:]
    length = k_ref.shape[0]
    rows = block_rows(length)
    low = lanes_of((length, PAIR)) < HEAD
    keys, values, key_base = k_ref[...], v_ref[...], key_base_ref[...]
    ones = jnp.ones((length, PAIR), BF16)
    lane = lanes_of((rows, PAIR))
    low_rows = lane < HEAD
    steps = length // rows
    grad_q, grad_k, grad_v = [], [], []
    sum_q = jnp.zeros((1, PAIR), F32)
    for head in range(2):
        base = HEAD * (1 - head)
        own = low if head == 0 else jnp.logical_not(low)
        own_rows = low_rows if head == 0 else jnp.logical_not(low_rows)
        head_keys = jnp.where(own, keys, key_base)
        head_values = jnp.where(own, values, ones)
        sum_k = jnp.zeros((length, PAIR), F32)
        sum_v = jnp.zeros((length, PAIR), F32)
        for step in range(steps):
            span = slice(step * rows, (step + 1) * rows)
            queries = query_ref[head, span, :]
            grads = grad_ref[span, :]
            product = grads.astype(F32) * context_ref[span, :].astype(F32)
            inner = jnp.sum(jnp.where(own_rows, product, 0.0), axis=1, keepdims=True)
            high, middle, rest = three_parts(-inner)
            extra = jnp.where(lane == base + 2, rest, 0.0)
            extra = jnp.where(lane == base + 1, middle, extra)
            extra = jnp.where(lane == base, high, extra)
            head_grads = jnp.where(own_rows, grads, extra.astype(BF16))
            probs = jnp.exp(dot(head_keys, queries, NT))
            grad_scores = (probs * dot(head_values, head_grads, NT)).astype(BF16)
            sum_v = sum_v + dot(probs.astype(BF16), grads)
            sum_k = sum_k + dot(grad_scores, queries)
            part = dot(grad_scores, keys, TN)
            if head == 0:
                grad_q.append(part)
            else:
                both = jnp.where(low_rows, grad_q[step], part).astype(BF16)
                both = both * (HEAD ** (-0.5))
                grad_mixed_ref[span, :PAIR] = both
                sum_q = sum_q + jnp.sum(both.astype(F32), axis=0, keepdims=True)
        grad_k.append(sum_k)
        grad_v.append(sum_v)
    grad_mixed_ref[:, PAIR : 2 * PAIR] = jnp.where(low, grad_k[0], grad_k[1]).astype(BF16)
    both = jnp.where(low, grad_v[0], grad_v[1]).astype(BF16)
    grad_mixed_ref[:, 2 * PAIR :] = both
    sums_ref[0:1, :] = sum_q
    sums_ref[1:2, :] = jnp.sum(both.astype(F32), axis=0, keepdims=True)


def attend_back(queries, mixed, grad_context, context, key_base, pair, place, grad_mixed):
    length = mixed.shape[0]
    tile = lambda column: pl.BlockSpec((length, PAIR), lambda i: (0, column))
    in_specs = [
        pl.BlockSpec((2, length, PAIR), lambda i: (0, 0, 0)),
        tile(3 * pair + 1),
        tile(3 * pair + 2),
        tile(place),
        tile(place),
        tile(0),
    ]
    operands = (queries, mixed, mixed, grad_context, context, key_base)
    aliases = {}
    if grad_mixed is not None:
        in_specs.append(pl.BlockSpec(memory_space=pl.ANY))
        operands += (grad_mixed,)
        aliases = {6: 0}
    return pl.pallas_call(
        attend_back_kernel,
        grid=(1,),
        in_specs=in_specs,
        out_specs=[
            pl.BlockSpec((length, 3 * PAIR), lambda i: (0, pair)),
            pl.BlockSpec((2, PAIR), lambda i: (0, 0)),
        ],
        out_shape=[
            jax.ShapeDtypeStruct((length, 6 * PAIR), BF16),
            jax.ShapeDtypeStruct((2, PAIR), F32),
        ],
        input_output_aliases=aliases,
        compiler_params=pltpu.CompilerParams(vmem_limit_bytes=VMEM_BYTES),
        cost_estimate=SMALL_COST,
        name="attend_back",
    )(*operands)


def normalize(values):
    center = values - jnp.mean(values, axis=-1, keepdims=True)
    spread = jnp.mean(center * center, axis=-1, keepdims=True)
    scale = lax.rsqrt(spread + EPS)
    return center * scale, scale


def rows_call(kernel, row_inputs, constants, kinds, sum_rows, name):
    rows, width = row_inputs[0].shape
    tile = rows // 7 if rows % 112 == 0 else rows
    block = lambda columns: pl.BlockSpec((tile, columns), lambda i: (i, 0))
    whole = lambda shape: pl.BlockSpec(shape, lambda i: (0, 0))
    out_specs = [block(width)] * len(kinds)
    out_shape = [jax.ShapeDtypeStruct((rows, width), kind) for kind in kinds]
    if sum_rows:
        out_specs.append(whole((sum_rows, width)))
        out_shape.append(jax.ShapeDtypeStruct((sum_rows, width), F32))
    return pl.pallas_call(
        kernel,
        grid=(rows // tile,),
        in_specs=[block(part.shape[1]) for part in row_inputs]
        + [whole(part.shape) for part in constants],
        out_specs=out_specs,
        out_shape=out_shape,
        compiler_params=pltpu.CompilerParams(vmem_limit_bytes=VMEM_BYTES),
        cost_estimate=SMALL_COST,
        name=name,
    )(*row_inputs, *constants)


def add_rows(sums_ref, parts):
    @pl.when(pl.program_id(0) == 0)
    def _():
        sums_ref[...] = jnp.zeros(sums_ref.shape, F32)

    lines = [jnp.sum(part, axis=0, keepdims=True) for part in parts]
    sums_ref[...] += jnp.concatenate(lines, axis=0)


def first_kernel(values_ref, gain_ref, bias_ref, out_ref):
    normal = normalize(values_ref[...].astype(F32))[0]
    out_ref[...] = (normal * gain_ref[...] + bias_ref[...]).astype(BF16)


def middle_kernel(
    own_ref, other_ref, inputs_ref, counted_ref, out_bias_ref, gain_ref, bias_ref, *out_refs
):
    middle_ref, low_ref, sums_ref = out_refs
    branch = own_ref[...] + other_ref[...].astype(F32) + out_bias_ref[...]
    middle = inputs_ref[...].astype(F32) + branch
    middle_ref[...] = middle
    low_ref[...] = (normalize(middle)[0] * gain_ref[...] + bias_ref[...]).astype(BF16)
    counted = counted_ref[...]
    add_rows(sums_ref, [counted * branch * branch, jnp.broadcast_to(counted, branch.shape)])


def end_kernel(own_ref, other_ref, middle_ref, counted_ref, bias_ref, low_ref, sums_ref):
    branch = own_ref[...] + other_ref[...].astype(F32) + bias_ref[...]
    result = middle_ref[...] + branch
    low_ref[...] = result.astype(BF16)
    counted = counted_ref[...]
    add_rows(sums_ref, [counted * result * result, counted * branch * branch])


def norm_back_kernel(own_ref, other_ref, values_ref, residual_ref, gain_ref, *out_refs):
    grad = own_ref[...] + other_ref[...].astype(F32)
    normal, scale = normalize(values_ref[...].astype(F32))
    inner = grad * gain_ref[...]
    first = jnp.mean(inner, axis=-1, keepdims=True)
    second = jnp.mean(inner * normal, axis=-1, keepdims=True)
    total = residual_ref[...].astype(F32) + scale * (inner - first - normal * second)
    low = total.astype(BF16)
    if len(out_refs) == 3:
        out_refs[0][...] = total
    out_refs[-2][...] = low
    add_rows(out_refs[-1], [grad * normal, grad, low.astype(F32)])


def weight_kernel(left_ref, right_ref, kept_ref, sent_ref):
    chip = lax.axis_index("seq") // 2
    left, half = left_ref[...], kept_ref.shape[1]
    for part, out_ref in ((chip, kept_ref), (1 - chip, sent_ref)):
        columns = pl.ds(pl.multiple_of(part * half, half), half)
        out_ref[...] = dot(left, right_ref[:, columns], TN).astype(BF16)


def weight_halves(left, right):
    rows, depth = left.shape
    columns = right.shape[1]
    tile = min(depth, 512)
    half = pl.BlockSpec((tile, columns // 2), lambda i: (i, 0))
    return pl.pallas_call(
        weight_kernel,
        grid=(depth // tile,),
        in_specs=[
            pl.BlockSpec((rows, tile), lambda i: (0, i)),
            pl.BlockSpec((rows, columns), lambda i: (0, 0)),
        ],
        out_specs=[half, half],
        out_shape=[jax.ShapeDtypeStruct((depth, columns // 2), BF16)] * 2,
        compiler_params=pltpu.CompilerParams(vmem_limit_bytes=VMEM_BYTES),
        cost_estimate=SMALL_COST,
        name="weight_halves",
    )(left, right)


def gelu_both(values):
    half = 0.5 * (1.0 + lax.erf(values * (0.5**0.5)))
    density = jnp.exp(-0.5 * values * values) * (0.5 / jnp.pi) ** 0.5
    return values * half, half + values * density


def hidden_kernel(grad_ref, weight_ref, slope_ref, hidden_ref, sums_ref):
    rows = grad_ref.shape[0] // 2
    weight = weight_ref[...]
    total = jnp.zeros((1, weight.shape[0]), F32)
    for span in (slice(0, rows), slice(rows, 2 * rows)):
        hidden = (dot(grad_ref[span, :], weight, NT) * slope_ref[span, :].astype(F32)).astype(BF16)
        hidden_ref[span, :] = hidden
        total = total + jnp.sum(hidden.astype(F32), axis=0, keepdims=True)
    sums_ref[...] = total


def hidden_gradient(grads, weight, slope):
    rows, depth = grads.shape
    columns = weight.shape[0]
    tile = min(columns, 512)
    block = pl.BlockSpec((rows, tile), lambda i: (0, i))
    return pl.pallas_call(
        hidden_kernel,
        grid=(columns // tile,),
        in_specs=[
            pl.BlockSpec((rows, depth), lambda i: (0, 0)),
            pl.BlockSpec((tile, depth), lambda i: (i, 0)),
            block,
        ],
        out_specs=[block, pl.BlockSpec((1, tile), lambda i: (0, i))],
        out_shape=[
            jax.ShapeDtypeStruct((rows, columns), BF16),
            jax.ShapeDtypeStruct((1, columns), F32),
        ],
        compiler_params=pltpu.CompilerParams(vmem_limit_bytes=VMEM_BYTES),
        cost_estimate=SMALL_COST,
        name="hidden_gradient",
    )(grads, weight, slope)


def half_kernel(dims, *refs):
    total = dot(refs[0][...], refs[1][...], dims)
    for n in range(2, len(refs) - 1, 2):
        total = total + dot(refs[n][...], refs[n + 1][...], dims)
    refs[-1][...] = total.astype(refs[-1].dtype)


def half_product(pairs, dims, part, kind):
    rows = pairs[0][0].shape[0] if part is None else pairs[0][0].shape[0] // 2
    part = part or 0
    columns = pairs[0][1].shape[1 if dims is NN else 0]
    tile = min(columns, 512)
    in_specs, operands = [], []
    for left, right in pairs:
        depth = left.shape[1]
        in_specs.append(pl.BlockSpec((rows, depth), lambda i: (part, 0)))
        if dims is NN:
            in_specs.append(pl.BlockSpec((depth, tile), lambda i: (0, i)))
        else:
            in_specs.append(pl.BlockSpec((tile, depth), lambda i: (i, 0)))
        operands += [left, right]
    return pl.pallas_call(
        partial(half_kernel, dims),
        grid=(columns // tile,),
        in_specs=in_specs,
        out_specs=pl.BlockSpec((rows, tile), lambda i: (0, i)),
        out_shape=jax.ShapeDtypeStruct((rows, columns), kind),
        compiler_params=pltpu.CompilerParams(vmem_limit_bytes=VMEM_BYTES),
        cost_estimate=SMALL_COST,
        name="half_product",
    )(*operands)


def both_halves_product(pairs, dims):
    other = half_product(pairs, dims, 1, BF16)
    own = [(after(left, other), right) for left, right in pairs]
    return half_product(own, dims, 0, F32), swap_core(other)


def join_kernel(places, *refs):
    out_ref = refs[-1]
    core = lax.rem(lax.axis_index("seq"), 2)
    for n, (source, start, width, first, second) in enumerate(places):
        for other in range(2):
            target = pl.multiple_of(jnp.where(core == other, first, second), PAIR)
            block = refs[2 * source + other][:, start : start + width]
            out_ref[:, pl.ds(target, width)] = block.astype(F32)


def join_columns(parts, places, columns):
    rows = parts[0].shape[0]
    return pl.pallas_call(
        partial(join_kernel, places),
        in_specs=[pl.BlockSpec(memory_space=pltpu.VMEM)] * len(parts),
        out_specs=pl.BlockSpec(memory_space=pltpu.VMEM),
        out_shape=jax.ShapeDtypeStruct((rows, columns), F32),
        cost_estimate=SMALL_COST,
        name="join_columns",
    )(*parts)


def column_sum(values):
    return jnp.sum(values, axis=0, dtype=F32)


def swap_core(values):
    return lax.ppermute(values, "seq", [(0, 1), (1, 0), (2, 3), (3, 2)])


def swap_chip(values):
    return lax.ppermute(values, "seq", [(0, 2), (2, 0), (1, 3), (3, 1)])


def stack_kernel(own_ref, other_ref, out_ref, sems):
    rows = own_ref.shape[0]
    copies = [
        pltpu.make_async_copy(ref, out_ref.at[pl.ds(n * rows, rows)], sems.at[n])
        for n, ref in enumerate((own_ref, other_ref))
    ]
    for copy in copies:
        copy.start()
    for copy in copies:
        copy.wait()


def with_partner(values):
    rows, columns = values.shape
    return pl.pallas_call(
        stack_kernel,
        in_specs=[pl.BlockSpec(memory_space=pltpu.VMEM)] * 2,
        out_specs=pl.BlockSpec(memory_space=pl.ANY),
        out_shape=jax.ShapeDtypeStruct((2 * rows, columns), values.dtype),
        scratch_shapes=[pltpu.SemaphoreType.DMA((2,))],
        compiler_params=pltpu.CompilerParams(vmem_limit_bytes=16 * 2**20),
        cost_estimate=SMALL_COST,
        name="stack_rows",
    )(values, swap_core(values))


def swap_group(values, bit):
    return lax.ppermute(values, "fsdp", [(i, i ^ bit) for i in range(8)])


def order_kernel(count, *refs):
    pieces, full_ref, held, arrived, sent = refs[:count], refs[count], *refs[-3:]
    group = lax.axis_index("fsdp")
    rows = full_ref.shape[0] // count
    loads = [
        pltpu.make_async_copy(piece, held.at[relative], arrived.at[relative])
        for relative, piece in enumerate(pieces)
    ]
    for load in loads:
        load.start()
    stores = []
    for relative in range(count):
        start = pl.multiple_of((group ^ relative) * rows, rows)
        store = pltpu.make_async_copy(
            held.at[relative, pl.ds(0, rows)], full_ref.at[pl.ds(start, rows)], sent.at[relative]
        )
        loads[relative].wait()
        store.start()
        stores.append(store)
    if len(refs) > count + 4:
        own_width, core = 128, lax.rem(lax.axis_index("seq"), 2)
        wide_ref, bias_ref = refs[count + 1], refs[count + 2]
        for relative in range(count):
            place = group ^ relative
            columns = pl.ds(pl.multiple_of(place * own_width, own_width), own_width)
            extra = held[relative, rows : rows + 8, :].astype(F32)
            lines = [
                extra[k : k + 1, own_width * n : own_width * (n + 1)]
                for k in range(2)
                for n in range(6)
            ]
            for n in range(8):
                wide_ref[n : n + 1, columns] = lines[n]
            for n in range(2):
                start = pl.multiple_of((place * 2 + n) * own_width, own_width)
                bias_ref[:, pl.ds(start, own_width)] = jnp.where(
                    core == 0, lines[8 + n], lines[10 + n]
                )
    for store in stores:
        store.wait()


def in_order(pieces, rows, with_vectors=False):
    count, columns = len(pieces), pieces[0].shape[1]
    out_specs = [pl.BlockSpec(memory_space=pl.ANY)]
    out_shape = [jax.ShapeDtypeStruct((count * rows, columns), pieces[0].dtype)]
    if with_vectors:
        out_specs += [pl.BlockSpec(memory_space=pltpu.VMEM)] * 2
        out_shape += [jax.ShapeDtypeStruct((8, 1024), F32), jax.ShapeDtypeStruct((1, 2048), F32)]
    result = pl.pallas_call(
        partial(order_kernel, count),
        in_specs=[pl.BlockSpec(memory_space=pl.ANY)] * count,
        out_specs=out_specs,
        out_shape=out_shape,
        scratch_shapes=[
            pltpu.VMEM((count,) + pieces[0].shape, pieces[0].dtype),
            pltpu.SemaphoreType.DMA((count,)),
            pltpu.SemaphoreType.DMA((count,)),
        ],
        compiler_params=pltpu.CompilerParams(vmem_limit_bytes=16 * 2**20),
        cost_estimate=SMALL_COST,
        name="in_order",
    )(*pieces)
    return result if with_vectors else result[0]


def own_kernel(qkv_ref, out_ref, *refs):
    vector_refs, (first_ref, second_ref) = refs[:-2], refs[-2:]
    core = lax.rem(lax.axis_index("seq"), 2)
    rows = qkv_ref.shape[0]
    for n in range(3):
        for pair in range(4):
            block_ref = second_ref if pair >= 2 else first_ref
            start = pl.multiple_of((8 * n + pair + 4 * core) * PAIR, PAIR)
            target = (3 * (pair % 2) + n) * PAIR
            block_ref[:rows, target : target + PAIR] = qkv_ref[:, pl.ds(start, PAIR)]
    out_half = out_ref.shape[1] // 2
    start = pl.multiple_of(core * out_half, out_half)
    second_ref[:, 6 * PAIR :] = out_ref[:, pl.ds(start, out_half)]
    lines = []
    for ref in vector_refs:
        vector = ref[...].astype(F32).reshape(ref.shape[0] // PAIR, PAIR)
        lines += [vector[n : n + 1] for n in range(ref.shape[0] // PAIR)]
    row = lax.broadcasted_iota(jnp.int32, (8, PAIR), 0)
    for n in range(6):
        block = jnp.where(row == 0, lines[n], jnp.where(row == 1, lines[n + 6], 0.0))
        first_ref[rows:, PAIR * n : PAIR * (n + 1)] = block.astype(BF16)


def own_qkv_blocks(qkv_weight, out_weight, vectors):
    rows, columns = qkv_weight.shape[0], qkv_weight.shape[1] // 4
    out_half = out_weight.shape[1] // 2
    return pl.pallas_call(
        own_kernel,
        in_specs=[pl.BlockSpec(memory_space=pltpu.VMEM)] * (2 + len(vectors)),
        out_specs=[pl.BlockSpec(memory_space=pltpu.VMEM)] * 2,
        out_shape=[
            jax.ShapeDtypeStruct((rows + 8, columns), BF16),
            jax.ShapeDtypeStruct((rows, columns + out_half), BF16),
        ],
        cost_estimate=SMALL_COST,
        name="own_qkv",
    )(qkv_weight, out_weight, *vectors)


def own_rest_kernel(fc1_ref, fc2_ref, first_ref, second_ref):
    core = lax.rem(lax.axis_index("seq"), 2)
    rows = second_ref.shape[0]
    for n in range(fc1_ref.shape[1] // (2 * rows)):
        start = pl.multiple_of((2 * n + core) * rows, rows)
        first_ref[:, n * rows : (n + 1) * rows] = fc1_ref[:, pl.ds(start, rows)]
    second_ref[...] = fc2_ref[pl.ds(pl.multiple_of(core * rows, rows), rows), :]


def own_rest_blocks(fc1_weight, fc2_weight):
    return pl.pallas_call(
        own_rest_kernel,
        in_specs=[pl.BlockSpec(memory_space=pltpu.VMEM)] * 2,
        out_specs=[pl.BlockSpec(memory_space=pltpu.VMEM)] * 2,
        out_shape=[
            jax.ShapeDtypeStruct((fc1_weight.shape[0], fc1_weight.shape[1] // 2), BF16),
            jax.ShapeDtypeStruct((fc2_weight.shape[0] // 2, fc2_weight.shape[1]), BF16),
        ],
        cost_estimate=SMALL_COST,
        name="own_rest",
    )(fc1_weight, fc2_weight)


def after(values, *others):
    return lax.optimization_barrier((values,) + others)[0] if others else values


class Gather:
    SOURCE = {4: 0, 2: 0, 1: 0, 6: 4, 3: 2, 5: 4, 7: 6}
    STEP = {4: 4, 2: 2, 1: 1, 6: 2, 3: 1, 5: 1, 7: 1}

    def __init__(self, own):
        self.pieces = [own] + [None] * 7
        self.grouped = lax.axis_size("fsdp") == 8

    def send(self, *parts, ready=()):
        if not self.grouped:
            return
        sources = [self.pieces[self.SOURCE[part]] for part in parts]
        if ready:
            sources = lax.optimization_barrier(tuple(sources) + tuple(ready))
        for part, source in zip(parts, sources):
            self.pieces[part] = swap_group(source, self.STEP[part])

    def got(self, *parts):
        return tuple(self.pieces[part] for part in parts) if self.grouped else ()

    def result(self):
        if not self.grouped:
            return lax.all_gather(self.pieces[0], "fsdp", axis=0, tiled=True)
        return in_order(self.pieces, self.pieces[0].shape[0])


def add_low(left, right):
    return (left.astype(F32) + right.astype(F32)).astype(BF16)


def split_kernel(full_ref, *refs):
    sems = refs[2]
    group = lax.axis_index("fsdp")
    rows = full_ref.shape[0] // 8
    copies = []
    for n in range(8):
        far, near, side = n % 2, (n // 2) % 2, n // 4
        start = pl.multiple_of((group ^ (4 * far + 2 * near + side)) * rows, rows)
        target = refs[side].at[pl.ds((n % 4) * rows, rows)]
        copies.append(
            pltpu.make_async_copy(full_ref.at[pl.ds(start, rows)], target, sems.at[n])
        )
    for copy in copies:
        copy.start()
    for copy in copies:
        copy.wait()


def split_blocks(values):
    rows, columns = values.shape
    return pl.pallas_call(
        split_kernel,
        in_specs=[pl.BlockSpec(memory_space=pltpu.VMEM)],
        out_specs=[pl.BlockSpec(memory_space=pl.ANY)] * 2,
        out_shape=[jax.ShapeDtypeStruct((rows // 2, columns), values.dtype)] * 2,
        scratch_shapes=[pltpu.SemaphoreType.DMA((8,))],
        compiler_params=pltpu.CompilerParams(vmem_limit_bytes=16 * 2**20),
        cost_estimate=SMALL_COST,
        name="split_blocks",
    )(values)


def pack_kernel(
    one_ref, two_ref, grads_ref, hidden_ref, end_ref, middle_ref, *refs
):
    sum_refs, packed_ref = refs[:4], refs[4]
    group = lax.axis_index("fsdp")
    core = lax.rem(lax.axis_index("seq"), 2)
    squares = jnp.zeros((4, PAIR), F32)
    for n in range(end_ref.shape[1] // PAIR):
        span = slice(n * PAIR, (n + 1) * PAIR)
        end, middle = end_ref[:, span], middle_ref[:, span]
        squares = squares + jnp.concatenate([end[:1], middle[:1], end[1:], middle[1:]], axis=0)
    for n in range(8):
        far, near, side = n % 2, (n // 2) % 2, n // 4
        target = group ^ (4 * far + 2 * near + side)
        columns = pl.ds(pl.multiple_of(target * PAIR, PAIR), PAIR)
        mine = (target // 4) == core
        pair = lax.rem(target, 4)
        head_sums = jnp.zeros((2, PAIR), F32)
        for k in range(4):
            head_sums = jnp.where(jnp.logical_and(mine, pair == k), sum_refs[k][...], head_sums)
        one, two = one_ref[:, columns], two_ref[:, columns]
        hidden = [
            hidden_ref[:, pl.ds(pl.multiple_of(target * 2 * PAIR + k * PAIR, PAIR), PAIR)]
            for k in range(2)
        ]
        empty = jnp.zeros((1, PAIR), F32)
        rows = [one[:2], head_sums, two[2:3], two[:2], grads_ref[:, columns]]
        rows += [jnp.where(core == 0, part, empty) for part in hidden]
        rows += [jnp.where(core == 0, empty, part) for part in hidden]
        rows.append(squares)
        packed_ref[16 * n : 16 * (n + 1), :] = jnp.concatenate(rows, axis=0).astype(BF16)


def pack_lines(lines, sums):
    return pl.pallas_call(
        pack_kernel,
        in_specs=[pl.BlockSpec(memory_space=pltpu.VMEM)] * 10,
        out_specs=pl.BlockSpec(memory_space=pltpu.VMEM),
        out_shape=jax.ShapeDtypeStruct((128, PAIR), BF16),
        cost_estimate=SMALL_COST,
        name="pack_lines",
    )(*lines, *sums)


class Scatter:
    def __init__(self, values, *ready, halves=None, ordered=False):
        self.grouped = lax.axis_size("fsdp") == 8
        self.halved = halves is not None
        values = values.astype(BF16)
        if self.halved:
            self.kept, self.sent = halves
            self.crossed = swap_chip(self.sent)
        elif self.grouped:
            middle = values.shape[0] // 2
            split = (values[:middle], values[middle:]) if ordered else split_blocks(values)
            self.keep, self.side_send = split
            self.side = swap_group(after(self.side_send, *ready), 1)
        else:
            self.sums = lax.psum_scatter(values, "fsdp", scatter_dimension=0, tiled=True)

    def cross(self, *ready):
        values = add_low(self.kept, after(self.crossed, *ready))
        if self.grouped:
            self.keep, self.side_send = split_blocks(values)
            self.side = swap_group(self.side_send, 1)
        else:
            self.sums = lax.psum_scatter(values, "fsdp", scatter_dimension=0, tiled=True)

    def got(self, *names):
        return tuple(getattr(self, name) for name in names if hasattr(self, name))

    def step(self, name, next_name, bit, ready):
        if self.grouped:
            received = after(getattr(self, name), *ready)
            half = self.keep.shape[0] // 2
            send = add_low(self.keep[half:], received[half:])
            self.keep = add_low(self.keep[:half], received[:half])
            setattr(self, next_name, swap_group(send, bit))

    def near(self, *ready):
        self.step("side", "near_sums", 2, ready)

    def far(self, *ready):
        self.step("near_sums", "far_sums", 4, ready)

    def chips(self, *ready):
        if self.grouped:
            self.sums = add_low(self.keep, after(self.far_sums, *ready))
        self.other_chip = swap_chip(self.sums)

    def cores(self, *ready):
        other_chip = after(self.other_chip, *ready)
        if self.halved:
            chip = lax.axis_index("seq") // 2
            first = jnp.where(chip == 0, self.sums, other_chip)
            second = jnp.where(chip == 0, other_chip, self.sums)
            self.total = jnp.concatenate([first, second], axis=1)
        else:
            self.total = add_low(self.sums, other_chip)
        self.other_core = swap_core(self.total)

    def last(self):
        if not self.grouped:
            return self.sums.astype(F32)
        return self.keep.astype(F32) + self.far_sums.astype(F32)


def take(values, index):
    return lax.dynamic_index_in_dim(values, index, 0, keepdims=False)


def in_core_order(own, other, core, axis):
    first = jnp.where(core == 0, own, other)
    second = jnp.where(core == 0, other, own)
    return first, second


def body(
    inputs,
    cotangent,
    valid,
    ln1_gain,
    ln1_bias,
    qkv_weight,
    q_bias,
    v_bias,
    out_weight,
    out_bias,
    ln2_gain,
    ln2_bias,
    fc1_weight,
    fc1_bias,
    fc2_weight,
    fc2_bias,
):
    clips, rows, width = inputs.shape
    groups = lax.axis_size("fsdp")
    place = lax.axis_index("seq")
    group = lax.axis_index("fsdp")
    chip, core = place // 2, place % 2
    half = width // 2
    hidden_rows = fc2_weight.shape[0]
    half_rows = hidden_rows // 2
    own_rows = clips * rows
    scale_factor = HEAD ** (-0.5)

    def all_clips(values, back):
        mine = values[:rows]
        first = jnp.where(chip == 0, mine, back)
        second = jnp.where(chip == 0, back, mine)
        return jnp.stack([first, second])

    own_width = width // groups
    vectors = (ln1_gain, ln1_bias, q_bias, v_bias, out_bias, ln2_gain, ln2_bias, fc2_bias, fc1_bias)
    quarter = half // 2
    row_width = 3 * quarter
    used = 8 * own_width + fc1_bias.shape[0]
    if groups == 8:
        own_first, own_second = own_qkv_blocks(qkv_weight, out_weight, vectors)
    else:
        by_head = qkv_weight.reshape(own_width, 3, 2, 2, 2, PAIR)
        by_head = lax.dynamic_index_in_dim(by_head, core, 2, keepdims=False)
        by_head = by_head.transpose(0, 2, 3, 1, 4).reshape(own_width, 2, row_width)
        out_columns = lax.dynamic_slice_in_dim(out_weight, core * half, half, 1)
        own_first = by_head[:, 0]
        own_second = jnp.concatenate([by_head[:, 1], out_columns], axis=1)

    qkv_a, qkv_b = Gather(own_first), Gather(own_second)
    qkv_a.send(4, 2, 1)
    other_inputs = swap_chip(take(after(inputs, *qkv_a.got(4, 2, 1)), 1 - chip))
    qkv_a.send(6, 3, 5, ready=qkv_a.got(4, 2, 1))
    qkv_b.send(4, ready=qkv_a.got(4, 2, 1))
    fc1_weight, fc2_weight = after((fc1_weight, fc2_weight), own_first)
    if groups == 8:
        own_fc1, own_fc2 = own_rest_blocks(fc1_weight, fc2_weight)
    else:
        own_fc1 = lax.dynamic_index_in_dim(
            fc1_weight.reshape(own_width, groups, 2, half_rows), core, 2, keepdims=False
        ).reshape(own_width, groups * half_rows)
        own_fc2 = lax.dynamic_slice_in_dim(fc2_weight, core * half_rows, half_rows, 0)
    full_fc1 = lax.all_gather(own_fc1, "fsdp", axis=0, tiled=True)
    full_fc2 = lax.all_gather(own_fc2, "fsdp", axis=0, tiled=True)
    qkv_a.send(7, ready=qkv_a.got(6, 3, 5))
    other_inputs = after(other_inputs, own_fc1, *qkv_a.got(6, 3, 5))
    qkv_b.send(2, 1, ready=qkv_a.got(6, 3, 5))
    own_inputs = jnp.concatenate([take(inputs, chip), other_inputs], axis=0)
    all_inputs = with_partner(own_inputs)
    if groups == 8:
        qkv_first, wide, bias_fc1 = in_order(qkv_a.pieces, own_width, True)
    else:
        qkv_first = qkv_a.result()
        packed = lax.all_gather(jnp.concatenate(vectors), "fsdp", axis=0)
        wide = [
            packed[:, i * own_width : (i + 1) * own_width].reshape(width).astype(F32)
            for i in range(8)
        ]
        bias_fc1 = packed[:, 8 * own_width : used].reshape(groups, 2, half_rows)
        bias_fc1 = take(jnp.moveaxis(bias_fc1, 1, 0), core)
        bias_fc1 = bias_fc1.reshape(groups * half_rows).astype(F32)
    gain_one, bias_one, bias_q, bias_v, bias_out, gain_two, bias_two, bias_fc2 = [
        wide[i] for i in range(8)
    ]
    bias_q = take(bias_q.reshape(2, 2, 2, PAIR), core)
    bias_v = take(bias_v.reshape(2, 2, 2, PAIR), core)
    bias_mixed = jnp.stack([bias_q, jnp.zeros_like(bias_q), bias_v], axis=2).reshape(2, row_width)
    scale_mixed = jnp.array([scale_factor, 1.0, 1.0] * 2, F32).repeat(PAIR)
    clip_valid = take(valid, chip).reshape(2 * clips, rows)
    own_valid = jnp.concatenate([take(clip_valid, place), take(clip_valid, place ^ 2)])
    other_valid = jnp.concatenate([take(clip_valid, place ^ 1), take(clip_valid, place ^ 3)])
    key_valid = jnp.concatenate([own_valid, other_valid])
    lane = jnp.arange(PAIR) % HEAD
    key_mask = jnp.where(key_valid > 0, 0.0, MASKED)[:, None]
    key_base = jnp.where(lane == 0, key_mask, jnp.where(lane < 4, 1.0, 0.0)).astype(BF16)


    def project(weight, i):
        return ((dot(h_one, weight) + bias_mixed[i]) * scale_mixed).astype(BF16)

    h_one = rows_call(
        first_kernel, [all_inputs], [gain_one[None], bias_one[None]], [BF16], 0, "first_norm"
    )[0]
    mixed = [project(qkv_first, 0)]
    context, queries = [], []

    def attend_pair(pair, *ready):
        before = context[-1] if context else None
        base = after(key_base, *ready)
        results = attend(mixed[pair // 2], base, pair % 2, before, pair, 4)
        context.append(results[0])
        queries.append(results[1])

    ready = (h_one,) + qkv_b.got(4, 2, 1)
    qkv_b.send(6, 3, 5, ready=ready)
    attend_pair(0, *ready)
    ready = (queries[0],) + qkv_b.got(6, 3, 5)
    qkv_b.send(7, ready=ready)
    other_grads = swap_chip(after(take(cotangent, 1 - chip), *ready))
    attend_pair(1, *ready)
    second_columns = qkv_b.result()
    mixed.append(project(second_columns[:, :row_width], 1))
    ready = (queries[1], mixed[1], other_grads)
    kept = lax.dynamic_slice(second_columns, (core * half, row_width), (half, half))
    received = lax.dynamic_slice(second_columns, ((1 - core) * half, row_width), (half, half))
    received = swap_core(after(received, mixed[1]))
    attend_pair(2, kept, *ready)
    ready = (queries[2], received)
    attend_pair(3, *ready)
    own_grads = jnp.concatenate([take(cotangent, chip), after(other_grads, queries[3])], axis=0)
    full_out = jnp.concatenate(in_core_order(kept, received, core, 1), axis=1)
    all_context = context[3]
    own_part, other_part = both_halves_product([(all_context, full_out)], NN)
    ready = (own_grads, own_part)
    counted = own_valid.astype(F32)[:, None]
    residual_mid, h_two, middle_sums = rows_call(
        middle_kernel,
        [own_part, after(other_part, *ready), own_inputs, counted],
        [bias_out[None], gain_two[None], bias_two[None]],
        [F32, BF16],
        2,
        "middle",
    )
    h_two = with_partner(h_two)
    all_grads = with_partner(after(own_grads, residual_mid))
    grad_sums = column_sum(own_grads)
    h_two = after(h_two, grad_sums)
    active, slope = gelu_both(dot(h_two, full_fc1) + bias_fc1)
    active, slope = active.astype(BF16), slope.astype(BF16)
    active = after(active, full_fc2)
    fc2_product = dot(active, all_grads, TN).astype(BF16)
    fc2_scatter = Scatter(fc2_product)

    late_grads = after(all_grads, *fc2_scatter.got("keep"))
    grad_hidden, hidden_sums = hidden_gradient(late_grads, full_fc2, slope)
    fc1_halves = weight_halves(h_two, grad_hidden)
    fc1_scatter = Scatter(fc1_halves[0], halves=fc1_halves)
    own_part, other_part = both_halves_product(
        [(after(grad_hidden, fc1_scatter.sent), full_fc1)], NT
    )
    grad_residual, own_grad_attn, two_sums = rows_call(
        norm_back_kernel,
        [own_part, other_part, residual_mid, own_grads],
        [gain_two[None]],
        [F32, BF16],
        3,
        "norm_back",
    )
    grad_attn = with_partner(own_grad_attn)
    grad_context = half_product([(grad_attn, full_out)], NT, None, BF16)
    halves, sums = [None, None], []

    def back_pair(pair, *ready):
        grad_mixed, parts = attend_back(
            queries[pair],
            mixed[pair // 2],
            grad_context,
            all_context,
            after(key_base, *ready),
            pair % 2,
            pair,
            halves[pair // 2],
        )
        halves[pair // 2] = grad_mixed
        sums.append(parts)

    back_pair(0, grad_context)
    own_mlp, other_mlp = both_halves_product([(after(active, sums[0]), full_fc2)], NN)
    low_output, end_sums = rows_call(
        end_kernel,
        [own_mlp, other_mlp, residual_mid, counted],
        [bias_fc2[None]],
        [BF16],
        2,
        "end",
    )
    ready = (low_output, fc1_scatter.crossed) + fc2_scatter.got("side")
    output_back = swap_chip(after(low_output, *ready)[rows:])
    grad_out = dot(all_context, after(grad_attn, *ready), TN).astype(BF16)
    kept = lax.dynamic_slice_in_dim(grad_out, core * half, half, 1)
    received = swap_core(lax.dynamic_slice_in_dim(grad_out, (1 - core) * half, half, 1))
    fc2_scatter.near(*ready)
    fc1_scatter.cross(*ready)
    back_pair(1, kept, *ready, *fc2_scatter.got("keep"), *fc1_scatter.got("keep"))
    received = after(received, sums[1])
    grad_out = jnp.concatenate(in_core_order(kept, received, core, 0), axis=0)
    early = jnp.concatenate([dot(h_one, halves[0], TN).astype(BF16), grad_out], axis=1)
    ready = (sums[1], output_back) + fc2_scatter.got("near_sums") + fc1_scatter.got("side")
    fc2_scatter.far(*ready)
    fc1_scatter.near(*ready)
    early_scatter = Scatter(early, *ready)
    ready += fc2_scatter.got("keep") + fc1_scatter.got("keep") + early_scatter.got("keep")
    back_pair(2, *ready)
    ready = (sums[2],) + fc1_scatter.got("near_sums") + fc2_scatter.got("far_sums")
    ready += early_scatter.got("side")
    fc1_scatter.far(*ready)
    early_scatter.near(*ready)
    ready += fc1_scatter.got("keep") + early_scatter.got("keep")
    back_pair(3, *ready)
    ready = (sums[3],) + fc1_scatter.got("far_sums")
    ready += early_scatter.got("near_sums")
    early_scatter.far(*ready)
    fc2_scatter.chips(*ready)
    fc1_scatter.chips(*ready)
    late_scatter = Scatter(dot(after(h_one, *ready), halves[1], TN))
    gm_first, gm_second = after(tuple(halves), *late_scatter.got("keep"))
    own_one, other_one = both_halves_product(
        [(gm_first, qkv_first), (gm_second, second_columns)], NT
    )
    low_input_grad, one_sums = rows_call(
        norm_back_kernel,
        [own_one, other_one, own_inputs, grad_residual],
        [gain_one[None]],
        [BF16],
        3,
        "norm_back",
    )
    ready = late_scatter.got("side") + (low_input_grad,)
    late_scatter.near(*ready)
    one_sums = after(one_sums, *ready)

    if groups == 8:
        packed = pack_lines(
            [one_sums, two_sums, grad_sums[None], hidden_sums, end_sums, middle_sums], sums
        )
    else:
        lines = [one_sums[0], one_sums[1], two_sums[2], two_sums[0], two_sums[1], grad_sums]
        lines.append(hidden_sums[0])
        squares = [end_sums[0], middle_sums[0], end_sums[1], middle_sums[1]]
        squares = [jnp.sum(line.reshape(-1, PAIR), axis=0) for line in squares]

        def by_core(values):
            full = jnp.zeros((2, values.shape[0]), F32)
            return lax.dynamic_update_index_in_dim(full, values, core, 0).reshape(-1)

        wide = lines[:2] + [by_core(jnp.concatenate([part[n] for part in sums])) for n in range(2)]
        wide = [line.reshape(groups, own_width) for line in wide + lines[2:6]]
        all_sums = jnp.zeros((groups, 2, half_rows), F32)
        all_sums = lax.dynamic_update_index_in_dim(
            all_sums, lines[6].reshape(groups, half_rows), core, 1
        )
        wide.append(all_sums.reshape(groups, hidden_rows))
        wide.append(jnp.zeros((groups, 12 * PAIR - used)))
        wide.append(jnp.broadcast_to(jnp.concatenate(squares), (groups, 4 * PAIR)))
        packed = jnp.concatenate(wide, axis=1).astype(BF16).reshape(groups * 16, PAIR)
    ready = early_scatter.got("far_sums") + (fc1_scatter.other_chip, fc2_scatter.other_chip)
    packed = add_low(packed, after(swap_chip(packed), *ready))
    early_scatter.chips(packed)
    input_back = swap_chip(after(low_input_grad, early_scatter.sums)[rows:])
    fc1_scatter.cores(packed)
    fc2_scatter.cores(packed)
    ready = late_scatter.got("near_sums")
    packed = add_low(packed, after(swap_core(packed), *ready))
    late_scatter.far(packed)
    vector_scatter = Scatter(packed, ordered=True)
    vector_scatter.near(early_scatter.other_chip)
    early_scatter.cores(*vector_scatter.got("keep"))
    late_scatter.chips(*vector_scatter.got("keep"))
    vector_scatter.far(late_scatter.sums)
    input_back = after(input_back, late_scatter.other_chip)
    late_scatter.cores()
    ready_last = (packed,)
    output = all_clips(low_output, after(output_back, packed))
    input_grad = all_clips(low_input_grad, input_back)

    def in_columns(values, other, blocks):
        size = values.shape[1] // blocks
        parts = in_core_order(values, other, core, 0)
        parts = [part.reshape(own_width, blocks, 1, size) for part in parts]
        return jnp.concatenate(parts, axis=2).reshape(own_width, -1).astype(F32)

    fc2_parts = after((fc2_scatter.total, fc2_scatter.other_core), *ready_last)
    fc2_grad = in_core_order(*fc2_parts, core, 0)
    fc2_grad = jnp.concatenate(fc2_grad, axis=0).astype(F32)
    early_parts = [early_scatter.total, early_scatter.other_core]
    late_parts = [late_scatter.total, late_scatter.other_core]
    fc1_parts = after((fc1_scatter.total, fc1_scatter.other_core), *ready_last)
    if groups == 8:
        fc1_places = [
            (0, n * half_rows, half_rows, 2 * n * half_rows, (2 * n + 1) * half_rows)
            for n in range(groups)
        ]
        fc1_grad = join_columns(fc1_parts, fc1_places, 2 * groups * half_rows)
        out_grad = join_columns(early_parts, [(0, row_width, half, 0, half)], width)
        qkv_places = []
        for n in range(3):
            for pair in range(4):
                target = n * width + pair * PAIR
                start = (3 * (pair % 2) + n) * PAIR
                qkv_places.append((pair // 2, start, PAIR, target, target + half))
        qkv_grad = join_columns(early_parts + late_parts, qkv_places, 3 * width)
    else:
        fc1_grad = in_columns(*fc1_parts, groups)
        out_grad = in_columns(*[part[:, row_width:] for part in early_parts], 1)

        def both_halves(left, right):
            left = left[:, :row_width].reshape(own_width, 1, 2, 3, PAIR)
            right = right.reshape(own_width, 1, 2, 3, PAIR)
            both = jnp.concatenate([left, right], axis=1).transpose(0, 3, 1, 2, 4)
            return both.reshape(own_width, 3 * half)

        qkv_grad = in_columns(*[both_halves(*pair) for pair in zip(early_parts, late_parts)], 3)
    lines = vector_scatter.last()
    flat = lines[:12].reshape(-1)
    own_vectors = [flat[i * own_width : (i + 1) * own_width] for i in range(8)]
    own_hidden = flat[8 * own_width : used]
    totals = jnp.sum(lines[12:], axis=1)
    branch_rms = jnp.sqrt(totals[:3] / totals[3])
    return (
        output,
        input_grad,
        own_vectors[0],
        own_vectors[1],
        qkv_grad,
        own_vectors[2],
        own_vectors[3],
        out_grad,
        own_vectors[4],
        own_vectors[5],
        own_vectors[6],
        fc1_grad,
        own_hidden,
        fc2_grad,
        own_vectors[7],
        branch_rms,
    )


def solution(mesh):
    tokens, rows, vector = P("fsdp", "seq", None), P("fsdp", None), P("fsdp")
    return jax.shard_map(
        body,
        mesh=mesh,
        in_specs=(
            tokens,
            tokens,
            rows,
            vector,
            vector,
            rows,
            vector,
            vector,
            rows,
            vector,
            vector,
            vector,
            rows,
            vector,
            rows,
            vector,
        ),
        out_specs=(
            tokens,
            tokens,
            vector,
            vector,
            rows,
            vector,
            vector,
            rows,
            vector,
            vector,
            vector,
            rows,
            vector,
            rows,
            vector,
            P(),
        ),
        check_vma=False,
    )
```
